32 devices in a mesh: dp: 4 (over x, core), mp: 8 (over z, y).
Axes of the slice: x: 2, y: 2, z: 4, core: 2. Of those that a mesh axis runs over, the one named last changes fastest.
Arguments:
- fast_in: bfloat16 [128, 8, 4, 256], P(None, 'mp', 'dp'), may hold values from -6 to 6
- slow_in: bfloat16 [1024, 2, 4, 256], P('mp', None, 'dp'), may hold values from -6 to 6
- fast_cot: bfloat16 [128, 8, 4, 256], P(None, 'mp', 'dp'), may hold values from -6 to 6
- slow_cot: bfloat16 [1024, 2, 4, 256], P('mp', None, 'dp'), may hold values from -6 to 6
- crop_tiles: int32 [4], P('dp'), may hold values from 10 to 16, as said below
- owner: int32 [7591], replicated, may hold values from 0 to 31, as said below
- master: float32 [15232, 128], P(('dp', 'mp')), as said below
- moment_one: float32 [15232, 128], P(('dp', 'mp')), as said below
- moment_two: float32 [15232, 128], P(('dp', 'mp')), as said below
Outputs:
- fast_out: float32 [128, 8, 4, 256], P(None, 'mp', 'dp')
- slow_out: float32 [1024, 2, 4, 256], P('mp', None, 'dp')
- fast_grad: float32 [128, 8, 4, 256], P(None, 'mp', 'dp')
- slow_grad: float32 [1024, 2, 4, 256], P('mp', None, 'dp')
- new_master: float32 [15232, 128], P(('dp', 'mp'))
- new_moment_one: float32 [15232, 128], P(('dp', 'mp'))
- new_moment_two: float32 [15232, 128], P(('dp', 'mp'))
- new_weights: bfloat16 [15232, 128], P(('dp', 'mp'))
The draws below stay inside these ranges and needn't reach their ends.
Inputs may be any that keep to these rules, and one draw needn't show every extreme that they name: `crop_tiles`: each value is 10, 14 or 16. `owner`: blocks of 128 flattened parameters; each device owns one contiguous run of 1 to 476 blocks, one device exactly 476; runs follow a drawn order of devices. `master`: row j of device d's 476 rows holds the j-th block d owns; other rows are ignored. `moment_one`: rows laid out as master's. `moment_two`: positive; rows laid out as master's.
All inputs are finite; a program needn't handle non-finite values.
Results may differ from the reference program's by a relative error of at most 0.012.
The reference program's roundings to bfloat16 on the way count: a program that leaves them out, or rounds other values in their place, can miss the bound.
Values may be sent and summed in bfloat16 or wider, within the bound.
A program may use at most 128 MiB of HBM per device.

```python
import math
import jax
import jax.numpy as jnp
from jax import lax

C_FAST = 128
B_FAST = 32
C_SLOW = 1024
B_SLOW = 256
C_LAT = 256
TILE = 16
BLK = 128
STEP = 10
POS = 256
CLIPS = 4
T_FAST = 8
T_SLOW = 2
PARAMS = 971648
NBLK = 7591
SLOTS = 476
DEVICES = 32


def segment_list_drawn():
    mats = [('fast_one', (B_FAST, 3 * C_FAST)), ('fast_two', (B_FAST, B_FAST)), ('fast_three', (C_FAST, B_FAST)), ('lateral', (C_LAT, 5 * C_FAST)), ('slow_one', (B_SLOW, C_SLOW + C_LAT)), ('slow_two', (B_SLOW, 3 * B_SLOW)), ('slow_three', (C_SLOW, B_SLOW))]
    norms = []
    for label, width in (('fast_one', B_FAST), ('fast_two', B_FAST), ('fast_three', C_FAST), ('lateral', C_LAT), ('slow_one', B_SLOW), ('slow_two', B_SLOW), ('slow_three', C_SLOW)):
        norms.append(('gain_' + label, (width,)))
        norms.append(('bias_' + label, (width,)))
    return mats + norms


def owner_plan(key):
    key_order, key_weight = jax.random.split(key)
    order = jax.random.permutation(key_order, DEVICES).astype(jnp.int32)
    weight = jax.random.randint(key_weight, (DEVICES,), 2, 4)
    weight = jnp.where(jnp.arange(DEVICES) == 0, 0, weight)
    running = jnp.cumsum(weight)
    ends = SLOTS + (NBLK - SLOTS) * running // running[DEVICES - 1]
    counts = ends - jnp.concatenate([jnp.zeros((1,), ends.dtype), ends[:-1]])
    blocks = jnp.arange(NBLK)
    which = jnp.sum((blocks[:, None] >= ends[None, :]).astype(jnp.int32), axis=1)
    owner = order[which]
    rank = jnp.argsort(order)
    starts = ends - counts
    slot = jnp.arange(SLOTS)
    ids = starts[rank][:, None] + slot[None, :]
    living = slot[None, :] < counts[rank][:, None]
    return (owner.astype(jnp.int32), jnp.where(living, ids, -1).reshape(-1))


def segment_table(element):
    spread = jnp.ones(element.shape, jnp.float32)
    grad = jnp.ones(element.shape, jnp.float32)
    kind = jnp.zeros(element.shape, jnp.int32)
    offset = 0
    for label, shape in segment_list_drawn():
        size = math.prod(shape)
        inside = (element >= offset) & (element < offset + size)
        frames = T_FAST if 'fast' in label else T_SLOW
        grad = jnp.where(inside, 0.3 * math.sqrt(0.5 * CLIPS * frames * POS), grad)
        if len(shape) == 2:
            spread = jnp.where(inside, 1.0 / math.sqrt(shape[1]), spread)
        elif label[:4] == 'gain':
            kind = jnp.where(inside, 1, kind)
        else:
            spread = jnp.where(inside, 0.3, spread)
        offset += size
    return (spread, grad, kind)


def packed_elements(key):
    owner, ids = owner_plan(key)
    return ids[:, None] * BLK + jnp.arange(BLK)[None, :]


def draw_owner(key, part):
    owner, ids = owner_plan(key)
    return owner


def draw_master(key, part):
    element = packed_elements(key)
    key = jax.random.fold_in(key, 2)
    spread, grad, kind = segment_table(element)
    noise = jax.random.normal(key, element.shape, jnp.float32)
    gain = 1.0 + 0.4 * jax.random.uniform(jax.random.fold_in(key, 7), element.shape, jnp.float32, -1.0, 1.0)
    return jnp.where(kind == 1, gain, spread * noise)


def draw_moment_one(key, part):
    element = packed_elements(key)
    key = jax.random.fold_in(key, 3)
    spread, grad, kind = segment_table(element)
    noise = jax.random.normal(key, element.shape, jnp.float32)
    return grad * noise


def draw_moment_two(key, part):
    element = packed_elements(key)
    key = jax.random.fold_in(key, 4)
    spread, grad, kind = segment_table(element)
    factor = jnp.exp(jax.random.uniform(key, element.shape, jnp.float32, 0.0, math.log(4.0)))
    return grad * grad * factor


def draw_crop_tiles(key, part):
    key = jax.random.fold_in(key, 5)
    key_level, key_top, key_low = jax.random.split(key, 3)
    level = jax.random.randint(key_level, (CLIPS,), 0, 3)
    top = jax.random.randint(key_top, (), 0, CLIPS)
    bottom = (top + 1 + jax.random.randint(key_low, (), 0, CLIPS - 1)) % CLIPS
    clip = jnp.arange(CLIPS)
    level = jnp.where(clip == top, 2, jnp.where(clip == bottom, 0, level))
    sides = jnp.array([10 * TILE // 16, 14 * TILE // 16, TILE], dtype=jnp.int32)
    return sides[level].astype(jnp.int32)


def block_levels(stream_key, extent, cuts, least, largest):
    def one(dim, blocks):
        steps = jax.random.uniform(jax.random.fold_in(jax.random.fold_in(stream_key, 6), dim), (blocks,), jnp.float32, least / len(cuts), largest / len(cuts))
        return jnp.repeat(jnp.exp(steps), extent[dim] // blocks).reshape((-1,) + (1,) * (len(extent) - dim - 1))

    factor_of = one(*cuts[0])
    for cut in cuts[1:]:
        factor_of = factor_of * one(*cut)
    return factor_of


def gaussian(own_key, dims, scale, reach, cuts=(), held_as=jnp.bfloat16):
    level = block_levels(own_key, dims, cuts, -0.22, 0.18) if cuts else 1.0
    values = jax.random.normal(own_key, dims, jnp.float32) * scale * level
    return jnp.minimum(jnp.maximum(values, -reach), reach).astype(held_as)


def setup_inputs(seed: int = 0) -> dict:
    seeds = jax.random.split(jax.random.key(seed), 10)
    return {
        "fast_in": gaussian(seeds[0], (C_FAST, T_FAST, CLIPS, POS), 1.0, 6.0, ((1, 8), (2, 4))),
        "slow_in": gaussian(seeds[1], (C_SLOW, T_SLOW, CLIPS, POS), 1.0, 6.0, ((0, 8), (2, 4))),
        "fast_cot": gaussian(seeds[2], (C_FAST, T_FAST, CLIPS, POS), 1.0, 6.0, ((1, 8), (2, 4))),
        "slow_cot": gaussian(seeds[3], (C_SLOW, T_SLOW, CLIPS, POS), 1.0, 6.0, ((0, 8), (2, 4))),
        "crop_tiles": draw_crop_tiles(jax.random.fold_in(seeds[9], 71), 0),
        "owner": draw_owner(jax.random.fold_in(seeds[9], 71), 0),
        "master": draw_master(jax.random.fold_in(seeds[9], 71), 0),
        "moment_one": draw_moment_one(jax.random.fold_in(seeds[9], 71), 0),
        "moment_two": draw_moment_two(jax.random.fold_in(seeds[9], 71), 0),
    }


norm_eps = 1e-05
beta_first = 0.5
beta_second = 0.5
adam_eps = 1e-08
decay_rate = 0.05
highest = lax.Precision.HIGHEST

@jax.custom_vjp
def low(v):
    return lax.optimization_barrier(v.astype(jnp.bfloat16)).astype(jnp.float32)

@jax.custom_vjp
def low_back(v):
    return v

def low_keep(v):
    return (low(v), None)

def low_pass(kept, grad):
    return (grad,)

def back_keep(v):
    return (v, None)

def back_low(kept, grad):
    return (low(grad),)
low.defvjp(low_keep, low_pass)
low_back.defvjp(back_keep, back_low)

def segment_list():
    mats = [('fast_one', (B_FAST, 3 * C_FAST)), ('fast_two', (B_FAST, B_FAST)), ('fast_three', (C_FAST, B_FAST)), ('lateral', (C_LAT, 5 * C_FAST)), ('slow_one', (B_SLOW, C_SLOW + C_LAT)), ('slow_two', (B_SLOW, 3 * B_SLOW)), ('slow_three', (C_SLOW, B_SLOW))]
    norms = []
    for label, width in (('fast_one', B_FAST), ('fast_two', B_FAST), ('fast_three', C_FAST), ('lateral', C_LAT), ('slow_one', B_SLOW), ('slow_two', B_SLOW), ('slow_three', C_SLOW)):
        norms.append(('gain_' + label, (width,)))
        norms.append(('bias_' + label, (width,)))
    return mats + norms

def unpack(flat):
    result = {}
    offset = 0
    for label, shape in segment_list():
        size = math.prod(shape)
        result[label] = flat[offset:offset + size].reshape(shape)
        offset += size
    return result

def element_rates(element):
    rate = jnp.zeros(element.shape, jnp.float32)
    decay = jnp.zeros(element.shape, jnp.float32)
    offset = 0
    for label, shape in segment_list():
        size = math.prod(shape)
        inside = (element >= offset) & (element < offset + size)
        if len(shape) == 2:
            rate = jnp.where(inside, 0.5 / math.sqrt(shape[1]), rate)
            decay = jnp.where(inside, decay_rate, decay)
        else:
            rate = jnp.where(inside, 0.2, rate)
        offset += size
    return (rate, decay)

def block_positions(owner, devices, slots):
    onehot = (owner[:, None] == jnp.arange(devices, dtype=jnp.int32)[None, :]).astype(jnp.int32)
    before = jnp.cumsum(onehot, axis=0) - onehot
    return (owner * slots + lax.optimization_barrier(jnp.sum(before * onehot, axis=1))).astype(jnp.int32)

def clip_mask(crop_tiles, times):
    spot = jnp.arange(TILE * TILE, dtype=jnp.int32)
    inside = ((spot // TILE)[None, :] < crop_tiles[:, None]) & ((spot % TILE)[None, :] < crop_tiles[:, None])
    living = (times[:, None] >= 0) & (crop_tiles[None, :] > 0)
    return (living[:, :, None] & inside[None]).astype(jnp.float32)

def adam(weight, grad, first, second, rate, decay):
    first = beta_first * first + (1.0 - beta_first) * grad
    second = beta_second * second + (1.0 - beta_second) * grad * grad
    lift_one = 1.0 - beta_first ** STEP
    lift_two = 1.0 - beta_second ** STEP
    update = first / lift_one / (jnp.sqrt(second / lift_two) + adam_eps)
    return (first, second, weight - rate * (update + decay * weight))

def conv(weight, inputs):
    return jnp.einsum('oc,ctnp->otnp', weight, inputs, precision=highest)

def norm_act(value, mask, gain, bias, extra):
    count = jnp.sum(mask)
    mean = lax.optimization_barrier(jnp.sum(value * mask[None], axis=(1, 2, 3))) / count
    square = lax.optimization_barrier(jnp.sum(value * value * mask[None], axis=(1, 2, 3))) / count
    scale = lax.rsqrt(square - mean * mean + norm_eps)
    normed = (value - mean[:, None, None, None]) * scale[:, None, None, None]
    pre = gain[:, None, None, None] * normed + bias[:, None, None, None] + extra
    return jax.nn.gelu(pre) * mask[None]

def forward(flat, fast_x, slow_x, fast_mask, slow_mask):
    par = unpack(low(flat))
    masked = fast_x * fast_mask[None]
    frames = masked.shape[1]
    slow_frames = slow_x.shape[1]
    padded = jnp.pad(masked, ((0, 0), (2, 2), (0, 0), (0, 0)))
    window = jnp.concatenate([padded[:, tap + 1:tap + 1 + frames] for tap in range(3)], 0)
    first_raw = low_back(conv(par['fast_one'], window))
    first_act = low(norm_act(first_raw, fast_mask, par['gain_fast_one'], par['bias_fast_one'], 0.0))
    second_raw = low_back(conv(par['fast_two'], first_act))
    second_act = low(norm_act(second_raw, fast_mask, par['gain_fast_two'], par['bias_fast_two'], 0.0))
    third_raw = low_back(conv(par['fast_three'], second_act))
    fast_out = norm_act(third_raw, fast_mask, par['gain_fast_three'], par['bias_fast_three'], masked)
    wide = jnp.concatenate([padded[:, tap:tap + 4 * slow_frames:4] for tap in range(5)], 0)
    lateral_raw = low_back(low(conv(par['lateral'], wide)))
    lateral_act = low(norm_act(lateral_raw, slow_mask, par['gain_lateral'], par['bias_lateral'], 0.0))
    slow_masked = slow_x * slow_mask[None]
    joined = jnp.concatenate([slow_masked, lateral_act], 0)
    one_raw = low_back(conv(par['slow_one'], joined))
    one_act = low(norm_act(one_raw, slow_mask, par['gain_slow_one'], par['bias_slow_one'], 0.0))
    spad = jnp.pad(one_act, ((0, 0), (1, 1), (0, 0), (0, 0)))
    slow_window = jnp.concatenate([spad[:, tap:tap + slow_frames] for tap in range(3)], 0)
    two_raw = low_back(conv(par['slow_two'], slow_window))
    two_act = low(norm_act(two_raw, slow_mask, par['gain_slow_two'], par['bias_slow_two'], 0.0))
    three_raw = low_back(conv(par['slow_three'], two_act))
    slow_out = norm_act(three_raw, slow_mask, par['gain_slow_three'], par['bias_slow_three'], slow_masked)
    return (fast_out, slow_out)

def reference(fast_in, slow_in, fast_cot, slow_cot, crop_tiles, owner, master, moment_one, moment_two):
    position = block_positions(owner, DEVICES, SLOTS)
    flat = master[position].reshape(-1)
    fast_mask = clip_mask(crop_tiles, jnp.arange(T_FAST, dtype=jnp.int32))
    slow_mask = clip_mask(crop_tiles, 4 * jnp.arange(T_SLOW, dtype=jnp.int32))

    def run(params, fast_x, slow_x):
        return forward(params, fast_x, slow_x, fast_mask, slow_mask)
    outputs, pull = jax.vjp(run, flat, fast_in.astype(jnp.float32), slow_in.astype(jnp.float32))
    grads, fast_grad, slow_grad = pull((fast_cot.astype(jnp.float32), slow_cot.astype(jnp.float32)))
    rate, decay = element_rates(jnp.arange(PARAMS, dtype=jnp.int32))
    first = moment_one[position].reshape(-1)
    second = moment_two[position].reshape(-1)
    new_first, new_second, new_weight = adam(flat, grads, first, second, rate, decay)

    def pack(values):
        return jnp.zeros(master.shape, values.dtype).at[position].set(values.reshape(NBLK, BLK))
    packed_master = pack(new_weight)
    return (outputs[0], outputs[1], fast_grad, slow_grad, packed_master, pack(new_first), pack(new_second), packed_master.astype(jnp.bfloat16))
```

```python
import functools
import math

import jax
import jax.numpy as jnp
from jax import lax
from jax.experimental import pallas as pl
from jax.experimental.pallas import tpu as pltpu
from jax.sharding import PartitionSpec as P

C_FAST = 128
B_FAST = 32
C_SLOW = 1024
B_SLOW = 256
C_LAT = 256
TILE = 16
POS = TILE * TILE
BLK = 128
STEP = 10
NBLK = 7591

norm_eps = 1e-05
beta_first = 0.5
beta_second = 0.5
adam_eps = 1e-08
decay_rate = 0.05

MESH = pl.DeviceIdType.MESH
f32 = jnp.float32
bf16 = jnp.bfloat16
RC = 32
GROUPS = BLK // B_FAST

AT_F1 = 0
AT_F2 = AT_F1 + B_FAST * 3 * C_FAST // BLK
AT_F3 = AT_F2 + B_FAST * B_FAST // BLK
AT_LAT = AT_F3 + C_FAST * B_FAST // BLK
AT_S1 = AT_LAT + C_LAT * 5 * C_FAST // BLK
AT_S2 = AT_S1 + B_SLOW * (C_SLOW + C_LAT) // BLK
AT_S3 = AT_S2 + B_SLOW * 3 * B_SLOW // BLK
AT_VEC = AT_S3 + C_SLOW * B_SLOW // BLK
VECS = NBLK - AT_VEC
V_F3 = (1, 2, 1)
V_LAT = (3, 5, 2)
V_S1 = (7, 9, 2)
V_S2 = (11, 13, 2)
V_S3 = (15, 23, 8)


def up(n, m):
    return (n + m - 1) // m * m


def dot_nt(a, b):
    return lax.dot_general(a, b, (((1,), (1,)), ((), ())), preferred_element_type=f32)


def dot_tn(a, b):
    return lax.dot_general(a, b, (((0,), (0,)), ((), ())), preferred_element_type=f32)


def dot_nn(a, b):
    return lax.dot_general(a, b, (((1,), (0,)), ((), ())), preferred_element_type=f32)


G0 = math.sqrt(2.0 / math.pi)
G1 = 0.044715


def gelu(x):
    t = jnp.tanh(x * (G0 + (G0 * G1) * (x * x)))
    return 0.5 * x * (1.0 + t)


def gelu_slope(x):
    xx = x * x
    t = jnp.tanh(x * (G0 + (G0 * G1) * xx))
    return 0.5 * (1.0 + t) + (0.5 * x) * (1.0 - t * t) * (G0 + (3.0 * G0 * G1) * xx)


def position_mask(crop):
    spot = lax.broadcasted_iota(jnp.int32, (POS, BLK), 0)
    inside = (spot // TILE < crop) & (lax.rem(spot, TILE) < crop)
    return jnp.where(inside, 1.0, 0.0).astype(f32)


class Sender:
    def __init__(self, sems):
        self.sems = sems
        self.copies = []

    def send(self, view, recv_sem, device):
        copy = pltpu.make_async_remote_copy(
            src_ref=view,
            dst_ref=view,
            send_sem=self.sems.at[len(self.copies)],
            recv_sem=recv_sem,
            device_id=device,
            device_id_type=MESH,
        )
        copy.start()
        self.copies.append(copy)

    def drain(self):
        for copy in self.copies:
            copy.wait_send()
        self.copies = []


def arrived(view, sem):
    pltpu.make_async_copy(view, view, sem).wait()


class Place:
    def __init__(self, nd, nm):
        self.nd, self.nm = nd, nm
        self.nc = 2
        self.nx = nd // 2
        self.nb = 2 if nm % 2 == 0 else 1
        self.na = nm // self.nb
        self.dp = lax.axis_index("dp")
        self.mp = lax.axis_index("mp")
        self.x, self.c = self.dp // 2, lax.rem(self.dp, 2)
        self.a, self.b = self.mp // self.nb, lax.rem(self.mp, self.nb)

    def off_a(self, i):
        return lax.rem(self.a + i, self.na)

    def off_b(self, i):
        return lax.rem(self.b + i, self.nb)

    def off_x(self, i):
        return lax.rem(self.x + i, self.nx)

    def dev(self, x, c, a, b):
        return (x * 2 + c, a * self.nb + b)

    def slot(self, x, c, a, b):
        return (x * 2 + c) * self.nm + a * self.nb + b


class Gather:
    def __init__(self, place, view, sender, recv):
        self.p, self.view, self.sender, self.recv = place, view, sender, recv

    def rank(self, a, b):
        return a * self.p.nb + b

    def forward(self, a):
        p = self.p
        r = self.rank(a, p.b)
        for i in range(1, p.nb):
            self.sender.send(self.view(r), self.recv.at[r], (p.dp, self.rank(p.a, p.off_b(i))))

    def start(self):
        p = self.p
        for i in range(1, p.na):
            self.sender.send(
                self.view(p.mp), self.recv.at[p.mp], (p.dp, self.rank(p.off_a(i), p.b))
            )
        self.forward(p.a)

    def relay(self):
        p = self.p
        for i in range(1, p.na):
            a = p.off_a(p.na - i)
            arrived(self.view(self.rank(a, p.b)), self.recv.at[self.rank(a, p.b)])
            self.forward(a)

    def finish(self):
        p = self.p
        for j in range(1, p.nb):
            for i in range(p.na):
                r = self.rank(p.off_a(p.na - i), p.off_b(j))
                arrived(self.view(r), self.recv.at[r])


def signal_all(devices):
    barrier = pltpu.get_barrier_semaphore()
    for device in devices:
        pl.semaphore_signal(barrier, inc=1, device_id=device, device_id_type=MESH)


def gather_sizes(nd, nm):
    nb = 2 if nm % 2 == 0 else 1
    na, nx = nm // nb, nd // 2
    params = (na - 1) + (nb - 1) + (nx - 1) + 1
    params += (na - 1) * ((nb - 1) + (nx - 1) + 1)
    params += na * (nb - 1) * (1 + nx - 1) + na * (nx - 1) * (1 + nb - 1)
    params += na * (nb - 1) * (nx - 1)
    arrays = nm - 1
    return params, arrays


def gather_kernel(
    cfg, start_ref, count_ref, crop_ref, master_ref, fast_ref, slow_ref,
    p_ref, xt_ref, xs_ref, shift_ref, natural_ref, p_recv, f_recv, s_recv, send_sems
):
    nd, nm, frames, slow_frames, share, slots = cfg
    rows = up(slots + 15, 16)
    p = Place(nd, nm)
    peers = [p.dev(p.x, p.c, p.off_a(i), p.b) for i in range(1, p.na)]
    peers += [p.dev(p.x, p.c, p.a, p.off_b(i)) for i in range(1, p.nb)]
    peers += [p.dev(p.off_x(i), p.c, p.a, p.b) for i in range(1, p.nx)]
    peers += [p.dev(p.x, 1 - p.c, p.a, p.b)]
    signal_all(peers)

    me = p.dp * nm + p.mp
    start = start_ref[me]
    shift = lax.rem(start, 16)
    shift_ref[...] = jnp.zeros_like(shift_ref)
    shift_ref[16 : 16 + slots] = master_ref[...]
    moved = shift_ref[pl.ds(16 - shift, rows), :]
    row = lax.broadcasted_iota(jnp.int32, (rows, BLK), 0)
    own = (row >= shift) & (row < shift + count_ref[me])
    p_ref[me] = jnp.where(own, moved, 0.0).astype(bf16)

    pl.semaphore_wait(pltpu.get_barrier_semaphore(), len(peers))

    out = Sender(send_sems)

    def view(x, c, a, b):
        return p_ref.at[p.slot(x, c, a, b)]

    def pass_on(source, along_a=False, along_b=False, along_x=False, along_c=False):
        piece, sem = view(*source), p_recv.at[p.slot(*source)]
        if along_a:
            for i in range(1, p.na):
                out.send(piece, sem, p.dev(p.x, p.c, p.off_a(i), p.b))
        if along_x:
            for i in range(1, p.nx):
                out.send(piece, sem, p.dev(p.off_x(i), p.c, p.a, p.b))
        if along_b:
            for i in range(1, p.nb):
                out.send(piece, sem, p.dev(p.x, p.c, p.a, p.off_b(i)))
        if along_c:
            out.send(piece, sem, p.dev(p.x, 1 - p.c, p.a, p.b))

    def take(source):
        arrived(view(*source), p_recv.at[p.slot(*source)])

    pass_on((p.x, p.c, p.a, p.b), along_a=True, along_b=True, along_x=True, along_c=True)

    mask = position_mask(crop_ref[0])
    xt_ref[: 2 * POS] = jnp.zeros((2 * POS, BLK), bf16)
    xt_ref[(frames + 2) * POS :] = jnp.zeros((2 * POS, BLK), bf16)

    def frame_view(r):
        return xt_ref.at[pl.ds(pl.multiple_of((r + 2) * POS, POS), POS)]

    frame_view(p.mp)[...] = (fast_ref[...].astype(f32).T * mask).astype(bf16)
    fast_gather = Gather(p, frame_view, out, f_recv)
    fast_gather.start()

    if share == BLK:

        def slow_view(r):
            return xs_ref.at[:, pl.ds(pl.multiple_of(r * BLK, BLK), BLK)]

        for s in range(slow_frames):
            piece = slow_ref[:, s * POS : (s + 1) * POS].astype(f32).T * mask
            slow_view(p.mp)[s * POS : (s + 1) * POS, :] = piece.astype(bf16)
    else:

        def slow_view(r):
            return natural_ref.at[pl.ds(pl.multiple_of(r * share, share), share)]

        slow_view(p.mp)[...] = slow_ref[...]
    slow_gather = Gather(p, slow_view, out, s_recv)
    slow_gather.start()

    for i in range(1, p.na):
        source = (p.x, p.c, p.off_a(p.na - i), p.b)
        take(source)
        pass_on(source, along_b=True, along_x=True, along_c=True)
    fast_gather.relay()
    across = p.na * 3 // 4
    for i in range(p.na):
        for j in range(1, p.nb):
            source = (p.x, p.c, p.off_a(p.na - i), p.off_b(j))
            take(source)
            pass_on(source, along_x=i < across, along_c=True)
        for j in range(1, p.nx):
            source = (p.off_x(j), p.c, p.off_a(p.na - i), p.b)
            take(source)
            pass_on(source, along_b=i >= across, along_c=True)
    slow_gather.relay()
    for i in range(p.na):
        for j in range(1, p.nb):
            for k in range(1, p.nx):
                source = (p.off_x(k), p.c, p.off_a(p.na - i), p.off_b(j))
                take(source)
                pass_on(source, along_c=True)
    for i in range(p.na):
        for j in range(p.nb):
            for k in range(p.nx):
                take((p.off_x(k), 1 - p.c, p.off_a(i), p.off_b(j)))
    fast_gather.finish()
    slow_gather.finish()
    out.drain()
    if share != BLK:
        from_natural(natural_ref, xs_ref, mask, slow_frames)


def from_natural(natural_ref, wide_ref, mask, slow_frames):
    def block(i, _):
        s, j = i // (C_SLOW // BLK), lax.rem(i, C_SLOW // BLK)
        at_row = pl.ds(pl.multiple_of(s * POS, POS), POS)
        at_lane = pl.ds(pl.multiple_of(j * BLK, BLK), BLK)
        piece = natural_ref[at_lane, at_row].astype(f32).T * mask
        wide_ref[at_row, at_lane] = piece.astype(bf16)
        return 0

    lax.fori_loop(0, slow_frames * (C_SLOW // BLK), block, 0)


def call_gather(cfg, starts, counts, crop, master, fast, slow):
    nd, nm, frames, slow_frames, share, slots = cfg
    rows = up(slots + 15, 16)
    params, arrays = gather_sizes(nd, nm)
    smem = pl.BlockSpec(memory_space=pltpu.SMEM)
    vmem = pl.BlockSpec(memory_space=pltpu.VMEM)
    dma = pltpu.SemaphoreType.DMA
    natural = (C_SLOW, slow_frames * POS) if share != BLK else (16, BLK)
    return pl.pallas_call(
        functools.partial(gather_kernel, cfg),
        out_shape=(
            jax.ShapeDtypeStruct((nd * nm, rows, BLK), bf16),
            jax.ShapeDtypeStruct(((frames + 4) * POS, BLK), bf16),
            jax.ShapeDtypeStruct((slow_frames * POS, C_SLOW), bf16),
        ),
        in_specs=[smem, smem, smem, vmem, vmem, vmem],
        out_specs=(vmem, vmem, vmem),
        scratch_shapes=[
            pltpu.VMEM((rows + 16, BLK), f32),
            pltpu.VMEM(natural, bf16),
            dma((nd * nm,)),
            dma((nm,)),
            dma((nm,)),
            dma((params + 2 * arrays,)),
        ],
        compiler_params=pltpu.CompilerParams(
            collective_id=0, has_side_effects=True, vmem_limit_bytes=48 << 20
        ),
        name="gather",
    )(starts, counts, crop, master, fast, slow)


def lane_group():
    return lax.broadcasted_iota(jnp.int32, (1, BLK), 1) // B_FAST


def fold_lanes(v):
    v = v + pltpu.roll(v, B_FAST, 1)
    return v + pltpu.roll(v, 2 * B_FAST, 1)


def weights_kernel(
    cfg, start_ref, p_ref, lat_ref, s1_ref, s2_ref, s3_ref, f1_ref, f2_ref, f3_ref, vec_ref,
    flat_ref, square_ref
):
    nd, nm, frames, slow_frames, share, slots = cfg
    rows = up(slots + 15, 16)
    chunk = 64

    def clear(i, _):
        flat_ref[pl.ds(pl.multiple_of(i * chunk, chunk), chunk), :] = jnp.zeros((chunk, BLK), f32)
        return 0

    lax.fori_loop(0, flat_ref.shape[0] // chunk, clear, 0)

    def add(d, _):
        base = pl.multiple_of(start_ref[d] // 16 * 16, 16)
        flat_ref[pl.ds(base, rows), :] += p_ref[d].astype(f32)
        return 0

    lax.fori_loop(0, nd * nm, add, 0)

    def matrix(out_ref, at, tall, blocks):
        for j in range(blocks):
            for o in range(0, tall, 256):
                out_ref[o : o + 256, j * BLK : (j + 1) * BLK] = flat_ref[
                    pl.ds(at + o * blocks + j, 256, stride=blocks), :
                ].astype(bf16)

    matrix(lat_ref, AT_LAT, C_LAT, 5)
    matrix(s1_ref, AT_S1, B_SLOW, 10)
    matrix(s2_ref, AT_S2, B_SLOW, 6)
    matrix(s3_ref, AT_S3, C_SLOW, 2)
    for k in range(3):
        tap = flat_ref[pl.ds(AT_F1 + k, B_FAST, stride=3), :].astype(bf16)
        for g in range(GROUPS):
            f1_ref[g * B_FAST : (g + 1) * B_FAST, k * BLK : (k + 1) * BLK] = tap
    group = lane_group()

    def spread(at, tall):
        for r in range(GROUPS):
            part = jnp.where(group == r, flat_ref[at : at + tall // GROUPS, :], 0.0)
            square_ref[pl.ds(r, tall // GROUPS, stride=GROUPS), :] = fold_lanes(part)
        return square_ref[:tall, :]

    two = spread(AT_F2, B_FAST)
    for g in range(GROUPS):
        f2_ref[g * B_FAST : (g + 1) * B_FAST, :] = jnp.where(group == g, two, 0.0).astype(bf16)
    f3_ref[...] = spread(AT_F3, C_FAST).astype(bf16)
    vec_ref[...] = flat_ref[AT_VEC : AT_VEC + 32, :]


def call_weights(cfg, starts, gathered):
    nd, nm, frames, slow_frames, share, slots = cfg
    rows = up(slots + 15, 16)
    smem = pl.BlockSpec(memory_space=pltpu.SMEM)
    vmem = pl.BlockSpec(memory_space=pltpu.VMEM)
    shapes = [
        ((C_LAT, 5 * C_FAST), bf16),
        ((B_SLOW, C_SLOW + C_LAT), bf16),
        ((B_SLOW, 3 * B_SLOW), bf16),
        ((C_SLOW, B_SLOW), bf16),
        ((BLK, 3 * C_FAST), bf16),
        ((BLK, BLK), bf16),
        ((BLK, BLK), bf16),
        ((32, BLK), f32),
    ]
    return pl.pallas_call(
        functools.partial(weights_kernel, cfg),
        out_shape=tuple(jax.ShapeDtypeStruct(s, t) for s, t in shapes),
        in_specs=[smem, vmem],
        out_specs=tuple(vmem for _ in shapes),
        scratch_shapes=[
            pltpu.VMEM((up(NBLK + rows, 64), BLK), f32),
            pltpu.VMEM((BLK, BLK), f32),
        ],
        compiler_params=pltpu.CompilerParams(vmem_limit_bytes=48 << 20),
        name="weights",
    )(starts, gathered)


EX_LAT, EX_S1, EX_S2, EX_B2, EX_B1, EX_BLAT = range(6)
EX_F1, EX_F2, EX_F3, EX_BF3, EX_BF2, EX_BF1 = range(6, 12)
EX_S3, EX_BS3 = 12, 13
EXCHANGES = 14


def main_kernel(
    cfg, start_ref, crop_ref, xt_ref, xs_ref, lat_w, s1_w, s2_w, s3_w, f1_w, f2_w, f3_w, vec_ref,
    fcot_ref, scot_ref,
    fast_out, slow_out, fast_grad, slow_grad, grad_out,
    mask_ref, fc_ref, sc_ref, natural_ref, zb, latb, s1b, s2b, dz, da1, da2, c1, c2, c3, e, e3,
    a1p, a2p, h1p, h2p, d1p, d2p, ep, a3, e3f, square_ref, flat_ref, own3_ref, win_ref,
    st_ref, st16_ref, f_recv, s_recv, gather_sems, ex_send, ex_recv, g_send, g_recv
):
    nd, nm, frames, slow_frames, share, slots = cfg
    p = Place(nd, nm)
    slow_rows, fast_rows = slow_frames * POS, frames * POS
    per_group = frames // GROUPS
    group_rows = per_group * POS
    keep = share == BLK
    da3, da3f = sc_ref, fc_ref

    peers = [(lax.rem(p.dp + i, nd), p.mp) for i in range(1, nd)]
    near = [p.dev(p.x, p.c, p.off_a(i), p.b) for i in range(1, p.na)]
    near += [p.dev(p.x, p.c, p.a, p.off_b(i)) for i in range(1, p.nb)]
    signal_all(peers + near)

    crop = crop_ref[0]
    mask_ref[...] = position_mask(crop)
    tall = crop.astype(f32)
    area = tall * tall

    mask = mask_ref[...]

    def frame_view(r):
        return fc_ref.at[pl.ds(pl.multiple_of(r * POS, POS), POS)]

    frame_view(p.mp)[...] = (fcot_ref[...].astype(f32).T * mask).astype(bf16)
    if keep:

        def slow_view(r):
            return sc_ref.at[:, pl.ds(pl.multiple_of(r * BLK, BLK), BLK)]

        for s in range(slow_frames):
            piece = scot_ref[:, s * POS : (s + 1) * POS].astype(f32).T * mask
            slow_view(p.mp)[s * POS : (s + 1) * POS, :] = piece.astype(bf16)
    else:

        def slow_view(r):
            return natural_ref.at[pl.ds(pl.multiple_of(r * share, share), share)]

        slow_view(p.mp)[...] = scot_ref[...]

    pl.semaphore_wait(pltpu.get_barrier_semaphore(), len(peers) + len(near))
    out = Sender(gather_sems)
    slow_gather = Gather(p, slow_view, out, s_recv)
    fast_gather = Gather(p, frame_view, out, f_recv)
    fast_gather.start()
    slow_gather.start()

    ex_copies = []

    def stat(which):
        return st_ref.at[which] if which < 12 else st16_ref.at[which - 12]

    def exchange(which):
        own = stat(which).at[p.dp]
        for i in range(1, nd):
            copy = pltpu.make_async_remote_copy(
                src_ref=own,
                dst_ref=own,
                send_sem=ex_send.at[which, i - 1],
                recv_sem=ex_recv.at[which, i - 1],
                device_id=peers[i - 1],
                device_id_type=MESH,
            )
            copy.start()
            ex_copies.append(copy)

    def exchanged(which):
        buffer = stat(which)
        for i in range(1, nd):
            arrived(buffer.at[lax.rem(p.dp + nd - i, nd)], ex_recv.at[which, i - 1])
        total = buffer[0]
        for i in range(1, nd):
            total = total + buffer[i]
        return total

    def put(which, at, vector):
        ref = stat(which)
        for j in range(vector.shape[1] // BLK):
            ref[p.dp, at + j : at + j + 1, :] = vector[:, j * BLK : (j + 1) * BLK]

    def row_of(block, at, n):
        return jnp.concatenate([block[at + j : at + j + 1, :] for j in range(n)], 1)

    def vectors(place):
        g, b, n = place
        return row_of(vec_ref[...], g, n), row_of(vec_ref[...], b, n)

    def rows_at(i, size):
        return pl.ds(pl.multiple_of(i * size, size), size)

    def mask_at(i, width):
        part = mask_ref[pl.ds(pl.multiple_of(lax.rem(i * RC, POS), RC), RC), :]
        return jnp.concatenate([part] * (width // BLK), 1) if width > BLK else part

    def eights(v):
        return jnp.sum(v.reshape(v.shape[0] // 8, 8, v.shape[1]), 0)

    def total_row(v):
        return jnp.sum(v, 0, keepdims=True)

    def affine(sums, squares, count, gain, bias):
        mean = sums / count
        scale = lax.rsqrt(squares / count - mean * mean + norm_eps)
        grow = gain * scale
        return mean, scale, grow, bias - mean * grow

    def sums_of(ref, n_rows, width):
        def body(i, acc):
            v = ref[rows_at(i, RC), :].astype(f32)
            return acc[0] + eights(v), acc[1] + eights(v * v)

        zero = jnp.zeros((8, width), f32)
        one, two = lax.fori_loop(0, n_rows // RC, body, (zero, zero))
        return total_row(one), total_row(two)

    def activate(src, dst, n_rows, width, grow, base):
        def body(i, _):
            at = rows_at(i, RC)
            pre = src[at, :].astype(f32) * grow + base
            dst[at, :] = (gelu(pre) * mask_at(i, width)).astype(bf16)
            return 0

        lax.fori_loop(0, n_rows // RC, body, 0)

    def slopes(src, incoming, n_rows, width, norm):
        mean, scale, grow, base = norm

        def body(i, acc):
            at = rows_at(i, RC)
            a = src[at, :].astype(f32)
            d = gelu_slope(a * grow + base) * incoming[at, :] * mask_at(i, width)
            incoming[at, :] = d
            return acc[0] + eights(d), acc[1] + eights(d * ((a - mean) * scale))

        zero = jnp.zeros((8, width), f32)
        one, two = lax.fori_loop(0, n_rows // RC, body, (zero, zero))
        return total_row(one), total_row(two)

    def back_vectors(bias_sum, gain_sum, count, norm):
        mean, scale, grow, base = norm
        k1 = grow * gain_sum / count
        return grow * bias_sum / count - k1 * (mean * scale), k1 * scale

    def raw_grads(src, pres, dst, n_rows, width, norm, q0, q1):
        grow = norm[2]

        def body(i, _):
            at = rows_at(i, RC)
            a = src[at, :].astype(f32)
            da = grow * pres[at, :] - mask_at(i, width) * (q0 + a * q1)
            dst[at, :] = da.astype(bf16)
            return 0

        lax.fori_loop(0, n_rows // RC, body, 0)

    def put_vector(row, vector):
        for j in range(vector.shape[1] // BLK):
            at = AT_VEC + row + j
            flat_ref[at : at + 1, :] = vector[:, j * BLK : (j + 1) * BLK]

    def frame(ref, s):
        return ref[s * POS : (s + 1) * POS, :]

    group = lane_group()

    for s in range(slow_frames):
        window = jnp.concatenate([frame(xt_ref, 4 * s + k) for k in range(5)], 1)
        zb[s * POS : (s + 1) * POS, :] = dot_nt(window, lat_w[...]).astype(bf16)
    one, two = sums_of(zb, slow_rows, C_LAT)
    put(EX_LAT, 0, one)
    put(EX_LAT, 2, two)
    st_ref[EX_LAT, p.dp, 4:8, :] = jnp.full((4, BLK), area, f32)
    exchange(EX_LAT)

    def first(j, _):
        total = jnp.zeros((POS, BLK), f32)
        for g in range(GROUPS):
            at = (g * per_group + j + 1) * POS
            window = jnp.concatenate(
                [xt_ref[pl.ds(pl.multiple_of(at + k * POS, POS), POS), :] for k in range(3)], 1
            )
            total = total + jnp.where(group == g, dot_nt(window, f1_w[...]), 0.0)
        a1p[rows_at(j, POS), :] = total
        return 0

    lax.fori_loop(0, per_group, first, 0)
    one, two = sums_of(a1p, group_rows, BLK)
    put(EX_F1, 0, fold_lanes(one))
    put(EX_F1, 1, fold_lanes(two))
    st_ref[EX_F1, p.dp, 2:8, :] = jnp.full((6, BLK), area, f32)
    exchange(EX_F1)

    for s in range(slow_frames):
        c1[s * POS : (s + 1) * POS, :] = dot_nt(frame(xs_ref, s), s1_w[:, :C_SLOW])

    total = exchanged(EX_LAT)
    area_all = total[4:5, :]
    slow_count = jnp.concatenate([area_all * float(slow_frames)] * 2, 1)
    slow_count8 = jnp.concatenate([slow_count] * 4, 1)
    fast_count = area_all * float(frames)
    lat_norm = affine(row_of(total, 0, 2), row_of(total, 2, 2), slow_count, *vectors(V_LAT))
    activate(zb, latb, slow_rows, C_LAT, lat_norm[2], lat_norm[3])
    for s in range(slow_frames):
        at = slice(s * POS, (s + 1) * POS)
        c1[at, :] = c1[at, :] + dot_nt(latb[at, :], s1_w[:, C_SLOW:])
    one, two = sums_of(c1, slow_rows, B_SLOW)
    put(EX_S1, 0, one)
    put(EX_S1, 2, two)
    st_ref[EX_S1, p.dp, 4:8, :] = jnp.zeros((4, BLK), f32)
    exchange(EX_S1)

    packed = vec_ref[0:1, :]

    def spread(which):
        return fold_lanes(jnp.where(group == which, packed, 0.0))

    def exchanged_two(which):
        total = exchanged(which)
        return total[0:1, :], total[1:2, :]

    f1_norm = affine(*exchanged_two(EX_F1), fast_count, spread(0), spread(1))
    activate(a1p, h1p, group_rows, BLK, f1_norm[2], f1_norm[3])
    for j in range(per_group):
        a2p[j * POS : (j + 1) * POS, :] = dot_nt(frame(h1p, j), f2_w[...])
    one, two = sums_of(a2p, group_rows, BLK)
    put(EX_F2, 0, fold_lanes(one))
    put(EX_F2, 1, fold_lanes(two))
    st_ref[EX_F2, p.dp, 2:8, :] = jnp.zeros((6, BLK), f32)
    exchange(EX_F2)
    fast_gather.relay()

    total = exchanged(EX_S1)
    s1_norm = affine(row_of(total, 0, 2), row_of(total, 2, 2), slow_count, *vectors(V_S1))
    activate(c1, s1b, slow_rows, B_SLOW, s1_norm[2], s1_norm[3])
    for s in range(slow_frames):
        low, high = max(0, 1 - s), min(3, slow_frames - s + 1)
        window = jnp.concatenate([frame(s1b, s + k - 1) for k in range(low, high)], 1)
        c2[s * POS : (s + 1) * POS, :] = dot_nt(window, s2_w[:, low * B_SLOW : high * B_SLOW])
    one, two = sums_of(c2, slow_rows, B_SLOW)
    put(EX_S2, 0, one)
    put(EX_S2, 2, two)
    st_ref[EX_S2, p.dp, 4:8, :] = jnp.zeros((4, BLK), f32)
    exchange(EX_S2)

    f2_norm = affine(*exchanged_two(EX_F2), fast_count, spread(2), spread(3))
    activate(a2p, h2p, group_rows, BLK, f2_norm[2], f2_norm[3])
    for g in range(GROUPS):

        def third(j, _, g=g):
            part = jnp.where(group == g, h2p[rows_at(j, POS), :], 0.0).astype(bf16)
            a3[rows_at(g * per_group + j, POS), :] = dot_nt(part, f3_w[...])
            return 0

        lax.fori_loop(0, per_group, third, 0)
    one, two = sums_of(a3, fast_rows, BLK)
    put(EX_F3, 0, one)
    put(EX_F3, 1, two)
    st_ref[EX_F3, p.dp, 2:8, :] = jnp.zeros((6, BLK), f32)
    exchange(EX_F3)
    slow_gather.relay()

    total = exchanged(EX_S2)
    s2_norm = affine(row_of(total, 0, 2), row_of(total, 2, 2), slow_count, *vectors(V_S2))
    activate(c2, s2b, slow_rows, B_SLOW, s2_norm[2], s2_norm[3])
    quarter = C_SLOW // 4
    for n in range(4):
        lanes = slice(n * quarter, (n + 1) * quarter)
        for s in range(slow_frames):
            c3[s * POS : (s + 1) * POS, lanes] = dot_nt(frame(s2b, s), s3_w[lanes, :])
        one, two = sums_of(c3.at[:, lanes], slow_rows, quarter)
        put(EX_S3, 2 * n, one)
        put(EX_S3, 8 + 2 * n, two)
    exchange(EX_S3)

    f3_norm = affine(*exchanged_two(EX_F3), fast_count, *vectors(V_F3))
    fast_gather.finish()
    own = a3[rows_at(p.mp, POS), :] * f3_norm[2] + f3_norm[3]
    own = own + xt_ref[rows_at(p.mp + 2, POS), :].astype(f32)
    fast_out[...] = (gelu(own) * mask_ref[...]).T

    def fast_slopes(i, acc):
        mean, scale, grow, base = f3_norm
        at = rows_at(i, RC)
        a = a3[at, :]
        x = xt_ref[pl.ds(pl.multiple_of(i * RC + 2 * POS, RC), RC), :].astype(f32)
        d = gelu_slope(a * grow + base + x) * fc_ref[at, :].astype(f32)
        e3f[at, :] = d
        return acc[0] + eights(d), acc[1] + eights(d * ((a - mean) * scale))

    zero = jnp.zeros((8, BLK), f32)
    one, two = lax.fori_loop(0, fast_rows // RC, fast_slopes, (zero, zero))
    one, two = total_row(one), total_row(two)
    put(EX_BF3, 0, one)
    put(EX_BF3, 1, two)
    st_ref[EX_BF3, p.dp, 2:8, :] = jnp.zeros((6, BLK), f32)
    exchange(EX_BF3)
    put_vector(V_F3[0], two)
    put_vector(V_F3[1], one)

    slow_gather.finish()
    out.drain()
    if not keep:
        from_natural(natural_ref, sc_ref, mask_ref[...], slow_frames)
    total = exchanged(EX_S3)
    s3_norm = affine(row_of(total, 0, 8), row_of(total, 8, 8), slow_count8, *vectors(V_S3))

    def slope_three(at, lanes, norm):
        a = c3[at, lanes]
        pre = a * norm[2] + norm[3] + xs_ref[at, lanes].astype(f32)
        return a, gelu_slope(pre) * sc_ref[at, lanes].astype(f32)

    for n in range(4):
        lanes = slice(n * quarter, (n + 1) * quarter)
        norm = [v[:, lanes] for v in s3_norm]

        def slow_slopes(i, acc, lanes=lanes, norm=norm):
            at = rows_at(i, RC)
            a, d = slope_three(at, lanes, norm)
            if keep:
                e3[at, lanes] = d
            return acc[0] + eights(d), acc[1] + eights(d * ((a - norm[0]) * norm[1]))

        zero = jnp.zeros((8, quarter), f32)
        one, two = lax.fori_loop(0, slow_rows // RC, slow_slopes, (zero, zero))
        one, two = total_row(one), total_row(two)
        put(EX_BS3, 2 * n, one)
        put(EX_BS3, 8 + 2 * n, two)
        put_vector(V_S3[0] + 2 * n, two)
        put_vector(V_S3[1] + 2 * n, one)
    exchange(EX_BS3)

    first_channel = p.mp * share
    at_lane = pl.ds(pl.multiple_of(first_channel // BLK * BLK, BLK), BLK)
    lane_shift = lax.rem(first_channel, BLK)
    own_rows = first_channel // BLK
    own_norm = [
        sum(
            jnp.where(own_rows == j, v[:, j * BLK : (j + 1) * BLK], 0.0)
            for j in range(C_SLOW // BLK)
        )
        for v in s3_norm
    ]

    def to_channels(block):
        turned = block.T
        if share == BLK:
            return turned
        return sum(
            jnp.where(lane_shift == k * share, turned[k * share : (k + 1) * share, :], 0.0)
            for k in range(BLK // share)
        )

    for s in range(slow_frames):
        at = slice(s * POS, (s + 1) * POS)
        pre = c3[at, at_lane] * own_norm[2] + own_norm[3] + xs_ref[at, at_lane].astype(f32)
        slow_out[:, at] = to_channels(gelu(pre) * mask_ref[...])
        own3_ref[at, :] = gelu_slope(pre) * sc_ref[at, at_lane].astype(f32)

    q0, q1 = back_vectors(*exchanged_two(EX_BF3), fast_count, f3_norm)
    raw_grads(a3, e3f, da3f, fast_rows, BLK, f3_norm, q0, q1)
    for j in range(per_group):
        total = jnp.zeros((POS, BLK), f32)
        for g in range(GROUPS):
            part = dot_nn(frame(da3f, g * per_group + j), f3_w[...])
            total = total + jnp.where(group == g, part, 0.0)
        ep[j * POS : (j + 1) * POS, :] = total
    one, two = slopes(a2p, ep, group_rows, BLK, f2_norm)
    put(EX_BF2, 0, fold_lanes(one))
    put(EX_BF2, 1, fold_lanes(two))
    st_ref[EX_BF2, p.dp, 2:8, :] = jnp.zeros((6, BLK), f32)
    exchange(EX_BF2)
    vec_two = jnp.where(group == 2, fold_lanes(two), 0.0)
    vec_two = vec_two + jnp.where(group == 3, fold_lanes(one), 0.0)

    total = exchanged(EX_BS3)
    q0, q1 = back_vectors(row_of(total, 0, 8), row_of(total, 8, 8), slow_count8, s3_norm)
    for n in range(4):
        lanes = slice(n * quarter, (n + 1) * quarter)
        norm = [v[:, lanes] for v in s3_norm]
        q0n, q1n = q0[:, lanes], q1[:, lanes]

        def raw_three(i, _, lanes=lanes, norm=norm, q0n=q0n, q1n=q1n):
            at = rows_at(i, RC)
            if keep:
                a, d = c3[at, lanes], e3[at, lanes]
            else:
                a, d = slope_three(at, lanes, norm)
            da = norm[2] * d - mask_at(i, quarter) * (q0n + a * q1n)
            da3[at, lanes] = da.astype(bf16)
            return 0

        lax.fori_loop(0, slow_rows // RC, raw_three, 0)
    for s in range(slow_frames):
        at = slice(s * POS, (s + 1) * POS)
        e[at, :] = dot_nn(da3[at, :], s3_w[...])
    one, two = slopes(c2, e, slow_rows, B_SLOW, s2_norm)
    put(EX_B2, 0, one)
    put(EX_B2, 2, two)
    st_ref[EX_B2, p.dp, 4:8, :] = jnp.zeros((4, BLK), f32)
    exchange(EX_B2)
    put_vector(V_S2[0], two)
    put_vector(V_S2[1], one)

    def to_flat(at, blocks, offset, tall, lane, value):
        flat_ref[pl.ds(at + offset * blocks + lane, tall, stride=blocks), :] = value

    for n in range(4):
        part = dot_tn(da3[:, n * quarter : (n + 1) * quarter], s2b[...])
        for j in range(2):
            to_flat(AT_S3, 2, n * quarter, quarter, j, part[:, j * BLK : (j + 1) * BLK])

    q0, q1 = back_vectors(*exchanged_two(EX_BF2), fast_count, f2_norm)
    raw_grads(a2p, ep, d2p, group_rows, BLK, f2_norm, q0, q1)
    for j in range(per_group):
        ep[j * POS : (j + 1) * POS, :] = dot_nn(frame(d2p, j), f2_w[...])
    one, two = slopes(a1p, ep, group_rows, BLK, f1_norm)
    put(EX_BF1, 0, fold_lanes(one))
    put(EX_BF1, 1, fold_lanes(two))
    st_ref[EX_BF1, p.dp, 2:8, :] = jnp.zeros((6, BLK), f32)
    exchange(EX_BF1)
    vec_one = jnp.where(group == 0, fold_lanes(two), 0.0)
    vec_one = vec_one + jnp.where(group == 1, fold_lanes(one), 0.0)
    put_vector(0, vec_one + vec_two)

    total = exchanged(EX_B2)
    q0, q1 = back_vectors(row_of(total, 0, 2), row_of(total, 2, 2), slow_count, s2_norm)
    raw_grads(c2, e, da2, slow_rows, B_SLOW, s2_norm, q0, q1)
    for s in range(slow_frames):
        parts = [
            dot_nn(frame(da2, s - k + 1), s2_w[:, k * B_SLOW : (k + 1) * B_SLOW])
            for k in range(3)
            if 0 <= s - k + 1 < slow_frames
        ]
        e[s * POS : (s + 1) * POS, :] = functools.reduce(lambda u, v: u + v, parts)
    one, two = slopes(c1, e, slow_rows, B_SLOW, s1_norm)
    put(EX_B1, 0, one)
    put(EX_B1, 2, two)
    st_ref[EX_B1, p.dp, 4:8, :] = jnp.zeros((4, BLK), f32)
    exchange(EX_B1)
    put_vector(V_S1[0], two)
    put_vector(V_S1[1], one)

    for k in range(3):
        low, high = max(0, 1 - k), min(slow_frames, slow_frames + 1 - k)
        part = dot_tn(
            da2[low * POS : high * POS, :], s1b[(low + k - 1) * POS : (high + k - 1) * POS, :]
        )
        for j in range(2):
            to_flat(AT_S2, 6, 0, B_SLOW, 2 * k + j, part[:, j * BLK : (j + 1) * BLK])

    total = jnp.zeros((BLK, BLK), f32)
    for g in range(GROUPS):
        at = slice(g * group_rows, (g + 1) * group_rows)
        total = total + jnp.where(group == g, dot_tn(da3f[at, :], h2p[...]), 0.0)

    def to_blocks(value, at):
        n = value.shape[0] // GROUPS
        square_ref[: value.shape[0], :] = fold_lanes(value)
        flat_ref[at : at + n, :] = sum(
            jnp.where(group == r, square_ref[pl.ds(r, n, stride=GROUPS), :], 0.0)
            for r in range(GROUPS)
        )

    to_blocks(total, AT_F3)
    square = dot_tn(d2p[...], h1p[...])
    to_blocks(
        sum(
            jnp.where(group == g, square[g * B_FAST : (g + 1) * B_FAST, :], 0.0)
            for g in range(GROUPS)
        ),
        AT_F2,
    )

    total = exchanged(EX_B1)
    q0, q1 = back_vectors(row_of(total, 0, 2), row_of(total, 2, 2), slow_count, s1_norm)
    raw_grads(c1, e, da1, slow_rows, B_SLOW, s1_norm, q0, q1)
    for s in range(slow_frames):
        at = slice(s * POS, (s + 1) * POS)
        e[at, :] = dot_nn(da1[at, :], s1_w[:, C_SLOW:])
    one, two = slopes(zb, e, slow_rows, C_LAT, lat_norm)
    put(EX_BLAT, 0, one)
    put(EX_BLAT, 2, two)
    st_ref[EX_BLAT, p.dp, 4:8, :] = jnp.zeros((4, BLK), f32)
    exchange(EX_BLAT)
    put_vector(V_LAT[0], two)
    put_vector(V_LAT[1], one)

    for s in range(slow_frames):
        at = slice(s * POS, (s + 1) * POS)
        value = own3_ref[at, :] + dot_nn(da1[at, :], s1_w[:, at_lane])
        slow_grad[:, at] = to_channels(value * mask_ref[...])

    q0, q1 = back_vectors(*exchanged_two(EX_BF1), fast_count, f1_norm)
    raw_grads(a1p, ep, d1p, group_rows, BLK, f1_norm, q0, q1)
    for k in range(3):
        tap = jnp.zeros((B_FAST, BLK), f32)
        for g in range(GROUPS):
            at = (g * per_group + k + 1) * POS
            part = dot_tn(d1p[...], xt_ref[at : at + group_rows, :])
            tap = tap + part[g * B_FAST : (g + 1) * B_FAST, :]
        to_flat(AT_F1, 3, 0, B_FAST, k, tap)

    for n in range((C_SLOW + C_LAT) // quarter):
        if n < 4:
            right = xs_ref[:, n * quarter : (n + 1) * quarter]
        else:
            right = latb[...]
        part = dot_tn(da1[...], right)
        for j in range(2):
            to_flat(AT_S1, 10, 0, B_SLOW, 2 * n + j, part[:, j * BLK : (j + 1) * BLK])

    near_grad = e3f[rows_at(p.mp, POS), :]
    for k in range(3):
        f = p.mp - k + 1
        there = (f >= 0) & (f < frames)
        g, j = f // per_group, lax.rem(f, per_group)
        g, j = jnp.where(there, g, 0), jnp.where(there, j, 0)
        left = jnp.where((group == g) & there, d1p[rows_at(j, POS), :], 0.0).astype(bf16)
        near_grad = near_grad + dot_nn(left, f1_w[:, k * BLK : (k + 1) * BLK])

    total = exchanged(EX_BLAT)
    q0, q1 = back_vectors(row_of(total, 0, 2), row_of(total, 2, 2), slow_count, lat_norm)
    raw_grads(zb, e, dz, slow_rows, C_LAT, lat_norm, q0, q1)
    for k in range(5):
        tap = functools.reduce(
            lambda u, v: u + v,
            [dot_tn(frame(dz, s), frame(xt_ref, 4 * s + k)) for s in range(slow_frames)],
        )
        to_flat(AT_LAT, 5, 0, C_LAT, k, tap)

    height = up(slots, 16)
    g_copies = []

    def window_of(device):
        return flat_ref[pl.ds(start_ref[device], height), :]

    for i in range(1, nd):
        peer = lax.rem(p.dp + i, nd)
        win_ref[0, i - 1] = window_of(peer * nm + p.mp).astype(bf16)
        copy = pltpu.make_async_remote_copy(
            src_ref=win_ref.at[0, i - 1],
            dst_ref=win_ref.at[1, i - 1],
            send_sem=g_send.at[i - 1],
            recv_sem=g_recv.at[i - 1],
            device_id=peers[i - 1],
            device_id_type=MESH,
        )
        copy.start()
        g_copies.append(copy)

    later = lax.rem(p.mp + 2, 4)
    s = (p.mp + 2) // 4
    for tap, at, there in (
        (later, s, s < slow_frames),
        (later + 4, s - 1, (later == 0) & (s > 0)),
    ):
        tap, at = jnp.where(there, tap, 0), jnp.where(there, at, 0)
        left = jnp.where(there, dz[rows_at(at, POS), :], 0.0).astype(bf16)
        weight = lat_w[:, pl.ds(pl.multiple_of(tap * BLK, BLK), BLK)]
        near_grad = near_grad + dot_nn(left, weight)
    fast_grad[...] = (near_grad * mask_ref[...]).T

    total = window_of(p.dp * nm + p.mp)
    for i in range(1, nd):
        arrived(win_ref.at[1, i - 1], g_recv.at[i - 1])
        total = total + win_ref[1, i - 1].astype(f32)
    grad_out[...] = total
    for copy in ex_copies + g_copies:
        copy.wait_send()


def call_main(cfg, starts, crop, xt, xs, weights, fcot, scot):
    nd, nm, frames, slow_frames, share, slots = cfg
    height = up(slots, 16)
    slow_rows, fast_rows = slow_frames * POS, frames * POS
    group_rows = fast_rows // GROUPS
    keep = share == BLK
    smem = pl.BlockSpec(memory_space=pltpu.SMEM)
    vmem = pl.BlockSpec(memory_space=pltpu.VMEM)
    dma = pltpu.SemaphoreType.DMA
    out_shapes = (
        (C_FAST, POS), (share, slow_rows), (C_FAST, POS), (share, slow_rows), (height, BLK)
    )
    scratch = [
        ((POS, BLK), f32),
        ((fast_rows, BLK), bf16),
        ((slow_rows, C_SLOW), bf16),
        ((16, BLK) if keep else (C_SLOW, slow_rows), bf16),
    ]
    scratch += [((slow_rows, 256), bf16)] * 7
    scratch += [
        ((slow_rows, 256), f32),
        ((slow_rows, 256), f32),
        ((slow_rows, C_SLOW), f32),
        ((slow_rows, 256), f32),
        ((slow_rows, C_SLOW) if keep else (8, BLK), f32),
        ((group_rows, BLK), f32),
        ((group_rows, BLK), f32),
        ((group_rows, BLK), bf16),
        ((group_rows, BLK), bf16),
        ((group_rows, BLK), bf16),
        ((group_rows, BLK), bf16),
        ((group_rows, BLK), f32),
        ((fast_rows, BLK), f32),
        ((fast_rows, BLK), f32),
        ((BLK, BLK), f32),
        ((up(NBLK + height, 64), BLK), f32),
        ((slow_rows, BLK), f32),
        ((2, nd - 1, height, BLK), bf16),
        ((12, nd, 8, BLK), f32),
        ((2, nd, 16, BLK), f32),
    ]
    return pl.pallas_call(
        functools.partial(main_kernel, cfg),
        out_shape=tuple(jax.ShapeDtypeStruct(s, f32) for s in out_shapes),
        in_specs=[smem, smem] + [vmem] * 12,
        out_specs=tuple(vmem for _ in out_shapes),
        scratch_shapes=[pltpu.VMEM(s, t) for s, t in scratch]
        + [
            dma((nm,)),
            dma((nm,)),
            dma((2 * (nm - 1),)),
            dma((EXCHANGES, nd - 1)),
            dma((EXCHANGES, nd - 1)),
            dma((nd - 1,)),
            dma((nd - 1,)),
        ],
        compiler_params=pltpu.CompilerParams(
            collective_id=1, has_side_effects=True, vmem_limit_bytes=60 << 20
        ),
        name="block",
    )(starts, crop, xt, xs, *weights, fcot, scot)


def adam_kernel(cfg, start_ref, count_ref, grad, master, one, two, w_out, one_out, two_out, low_out):
    nd, nm, frames, slow_frames, share, slots = cfg
    me = lax.axis_index("dp") * nm + lax.axis_index("mp")
    row = lax.broadcasted_iota(jnp.int32, (slots, BLK), 0)
    living = row < count_ref[me]
    block = row + start_ref[me]
    rate = jnp.full((slots, BLK), 0.2, f32)
    for at, width in (
        (AT_VEC, B_SLOW),
        (AT_S3, 3 * B_SLOW),
        (AT_S2, C_SLOW + C_LAT),
        (AT_S1, 5 * C_FAST),
        (AT_LAT, B_FAST),
        (AT_F2, 3 * C_FAST),
    ):
        rate = jnp.where(block < at, 0.5 / math.sqrt(width), rate)
    decay = jnp.where(block < AT_VEC, decay_rate, 0.0)
    g = grad[:slots, :]
    first = beta_first * one[...] + (1.0 - beta_first) * g
    second = beta_second * two[...] + (1.0 - beta_second) * g * g
    lift_one = 1.0 - beta_first**STEP
    lift_two = 1.0 - beta_second**STEP
    update = first / lift_one / (jnp.sqrt(second / lift_two) + adam_eps)
    weight = master[...]
    weight = jnp.where(living, weight - rate * (update + decay * weight), 0.0)
    w_out[...] = weight
    one_out[...] = jnp.where(living, first, 0.0)
    two_out[...] = jnp.where(living, second, 0.0)
    low_out[...] = weight.astype(bf16)


def call_adam(cfg, starts, counts, grad, master, one, two):
    shape = master.shape
    smem = pl.BlockSpec(memory_space=pltpu.SMEM)
    vmem = pl.BlockSpec(memory_space=pltpu.VMEM)
    return pl.pallas_call(
        functools.partial(adam_kernel, cfg),
        out_shape=tuple(jax.ShapeDtypeStruct(shape, t) for t in (f32, f32, f32, bf16)),
        in_specs=[smem, smem] + [vmem] * 4,
        out_specs=(vmem,) * 4,
        compiler_params=pltpu.CompilerParams(vmem_limit_bytes=32 << 20),
        name="adam",
    )(starts, counts, grad, master, one, two)


def solution(mesh):
    nd, nm = mesh.shape["dp"], mesh.shape["mp"]

    def local(fast_in, slow_in, fast_cot, slow_cot, crop, owner, master, one, two):
        cfg = (nd, nm, fast_in.shape[1] * nm, slow_in.shape[1], slow_in.shape[0], master.shape[0])
        devices = jnp.arange(nd * nm, dtype=jnp.int32)[:, None]
        mine = owner[None, :] == devices
        spot = jnp.arange(NBLK, dtype=jnp.int32)[None, :]
        starts = jnp.min(jnp.where(mine, spot, NBLK), 1)
        counts = jnp.sum(mine.astype(jnp.int32), 1)
        fast = fast_in.reshape(C_FAST, -1)
        slow = slow_in.reshape(slow_in.shape[0], -1)
        fcot = fast_cot.reshape(C_FAST, -1)
        scot = slow_cot.reshape(slow_in.shape[0], -1)
        gathered, xt, xs = call_gather(cfg, starts, counts, crop, master, fast, slow)
        weights = call_weights(cfg, starts, gathered)
        fast_out, slow_out, fast_grad, slow_grad, grad = call_main(
            cfg, starts, crop, xt, xs, weights, fcot, scot
        )
        new = call_adam(cfg, starts, counts, grad, master, one, two)
        return (
            fast_out.reshape(fast_in.shape),
            slow_out.reshape(slow_in.shape),
            fast_grad.reshape(fast_in.shape),
            slow_grad.reshape(slow_in.shape),
            *new,
        )

    return jax.shard_map(
        local,
        mesh=mesh,
        in_specs=(
            P(None, "mp", "dp", None),
            P("mp", None, "dp", None),
            P(None, "mp", "dp", None),
            P("mp", None, "dp", None),
            P("dp"),
            P(),
            P(("dp", "mp"), None),
            P(("dp", "mp"), None),
            P(("dp", "mp"), None),
        ),
        out_specs=(
            P(None, "mp", "dp", None),
            P("mp", None, "dp", None),
            P(None, "mp", "dp", None),
            P("mp", None, "dp", None),
            P(("dp", "mp"), None),
            P(("dp", "mp"), None),
            P(("dp", "mp"), None),
            P(("dp", "mp"), None),
        ),
        check_vma=False,
    )
```

```python
import functools
import math

import jax
import jax.numpy as jnp
from jax import lax
from jax.experimental import pallas as pl
from jax.experimental.pallas import tpu as pltpu
from jax.sharding import PartitionSpec as P

C_FAST = 128
B_FAST = 32
C_SLOW = 1024
B_SLOW = 256
C_LAT = 256
TILE = 16
POS = TILE * TILE
BLK = 128
STEP = 10
NBLK = 7591

norm_eps = 1e-05
beta_first = 0.5
beta_second = 0.5
adam_eps = 1e-08
decay_rate = 0.05

MESH = pl.DeviceIdType.MESH
f32 = jnp.float32
bf16 = jnp.bfloat16
RC = 32
GROUPS = BLK // B_FAST

AT_F1 = 0
AT_F2 = AT_F1 + B_FAST * 3 * C_FAST // BLK
AT_F3 = AT_F2 + B_FAST * B_FAST // BLK
AT_LAT = AT_F3 + C_FAST * B_FAST // BLK
AT_S1 = AT_LAT + C_LAT * 5 * C_FAST // BLK
AT_S2 = AT_S1 + B_SLOW * (C_SLOW + C_LAT) // BLK
AT_S3 = AT_S2 + B_SLOW * 3 * B_SLOW // BLK
AT_VEC = AT_S3 + C_SLOW * B_SLOW // BLK
VECS = NBLK - AT_VEC
V_F3 = (1, 2, 1)
V_LAT = (3, 5, 2)
V_S1 = (7, 9, 2)
V_S2 = (11, 13, 2)
V_S3 = (15, 23, 8)


def up(n, m):
    return (n + m - 1) // m * m


def dot_nt(a, b):
    return lax.dot_general(a, b, (((1,), (1,)), ((), ())), preferred_element_type=f32)


def dot_tn(a, b):
    return lax.dot_general(a, b, (((0,), (0,)), ((), ())), preferred_element_type=f32)


def dot_nn(a, b):
    return lax.dot_general(a, b, (((1,), (0,)), ((), ())), preferred_element_type=f32)


G0 = math.sqrt(2.0 / math.pi)
G1 = 0.044715


def gelu(x):
    t = jnp.tanh(x * (G0 + (G0 * G1) * (x * x)))
    return 0.5 * x * (1.0 + t)


def gelu_slope(x):
    xx = x * x
    t = jnp.tanh(x * (G0 + (G0 * G1) * xx))
    return 0.5 * (1.0 + t) + (0.5 * x) * (1.0 - t * t) * (G0 + (3.0 * G0 * G1) * xx)


def position_mask(crop):
    spot = lax.broadcasted_iota(jnp.int32, (POS, BLK), 0)
    inside = (spot // TILE < crop) & (lax.rem(spot, TILE) < crop)
    return jnp.where(inside, 1.0, 0.0).astype(f32)


class Sender:
    def __init__(self, sems):
        self.sems = sems
        self.copies = []

    def send(self, view, recv_sem, device):
        copy = pltpu.make_async_remote_copy(
            src_ref=view,
            dst_ref=view,
            send_sem=self.sems.at[len(self.copies)],
            recv_sem=recv_sem,
            device_id=device,
            device_id_type=MESH,
        )
        copy.start()
        self.copies.append(copy)

    def drain(self):
        for copy in self.copies:
            copy.wait_send()
        self.copies = []


def arrived(view, sem):
    pltpu.make_async_copy(view, view, sem).wait()


class Place:
    def __init__(self, nd, nm):
        self.nd, self.nm = nd, nm
        self.nc = 2
        self.nx = nd // 2
        self.nb = 2 if nm % 2 == 0 else 1
        self.na = nm // self.nb
        self.dp = lax.axis_index("dp")
        self.mp = lax.axis_index("mp")
        self.x, self.c = self.dp // 2, lax.rem(self.dp, 2)
        self.a, self.b = self.mp // self.nb, lax.rem(self.mp, self.nb)

    def off_a(self, i):
        return lax.rem(self.a + i, self.na)

    def off_b(self, i):
        return lax.rem(self.b + i, self.nb)

    def off_x(self, i):
        return lax.rem(self.x + i, self.nx)

    def dev(self, x, c, a, b):
        return (x * 2 + c, a * self.nb + b)

    def slot(self, x, c, a, b):
        return (x * 2 + c) * self.nm + a * self.nb + b


class Gather:
    def __init__(self, place, view, sender, recv):
        self.p, self.view, self.sender, self.recv = place, view, sender, recv

    def rank(self, a, b):
        return a * self.p.nb + b

    def forward(self, a):
        p = self.p
        r = self.rank(a, p.b)
        for i in range(1, p.nb):
            self.sender.send(self.view(r), self.recv.at[r], (p.dp, self.rank(p.a, p.off_b(i))))

    def start(self):
        p = self.p
        for i in range(1, p.na):
            self.sender.send(
                self.view(p.mp), self.recv.at[p.mp], (p.dp, self.rank(p.off_a(i), p.b))
            )
        self.forward(p.a)

    def relay(self):
        p = self.p
        for i in range(1, p.na):
            a = p.off_a(p.na - i)
            arrived(self.view(self.rank(a, p.b)), self.recv.at[self.rank(a, p.b)])
            self.forward(a)

    def finish(self):
        p = self.p
        for j in range(1, p.nb):
            for i in range(p.na):
                r = self.rank(p.off_a(p.na - i), p.off_b(j))
                arrived(self.view(r), self.recv.at[r])


def signal_all(devices):
    barrier = pltpu.get_barrier_semaphore()
    for device in devices:
        pl.semaphore_signal(barrier, inc=1, device_id=device, device_id_type=MESH)


def lane_group():
    return lax.broadcasted_iota(jnp.int32, (1, BLK), 1) // B_FAST


def fold_lanes(v):
    v = v + pltpu.roll(v, B_FAST, 1)
    return v + pltpu.roll(v, 2 * B_FAST, 1)


EX_LAT, EX_S1, EX_S2, EX_B2, EX_B1, EX_BLAT = range(6)
EX_F1, EX_F2, EX_F3, EX_BF3, EX_BF2, EX_BF1 = range(6, 12)
EX_S3, EX_BS3 = 12, 13
EXCHANGES = 14

ARGS = ("crop", "owner", "owners", "master", "fast", "slow", "fcot", "scot")


def sizes(cfg):
    nd, nm, frames, slow_frames, share, slots = cfg
    nb = 2 if nm % 2 == 0 else 1
    na, nx = nm // nb, nd // 2
    params = (na - 1) + (nb - 1) + (nx - 1) + 1
    params += (na - 1) * ((nb - 1) + (nx - 1) + 1)
    params += na * (nb - 1) * (1 + nx - 1) + na * (nx - 1) * (1 + nb - 1)
    params += na * (nb - 1) * (nx - 1)
    return params + 4 * (nm - 1)


def outputs(cfg):
    nd, nm, frames, slow_frames, share, slots = cfg
    halves = POS // BLK
    result = [
        ("fast_out", (C_FAST * halves, BLK), f32),
        ("slow_out", (share * slow_frames * halves, BLK), f32),
        ("fast_grad", (C_FAST * halves, BLK), f32),
        ("slow_grad", (share * slow_frames * halves, BLK), f32),
        ("grad", (up(slots, 16), BLK), f32),
    ]
    if share != BLK:
        result += [
            ("natural_x", (C_SLOW, slow_frames * POS), bf16),
            ("natural_c", (C_SLOW, slow_frames * POS), bf16),
        ]
    return result


def scratch(cfg):
    nd, nm, frames, slow_frames, share, slots = cfg
    keep = share == BLK
    devices = nd * nm
    rows = up(slots + 15, 16)
    height = up(slots, 16)
    halves = POS // BLK
    slow_rows, fast_rows = slow_frames * POS, frames * POS
    group_rows = fast_rows // GROUPS
    vmem, smem, dma = pltpu.VMEM, pltpu.SMEM, pltpu.SemaphoreType.DMA
    result = [
        ("owner_v", vmem((up(NBLK, 1024) // BLK, BLK), jnp.int32)),
        ("owner_s", smem((NBLK,), jnp.int32)),
        ("run_device", smem((devices,), jnp.int32)),
        ("run_start", smem((devices,), jnp.int32)),
        ("run_count", smem((devices,), jnp.int32)),
        ("table_v", vmem((8, BLK), jnp.int32)),
        ("table_s", smem((8, BLK), jnp.int32)),
        ("shift", vmem((rows + 16, BLK), f32)),
        ("p", vmem((devices * (rows // 16), 16, BLK), bf16)),
        ("q", vmem((devices, 16, BLK), bf16)),
        ("fast_v", vmem((C_FAST, POS), bf16)),
        ("slow_v", vmem((share * slow_frames * halves, BLK), bf16)),
        ("fcot_v", vmem((C_FAST, POS), bf16)),
        ("scot_v", vmem((share * slow_frames * halves, BLK), bf16)),
        ("stage", vmem((share * slow_frames * halves, BLK), f32)),
        ("xt", vmem(((frames + 4) * POS, BLK), bf16)),
        ("xs", vmem((slow_rows, C_SLOW), bf16)),
        ("fc", vmem((fast_rows, BLK), bf16)),
        ("sc", vmem((slow_rows, C_SLOW), bf16)),
        ("lat_w", vmem((C_LAT, 5 * C_FAST), bf16)),
        ("s1_w", vmem((B_SLOW, C_SLOW + C_LAT), bf16)),
        ("s2_w", vmem((B_SLOW, 3 * B_SLOW), bf16)),
        ("s3_w", vmem((C_SLOW, B_SLOW), bf16)),
        ("f1_w", vmem((BLK, 3 * C_FAST), bf16)),
        ("f2_w", vmem((BLK, BLK), bf16)),
        ("f3_w", vmem((BLK, BLK), bf16)),
        ("vec", vmem((32, BLK), f32)),
        ("mask", vmem((POS, BLK), f32)),
    ]
    if not keep:
        result += [
            ("piece", vmem((share, slow_rows), bf16)),
            ("turn", vmem((BLK, POS), bf16)),
        ]
    result += [
        (name, vmem((slow_rows, 256), bf16))
        for name in ("zb", "latb", "s1b", "s2b", "da1", "da2")
    ]
    result += [
        ("c1", vmem((slow_rows, 256), f32)),
        ("c2", vmem((slow_rows, 256), f32)),
        ("c3", vmem((slow_rows, C_SLOW), f32)),
        ("e", vmem((slow_rows, 256), f32)),
        ("e3", vmem((slow_rows, C_SLOW) if keep else (8, BLK), f32)),
        ("a1p", vmem((group_rows, BLK), f32)),
        ("a2p", vmem((group_rows, BLK), f32)),
        ("h1p", vmem((group_rows, BLK), bf16)),
        ("h2p", vmem((group_rows, BLK), bf16)),
        ("d1p", vmem((group_rows, BLK), bf16)),
        ("d2p", vmem((group_rows, BLK), bf16)),
        ("ep", vmem((group_rows, BLK), f32)),
        ("a3", vmem((fast_rows, BLK), f32)),
        ("e3f", vmem((fast_rows, BLK), f32)),
        ("square", vmem((BLK, BLK), f32)),
        ("flat", vmem((up(NBLK + height, 64), BLK), f32)),
        ("own3", vmem((slow_rows, BLK), f32)),
        ("win", vmem((2, nd - 1, height, BLK), bf16)),
        ("st", vmem((12, nd, 8, BLK), f32)),
        ("st16", vmem((2, nd, 16, BLK), f32)),
        ("out_fast", vmem((C_FAST * halves, BLK), f32)),
        ("out_slow", vmem((share * slow_frames * halves, BLK), f32)),
        ("out_fgrad", vmem((C_FAST * halves, BLK), f32)),
        ("out_sgrad", vmem((share * slow_frames * halves, BLK), f32)),
        ("out_grad", vmem((height, BLK), f32)),
        ("p_recv", dma((devices,))),
        ("x_recv", dma((nm,))),
        ("xs_recv", dma((nm,))),
        ("fc_recv", dma((nm,))),
        ("sc_recv", dma((nm,))),
        ("sends", dma((sizes(cfg),))),
        ("ex_send", dma((EXCHANGES, nd - 1))),
        ("ex_recv", dma((EXCHANGES, nd - 1))),
        ("g_send", dma((nd - 1,))),
        ("g_recv", dma((nd - 1,))),
        ("local", dma((16,))),
    ]
    return result


def main_kernel(cfg, *refs):
    nd, nm, frames, slow_frames, share, slots = cfg
    out_names = [name for name, _, _ in outputs(cfg)]
    names = list(ARGS) + ["out:" + n for n in out_names] + [n for n, _ in scratch(cfg)]
    R = dict(zip(names, refs, strict=True))
    p = Place(nd, nm)
    devices = nd * nm
    halves = POS // BLK
    rows = up(slots + 15, 16)
    tiles = rows // 16
    slow_rows, fast_rows = slow_frames * POS, frames * POS
    per_group = frames // GROUPS
    group_rows = per_group * POS
    keep = share == BLK
    me = p.dp * nm + p.mp

    peers = [(lax.rem(p.dp + i, nd), p.mp) for i in range(1, nd)]
    near = [p.dev(p.x, p.c, p.off_a(i), p.b) for i in range(1, p.na)]
    near += [p.dev(p.x, p.c, p.a, p.off_b(i)) for i in range(1, p.nb)]
    signal_all(peers + near)

    local_copies = []

    def fetch(source, target):
        copy = pltpu.make_async_copy(source, target, R["local"].at[len(local_copies)])
        copy.start()
        local_copies.append(copy)
        return copy

    get_owner = fetch(R["owners"], R["owner_v"])
    get_master = fetch(R["master"], R["shift"].at[pl.ds(16, slots)])
    get_fast = fetch(R["fast"], R["fast_v"])
    get_slow = fetch(R["slow"], R["slow_v"])
    get_fcot = fetch(R["fcot"], R["fcot_v"])
    get_scot = fetch(R["scot"], R["scot_v"])
    get_owner_s = fetch(R["owner"], R["owner_s"])

    crop = R["crop"][0]
    R["mask"][...] = position_mask(crop)
    tall = crop.astype(f32)
    area = tall * tall
    xt_ref, xs_ref, fc_ref, sc_ref = R["xt"], R["xs"], R["fc"], R["sc"]
    xt_ref[: 2 * POS] = jnp.zeros((2 * POS, BLK), bf16)
    xt_ref[(frames + 2) * POS :] = jnp.zeros((2 * POS, BLK), bf16)

    get_owner.wait()
    spot = lax.broadcasted_iota(jnp.int32, (8, BLK), 0) * BLK
    spot = spot + lax.broadcasted_iota(jnp.int32, (8, BLK), 1)
    lowest = jnp.full((8, BLK), NBLK, jnp.int32)
    number = jnp.zeros((8, BLK), jnp.int32)
    for i in range(up(NBLK, 1024) // 1024):
        block = spot + i * 1024
        mine = R["owner_v"][i * 8 : (i + 1) * 8, :] == me
        mine = mine & (block < NBLK)
        lowest = jnp.minimum(lowest, jnp.where(mine, block, NBLK))
        number = number + jnp.where(mine, 1, 0)
    my_start, my_count = jnp.min(lowest), jnp.sum(number)
    shift = lax.rem(my_start, 16)
    get_master.wait()
    moved = R["shift"][pl.ds(16 - shift, rows), :]
    row = lax.broadcasted_iota(jnp.int32, (rows, BLK), 0)
    own = (row >= shift) & (row < shift + my_count)
    p_ref = R["p"]

    def p_slot(slot):
        return p_ref.at[pl.ds(slot * tiles, tiles)]

    p_slot(me)[...] = jnp.where(own, moved, 0.0).astype(bf16).reshape(tiles, 16, BLK)

    pl.semaphore_wait(pltpu.get_barrier_semaphore(), len(peers) + len(near))
    out = Sender(R["sends"])

    def view(x, c, a, b):
        return p_slot(p.slot(x, c, a, b))

    def pass_on(source, along_a=False, along_b=False, along_x=False, along_c=False):
        piece, sem = view(*source), R["p_recv"].at[p.slot(*source)]
        if along_a:
            for i in range(1, p.na):
                out.send(piece, sem, p.dev(p.x, p.c, p.off_a(i), p.b))
        if along_x:
            for i in range(1, p.nx):
                out.send(piece, sem, p.dev(p.off_x(i), p.c, p.a, p.b))
        if along_b:
            for i in range(1, p.nb):
                out.send(piece, sem, p.dev(p.x, p.c, p.a, p.off_b(i)))
        if along_c:
            out.send(piece, sem, p.dev(p.x, 1 - p.c, p.a, p.b))

    def take(source):
        arrived(view(*source), R["p_recv"].at[p.slot(*source)])

    pass_on((p.x, p.c, p.a, p.b), along_a=True, along_b=True, along_x=True, along_c=True)

    mask = R["mask"][...]

    def frame_view(ref, skip):
        return lambda r: ref.at[pl.ds(pl.multiple_of((r + skip) * POS, POS), POS)]

    def own_frame(target, source):
        target(p.mp)[...] = (source[...].astype(f32).T * mask).astype(bf16)

    def lane_view(ref):
        return lambda r: ref.at[:, pl.ds(pl.multiple_of(r * BLK, BLK), BLK)]

    def natural_view(ref):
        return lambda r: ref.at[pl.ds(pl.multiple_of(r * share, share), share)]

    def own_slow(target, source):
        stage = R["stage"]
        stage[...] = source[...].astype(f32)
        for s in range(slow_frames):
            for h in range(halves):
                part = stage[pl.ds(h * slow_frames + s, share, stride=halves * slow_frames), :]
                at = slice(s * POS + h * BLK, s * POS + (h + 1) * BLK)
                if keep:
                    turned = part.T * mask[h * BLK : (h + 1) * BLK, :]
                    target(p.mp)[at, :] = turned.astype(bf16)
                else:
                    R["piece"][:, at] = part.astype(bf16)
        if not keep:
            pltpu.sync_copy(R["piece"], target(p.mp))

    def from_natural(natural, wide):
        def block(i, _):
            s, j = i // (C_SLOW // BLK), lax.rem(i, C_SLOW // BLK)
            at_row = pl.ds(pl.multiple_of(s * POS, POS), POS)
            at_lane = pl.ds(pl.multiple_of(j * BLK, BLK), BLK)
            pltpu.sync_copy(natural.at[at_lane, at_row], R["turn"])
            piece = R["turn"][...].astype(f32).T * R["mask"][...]
            wide[at_row, at_lane] = piece.astype(bf16)
            return 0

        lax.fori_loop(0, slow_frames * (C_SLOW // BLK), block, 0)

    x_view, fc_view = frame_view(xt_ref, 2), frame_view(fc_ref, 0)
    if keep:
        xs_view, sc_view = lane_view(xs_ref), lane_view(sc_ref)
    else:
        xs_view, sc_view = natural_view(R["out:natural_x"]), natural_view(R["out:natural_c"])
    x_gather = Gather(p, x_view, out, R["x_recv"])
    xs_gather = Gather(p, xs_view, out, R["xs_recv"])
    fc_gather = Gather(p, fc_view, out, R["fc_recv"])
    sc_gather = Gather(p, sc_view, out, R["sc_recv"])
    get_fast.wait()
    own_frame(x_view, R["fast_v"])
    x_gather.start()
    get_slow.wait()
    own_slow(xs_view, R["slow_v"])

    get_owner_s.wait()
    steps = [1 << i for i in reversed(range(max(1, (slots - 1).bit_length())))]
    owner_s, run_device, run_start, run_count = (
        R[n] for n in ("owner_s", "run_device", "run_start", "run_count")
    )

    def run(k, at):
        device = owner_s[jnp.minimum(at, NBLK - 1)]
        n = jnp.int32(1)
        for step in steps:
            more = n + step
            last = at + more - 1
            inside = owner_s[jnp.minimum(last, NBLK - 1)] == device
            n = jnp.where((more <= slots) & (last < NBLK) & inside, more, n)
        run_device[k] = device
        run_start[k] = at
        run_count[k] = n
        return at + n

    lax.fori_loop(0, devices, run, jnp.int32(0))

    for i in range(1, p.na):
        source = (p.x, p.c, p.off_a(p.na - i), p.b)
        take(source)
        pass_on(source, along_b=True, along_x=True, along_c=True)
    x_gather.relay()
    xs_gather.start()

    def tile_of(k):
        return run_device[k] * tiles - run_start[k] // 16

    def table(k, found):
        start, last = run_start[k], run_start[k] + run_count[k] - 1
        final = jnp.minimum(spot * 16 + 15, NBLK - 1)
        holds = (final >= start) & (final <= last)
        tile = jnp.where(spot == start // 16, devices * tiles + k, spot + tile_of(k))
        return jnp.where(holds, tile, found)

    R["table_v"][...] = lax.fori_loop(0, devices, table, jnp.zeros((8, BLK), jnp.int32))
    get_table = fetch(R["table_v"], R["table_s"])

    across = p.na * 3 // 4
    for i in range(p.na):
        for j in range(1, p.nb):
            source = (p.x, p.c, p.off_a(p.na - i), p.off_b(j))
            take(source)
            pass_on(source, along_x=i < across, along_c=True)
        for j in range(1, p.nx):
            source = (p.off_x(j), p.c, p.off_a(p.na - i), p.b)
            take(source)
            pass_on(source, along_b=i >= across, along_c=True)
    get_fcot.wait()
    own_frame(fc_view, R["fcot_v"])
    get_scot.wait()
    own_slow(sc_view, R["scot_v"])
    for i in range(p.na):
        for j in range(1, p.nb):
            for k in range(1, p.nx):
                source = (p.off_x(k), p.c, p.off_a(p.na - i), p.off_b(j))
                take(source)
                pass_on(source, along_c=True)
    sc_gather.start()
    fc_gather.start()
    xs_gather.relay()
    for i in range(p.na):
        for j in range(p.nb):
            for k in range(p.nx):
                take((p.off_x(k), 1 - p.c, p.off_a(i), p.off_b(j)))
    get_table.wait()

    def tile_rows(t):
        return pl.ds(pl.multiple_of(t * 16, 16), 16)

    q_ref = R["q"]

    def first_tile(k, before):
        tile = p_ref[run_device[k] * tiles].astype(f32)
        shared = lax.rem(run_start[k], 16) != 0
        tile = tile + jnp.where(shared, before, 0.0)
        q_ref[k] = tile.astype(bf16)
        last = (run_start[k] + run_count[k] - 1) // 16
        alone = last == run_start[k] // 16
        return jnp.where(alone, tile, p_ref[tile_of(k) + last].astype(f32))

    lax.fori_loop(0, devices, first_tile, jnp.zeros((16, BLK), f32))
    flat_ref, table_s = R["flat"], R["table_s"]

    def lay_out(first_block, end_block):
        first, end = first_block // 16, up(end_block, 16) // 16

        def one(t):
            source = table_s[t // BLK, lax.rem(t, BLK)]
            plain = p_ref[jnp.minimum(source, devices * tiles - 1)]
            shared = q_ref[jnp.maximum(source - devices * tiles, 0)]
            tile = jnp.where(source < devices * tiles, plain, shared)
            flat_ref[tile_rows(t), :] = tile.astype(f32)

        def eight(i, _):
            for k in range(8):
                one(first + i * 8 + k)
            return 0

        lax.fori_loop(0, (end - first) // 8, eight, 0)
        for t in range(first + (end - first) // 8 * 8, end):
            one(t)

    def matrix(out_ref, at, height, blocks):
        lay_out(at, at + height * blocks)
        for j in range(blocks):
            for o in range(0, height, 256):
                out_ref[o : o + 256, j * BLK : (j + 1) * BLK] = flat_ref[
                    pl.ds(at + o * blocks + j, 256, stride=blocks), :
                ].astype(bf16)

    group = lane_group()
    square_ref = R["square"]
    lat_w, s1_w, s2_w, s3_w = R["lat_w"], R["s1_w"], R["s2_w"], R["s3_w"]
    f1_w, f2_w, f3_w, vec_ref = R["f1_w"], R["f2_w"], R["f3_w"], R["vec"]

    def spread_rows(at, height):
        for r in range(GROUPS):
            part = jnp.where(group == r, flat_ref[at : at + height // GROUPS, :], 0.0)
            square_ref[pl.ds(r, height // GROUPS, stride=GROUPS), :] = fold_lanes(part)
        return square_ref[:height, :]

    def fast_weights():
        lay_out(AT_F1, AT_LAT)
        for k in range(3):
            tap = flat_ref[pl.ds(AT_F1 + k, B_FAST, stride=3), :].astype(bf16)
            for g in range(GROUPS):
                f1_w[g * B_FAST : (g + 1) * B_FAST, k * BLK : (k + 1) * BLK] = tap
        two = spread_rows(AT_F2, B_FAST)
        for g in range(GROUPS):
            f2_w[g * B_FAST : (g + 1) * B_FAST, :] = jnp.where(group == g, two, 0.0).astype(bf16)
        f3_w[...] = spread_rows(AT_F3, C_FAST).astype(bf16)

    matrix(lat_w, AT_LAT, C_LAT, 5)
    lay_out(AT_VEC, NBLK)
    vec_ref[...] = flat_ref[AT_VEC : AT_VEC + 32, :]

    x_gather.finish()
    zb, latb, s1b, s2b, da1, da2 = (R[n] for n in ("zb", "latb", "s1b", "s2b", "da1", "da2"))
    c1, c2, c3, e, e3 = (R[n] for n in ("c1", "c2", "c3", "e", "e3"))
    a1p, a2p, h1p, h2p, d1p, d2p, ep, a3, e3f = (
        R[n] for n in ("a1p", "a2p", "h1p", "h2p", "d1p", "d2p", "ep", "a3", "e3f")
    )
    mask_ref, own3_ref, win_ref, st_ref, st16_ref = (
        R[n] for n in ("mask", "own3", "win", "st", "st16")
    )
    ex_send, ex_recv, g_send, g_recv = (R[n] for n in ("ex_send", "ex_recv", "g_send", "g_recv"))
    da3, da3f, dz = sc_ref, fc_ref, s2b

    ex_copies = []

    def stat(which):
        return st_ref.at[which] if which < 12 else st16_ref.at[which - 12]

    def exchange(which):
        own = stat(which).at[p.dp]
        for i in range(1, nd):
            copy = pltpu.make_async_remote_copy(
                src_ref=own,
                dst_ref=own,
                send_sem=ex_send.at[which, i - 1],
                recv_sem=ex_recv.at[which, i - 1],
                device_id=peers[i - 1],
                device_id_type=MESH,
            )
            copy.start()
            ex_copies.append(copy)

    def exchanged(which):
        buffer = stat(which)
        for i in range(1, nd):
            arrived(buffer.at[lax.rem(p.dp + nd - i, nd)], ex_recv.at[which, i - 1])
        ref, at = (st_ref, which) if which < 12 else (st16_ref, which - 12)
        total = ref[at, 0]
        for i in range(1, nd):
            total = total + ref[at, i]
        return total

    def put(which, at, vector):
        ref = stat(which)
        for j in range(vector.shape[1] // BLK):
            ref[p.dp, at + j : at + j + 1, :] = vector[:, j * BLK : (j + 1) * BLK]

    def row_of(block, at, n):
        return jnp.concatenate([block[at + j : at + j + 1, :] for j in range(n)], 1)

    def vectors(place):
        g, b, n = place
        return row_of(vec_ref[...], g, n), row_of(vec_ref[...], b, n)

    def rows_at(i, size):
        return pl.ds(pl.multiple_of(i * size, size), size)

    def mask_at(i, width):
        part = mask_ref[pl.ds(pl.multiple_of(lax.rem(i * RC, POS), RC), RC), :]
        return jnp.concatenate([part] * (width // BLK), 1) if width > BLK else part

    def eights(v):
        return jnp.sum(v.reshape(v.shape[0] // 8, 8, v.shape[1]), 0)

    def total_row(v):
        return jnp.sum(v, 0, keepdims=True)

    def affine(sums, squares, count, gain, bias):
        mean = sums / count
        scale = lax.rsqrt(squares / count - mean * mean + norm_eps)
        grow = gain * scale
        return mean, scale, grow, bias - mean * grow

    def sums_of(ref, n_rows, width):
        def body(i, acc):
            v = ref[rows_at(i, RC), :].astype(f32)
            return acc[0] + eights(v), acc[1] + eights(v * v)

        zero = jnp.zeros((8, width), f32)
        one, two = lax.fori_loop(0, n_rows // RC, body, (zero, zero))
        return total_row(one), total_row(two)

    def activate(src, dst, n_rows, width, grow, base):
        def body(i, _):
            at = rows_at(i, RC)
            pre = src[at, :].astype(f32) * grow + base
            dst[at, :] = (gelu(pre) * mask_at(i, width)).astype(bf16)
            return 0

        lax.fori_loop(0, n_rows // RC, body, 0)

    def slopes(src, incoming, n_rows, width, norm):
        mean, scale, grow, base = norm

        def body(i, acc):
            at = rows_at(i, RC)
            a = src[at, :].astype(f32)
            d = gelu_slope(a * grow + base) * incoming[at, :] * mask_at(i, width)
            incoming[at, :] = d
            return acc[0] + eights(d), acc[1] + eights(d * ((a - mean) * scale))

        zero = jnp.zeros((8, width), f32)
        one, two = lax.fori_loop(0, n_rows // RC, body, (zero, zero))
        return total_row(one), total_row(two)

    def back_vectors(bias_sum, gain_sum, count, norm):
        mean, scale, grow, base = norm
        k1 = grow * gain_sum / count
        return grow * bias_sum / count - k1 * (mean * scale), k1 * scale

    def raw_grads(src, pres, dst, n_rows, width, norm, q0, q1):
        grow = norm[2]

        def body(i, _):
            at = rows_at(i, RC)
            a = src[at, :].astype(f32)
            da = grow * pres[at, :] - mask_at(i, width) * (q0 + a * q1)
            dst[at, :] = da.astype(bf16)
            return 0

        lax.fori_loop(0, n_rows // RC, body, 0)

    def put_vector(row, vector):
        for j in range(vector.shape[1] // BLK):
            at = AT_VEC + row + j
            flat_ref[at : at + 1, :] = vector[:, j * BLK : (j + 1) * BLK]

    deliveries = []

    def deliver(source, name):
        copy = pltpu.make_async_copy(
            source, R["out:" + name], R["local"].at[len(local_copies) + len(deliveries)]
        )
        copy.start()
        deliveries.append(copy)

    def put_frame(name, target, block):
        for h in range(halves):
            target[pl.ds(h, C_FAST, stride=halves), :] = block[h * BLK : (h + 1) * BLK, :].T
        deliver(target, name)

    def put_slow(target, s, block):
        for h in range(halves):
            target[pl.ds(s * halves + h, share, stride=slow_frames * halves), :] = to_channels(
                block[h * BLK : (h + 1) * BLK, :]
            )

    def frame(ref, s):
        return ref[s * POS : (s + 1) * POS, :]

    for s in range(slow_frames):
        window = jnp.concatenate([frame(xt_ref, 4 * s + k) for k in range(5)], 1)
        zb[s * POS : (s + 1) * POS, :] = dot_nt(window, lat_w[...]).astype(bf16)
    one, two = sums_of(zb, slow_rows, C_LAT)
    put(EX_LAT, 0, one)
    put(EX_LAT, 2, two)
    st_ref[EX_LAT, p.dp, 4:8, :] = jnp.full((4, BLK), area, f32)
    exchange(EX_LAT)

    fast_weights()

    def first(j, _):
        total = jnp.zeros((POS, BLK), f32)
        for g in range(GROUPS):
            at = (g * per_group + j + 1) * POS
            window = jnp.concatenate(
                [xt_ref[pl.ds(pl.multiple_of(at + k * POS, POS), POS), :] for k in range(3)], 1
            )
            total = total + jnp.where(group == g, dot_nt(window, f1_w[...]), 0.0)
        a1p[rows_at(j, POS), :] = total
        return 0

    lax.fori_loop(0, per_group, first, 0)
    one, two = sums_of(a1p, group_rows, BLK)
    put(EX_F1, 0, fold_lanes(one))
    put(EX_F1, 1, fold_lanes(two))
    st_ref[EX_F1, p.dp, 2:8, :] = jnp.full((6, BLK), area, f32)
    exchange(EX_F1)

    matrix(s1_w, AT_S1, B_SLOW, 10)
    xs_gather.finish()
    if not keep:
        from_natural(R["out:natural_x"], xs_ref)

    for s in range(slow_frames):
        c1[s * POS : (s + 1) * POS, :] = dot_nt(frame(xs_ref, s), s1_w[:, :C_SLOW])

    total = exchanged(EX_LAT)
    area_all = total[4:5, :]
    slow_count = jnp.concatenate([area_all * float(slow_frames)] * 2, 1)
    slow_count8 = jnp.concatenate([slow_count] * 4, 1)
    fast_count = area_all * float(frames)
    lat_norm = affine(row_of(total, 0, 2), row_of(total, 2, 2), slow_count, *vectors(V_LAT))
    activate(zb, latb, slow_rows, C_LAT, lat_norm[2], lat_norm[3])
    for s in range(slow_frames):
        at = slice(s * POS, (s + 1) * POS)
        c1[at, :] = c1[at, :] + dot_nt(latb[at, :], s1_w[:, C_SLOW:])
    one, two = sums_of(c1, slow_rows, B_SLOW)
    put(EX_S1, 0, one)
    put(EX_S1, 2, two)
    st_ref[EX_S1, p.dp, 4:8, :] = jnp.zeros((4, BLK), f32)
    exchange(EX_S1)

    matrix(s2_w, AT_S2, B_SLOW, 6)

    packed = vec_ref[0:1, :]

    def spread(which):
        return fold_lanes(jnp.where(group == which, packed, 0.0))

    def exchanged_two(which):
        total = exchanged(which)
        return total[0:1, :], total[1:2, :]

    f1_norm = affine(*exchanged_two(EX_F1), fast_count, spread(0), spread(1))
    activate(a1p, h1p, group_rows, BLK, f1_norm[2], f1_norm[3])
    for j in range(per_group):
        a2p[j * POS : (j + 1) * POS, :] = dot_nt(frame(h1p, j), f2_w[...])
    one, two = sums_of(a2p, group_rows, BLK)
    put(EX_F2, 0, fold_lanes(one))
    put(EX_F2, 1, fold_lanes(two))
    st_ref[EX_F2, p.dp, 2:8, :] = jnp.zeros((6, BLK), f32)
    exchange(EX_F2)
    fc_gather.relay()

    total = exchanged(EX_S1)
    s1_norm = affine(row_of(total, 0, 2), row_of(total, 2, 2), slow_count, *vectors(V_S1))
    activate(c1, s1b, slow_rows, B_SLOW, s1_norm[2], s1_norm[3])
    for s in range(slow_frames):
        low, high = max(0, 1 - s), min(3, slow_frames - s + 1)
        window = jnp.concatenate([frame(s1b, s + k - 1) for k in range(low, high)], 1)
        c2[s * POS : (s + 1) * POS, :] = dot_nt(window, s2_w[:, low * B_SLOW : high * B_SLOW])
    one, two = sums_of(c2, slow_rows, B_SLOW)
    put(EX_S2, 0, one)
    put(EX_S2, 2, two)
    st_ref[EX_S2, p.dp, 4:8, :] = jnp.zeros((4, BLK), f32)
    exchange(EX_S2)

    matrix(s3_w, AT_S3, C_SLOW, 2)

    f2_norm = affine(*exchanged_two(EX_F2), fast_count, spread(2), spread(3))
    activate(a2p, h2p, group_rows, BLK, f2_norm[2], f2_norm[3])
    for g in range(GROUPS):

        def third(j, _, g=g):
            part = jnp.where(group == g, h2p[rows_at(j, POS), :], 0.0).astype(bf16)
            a3[rows_at(g * per_group + j, POS), :] = dot_nt(part, f3_w[...])
            return 0

        lax.fori_loop(0, per_group, third, 0)
    one, two = sums_of(a3, fast_rows, BLK)
    put(EX_F3, 0, one)
    put(EX_F3, 1, two)
    st_ref[EX_F3, p.dp, 2:8, :] = jnp.zeros((6, BLK), f32)
    exchange(EX_F3)
    sc_gather.relay()

    total = exchanged(EX_S2)
    s2_norm = affine(row_of(total, 0, 2), row_of(total, 2, 2), slow_count, *vectors(V_S2))
    activate(c2, s2b, slow_rows, B_SLOW, s2_norm[2], s2_norm[3])
    quarter = C_SLOW // 4
    for n in range(4):
        lanes = slice(n * quarter, (n + 1) * quarter)
        for s in range(slow_frames):
            c3[s * POS : (s + 1) * POS, lanes] = dot_nt(frame(s2b, s), s3_w[lanes, :])
        one, two = sums_of(c3.at[:, lanes], slow_rows, quarter)
        put(EX_S3, 2 * n, one)
        put(EX_S3, 8 + 2 * n, two)
    exchange(EX_S3)

    f3_norm = affine(*exchanged_two(EX_F3), fast_count, *vectors(V_F3))
    fc_gather.finish()
    own = a3[rows_at(p.mp, POS), :] * f3_norm[2] + f3_norm[3]
    own = own + xt_ref[rows_at(p.mp + 2, POS), :].astype(f32)
    put_frame("fast_out", R["out_fast"], gelu(own) * mask_ref[...])

    def fast_slopes(i, acc):
        mean, scale, grow, base = f3_norm
        at = rows_at(i, RC)
        a = a3[at, :]
        x = xt_ref[pl.ds(pl.multiple_of(i * RC + 2 * POS, RC), RC), :].astype(f32)
        d = gelu_slope(a * grow + base + x) * fc_ref[at, :].astype(f32)
        e3f[at, :] = d
        return acc[0] + eights(d), acc[1] + eights(d * ((a - mean) * scale))

    zero = jnp.zeros((8, BLK), f32)
    one, two = lax.fori_loop(0, fast_rows // RC, fast_slopes, (zero, zero))
    one, two = total_row(one), total_row(two)
    put(EX_BF3, 0, one)
    put(EX_BF3, 1, two)
    st_ref[EX_BF3, p.dp, 2:8, :] = jnp.zeros((6, BLK), f32)
    exchange(EX_BF3)
    put_vector(V_F3[0], two)
    put_vector(V_F3[1], one)

    sc_gather.finish()
    out.drain()
    if not keep:
        from_natural(R["out:natural_c"], sc_ref)
    total = exchanged(EX_S3)
    s3_norm = affine(row_of(total, 0, 8), row_of(total, 8, 8), slow_count8, *vectors(V_S3))

    def slope_three(at, lanes, norm):
        a = c3[at, lanes]
        pre = a * norm[2] + norm[3] + xs_ref[at, lanes].astype(f32)
        return a, gelu_slope(pre) * sc_ref[at, lanes].astype(f32)

    for n in range(4):
        lanes = slice(n * quarter, (n + 1) * quarter)
        norm = [v[:, lanes] for v in s3_norm]

        def slow_slopes(i, acc, lanes=lanes, norm=norm):
            at = rows_at(i, RC)
            a, d = slope_three(at, lanes, norm)
            if keep:
                e3[at, lanes] = d
            return acc[0] + eights(d), acc[1] + eights(d * ((a - norm[0]) * norm[1]))

        zero = jnp.zeros((8, quarter), f32)
        one, two = lax.fori_loop(0, slow_rows // RC, slow_slopes, (zero, zero))
        one, two = total_row(one), total_row(two)
        put(EX_BS3, 2 * n, one)
        put(EX_BS3, 8 + 2 * n, two)
        put_vector(V_S3[0] + 2 * n, two)
        put_vector(V_S3[1] + 2 * n, one)
    exchange(EX_BS3)

    first_channel = p.mp * share
    at_lane = pl.ds(pl.multiple_of(first_channel // BLK * BLK, BLK), BLK)
    lane_shift = lax.rem(first_channel, BLK)
    own_rows = first_channel // BLK
    own_norm = [
        sum(
            jnp.where(own_rows == j, v[:, j * BLK : (j + 1) * BLK], 0.0)
            for j in range(C_SLOW // BLK)
        )
        for v in s3_norm
    ]

    def to_channels(block):
        turned = block.T
        if share == BLK:
            return turned
        return sum(
            jnp.where(lane_shift == k * share, turned[k * share : (k + 1) * share, :], 0.0)
            for k in range(BLK // share)
        )

    for s in range(slow_frames):
        at = slice(s * POS, (s + 1) * POS)
        pre = c3[at, at_lane] * own_norm[2] + own_norm[3] + xs_ref[at, at_lane].astype(f32)
        put_slow(R["out_slow"], s, gelu(pre) * mask_ref[...])
        own3_ref[at, :] = gelu_slope(pre) * sc_ref[at, at_lane].astype(f32)
    deliver(R["out_slow"], "slow_out")

    q0, q1 = back_vectors(*exchanged_two(EX_BF3), fast_count, f3_norm)
    raw_grads(a3, e3f, da3f, fast_rows, BLK, f3_norm, q0, q1)
    for j in range(per_group):
        total = jnp.zeros((POS, BLK), f32)
        for g in range(GROUPS):
            part = dot_nn(frame(da3f, g * per_group + j), f3_w[...])
            total = total + jnp.where(group == g, part, 0.0)
        ep[j * POS : (j + 1) * POS, :] = total
    one, two = slopes(a2p, ep, group_rows, BLK, f2_norm)
    put(EX_BF2, 0, fold_lanes(one))
    put(EX_BF2, 1, fold_lanes(two))
    st_ref[EX_BF2, p.dp, 2:8, :] = jnp.zeros((6, BLK), f32)
    exchange(EX_BF2)
    vec_two = jnp.where(group == 2, fold_lanes(two), 0.0)
    vec_two = vec_two + jnp.where(group == 3, fold_lanes(one), 0.0)

    total = exchanged(EX_BS3)
    q0, q1 = back_vectors(row_of(total, 0, 8), row_of(total, 8, 8), slow_count8, s3_norm)
    for n in range(4):
        lanes = slice(n * quarter, (n + 1) * quarter)
        norm = [v[:, lanes] for v in s3_norm]
        q0n, q1n = q0[:, lanes], q1[:, lanes]

        def raw_three(i, _, lanes=lanes, norm=norm, q0n=q0n, q1n=q1n):
            at = rows_at(i, RC)
            if keep:
                a, d = c3[at, lanes], e3[at, lanes]
            else:
                a, d = slope_three(at, lanes, norm)
            da = norm[2] * d - mask_at(i, quarter) * (q0n + a * q1n)
            da3[at, lanes] = da.astype(bf16)
            return 0

        lax.fori_loop(0, slow_rows // RC, raw_three, 0)
    for s in range(slow_frames):
        at = slice(s * POS, (s + 1) * POS)
        e[at, :] = dot_nn(da3[at, :], s3_w[...])
    one, two = slopes(c2, e, slow_rows, B_SLOW, s2_norm)
    put(EX_B2, 0, one)
    put(EX_B2, 2, two)
    st_ref[EX_B2, p.dp, 4:8, :] = jnp.zeros((4, BLK), f32)
    exchange(EX_B2)
    put_vector(V_S2[0], two)
    put_vector(V_S2[1], one)

    def to_flat(at, blocks, offset, tall, lane, value):
        flat_ref[pl.ds(at + offset * blocks + lane, tall, stride=blocks), :] = value

    for n in range(4):
        part = dot_tn(da3[:, n * quarter : (n + 1) * quarter], s2b[...])
        for j in range(2):
            to_flat(AT_S3, 2, n * quarter, quarter, j, part[:, j * BLK : (j + 1) * BLK])

    q0, q1 = back_vectors(*exchanged_two(EX_BF2), fast_count, f2_norm)
    raw_grads(a2p, ep, d2p, group_rows, BLK, f2_norm, q0, q1)
    for j in range(per_group):
        ep[j * POS : (j + 1) * POS, :] = dot_nn(frame(d2p, j), f2_w[...])
    one, two = slopes(a1p, ep, group_rows, BLK, f1_norm)
    put(EX_BF1, 0, fold_lanes(one))
    put(EX_BF1, 1, fold_lanes(two))
    st_ref[EX_BF1, p.dp, 2:8, :] = jnp.zeros((6, BLK), f32)
    exchange(EX_BF1)
    vec_one = jnp.where(group == 0, fold_lanes(two), 0.0)
    vec_one = vec_one + jnp.where(group == 1, fold_lanes(one), 0.0)
    put_vector(0, vec_one + vec_two)

    total = exchanged(EX_B2)
    q0, q1 = back_vectors(row_of(total, 0, 2), row_of(total, 2, 2), slow_count, s2_norm)
    raw_grads(c2, e, da2, slow_rows, B_SLOW, s2_norm, q0, q1)
    for s in range(slow_frames):
        parts = [
            dot_nn(frame(da2, s - k + 1), s2_w[:, k * B_SLOW : (k + 1) * B_SLOW])
            for k in range(3)
            if 0 <= s - k + 1 < slow_frames
        ]
        e[s * POS : (s + 1) * POS, :] = functools.reduce(lambda u, v: u + v, parts)
    one, two = slopes(c1, e, slow_rows, B_SLOW, s1_norm)
    put(EX_B1, 0, one)
    put(EX_B1, 2, two)
    st_ref[EX_B1, p.dp, 4:8, :] = jnp.zeros((4, BLK), f32)
    exchange(EX_B1)
    put_vector(V_S1[0], two)
    put_vector(V_S1[1], one)

    for k in range(3):
        low, high = max(0, 1 - k), min(slow_frames, slow_frames + 1 - k)
        part = dot_tn(
            da2[low * POS : high * POS, :], s1b[(low + k - 1) * POS : (high + k - 1) * POS, :]
        )
        for j in range(2):
            to_flat(AT_S2, 6, 0, B_SLOW, 2 * k + j, part[:, j * BLK : (j + 1) * BLK])

    total = jnp.zeros((BLK, BLK), f32)
    for g in range(GROUPS):
        at = slice(g * group_rows, (g + 1) * group_rows)
        total = total + jnp.where(group == g, dot_tn(da3f[at, :], h2p[...]), 0.0)

    def to_blocks(value, at):
        n = value.shape[0] // GROUPS
        square_ref[: value.shape[0], :] = fold_lanes(value)
        flat_ref[at : at + n, :] = sum(
            jnp.where(group == r, square_ref[pl.ds(r, n, stride=GROUPS), :], 0.0)
            for r in range(GROUPS)
        )

    to_blocks(total, AT_F3)
    square = dot_tn(d2p[...], h1p[...])
    to_blocks(
        sum(
            jnp.where(group == g, square[g * B_FAST : (g + 1) * B_FAST, :], 0.0)
            for g in range(GROUPS)
        ),
        AT_F2,
    )

    total = exchanged(EX_B1)
    q0, q1 = back_vectors(row_of(total, 0, 2), row_of(total, 2, 2), slow_count, s1_norm)
    raw_grads(c1, e, da1, slow_rows, B_SLOW, s1_norm, q0, q1)
    for s in range(slow_frames):
        at = slice(s * POS, (s + 1) * POS)
        e[at, :] = dot_nn(da1[at, :], s1_w[:, C_SLOW:])
    one, two = slopes(zb, e, slow_rows, C_LAT, lat_norm)
    put(EX_BLAT, 0, one)
    put(EX_BLAT, 2, two)
    st_ref[EX_BLAT, p.dp, 4:8, :] = jnp.zeros((4, BLK), f32)
    exchange(EX_BLAT)
    put_vector(V_LAT[0], two)
    put_vector(V_LAT[1], one)

    for s in range(slow_frames):
        at = slice(s * POS, (s + 1) * POS)
        value = own3_ref[at, :] + dot_nn(da1[at, :], s1_w[:, at_lane])
        put_slow(R["out_sgrad"], s, value * mask_ref[...])
    deliver(R["out_sgrad"], "slow_grad")

    q0, q1 = back_vectors(*exchanged_two(EX_BF1), fast_count, f1_norm)
    raw_grads(a1p, ep, d1p, group_rows, BLK, f1_norm, q0, q1)
    for k in range(3):
        tap = jnp.zeros((B_FAST, BLK), f32)
        for g in range(GROUPS):
            at = (g * per_group + k + 1) * POS
            part = dot_tn(d1p[...], xt_ref[at : at + group_rows, :])
            tap = tap + part[g * B_FAST : (g + 1) * B_FAST, :]
        to_flat(AT_F1, 3, 0, B_FAST, k, tap)

    for n in range((C_SLOW + C_LAT) // quarter):
        if n < 4:
            right = xs_ref[:, n * quarter : (n + 1) * quarter]
        else:
            right = latb[...]
        part = dot_tn(da1[...], right)
        for j in range(2):
            to_flat(AT_S1, 10, 0, B_SLOW, 2 * n + j, part[:, j * BLK : (j + 1) * BLK])

    near_grad = e3f[rows_at(p.mp, POS), :]
    for k in range(3):
        f = p.mp - k + 1
        there = (f >= 0) & (f < frames)
        g, j = f // per_group, lax.rem(f, per_group)
        g, j = jnp.where(there, g, 0), jnp.where(there, j, 0)
        left = jnp.where((group == g) & there, d1p[rows_at(j, POS), :], 0.0).astype(bf16)
        near_grad = near_grad + dot_nn(left, f1_w[:, k * BLK : (k + 1) * BLK])

    total = exchanged(EX_BLAT)
    q0, q1 = back_vectors(row_of(total, 0, 2), row_of(total, 2, 2), slow_count, lat_norm)
    raw_grads(zb, e, dz, slow_rows, C_LAT, lat_norm, q0, q1)
    for k in range(5):
        tap = functools.reduce(
            lambda u, v: u + v,
            [dot_tn(frame(dz, s), frame(xt_ref, 4 * s + k)) for s in range(slow_frames)],
        )
        to_flat(AT_LAT, 5, 0, C_LAT, k, tap)

    height = up(slots, 16)
    g_copies = []

    def start_of(device):
        def one(k, found):
            return jnp.where(run_device[k] == device, run_start[k], found)

        return lax.fori_loop(0, devices, one, jnp.int32(0))

    def window_of(device):
        return flat_ref[pl.ds(start_of(device), height), :]

    for i in range(1, nd):
        peer = lax.rem(p.dp + i, nd)
        win_ref[0, i - 1] = window_of(peer * nm + p.mp).astype(bf16)
        copy = pltpu.make_async_remote_copy(
            src_ref=win_ref.at[0, i - 1],
            dst_ref=win_ref.at[1, i - 1],
            send_sem=g_send.at[i - 1],
            recv_sem=g_recv.at[i - 1],
            device_id=peers[i - 1],
            device_id_type=MESH,
        )
        copy.start()
        g_copies.append(copy)

    later = lax.rem(p.mp + 2, 4)
    s = (p.mp + 2) // 4
    for tap, at, there in (
        (later, s, s < slow_frames),
        (later + 4, s - 1, (later == 0) & (s > 0)),
    ):
        tap, at = jnp.where(there, tap, 0), jnp.where(there, at, 0)
        left = jnp.where(there, dz[rows_at(at, POS), :], 0.0).astype(bf16)
        weight = lat_w[:, pl.ds(pl.multiple_of(tap * BLK, BLK), BLK)]
        near_grad = near_grad + dot_nn(left, weight)
    put_frame("fast_grad", R["out_fgrad"], near_grad * mask_ref[...])

    total = window_of(me)
    for i in range(1, nd):
        arrived(win_ref.at[1, i - 1], g_recv.at[i - 1])
        total = total + win_ref[1, i - 1].astype(f32)
    R["out_grad"][...] = total
    deliver(R["out_grad"], "grad")
    for copy in ex_copies + g_copies:
        copy.wait_send()
    for copy in deliveries:
        copy.wait()


def call_main(cfg, crop, owner, padded, master, fast, slow, fcot, scot):
    smem = pl.BlockSpec(memory_space=pltpu.SMEM)
    hbm = pl.BlockSpec(memory_space=pltpu.HBM)
    outs = outputs(cfg)
    return pl.pallas_call(
        functools.partial(main_kernel, cfg),
        out_shape=tuple(jax.ShapeDtypeStruct(s, t) for _, s, t in outs),
        in_specs=[smem] + [hbm] * 7,
        out_specs=tuple(hbm for _ in outs),
        scratch_shapes=[s for _, s in scratch(cfg)],
        compiler_params=pltpu.CompilerParams(
            collective_id=0, has_side_effects=True, vmem_limit_bytes=62 << 20
        ),
        name="block",
    )(crop, owner, padded, master, fast, slow, fcot, scot)[:5]


def adam_kernel(
    cfg, owner_ref, grad, master, one, two, a_in, b_in, c_in, d_in,
    w_out, one_out, two_out, low_out, a_out, b_out, c_out, d_out, sems
):
    nd, nm, frames, slow_frames, share, slots = cfg
    copies = [
        pltpu.make_async_copy(source, target, sems.at[i])
        for i, (source, target) in enumerate(
            ((a_in, a_out), (b_in, b_out), (c_in, c_out), (d_in, d_out))
        )
    ]
    for copy in copies:
        copy.start()
    me = lax.axis_index("dp") * nm + lax.axis_index("mp")
    spot = lax.broadcasted_iota(jnp.int32, (8, BLK), 0) * BLK
    spot = spot + lax.broadcasted_iota(jnp.int32, (8, BLK), 1)
    lowest = jnp.full((8, BLK), NBLK, jnp.int32)
    number = jnp.zeros((8, BLK), jnp.int32)
    for i in range(up(NBLK, 1024) // 1024):
        block = spot + i * 1024
        mine = (owner_ref[i * 8 : (i + 1) * 8, :] == me) & (block < NBLK)
        lowest = jnp.minimum(lowest, jnp.where(mine, block, NBLK))
        number = number + jnp.where(mine, 1, 0)
    start, count = jnp.min(lowest), jnp.sum(number)
    row = lax.broadcasted_iota(jnp.int32, (slots, BLK), 0)
    living = row < count
    block = row + start
    rate = jnp.full((slots, BLK), 0.2, f32)
    for at, width in (
        (AT_VEC, B_SLOW),
        (AT_S3, 3 * B_SLOW),
        (AT_S2, C_SLOW + C_LAT),
        (AT_S1, 5 * C_FAST),
        (AT_LAT, B_FAST),
        (AT_F2, 3 * C_FAST),
    ):
        rate = jnp.where(block < at, 0.5 / math.sqrt(width), rate)
    decay = jnp.where(block < AT_VEC, decay_rate, 0.0)
    g = grad[:slots, :]
    first = beta_first * one[...] + (1.0 - beta_first) * g
    second = beta_second * two[...] + (1.0 - beta_second) * g * g
    lift_one = 1.0 - beta_first**STEP
    lift_two = 1.0 - beta_second**STEP
    update = first / lift_one / (jnp.sqrt(second / lift_two) + adam_eps)
    weight = master[...]
    weight = jnp.where(living, weight - rate * (update + decay * weight), 0.0)
    w_out[...] = weight
    one_out[...] = jnp.where(living, first, 0.0)
    two_out[...] = jnp.where(living, second, 0.0)
    low_out[...] = weight.astype(bf16)
    for copy in copies:
        copy.wait()


def call_adam(cfg, owner, grad, master, one, two, passed):
    shape = master.shape
    vmem = pl.BlockSpec(memory_space=pltpu.VMEM)
    hbm = pl.BlockSpec(memory_space=pltpu.HBM)
    return pl.pallas_call(
        functools.partial(adam_kernel, cfg),
        out_shape=tuple(jax.ShapeDtypeStruct(shape, t) for t in (f32, f32, f32, bf16))
        + tuple(jax.ShapeDtypeStruct(a.shape, a.dtype) for a in passed),
        in_specs=[vmem] * 5 + [hbm] * 4,
        out_specs=(vmem,) * 4 + (hbm,) * 4,
        scratch_shapes=[pltpu.SemaphoreType.DMA((4,))],
        compiler_params=pltpu.CompilerParams(vmem_limit_bytes=32 << 20),
        name="adam",
    )(owner, grad, master, one, two, *passed)


def solution(mesh):
    nd, nm = mesh.shape["dp"], mesh.shape["mp"]

    def local(fast_in, slow_in, fast_cot, slow_cot, crop, owner, master, one, two):
        share, slow_frames = slow_in.shape[0], slow_in.shape[1]
        cfg = (nd, nm, fast_in.shape[1] * nm, slow_frames, share, master.shape[0])

        def halves(array):
            split = array.reshape(share, slow_frames, POS // BLK, BLK)
            return split.transpose(0, 2, 1, 3).reshape(-1, BLK)

        padded = jnp.pad(owner, (0, up(NBLK, 1024) - NBLK)).reshape(-1, BLK)
        *passed, grad = call_main(
            cfg,
            crop,
            owner,
            padded,
            master,
            fast_in.reshape(C_FAST, POS),
            halves(slow_in),
            fast_cot.reshape(C_FAST, POS),
            halves(slow_cot),
        )
        new = call_adam(cfg, padded, grad, master, one, two, passed)
        return (
            new[4].reshape(fast_in.shape),
            new[5].reshape(slow_in.shape),
            new[6].reshape(fast_in.shape),
            new[7].reshape(slow_in.shape),
            *new[:4],
        )

    return jax.shard_map(
        local,
        mesh=mesh,
        in_specs=(
            P(None, "mp", "dp", None),
            P("mp", None, "dp", None),
            P(None, "mp", "dp", None),
            P("mp", None, "dp", None),
            P("dp"),
            P(),
            P(("dp", "mp"), None),
            P(("dp", "mp"), None),
            P(("dp", "mp"), None),
        ),
        out_specs=(
            P(None, "mp", "dp", None),
            P("mp", None, "dp", None),
            P(None, "mp", "dp", None),
            P("mp", None, "dp", None),
            P(("dp", "mp"), None),
            P(("dp", "mp"), None),
            P(("dp", "mp"), None),
            P(("dp", "mp"), None),
        ),
        check_vma=False,
    )
```

```python
import functools
import math
import types

import jax
import jax.numpy as jnp
from jax import lax
from jax.experimental import pallas as pl
from jax.experimental.pallas import tpu as pltpu
from jax.sharding import PartitionSpec as P

C_FAST = 128
B_FAST = 32
C_SLOW = 1024
B_SLOW = 256
C_LAT = 256
TILE = 16
POS = TILE * TILE
BLK = 128
STEP = 10
NBLK = 7591

norm_eps = 1e-05
beta_first = 0.5
beta_second = 0.5
adam_eps = 1e-08
decay_rate = 0.05

MESH = pl.DeviceIdType.MESH
f32 = jnp.float32
bf16 = jnp.bfloat16
RC = 32
CH = 256
GROUPS = BLK // B_FAST
COLUMNS = 2
HALF = POS // COLUMNS
SLABS = C_SLOW // BLK

AT_F1 = 0
AT_F2 = AT_F1 + B_FAST * 3 * C_FAST // BLK
AT_F3 = AT_F2 + B_FAST * B_FAST // BLK
AT_LAT = AT_F3 + C_FAST * B_FAST // BLK
AT_S1 = AT_LAT + C_LAT * 5 * C_FAST // BLK
AT_S2 = AT_S1 + B_SLOW * (C_SLOW + C_LAT) // BLK
AT_S3 = AT_S2 + B_SLOW * 3 * B_SLOW // BLK
AT_VEC = AT_S3 + C_SLOW * B_SLOW // BLK
V_F3 = (1, 2, 1)
V_LAT = (3, 5, 2)
V_S1 = (7, 9, 2)
V_S2 = (11, 13, 2)
V_S3 = (15, 23, 8)


def up(n, m):
    return (n + m - 1) // m * m


def dot_nt(a, b):
    return lax.dot_general(a, b, (((1,), (1,)), ((), ())), preferred_element_type=f32)


def dot_tn(a, b):
    return lax.dot_general(a, b, (((0,), (0,)), ((), ())), preferred_element_type=f32)


def dot_nn(a, b):
    return lax.dot_general(a, b, (((1,), (0,)), ((), ())), preferred_element_type=f32)


G0 = math.sqrt(2.0 / math.pi)
G1 = 0.044715


def gelu(x):
    t = jnp.tanh(x * (G0 + (G0 * G1) * (x * x)))
    return 0.5 * x * (1.0 + t)


def gelu_slope(x):
    xx = x * x
    t = jnp.tanh(x * (G0 + (G0 * G1) * xx))
    return 0.5 * (1.0 + t) + (0.5 * x) * (1.0 - t * t) * (G0 + (3.0 * G0 * G1) * xx)


def position_mask(crop):
    spot = lax.broadcasted_iota(jnp.int32, (POS, BLK), 0)
    inside = (spot // TILE < crop) & (lax.rem(spot, TILE) < crop)
    return jnp.where(inside, 1.0, 0.0).astype(f32)


def lane_group():
    return lax.broadcasted_iota(jnp.int32, (1, BLK), 1) // B_FAST


def fold_lanes(v):
    v = v + pltpu.roll(v, B_FAST, 1)
    return v + pltpu.roll(v, 2 * B_FAST, 1)


def remote(source, target, send_sem, recv_sem, device):
    pltpu.make_async_remote_copy(
        src_ref=source,
        dst_ref=target,
        send_sem=send_sem,
        recv_sem=recv_sem,
        device_id=device,
        device_id_type=MESH,
    ).start()


def arrived(view, sem):
    pltpu.make_async_copy(view, view, sem).wait()


class Place:
    def __init__(self, nd, nm):
        self.nd, self.nm = nd, nm
        self.nx = nd // 2
        self.nb = COLUMNS
        self.na = nm // self.nb
        self.dp = lax.axis_index("dp")
        self.mp = lax.axis_index("mp")
        self.x, self.c = self.dp // 2, lax.rem(self.dp, 2)
        self.a, self.b = self.mp // self.nb, lax.rem(self.mp, self.nb)

    def off_a(self, i):
        return lax.rem(self.a + i, self.na)

    def off_b(self, i):
        return lax.rem(self.b + i, self.nb)

    def off_x(self, i):
        return lax.rem(self.x + i, self.nx)

    def dev(self, x, c, a, b):
        return (x * 2 + c, a * self.nb + b)

    def slot(self, x, c, a, b):
        return (x * 2 + c) * self.nm + a * self.nb + b


class Gather:
    def __init__(self, place, slabs, other, skip, send, near, far):
        self.p, self.slabs, self.other, self.skip = place, slabs, other, skip
        self.sems = send, near, far

    def view(self, rank):
        return self.slabs.at[rank + self.skip]

    def along(self, rank):
        p, (send, near, far) = self.p, self.sems
        for i in range(1, p.na):
            device = (p.dp, p.off_a(i) * p.nb + p.b)
            remote(self.view(rank), self.view(rank), send, far, device)

    def start(self):
        p, (send, near, far) = self.p, self.sems
        remote(self.other, self.view(p.mp), send, near, (p.dp, p.a * p.nb + p.off_b(1)))
        self.along(p.mp)

    def relay(self):
        p, (send, near, far) = self.p, self.sems
        rank = p.a * p.nb + p.off_b(1)
        arrived(self.view(rank), near)
        self.along(rank)

    def finish(self):
        arrived(self.slabs.at[pl.ds(0, (self.p.na - 1) * self.p.nb)], self.sems[2])

    def drain(self):
        arrived(self.slabs.at[pl.ds(0, self.p.nm - 1)], self.sems[0])


EX_LAT, EX_S1, EX_S2, EX_B2, EX_B1, EX_BLAT = range(6)
EX_F1, EX_F2, EX_F3, EX_BF3, EX_BF2, EX_BF1 = range(6, 12)
EX_S3, EX_BS3 = 12, 13
EXCHANGES = 14

FAST_OUT, SLOW_OUT, FAST_GRAD, SLOW_GRAD = range(4)
SENT, MINE, GOT = range(3)


def outputs(cfg):
    nd, nm, frames, slow_frames, share, slots = cfg
    halves = POS // BLK
    fast, slow = (C_FAST * halves, BLK), (share * slow_frames * halves, BLK)
    result = [(fast, f32), (slow, f32), (fast, f32), (slow, f32), ((up(slots, 16), BLK), f32)]
    if share != BLK:
        result += [((nm, share, slow_frames * HALF), bf16)] * 2
    return result


def scratch(cfg):
    nd, nm, frames, slow_frames, share, slots = cfg
    devices, group = nd * nm, nd * COLUMNS
    rows = up(slots + 15, 16)
    height = up(slots, 16)
    halves = POS // BLK
    slow_rows, fast_rows = slow_frames * HALF, frames * HALF
    group_rows = fast_rows // GROUPS
    windows = group // 2
    vmem, smem, dma = pltpu.VMEM, pltpu.SMEM, pltpu.SemaphoreType.DMA
    piece = (slow_rows, BLK) if share == BLK else (share, slow_rows)
    result = dict(
        owner_v=vmem((up(NBLK, 1024) // BLK, BLK), jnp.int32),
        owner_s=smem((NBLK,), jnp.int32),
        run_device=smem((devices,), jnp.int32),
        run_start=smem((devices,), jnp.int32),
        run_count=smem((devices,), jnp.int32),
        table_v=vmem((8, BLK), jnp.int32),
        table_s=smem((8, BLK), jnp.int32),
        shift=vmem((rows + 16, BLK), f32),
        p=vmem((devices * (rows // 16), 16, BLK), bf16),
        q=vmem((devices, 16, BLK), bf16),
        fast_v=vmem((C_FAST, POS), bf16),
        slow_v=vmem((share * slow_frames * halves, BLK), bf16),
        fcot_v=vmem((C_FAST, POS), bf16),
        scot_v=vmem((share * slow_frames * halves, BLK), bf16),
        stage=vmem((share * slow_frames * halves, BLK), f32),
        turned=vmem((POS, BLK), f32),
        x_other=vmem((HALF, BLK), bf16),
        fc_other=vmem((HALF, BLK), bf16),
        xs_other=vmem(piece, bf16),
        sc_other=vmem(piece, bf16),
        xt=vmem((frames + 4, HALF, BLK), bf16),
        xs=vmem((SLABS, slow_rows, BLK), bf16),
        fc=vmem((frames, HALF, BLK), bf16),
        sc=vmem((SLABS, slow_rows, BLK), bf16),
        wide=vmem((slow_rows, 5 * C_FAST), bf16),
        lat_w=vmem((C_LAT, 5 * C_FAST), bf16),
        s1_w=vmem((B_SLOW, C_SLOW + C_LAT), bf16),
        s2_w=vmem((B_SLOW, 3 * B_SLOW), bf16),
        s3_w=vmem((C_SLOW, B_SLOW), bf16),
        f1_w=vmem((BLK, 3 * C_FAST), bf16),
        f2_w=vmem((BLK, BLK), bf16),
        f3_w=vmem((BLK, BLK), bf16),
        vec=vmem((32, BLK), f32),
        mask_all=vmem((POS, BLK), f32),
        mask=vmem((HALF, BLK), f32),
    )
    if share != BLK:
        result.update(
            piece=vmem(piece, bf16),
            turn=vmem((BLK, HALF), bf16),
        )
    result.update(
        zb=vmem((slow_rows, 256), bf16),
        latb=vmem((slow_rows, 256), bf16),
        s2b=vmem((slow_rows, 256), bf16),
        dz=vmem((slow_rows, 256), bf16),
        da1=vmem((slow_rows, 256), bf16),
    )
    result.update(
        two_in=vmem(((slow_frames + 2) * HALF, 256), bf16),
        two_back=vmem(((slow_frames + 2) * HALF, 256), bf16),
        c1=vmem((slow_rows, 256), f32),
        c2=vmem((slow_rows, 256), f32),
        c3=vmem((slow_rows, C_SLOW), f32),
        e=vmem((slow_rows, 256), f32),
        e3=vmem((slow_rows, C_SLOW), f32),
        da3=vmem((slow_rows, C_SLOW), bf16),
        a1p=vmem((group_rows, BLK), f32),
        a2p=vmem((group_rows, BLK), f32),
        h1p=vmem((group_rows, BLK), bf16),
        h2p=vmem((group_rows, BLK), bf16),
        d1p=vmem((group_rows, BLK), bf16),
        d2p=vmem((group_rows, BLK), bf16),
        ep=vmem((group_rows, BLK), f32),
        a3=vmem((fast_rows, BLK), f32),
        e3f=vmem((fast_rows, BLK), f32),
        da3f=vmem((fast_rows, BLK), bf16),
        square=vmem((BLK, BLK), f32),
        flat=vmem((up(NBLK + height, 64), BLK), f32),
        own3=vmem((COLUMNS, slow_rows, BLK), f32),
        sib_out=vmem((windows, height, BLK), bf16),
        sib_in=vmem((windows, height, BLK), bf16),
        far_out=vmem((windows, height, BLK), bf16),
        far_in=vmem((windows, height, BLK), bf16),
        st=vmem((12, group, 8, BLK), f32),
        st16=vmem((2, group, 16, BLK), f32),
    )
    result.update(
        fast_out_box=vmem((3, HALF, BLK), f32),
        slow_out_box=vmem((3, slow_rows, BLK), f32),
        fast_grad_box=vmem((3, HALF, BLK), f32),
        slow_grad_box=vmem((3, slow_rows, BLK), f32),
        fast_out_end=vmem((C_FAST * halves, BLK), f32),
        slow_out_end=vmem((share * slow_frames * halves, BLK), f32),
        fast_grad_end=vmem((C_FAST * halves, BLK), f32),
        slow_grad_end=vmem((share * slow_frames * halves, BLK), f32),
        end_grad=vmem((height, BLK), f32),
        p_send=dma(()),
        p_recv=dma((devices,)),
        gather_sems=dma((4, 3)),
        ex_send=dma((EXCHANGES,)),
        ex_recv=dma((EXCHANGES,)),
        box_send=dma((4,)),
        box_recv=dma((4,)),
        sum_sems=dma((4,)),
        local=dma((16,)),
    )
    return result


def main_kernel(cfg, *refs):
    nd, nm, frames, slow_frames, share, slots = cfg
    n_out = len(outputs(cfg))
    args, results, held = refs[:8], refs[8 : 8 + n_out], refs[8 + n_out :]
    crop_in, owner_in, owners_in, master_in, fast_in, slow_in, fcot_in, scot_in = args
    R = types.SimpleNamespace(**dict(zip(scratch(cfg), held, strict=True)))
    p = Place(nd, nm)
    devices = nd * nm
    halves = POS // BLK
    rows = up(slots + 15, 16)
    tiles = rows // 16
    slow_rows, fast_rows = slow_frames * HALF, frames * HALF
    per_group = frames // GROUPS
    group_rows = per_group * HALF
    slabs = share == BLK
    me = p.dp * nm + p.mp
    partner = p.a * p.nb + p.off_b(1)

    members = nd * p.nb
    member = p.dp * p.nb + p.b
    group_peers = [
        (lax.rem(p.dp + i, nd), p.a * p.nb + p.off_b(k))
        for i in range(nd)
        for k in range(p.nb)
        if i or k
    ]
    near = [p.dev(p.x, p.c, p.off_a(i), p.b) for i in range(1, p.na)]
    barrier = pltpu.get_barrier_semaphore()
    for device in group_peers + near:
        pl.semaphore_signal(barrier, inc=1, device_id=device, device_id_type=MESH)

    local_copies = []

    def fetch(source, target):
        copy = pltpu.make_async_copy(source, target, R.local.at[len(local_copies)])
        copy.start()
        local_copies.append(copy)
        return copy

    get_owner = fetch(owners_in, R.owner_v)
    get_master = fetch(master_in, R.shift.at[pl.ds(16, slots)])
    get_fast = fetch(fast_in, R.fast_v)
    get_slow = fetch(slow_in, R.slow_v)
    get_owner_s = fetch(owner_in, R.owner_s)
    get_fcot = fetch(fcot_in, R.fcot_v)
    get_scot = fetch(scot_in, R.scot_v)

    crop = crop_in[0]
    R.mask_all[...] = position_mask(crop)
    R.mask[...] = R.mask_all[pl.ds(pl.multiple_of(p.b * HALF, HALF), HALF), :]
    tall = crop.astype(f32)
    area = tall * tall * (1.0 / COLUMNS)
    xt_ref, xs_ref, fc_ref, sc_ref = R.xt, R.xs, R.fc, R.sc
    for f in (0, 1, frames + 2, frames + 3):
        xt_ref[f] = jnp.zeros((HALF, BLK), bf16)
    two_in, two_back = R.two_in, R.two_back
    for ref in (two_in, two_back):
        ref[:HALF] = jnp.zeros((HALF, 256), bf16)
        ref[(slow_frames + 1) * HALF :] = jnp.zeros((HALF, 256), bf16)

    get_owner.wait()
    spot = lax.broadcasted_iota(jnp.int32, (8, BLK), 0) * BLK
    spot = spot + lax.broadcasted_iota(jnp.int32, (8, BLK), 1)
    lowest = jnp.full((8, BLK), NBLK, jnp.int32)
    number = jnp.zeros((8, BLK), jnp.int32)
    for i in range(up(NBLK, 1024) // 1024):
        block = spot + i * 1024
        mine = R.owner_v[i * 8 : (i + 1) * 8, :] == me
        mine = mine & (block < NBLK)
        lowest = jnp.minimum(lowest, jnp.where(mine, block, NBLK))
        number = number + jnp.where(mine, 1, 0)
    my_start, my_count = jnp.min(lowest), jnp.sum(number)
    shift = lax.rem(my_start, 16)
    get_master.wait()
    moved = R.shift[pl.ds(16 - shift, rows), :]
    row = lax.broadcasted_iota(jnp.int32, (rows, BLK), 0)
    own = (row >= shift) & (row < shift + my_count)
    p_ref = R.p

    def p_slot(slot):
        return p_ref.at[pl.ds(slot * tiles, tiles)]

    p_slot(me)[...] = jnp.where(own, moved, 0.0).astype(bf16).reshape(tiles, 16, BLK)

    pl.semaphore_wait(barrier, len(group_peers) + len(near))
    p_sends = []

    def view(x, c, a, b):
        return p_slot(p.slot(x, c, a, b))

    def pass_on(source, along_a=False, along_b=False, along_x=False, along_c=False):
        piece, sem = view(*source), R.p_recv.at[p.slot(*source)]
        to = []
        if along_a:
            to += [p.dev(p.x, p.c, p.off_a(i), p.b) for i in range(1, p.na)]
        if along_x:
            to += [p.dev(p.off_x(i), p.c, p.a, p.b) for i in range(1, p.nx)]
        if along_b:
            to += [p.dev(p.x, p.c, p.a, p.off_b(1))]
        if along_c:
            to += [p.dev(p.x, 1 - p.c, p.a, p.b)]
        for device in to:
            remote(piece, piece, R.p_send, sem, device)
            p_sends.append(device)

    def take(source):
        arrived(view(*source), R.p_recv.at[p.slot(*source)])

    pass_on((p.x, p.c, p.a, p.b), along_a=True, along_b=True, along_x=True, along_c=True)

    turned_ref = R.turned

    def half_of(b):
        return pl.ds(pl.multiple_of(b * HALF, HALF), HALF)

    def own_frame(slot, other, source):
        turned_ref[...] = source[...].astype(f32).T * R.mask_all[...]
        slot[...] = turned_ref[half_of(p.b), :].astype(bf16)
        other[...] = turned_ref[half_of(p.off_b(1)), :].astype(bf16)

    def own_slow(slot, other, source):
        stage = R.stage
        stage[...] = source[...].astype(f32)
        for s in range(slow_frames):
            at = slice(s * HALF, (s + 1) * HALF)
            for h in range(halves):
                part = stage[pl.ds(h * slow_frames + s, share, stride=halves * slow_frames), :]
                if slabs:
                    here = slice(h * BLK, (h + 1) * BLK)
                    turned_ref[here, :] = part.T * R.mask_all[here, :]
                else:
                    turned_ref[h * share : (h + 1) * share, :] = part
            if slabs:
                slot[at, :] = turned_ref[half_of(p.b), :].astype(bf16)
                other[at, :] = turned_ref[half_of(p.off_b(1)), :].astype(bf16)
            else:
                for ref, b in ((R.piece, p.b), (other, p.off_b(1))):
                    mine = pl.ds(pl.multiple_of(b * share, share), share)
                    ref[:, at] = turned_ref[mine, :].astype(bf16)
        if not slabs:
            pltpu.sync_copy(R.piece, slot)

    def from_natural(natural, wide):
        ranks = BLK // share

        def block(i, _):
            s, j = i // SLABS, lax.rem(i, SLABS)
            at_row = pl.ds(pl.multiple_of(s * HALF, HALF), HALF)
            for k in range(ranks):
                pltpu.sync_copy(
                    natural.at[j * ranks + k, :, at_row],
                    R.turn.at[pl.ds(k * share, share)],
                )
            piece = R.turn[...].astype(f32).T * R.mask[...]
            wide[j, at_row, :] = piece.astype(bf16)
            return 0

        lax.fori_loop(0, slow_frames * SLABS, block, 0)

    def gather(which, array, other, skip=0):
        sems = [R.gather_sems.at[which, i] for i in range(3)]
        return Gather(p, array, other, skip, *sems)

    x_gather = gather(0, xt_ref, R.x_other, 2)
    fc_gather = gather(1, fc_ref, R.fc_other)
    xs_gather = gather(2, xs_ref if slabs else results[5], R.xs_other)
    sc_gather = gather(3, sc_ref if slabs else results[6], R.sc_other)
    get_fast.wait()
    own_frame(x_gather.view(p.mp), R.x_other, R.fast_v)
    x_gather.start()
    get_slow.wait()
    own_slow(xs_gather.view(p.mp), R.xs_other, R.slow_v)

    get_owner_s.wait()
    steps = [1 << i for i in reversed(range(max(1, (slots - 1).bit_length())))]
    owner_s, run_device, run_start, run_count = (R.owner_s, R.run_device, R.run_start, R.run_count)

    def run(k, at):
        device = owner_s[jnp.minimum(at, NBLK - 1)]
        n = jnp.int32(1)
        for step in steps:
            more = n + step
            last = at + more - 1
            inside = owner_s[jnp.minimum(last, NBLK - 1)] == device
            n = jnp.where((more <= slots) & (last < NBLK) & inside, more, n)
        run_device[k] = device
        run_start[k] = at
        run_count[k] = n
        return at + n

    lax.fori_loop(0, devices, run, jnp.int32(0))

    for i in range(1, p.na):
        source = (p.x, p.c, p.off_a(p.na - i), p.b)
        take(source)
        pass_on(source, along_b=True, along_x=True, along_c=True)
    x_gather.relay()
    xs_gather.start()

    def tile_of(k):
        return run_device[k] * tiles - run_start[k] // 16

    def table(k, found):
        start, last = run_start[k], run_start[k] + run_count[k] - 1
        final = jnp.minimum(spot * 16 + 15, NBLK - 1)
        holds = (final >= start) & (final <= last)
        tile = jnp.where(spot == start // 16, devices * tiles + k, spot + tile_of(k))
        return jnp.where(holds, tile, found)

    R.table_v[...] = lax.fori_loop(0, devices, table, jnp.zeros((8, BLK), jnp.int32))
    get_table = fetch(R.table_v, R.table_s)

    across = p.na // 2
    for i in range(p.na):
        source = (p.x, p.c, p.off_a(p.na - i), p.off_b(1))
        take(source)
        pass_on(source, along_x=i < across, along_c=True)
        for j in range(1, p.nx):
            source = (p.off_x(j), p.c, p.off_a(p.na - i), p.b)
            take(source)
            pass_on(source, along_b=i >= across, along_c=True)
    xs_gather.relay()
    get_fcot.wait()
    own_frame(fc_gather.view(p.mp), R.fc_other, R.fcot_v)
    get_scot.wait()
    own_slow(sc_gather.view(p.mp), R.sc_other, R.scot_v)
    for i in range(p.na):
        for k in range(1, p.nx):
            source = (p.off_x(k), p.c, p.off_a(p.na - i), p.off_b(1))
            take(source)
            pass_on(source, along_c=True)
    fc_gather.start()
    sc_gather.start()
    for i in range(p.na):
        for j in range(p.nb):
            for k in range(p.nx):
                take((p.off_x(k), 1 - p.c, p.off_a(i), p.off_b(j)))
    get_table.wait()

    def tile_rows(t):
        return pl.ds(pl.multiple_of(t * 16, 16), 16)

    q_ref = R.q

    def first_tile(k, before):
        tile = p_ref[run_device[k] * tiles].astype(f32)
        shared = lax.rem(run_start[k], 16) != 0
        tile = tile + jnp.where(shared, before, 0.0)
        q_ref[k] = tile.astype(bf16)
        last = (run_start[k] + run_count[k] - 1) // 16
        alone = last == run_start[k] // 16
        return jnp.where(alone, tile, p_ref[tile_of(k) + last].astype(f32))

    lax.fori_loop(0, devices, first_tile, jnp.zeros((16, BLK), f32))
    flat_ref, table_s = R.flat, R.table_s

    def lay_out(first_block, end_block):
        first, end = first_block // 16, up(end_block, 16) // 16

        def one(t):
            source = table_s[t // BLK, lax.rem(t, BLK)]
            plain = p_ref[jnp.minimum(source, devices * tiles - 1)]
            shared = q_ref[jnp.maximum(source - devices * tiles, 0)]
            tile = jnp.where(source < devices * tiles, plain, shared)
            flat_ref[tile_rows(t), :] = tile.astype(f32)

        def eight(i, _):
            for k in range(8):
                one(first + i * 8 + k)
            return 0

        lax.fori_loop(0, (end - first) // 8, eight, 0)
        for t in range(first + (end - first) // 8 * 8, end):
            one(t)

    def matrix(out_ref, at, height, blocks):
        lay_out(at, at + height * blocks)
        for j in range(blocks):
            for o in range(0, height, 256):
                out_ref[o : o + 256, j * BLK : (j + 1) * BLK] = flat_ref[
                    pl.ds(at + o * blocks + j, 256, stride=blocks), :
                ].astype(bf16)

    group = lane_group()
    square_ref = R.square
    lat_w, s1_w, s2_w, s3_w = R.lat_w, R.s1_w, R.s2_w, R.s3_w
    f1_w, f2_w, f3_w, vec_ref = R.f1_w, R.f2_w, R.f3_w, R.vec

    def spread_rows(at, height):
        for r in range(GROUPS):
            part = jnp.where(group == r, flat_ref[at : at + height // GROUPS, :], 0.0)
            square_ref[pl.ds(r, height // GROUPS, stride=GROUPS), :] = fold_lanes(part)
        return square_ref[:height, :]

    def fast_weights():
        lay_out(AT_F1, AT_LAT)
        for k in range(3):
            tap = flat_ref[pl.ds(AT_F1 + k, B_FAST, stride=3), :].astype(bf16)
            for g in range(GROUPS):
                f1_w[g * B_FAST : (g + 1) * B_FAST, k * BLK : (k + 1) * BLK] = tap
        two = spread_rows(AT_F2, B_FAST)
        for g in range(GROUPS):
            f2_w[g * B_FAST : (g + 1) * B_FAST, :] = jnp.where(group == g, two, 0.0).astype(bf16)
        f3_w[...] = spread_rows(AT_F3, C_FAST).astype(bf16)

    matrix(lat_w, AT_LAT, C_LAT, 5)
    lay_out(AT_VEC, NBLK)
    vec_ref[...] = flat_ref[AT_VEC : AT_VEC + 32, :]
    x_gather.finish()

    zb, latb, s2b, dz, da1, wide_ref = (R.zb, R.latb, R.s2b, R.dz, R.da1, R.wide)
    c1, c2, c3, e, e3, da3 = (R.c1, R.c2, R.c3, R.e, R.e3, R.da3)
    a1p, a2p, h1p, h2p, d1p, d2p, ep, a3, e3f, da3f = (R.a1p, R.a2p, R.h1p, R.h2p, R.d1p, R.d2p, R.ep, R.a3, R.e3f, R.da3f)
    mask_ref, own3_ref, st_ref, st16_ref = (R.mask, R.own3, R.st, R.st16)
    s1b = two_in.at[pl.ds(HALF, slow_rows)]
    da2 = two_back.at[pl.ds(HALF, slow_rows)]

    def stat(which):
        return (st_ref, which) if which < 12 else (st16_ref, which - 12)

    def exchange(which):
        ref, at = stat(which)
        own = ref.at[at, member]
        for device in group_peers:
            remote(own, own, R.ex_send.at[which], R.ex_recv.at[which], device)

    def exchanged(which):
        ref, at = stat(which)
        arrived(ref.at[at, pl.ds(0, members - 1)], R.ex_recv.at[which])
        total = ref[at, 0]
        for i in range(1, members):
            total = total + ref[at, i]
        return total

    def put(which, at, vector):
        ref, index = stat(which)
        for j in range(vector.shape[1] // BLK):
            ref[index, member, at + j : at + j + 1, :] = vector[:, j * BLK : (j + 1) * BLK]

    def fill(which, at, value):
        ref, index = stat(which)
        ref[index, member, at:8, :] = jnp.full((8 - at, BLK), value, f32)

    def row_of(block, at, n):
        return jnp.concatenate([block[at + j : at + j + 1, :] for j in range(n)], 1)

    def vectors(place):
        g, b, n = place
        return row_of(vec_ref[...], g, n), row_of(vec_ref[...], b, n)

    def rows_at(i, size):
        return pl.ds(pl.multiple_of(i * size, size), size)

    def mask_at(i, width):
        part = mask_ref[pl.ds(pl.multiple_of(lax.rem(i * RC, HALF), RC), RC), :]
        return jnp.concatenate([part] * (width // BLK), 1) if width > BLK else part

    def eights(v):
        return jnp.sum(v.reshape(v.shape[0] // 8, 8, v.shape[1]), 0)

    def total_row(v):
        return jnp.sum(v, 0, keepdims=True)

    def affine(sums, squares, count, gain, bias):
        mean = sums / count
        scale = lax.rsqrt(squares / count - mean * mean + norm_eps)
        grow = gain * scale
        return mean, scale, grow, bias - mean * grow

    def sums_of(ref, n_rows, width):
        def body(i, acc):
            v = ref[rows_at(i, RC), :].astype(f32)
            return acc[0] + eights(v), acc[1] + eights(v * v)

        zero = jnp.zeros((8, width), f32)
        one, two = lax.fori_loop(0, n_rows // RC, body, (zero, zero))
        return total_row(one), total_row(two)

    def activate(src, dst, n_rows, width, grow, base):
        def body(i, _):
            at = rows_at(i, RC)
            pre = src[at, :].astype(f32) * grow + base
            dst[at, :] = (gelu(pre) * mask_at(i, width)).astype(bf16)
            return 0

        lax.fori_loop(0, n_rows // RC, body, 0)

    def slopes(src, incoming, n_rows, width, norm):
        mean, scale, grow, base = norm

        def body(i, acc):
            at = rows_at(i, RC)
            a = src[at, :].astype(f32)
            d = gelu_slope(a * grow + base) * incoming[at, :] * mask_at(i, width)
            incoming[at, :] = d
            return acc[0] + eights(d), acc[1] + eights(d * ((a - mean) * scale))

        zero = jnp.zeros((8, width), f32)
        one, two = lax.fori_loop(0, n_rows // RC, body, (zero, zero))
        return total_row(one), total_row(two)

    def back_vectors(bias_sum, gain_sum, count, norm):
        mean, scale, grow, base = norm
        k1 = grow * gain_sum / count
        return grow * bias_sum / count - k1 * (mean * scale), k1 * scale

    def raw_grads(src, pres, dst, n_rows, width, norm, q0, q1):
        grow = norm[2]

        def body(i, _):
            at = rows_at(i, RC)
            a = src[at, :].astype(f32)
            da = grow * pres[at, :] - mask_at(i, width) * (q0 + a * q1)
            dst[at, :] = da.astype(bf16)
            return 0

        lax.fori_loop(0, n_rows // RC, body, 0)

    def put_vector(row, vector):
        for j in range(vector.shape[1] // BLK):
            at = AT_VEC + row + j
            flat_ref[at : at + 1, :] = vector[:, j * BLK : (j + 1) * BLK]

    def put_pair(which, one, two, place=None):
        put(which, 0, one)
        put(which, one.shape[1] // BLK, two)
        if place is not None:
            put_vector(place[0], two)
            put_vector(place[1], one)

    slow_chunks = [slice(i, i + CH) for i in range(0, slow_rows, CH)]
    group_chunks = [slice(i, i + CH) for i in range(0, group_rows, CH)]

    def all_slabs(ref, at):
        return jnp.concatenate([ref[j, at, :] for j in range(SLABS)], 1)

    boxes = (
        (R.fast_out_box, R.fast_out_end),
        (R.slow_out_box, R.slow_out_end),
        (R.fast_grad_box, R.fast_grad_end),
        (R.slow_grad_box, R.slow_grad_end),
    )

    def box(which, kind):
        return boxes[which][0].at[kind]

    def hand_over(which):
        box_sems = R.box_send.at[which], R.box_recv.at[which]
        remote(box(which, SENT), box(which, GOT), *box_sems, (p.dp, partner))

    deliveries = []

    def deliver(source, which):
        sem = R.local.at[len(local_copies) + len(deliveries)]
        copy = pltpu.make_async_copy(source, results[which], sem)
        copy.start()
        deliveries.append(copy)

    def to_channels(block):
        turned = block.T
        if slabs:
            return turned
        lane_shift = lax.rem(p.mp * share, BLK)
        return sum(
            jnp.where(lane_shift == k * share, turned[k * share : (k + 1) * share, :], 0.0)
            for k in range(BLK // share)
        )

    def complete(which):
        ref, end = boxes[which]
        arrived(box(which, GOT), R.box_recv.at[which])
        fast = which in (FAST_OUT, FAST_GRAD)
        n = 1 if fast else slow_frames
        for s in range(n):
            at = slice(s * HALF, (s + 1) * HALF)
            for h in range(halves):
                block = jnp.where(p.b == h, ref[MINE, at, :], ref[GOT, at, :])
                block = block.T if fast else to_channels(block)
                end[pl.ds(s * halves + h, block.shape[0], stride=n * halves), :] = block
        deliver(end, which)

    for s in range(slow_frames):
        for k in range(5):
            wide_ref[s * HALF : (s + 1) * HALF, k * BLK : (k + 1) * BLK] = xt_ref[4 * s + k]
    for at in slow_chunks:
        zb[at, :] = dot_nt(wide_ref[at, :], lat_w[...]).astype(bf16)
    put_pair(EX_LAT, *sums_of(zb, slow_rows, C_LAT))
    fill(EX_LAT, 4, area)
    exchange(EX_LAT)

    fast_weights()

    def fast_rows_of(ref, first_frame, at):
        f = first_frame + at.start // HALF
        return jnp.concatenate([ref[f + i] for i in range(CH // HALF)], 0)

    for at in group_chunks:
        total = jnp.zeros((CH, BLK), f32)
        for g in range(GROUPS):
            window = jnp.concatenate(
                [fast_rows_of(xt_ref, g * per_group + 1 + k, at) for k in range(3)], 1
            )
            total = total + jnp.where(group == g, dot_nt(window, f1_w[...]), 0.0)
        a1p[at, :] = total

    def put_folded(which, one, two):
        put(which, 0, fold_lanes(one))
        put(which, 1, fold_lanes(two))

    put_folded(EX_F1, *sums_of(a1p, group_rows, BLK))
    fill(EX_F1, 2, area)
    exchange(EX_F1)
    fc_gather.relay()
    sc_gather.relay()

    matrix(s1_w, AT_S1, B_SLOW, 10)
    xs_gather.finish()
    if not slabs:
        from_natural(results[5], xs_ref)

    for at in slow_chunks:
        c1[at, :] = dot_nt(all_slabs(xs_ref, at), s1_w[:, :C_SLOW])

    total = exchanged(EX_LAT)
    area_all = total[4:5, :]
    slow_count = jnp.concatenate([area_all * float(slow_frames)] * 2, 1)
    slow_count8 = jnp.concatenate([slow_count] * 4, 1)
    fast_count = area_all * float(frames)
    lat_norm = affine(row_of(total, 0, 2), row_of(total, 2, 2), slow_count, *vectors(V_LAT))
    activate(zb, latb, slow_rows, C_LAT, lat_norm[2], lat_norm[3])
    for at in slow_chunks:
        c1[at, :] = c1[at, :] + dot_nt(latb[at, :], s1_w[:, C_SLOW:])
    put_pair(EX_S1, *sums_of(c1, slow_rows, B_SLOW))
    fill(EX_S1, 4, 0.0)
    exchange(EX_S1)

    matrix(s2_w, AT_S2, B_SLOW, 6)

    packed = vec_ref[0:1, :]

    def spread(which):
        return fold_lanes(jnp.where(group == which, packed, 0.0))

    def exchanged_two(which):
        total = exchanged(which)
        return total[0:1, :], total[1:2, :]

    f1_norm = affine(*exchanged_two(EX_F1), fast_count, spread(0), spread(1))
    activate(a1p, h1p, group_rows, BLK, f1_norm[2], f1_norm[3])
    for at in group_chunks:
        a2p[at, :] = dot_nt(h1p[at, :], f2_w[...])
    put_folded(EX_F2, *sums_of(a2p, group_rows, BLK))
    fill(EX_F2, 2, 0.0)
    exchange(EX_F2)

    total = exchanged(EX_S1)
    s1_norm = affine(row_of(total, 0, 2), row_of(total, 2, 2), slow_count, *vectors(V_S1))
    activate(c1, s1b, slow_rows, B_SLOW, s1_norm[2], s1_norm[3])

    def shifted(ref, at, k):
        return ref[at.start + k * HALF : at.stop + k * HALF, :]

    for at in slow_chunks:
        window = jnp.concatenate([shifted(two_in, at, k) for k in range(3)], 1)
        c2[at, :] = dot_nt(window, s2_w[...])
    put_pair(EX_S2, *sums_of(c2, slow_rows, B_SLOW))
    fill(EX_S2, 4, 0.0)
    exchange(EX_S2)

    matrix(s3_w, AT_S3, C_SLOW, 2)

    f2_norm = affine(*exchanged_two(EX_F2), fast_count, spread(2), spread(3))
    activate(a2p, h2p, group_rows, BLK, f2_norm[2], f2_norm[3])
    for g in range(GROUPS):
        for at in group_chunks:
            part = jnp.where(group == g, h2p[at, :], 0.0).astype(bf16)
            here = slice(g * group_rows + at.start, g * group_rows + at.stop)
            a3[here, :] = dot_nt(part, f3_w[...])
    put_pair(EX_F3, *sums_of(a3, fast_rows, BLK))
    fill(EX_F3, 2, 0.0)
    exchange(EX_F3)

    total = exchanged(EX_S2)
    s2_norm = affine(row_of(total, 0, 2), row_of(total, 2, 2), slow_count, *vectors(V_S2))
    activate(c2, s2b, slow_rows, B_SLOW, s2_norm[2], s2_norm[3])
    quarter = C_SLOW // 4
    quarters = [slice(n * quarter, (n + 1) * quarter) for n in range(4)]
    for n, lanes in enumerate(quarters):
        for at in slow_chunks:
            c3[at, lanes] = dot_nt(s2b[at, :], s3_w[lanes, :])
        one, two = sums_of(c3.at[:, lanes], slow_rows, quarter)
        put(EX_S3, 2 * n, one)
        put(EX_S3, 8 + 2 * n, two)
    exchange(EX_S3)

    f3_norm = affine(*exchanged_two(EX_F3), fast_count, *vectors(V_F3))
    for rank, kind in ((partner, SENT), (p.mp, MINE)):
        pre = a3[rows_at(rank, HALF), :] * f3_norm[2] + f3_norm[3]
        pre = pre + xt_ref[rank + 2].astype(f32)
        R.fast_out_box[kind] = gelu(pre) * mask_ref[...]
    hand_over(FAST_OUT)
    fc_gather.finish()

    def fast_slopes(i, acc):
        mean, scale, grow, base = f3_norm
        at = rows_at(i, RC)
        f, here = i // (HALF // RC), rows_at(lax.rem(i, HALF // RC), RC)
        a = a3[at, :]
        x = xt_ref[f + 2, here, :].astype(f32)
        d = gelu_slope(a * grow + base + x) * fc_ref[f, here, :].astype(f32)
        e3f[at, :] = d
        return acc[0] + eights(d), acc[1] + eights(d * ((a - mean) * scale))

    zero = jnp.zeros((8, BLK), f32)
    one, two = lax.fori_loop(0, fast_rows // RC, fast_slopes, (zero, zero))
    put_pair(EX_BF3, total_row(one), total_row(two), V_F3)
    fill(EX_BF3, 2, 0.0)
    exchange(EX_BF3)

    sc_gather.finish()
    if not slabs:
        from_natural(results[6], sc_ref)
    total = exchanged(EX_S3)
    s3_norm = affine(row_of(total, 0, 8), row_of(total, 8, 8), slow_count8, *vectors(V_S3))

    def pair_of(ref, n, at):
        return jnp.concatenate([ref[2 * n, at, :], ref[2 * n + 1, at, :]], 1).astype(f32)

    for n, lanes in enumerate(quarters):
        norm = [v[:, lanes] for v in s3_norm]

        def slow_slopes(i, acc, n=n, lanes=lanes, norm=norm):
            at = rows_at(i, RC)
            a = c3[at, lanes]
            pre = a * norm[2] + norm[3] + pair_of(xs_ref, n, at)
            d = gelu_slope(pre) * pair_of(sc_ref, n, at)
            e3[at, lanes] = d
            return acc[0] + eights(d), acc[1] + eights(d * ((a - norm[0]) * norm[1]))

        zero = jnp.zeros((8, quarter), f32)
        one, two = lax.fori_loop(0, slow_rows // RC, slow_slopes, (zero, zero))
        one, two = total_row(one), total_row(two)
        put(EX_BS3, 2 * n, one)
        put(EX_BS3, 8 + 2 * n, two)
        put_vector(V_S3[0] + 2 * n, two)
        put_vector(V_S3[1] + 2 * n, one)
    exchange(EX_BS3)

    places = []
    for kind, rank in enumerate((partner, p.mp)):
        slab = rank * share // BLK
        lanes = pl.ds(pl.multiple_of(slab * BLK, BLK), BLK)
        places.append((kind, lanes))
        norm = [
            sum(jnp.where(slab == k, v[:, k * BLK : (k + 1) * BLK], 0.0) for k in range(SLABS))
            for v in s3_norm
        ]
        for s in range(slow_frames):
            at = slice(s * HALF, (s + 1) * HALF)
            pre = c3[at, lanes] * norm[2] + norm[3] + xs_ref[slab, at, :].astype(f32)
            R.slow_out_box[kind, at, :] = gelu(pre) * mask_ref[...]
            own3_ref[kind, at, :] = e3[at, lanes]
        if kind == SENT:
            hand_over(SLOW_OUT)

    q0, q1 = back_vectors(*exchanged_two(EX_BF3), fast_count, f3_norm)
    raw_grads(a3, e3f, da3f, fast_rows, BLK, f3_norm, q0, q1)
    for at in group_chunks:
        total = jnp.zeros((CH, BLK), f32)
        for g in range(GROUPS):
            here = slice(g * group_rows + at.start, g * group_rows + at.stop)
            total = total + jnp.where(group == g, dot_nn(da3f[here, :], f3_w[...]), 0.0)
        ep[at, :] = total
    one, two = slopes(a2p, ep, group_rows, BLK, f2_norm)
    put_folded(EX_BF2, one, two)
    fill(EX_BF2, 2, 0.0)
    exchange(EX_BF2)
    vec_two = jnp.where(group == 2, fold_lanes(two), 0.0)
    vec_two = vec_two + jnp.where(group == 3, fold_lanes(one), 0.0)
    complete(FAST_OUT)

    total = exchanged(EX_BS3)
    q0, q1 = back_vectors(row_of(total, 0, 8), row_of(total, 8, 8), slow_count8, s3_norm)
    for lanes in quarters:
        norm = [v[:, lanes] for v in s3_norm]
        raw_grads(
            c3.at[:, lanes], e3.at[:, lanes], da3.at[:, lanes], slow_rows, quarter, norm,
            q0[:, lanes], q1[:, lanes]
        )
    for at in slow_chunks:
        e[at, :] = dot_nn(da3[at, :], s3_w[...])
    put_pair(EX_B2, *slopes(c2, e, slow_rows, B_SLOW, s2_norm), V_S2)
    fill(EX_B2, 4, 0.0)
    exchange(EX_B2)

    def to_flat(at, blocks, offset, lane, value):
        for j in range(value.shape[1] // BLK):
            here = pl.ds(at + offset * blocks + lane + j, value.shape[0], stride=blocks)
            flat_ref[here, :] = value[:, j * BLK : (j + 1) * BLK]

    for n, lanes in enumerate(quarters):
        to_flat(AT_S3, 2, n * quarter, 0, dot_tn(da3[:, lanes], s2b[...]))

    q0, q1 = back_vectors(*exchanged_two(EX_BF2), fast_count, f2_norm)
    raw_grads(a2p, ep, d2p, group_rows, BLK, f2_norm, q0, q1)
    for at in group_chunks:
        ep[at, :] = dot_nn(d2p[at, :], f2_w[...])
    one, two = slopes(a1p, ep, group_rows, BLK, f1_norm)
    put_folded(EX_BF1, one, two)
    fill(EX_BF1, 2, 0.0)
    exchange(EX_BF1)
    vec_one = jnp.where(group == 0, fold_lanes(two), 0.0)
    vec_one = vec_one + jnp.where(group == 1, fold_lanes(one), 0.0)
    put_vector(0, vec_one + vec_two)

    total = exchanged(EX_B2)
    q0, q1 = back_vectors(row_of(total, 0, 2), row_of(total, 2, 2), slow_count, s2_norm)
    raw_grads(c2, e, da2, slow_rows, B_SLOW, s2_norm, q0, q1)
    for at in slow_chunks:
        e[at, :] = functools.reduce(
            lambda u, v: u + v,
            [
                dot_nn(shifted(two_back, at, 2 - k), s2_w[:, k * B_SLOW : (k + 1) * B_SLOW])
                for k in range(3)
            ],
        )
    put_pair(EX_B1, *slopes(c1, e, slow_rows, B_SLOW, s1_norm), V_S1)
    fill(EX_B1, 4, 0.0)
    exchange(EX_B1)

    everything = slice(0, slow_rows)
    for k in range(3):
        part = dot_tn(two_back[HALF : HALF + slow_rows, :], shifted(two_in, everything, k))
        to_flat(AT_S2, 6, 0, 2 * k, part)

    total = jnp.zeros((BLK, BLK), f32)
    for g in range(GROUPS):
        at = slice(g * group_rows, (g + 1) * group_rows)
        total = total + jnp.where(group == g, dot_tn(da3f[at, :], h2p[...]), 0.0)

    def to_blocks(value, at):
        n = value.shape[0] // GROUPS
        square_ref[: value.shape[0], :] = fold_lanes(value)
        flat_ref[at : at + n, :] = sum(
            jnp.where(group == r, square_ref[pl.ds(r, n, stride=GROUPS), :], 0.0)
            for r in range(GROUPS)
        )

    to_blocks(total, AT_F3)
    square = dot_tn(d2p[...], h1p[...])
    to_blocks(
        sum(
            jnp.where(group == g, square[g * B_FAST : (g + 1) * B_FAST, :], 0.0)
            for g in range(GROUPS)
        ),
        AT_F2,
    )
    complete(SLOW_OUT)

    total = exchanged(EX_B1)
    q0, q1 = back_vectors(row_of(total, 0, 2), row_of(total, 2, 2), slow_count, s1_norm)
    raw_grads(c1, e, da1, slow_rows, B_SLOW, s1_norm, q0, q1)
    for at in slow_chunks:
        e[at, :] = dot_nn(da1[at, :], s1_w[:, C_SLOW:])
    put_pair(EX_BLAT, *slopes(zb, e, slow_rows, C_LAT, lat_norm), V_LAT)
    fill(EX_BLAT, 4, 0.0)
    exchange(EX_BLAT)

    for kind, lanes in places:
        for s in range(slow_frames):
            at = slice(s * HALF, (s + 1) * HALF)
            value = own3_ref[kind, at, :] + dot_nn(da1[at, :], s1_w[:, lanes])
            R.slow_grad_box[kind, at, :] = value * mask_ref[...]
        if kind == SENT:
            hand_over(SLOW_GRAD)

    q0, q1 = back_vectors(*exchanged_two(EX_BF1), fast_count, f1_norm)
    raw_grads(a1p, ep, d1p, group_rows, BLK, f1_norm, q0, q1)
    for k in range(3):
        tap = jnp.zeros((B_FAST, BLK), f32)
        for g in range(GROUPS):
            first = g * per_group + k + 1
            right = jnp.concatenate([xt_ref[first + i] for i in range(per_group)], 0)
            part = dot_tn(d1p[...], right)
            tap = tap + part[g * B_FAST : (g + 1) * B_FAST, :]
        to_flat(AT_F1, 3, 0, k, tap)

    for n in range(4):
        right = jnp.concatenate([xs_ref[2 * n], xs_ref[2 * n + 1]], 1)
        to_flat(AT_S1, 10, 0, 2 * n, dot_tn(da1[...], right))
    to_flat(AT_S1, 10, 0, 8, dot_tn(da1[...], latb[...]))

    def frame_grad(rank):
        grad = e3f[rows_at(rank, HALF), :]
        for k in range(3):
            f = rank - k + 1
            there = (f >= 0) & (f < frames)
            g, j = f // per_group, lax.rem(f, per_group)
            g, j = jnp.where(there, g, 0), jnp.where(there, j, 0)
            left = jnp.where((group == g) & there, d1p[rows_at(j, HALF), :], 0.0).astype(bf16)
            grad = grad + dot_nn(left, f1_w[:, k * BLK : (k + 1) * BLK])
        return grad

    def lateral_grad(rank):
        later, s = lax.rem(rank + 2, 4), (rank + 2) // 4
        grad = jnp.zeros((HALF, BLK), f32)
        for tap, at, there in (
            (later, s, s < slow_frames),
            (later + 4, s - 1, (later == 0) & (s > 0)),
        ):
            tap, at = jnp.where(there, tap, 0), jnp.where(there, at, 0)
            left = jnp.where(there, dz[rows_at(at, HALF), :], 0.0).astype(bf16)
            weight = lat_w[:, pl.ds(pl.multiple_of(tap * BLK, BLK), BLK)]
            grad = grad + dot_nn(left, weight)
        return grad

    R.fast_grad_box[SENT] = frame_grad(partner)
    R.fast_grad_box[MINE] = frame_grad(p.mp)

    total = exchanged(EX_BLAT)
    q0, q1 = back_vectors(row_of(total, 0, 2), row_of(total, 2, 2), slow_count, lat_norm)
    raw_grads(zb, e, dz, slow_rows, C_LAT, lat_norm, q0, q1)
    to_flat(AT_LAT, 5, 0, 0, dot_tn(dz[...], wide_ref[...]))

    height = up(slots, 16)
    sib_out, sib_in, far_out, far_in = (R.sib_out, R.sib_in, R.far_out, R.far_in)
    sib_send, sib_recv, far_send, far_recv = (R.sum_sems.at[i] for i in range(4))
    targets = [(i, j) for i in range(p.nx) for j in range(p.nb)]

    def start_of(device):
        def one(k, found):
            return jnp.where(run_device[k] == device, run_start[k], found)

        return lax.fori_loop(0, devices, one, jnp.int32(0))

    def window_of(c, target):
        x, b = p.off_x(target[0]), p.off_b(target[1])
        return flat_ref[pl.ds(start_of(p.slot(x, c, p.a, b)), height), :]

    for o, target in enumerate(targets):
        sib_out[o] = window_of(1 - p.c, target).astype(bf16)
    remote(sib_out, sib_in, sib_send, sib_recv, p.dev(p.x, 1 - p.c, p.a, p.b))

    for rank, kind in ((partner, SENT), (p.mp, MINE)):
        grad = R.fast_grad_box[kind] + lateral_grad(rank)
        R.fast_grad_box[kind] = grad * mask_ref[...]
    hand_over(FAST_GRAD)

    arrived(sib_in, sib_recv)
    for o, target in enumerate(targets[1:], 1):
        far_out[o] = (window_of(p.c, target) + sib_in[o].astype(f32)).astype(bf16)
        device = p.dev(p.off_x(target[0]), p.c, p.a, p.off_b(target[1]))
        remote(far_out.at[o], far_in.at[o], far_send, far_recv, device)
    complete(SLOW_GRAD)
    complete(FAST_GRAD)
    total = window_of(p.c, targets[0]) + sib_in[0].astype(f32)
    arrived(far_in.at[pl.ds(1, len(targets) - 1)], far_recv)
    for o in range(1, len(targets)):
        total = total + far_in[o].astype(f32)
    R.end_grad[...] = total
    deliver(R.end_grad, 4)

    sent = len(p_sends)
    while sent:
        n = min(sent, devices)
        arrived(p_ref.at[pl.ds(0, n * tiles)], R.p_send)
        sent -= n
    for each in (x_gather, xs_gather, fc_gather, sc_gather):
        each.drain()
    for which in range(EXCHANGES):
        ref, at = stat(which)
        arrived(ref.at[at, pl.ds(0, members - 1)], R.ex_send.at[which])
    for which in range(len(boxes)):
        arrived(box(which, SENT), R.box_send.at[which])
    arrived(sib_out, sib_send)
    arrived(far_out.at[pl.ds(1, len(targets) - 1)], far_send)
    for copy in deliveries:
        copy.wait()


def call_main(cfg, crop, owner, padded, master, fast, slow, fcot, scot):
    smem = pl.BlockSpec(memory_space=pltpu.SMEM)
    hbm = pl.BlockSpec(memory_space=pltpu.HBM)
    outs = outputs(cfg)
    return pl.pallas_call(
        functools.partial(main_kernel, cfg),
        out_shape=tuple(jax.ShapeDtypeStruct(s, t) for s, t in outs),
        in_specs=[smem] + [hbm] * 7,
        out_specs=tuple(hbm for _ in outs),
        scratch_shapes=list(scratch(cfg).values()),
        compiler_params=pltpu.CompilerParams(
            collective_id=0, has_side_effects=True, vmem_limit_bytes=62 << 20
        ),
        name="block",
    )(crop, owner, padded, master, fast, slow, fcot, scot)[:5]


def adam_kernel(cfg, *refs):
    nd, nm, frames, slow_frames, share, slots = cfg
    inputs, results, (sems, *held) = refs[:9], refs[9:17], refs[17:]
    owner_ref, grad, master, one, two = held[:5]
    w_out, one_out, two_out, low_out = held[9:]
    fetches = [
        pltpu.make_async_copy(source, target, sems.at[i])
        for i, (source, target) in enumerate(zip(inputs, held[:9], strict=True))
    ]
    for copy in fetches:
        copy.start()
    stores = [
        pltpu.make_async_copy(source, target, sems.at[9 + i])
        for i, (source, target) in enumerate(zip(held[9:] + held[5:9], results, strict=True))
    ]
    me = lax.axis_index("dp") * nm + lax.axis_index("mp")
    spot = lax.broadcasted_iota(jnp.int32, (8, BLK), 0) * BLK
    spot = spot + lax.broadcasted_iota(jnp.int32, (8, BLK), 1)
    lowest = jnp.full((8, BLK), NBLK, jnp.int32)
    number = jnp.zeros((8, BLK), jnp.int32)
    fetches[0].wait()
    for i in range(up(NBLK, 1024) // 1024):
        block = spot + i * 1024
        mine = (owner_ref[i * 8 : (i + 1) * 8, :] == me) & (block < NBLK)
        lowest = jnp.minimum(lowest, jnp.where(mine, block, NBLK))
        number = number + jnp.where(mine, 1, 0)
    start, count = jnp.min(lowest), jnp.sum(number)
    row = lax.broadcasted_iota(jnp.int32, (slots, BLK), 0)
    living = row < count
    block = row + start
    rate = jnp.full((slots, BLK), 0.2, f32)
    for at, width in (
        (AT_VEC, B_SLOW),
        (AT_S3, 3 * B_SLOW),
        (AT_S2, C_SLOW + C_LAT),
        (AT_S1, 5 * C_FAST),
        (AT_LAT, B_FAST),
        (AT_F2, 3 * C_FAST),
    ):
        rate = jnp.where(block < at, 0.5 / math.sqrt(width), rate)
    decay = jnp.where(block < AT_VEC, decay_rate, 0.0)
    for copy in fetches[5:]:
        copy.wait()
    for copy in stores[4:]:
        copy.start()
    for copy in fetches[1:5]:
        copy.wait()
    g = grad[:slots, :]
    first = beta_first * one[...] + (1.0 - beta_first) * g
    second = beta_second * two[...] + (1.0 - beta_second) * g * g
    lift_one = 1.0 - beta_first**STEP
    lift_two = 1.0 - beta_second**STEP
    update = first / lift_one / (jnp.sqrt(second / lift_two) + adam_eps)
    weight = master[...]
    weight = jnp.where(living, weight - rate * (update + decay * weight), 0.0)
    w_out[...] = weight
    one_out[...] = jnp.where(living, first, 0.0)
    two_out[...] = jnp.where(living, second, 0.0)
    low_out[...] = weight.astype(bf16)
    for copy in stores[:4]:
        copy.start()
    for copy in stores:
        copy.wait()


def call_adam(cfg, owner, grad, master, one, two, passed):
    arrays = (owner, grad, master, one, two, *passed)
    hbm = pl.BlockSpec(memory_space=pltpu.HBM)
    new = [jax.ShapeDtypeStruct(master.shape, t) for t in (f32, f32, f32, bf16)]
    results = new + [jax.ShapeDtypeStruct(a.shape, a.dtype) for a in passed]
    held = [pltpu.VMEM(a.shape, a.dtype) for a in (*arrays, *new)]
    return pl.pallas_call(
        functools.partial(adam_kernel, cfg),
        out_shape=tuple(results),
        in_specs=[hbm] * len(arrays),
        out_specs=(hbm,) * len(results),
        scratch_shapes=[pltpu.SemaphoreType.DMA((len(arrays) + len(results),)), *held],
        compiler_params=pltpu.CompilerParams(vmem_limit_bytes=62 << 20),
        name="adam",
    )(*arrays)


def solution(mesh):
    nd, nm = mesh.shape["dp"], mesh.shape["mp"]

    def local(fast_in, slow_in, fast_cot, slow_cot, crop, owner, master, one, two):
        share, slow_frames = slow_in.shape[0], slow_in.shape[1]
        cfg = (nd, nm, fast_in.shape[1] * nm, slow_frames, share, master.shape[0])

        def halves(array):
            split = array.reshape(share, slow_frames, POS // BLK, BLK)
            return split.transpose(0, 2, 1, 3).reshape(-1, BLK)

        padded = jnp.pad(owner, (0, up(NBLK, 1024) - NBLK)).reshape(-1, BLK)
        *passed, grad = call_main(
            cfg,
            crop,
            owner,
            padded,
            master,
            fast_in.reshape(C_FAST, POS),
            halves(slow_in),
            fast_cot.reshape(C_FAST, POS),
            halves(slow_cot),
        )
        new = call_adam(cfg, padded, grad, master, one, two, passed)
        return (
            new[4].reshape(fast_in.shape),
            new[5].reshape(slow_in.shape),
            new[6].reshape(fast_in.shape),
            new[7].reshape(slow_in.shape),
            *new[:4],
        )

    return jax.shard_map(
        local,
        mesh=mesh,
        in_specs=(
            P(None, "mp", "dp", None),
            P("mp", None, "dp", None),
            P(None, "mp", "dp", None),
            P("mp", None, "dp", None),
            P("dp"),
            P(),
            P(("dp", "mp"), None),
            P(("dp", "mp"), None),
            P(("dp", "mp"), None),
        ),
        out_specs=(
            P(None, "mp", "dp", None),
            P("mp", None, "dp", None),
            P(None, "mp", "dp", None),
            P("mp", None, "dp", None),
            P(("dp", "mp"), None),
            P(("dp", "mp"), None),
            P(("dp", "mp"), None),
            P(("dp", "mp"), None),
        ),
        check_vma=False,
    )
```

```python
import functools
import math
import types

import jax
import jax.numpy as jnp
from jax import lax
from jax.experimental import pallas as pl
from jax.experimental.pallas import tpu as pltpu
from jax.sharding import PartitionSpec as P

C_FAST = 128
B_FAST = 32
C_SLOW = 1024
B_SLOW = 256
C_LAT = 256
TILE = 16
POS = TILE * TILE
BLK = 128
STEP = 10
NBLK = 7591

norm_eps = 1e-05
beta_first = 0.5
beta_second = 0.5
adam_eps = 1e-08
decay_rate = 0.05

MESH = pl.DeviceIdType.MESH
f32 = jnp.float32
bf16 = jnp.bfloat16
RC = 32
CH = 256
GROUPS = BLK // B_FAST
COLUMNS = 2
HALF = POS // COLUMNS
SLABS = C_SLOW // BLK

AT_F1 = 0
AT_F2 = AT_F1 + B_FAST * 3 * C_FAST // BLK
AT_F3 = AT_F2 + B_FAST * B_FAST // BLK
AT_LAT = AT_F3 + C_FAST * B_FAST // BLK
AT_S1 = AT_LAT + C_LAT * 5 * C_FAST // BLK
AT_S2 = AT_S1 + B_SLOW * (C_SLOW + C_LAT) // BLK
AT_S3 = AT_S2 + B_SLOW * 3 * B_SLOW // BLK
AT_VEC = AT_S3 + C_SLOW * B_SLOW // BLK
V_F3 = (1, 2, 1)
V_LAT = (3, 5, 2)
V_S1 = (7, 9, 2)
V_S2 = (11, 13, 2)
V_S3 = (15, 23, 8)


def up(n, m):
    return (n + m - 1) // m * m


def dot_nt(a, b):
    return lax.dot_general(a, b, (((1,), (1,)), ((), ())), preferred_element_type=f32)


def dot_tn(a, b):
    return lax.dot_general(a, b, (((0,), (0,)), ((), ())), preferred_element_type=f32)


def dot_nn(a, b):
    return lax.dot_general(a, b, (((1,), (0,)), ((), ())), preferred_element_type=f32)


G0 = math.sqrt(2.0 / math.pi)
G1 = 0.044715


def gelu(x):
    t = jnp.tanh(x * (G0 + (G0 * G1) * (x * x)))
    return 0.5 * x * (1.0 + t)


def gelu_slope(x):
    xx = x * x
    t = jnp.tanh(x * (G0 + (G0 * G1) * xx))
    return 0.5 * (1.0 + t) + (0.5 * x) * (1.0 - t * t) * (G0 + (3.0 * G0 * G1) * xx)


def position_mask(crop):
    spot = lax.broadcasted_iota(jnp.int32, (POS, BLK), 0)
    inside = (spot // TILE < crop) & (lax.rem(spot, TILE) < crop)
    return jnp.where(inside, 1.0, 0.0).astype(f32)


def lane_group():
    return lax.broadcasted_iota(jnp.int32, (1, BLK), 1) // B_FAST


def fold_lanes(v):
    v = v + pltpu.roll(v, B_FAST, 1)
    return v + pltpu.roll(v, 2 * B_FAST, 1)


def remote(source, target, send_sem, recv_sem, device):
    pltpu.make_async_remote_copy(
        src_ref=source,
        dst_ref=target,
        send_sem=send_sem,
        recv_sem=recv_sem,
        device_id=device,
        device_id_type=MESH,
    ).start()


def arrived(view, sem):
    pltpu.make_async_copy(view, view, sem).wait()


class Place:
    def __init__(self, nd, nm):
        self.nd, self.nm = nd, nm
        self.nx = nd // 2
        self.nb = COLUMNS
        self.na = nm // self.nb
        self.dp = lax.axis_index("dp")
        self.mp = lax.axis_index("mp")
        self.x, self.c = self.dp // 2, lax.rem(self.dp, 2)
        self.a, self.b = self.mp // self.nb, lax.rem(self.mp, self.nb)

    def off_a(self, i):
        return lax.rem(self.a + i, self.na)

    def off_b(self, i):
        return lax.rem(self.b + i, self.nb)

    def off_x(self, i):
        return lax.rem(self.x + i, self.nx)

    def dev(self, x, c, a, b):
        return (x * 2 + c, a * self.nb + b)

    def slot(self, x, c, a, b):
        return (x * 2 + c) * self.nm + a * self.nb + b


class Gather:
    def __init__(self, place, slabs, other, skip, send, near, far):
        self.p, self.slabs, self.other, self.skip = place, slabs, other, skip
        self.sems = send, near, far

    def view(self, rank):
        return self.slabs.at[rank + self.skip]

    def along(self, rank):
        p, (send, near, far) = self.p, self.sems
        for i in range(1, p.na):
            device = (p.dp, p.off_a(i) * p.nb + p.b)
            remote(self.view(rank), self.view(rank), send, far, device)

    def start(self):
        p, (send, near, far) = self.p, self.sems
        remote(self.other, self.view(p.mp), send, near, (p.dp, p.a * p.nb + p.off_b(1)))
        self.along(p.mp)

    def relay(self):
        p, (send, near, far) = self.p, self.sems
        rank = p.a * p.nb + p.off_b(1)
        arrived(self.view(rank), near)
        self.along(rank)

    def finish(self):
        arrived(self.slabs.at[pl.ds(0, (self.p.na - 1) * self.p.nb)], self.sems[2])

    def drain(self):
        arrived(self.slabs.at[pl.ds(0, self.p.nm - 1)], self.sems[0])


EX_LAT, EX_S1, EX_S2, EX_B2, EX_B1, EX_BLAT = range(6)
EX_F1, EX_F2, EX_F3, EX_BF3, EX_BF2, EX_BF1 = range(6, 12)
EX_S3, EX_BS3 = 12, 13
EXCHANGES = 14

FAST_OUT, SLOW_OUT, FAST_GRAD, SLOW_GRAD = range(4)
SENT, MINE, GOT = range(3)


def outputs(cfg):
    nd, nm, frames, slow_frames, share, slots = cfg
    halves = POS // BLK
    fast, slow = (C_FAST * halves, BLK), (share * slow_frames * halves, BLK)
    result = [(fast, f32), (slow, f32), (fast, f32), (slow, f32), ((up(slots, 16), BLK), f32)]
    result += [((8, BLK), jnp.int32)]
    if share != BLK:
        result += [((nm, share, slow_frames * HALF), bf16)] * 2
    return result


def scratch(cfg):
    nd, nm, frames, slow_frames, share, slots = cfg
    devices, group = nd * nm, nd * COLUMNS
    rows = up(slots + 15, 16)
    height = up(slots, 16)
    halves = POS // BLK
    slow_rows, fast_rows = slow_frames * HALF, frames * HALF
    group_rows = fast_rows // GROUPS
    windows = group // 2
    vmem, smem, dma = pltpu.VMEM, pltpu.SMEM, pltpu.SemaphoreType.DMA
    piece = (slow_rows, BLK) if share == BLK else (share, slow_rows)
    result = dict(
        owner_v=vmem((NBLK,), jnp.int32),
        owner_s=smem((NBLK,), jnp.int32),
        run_device=smem((devices,), jnp.int32),
        run_start=smem((devices,), jnp.int32),
        run_count=smem((devices,), jnp.int32),
        win_start=smem((group,), jnp.int32),
        info=vmem((8, BLK), jnp.int32),
        table_v=vmem((8, BLK), jnp.int32),
        table_s=smem((8, BLK), jnp.int32),
        shift=vmem((rows + 16, BLK), f32),
        p=vmem((devices * (rows // 16), 16, BLK), bf16),
        q=vmem((devices, 16, BLK), bf16),
        fast_v=vmem((C_FAST, POS), bf16),
        slow_v=vmem((share * slow_frames * halves, BLK), bf16),
        fcot_v=vmem((C_FAST, POS), bf16),
        scot_v=vmem((share * slow_frames * halves, BLK), bf16),
        stage=vmem((share * slow_frames * halves, BLK), f32),
        turned=vmem((POS, BLK), f32),
        x_other=vmem((HALF, BLK), bf16),
        fc_other=vmem((HALF, BLK), bf16),
        xs_other=vmem(piece, bf16),
        sc_other=vmem(piece, bf16),
        xt=vmem((frames + 4, HALF, BLK), bf16),
        xs=vmem((SLABS, slow_rows, BLK), bf16),
        fc=vmem((frames, HALF, BLK), bf16),
        sc=vmem((SLABS, slow_rows, BLK), bf16),
        wide=vmem((slow_rows, 5 * C_FAST), bf16),
        lat_w=vmem((C_LAT, 5 * C_FAST), bf16),
        s1_w=vmem((B_SLOW, C_SLOW + C_LAT), bf16),
        s2_w=vmem((B_SLOW, 3 * B_SLOW), bf16),
        s3_w=vmem((C_SLOW, B_SLOW), bf16),
        f1_w=vmem((BLK, 3 * C_FAST), bf16),
        f2_w=vmem((BLK, BLK), bf16),
        f3_w=vmem((BLK, BLK), bf16),
        vec=vmem((32, BLK), f32),
        mask_all=vmem((POS, BLK), f32),
        mask=vmem((HALF, BLK), f32),
    )
    if share != BLK:
        result.update(
            piece=vmem(piece, bf16),
            turn=vmem((BLK, HALF), bf16),
        )
    result.update(
        zb=vmem((slow_rows, 256), bf16),
        latb=vmem((slow_rows, 256), bf16),
        s2b=vmem((slow_rows, 256), bf16),
        dz=vmem((slow_rows, 256), bf16),
        da1=vmem((slow_rows, 256), bf16),
    )
    result.update(
        two_in=vmem(((slow_frames + 2) * HALF, 256), bf16),
        two_back=vmem(((slow_frames + 2) * HALF, 256), bf16),
        c1=vmem((slow_rows, 256), f32),
        c2=vmem((slow_rows, 256), f32),
        c3=vmem((slow_rows, C_SLOW), f32),
        e=vmem((slow_rows, 256), f32),
        e3=vmem((slow_rows, C_SLOW), f32),
        da3=vmem((slow_rows, C_SLOW), bf16),
        a1p=vmem((group_rows, BLK), f32),
        a2p=vmem((group_rows, BLK), f32),
        h1p=vmem((group_rows, BLK), bf16),
        h2p=vmem((group_rows, BLK), bf16),
        d1p=vmem((group_rows, BLK), bf16),
        d2p=vmem((group_rows, BLK), bf16),
        ep=vmem((group_rows, BLK), f32),
        a3=vmem((fast_rows, BLK), f32),
        e3f=vmem((fast_rows, BLK), f32),
        da3f=vmem((fast_rows, BLK), bf16),
        square=vmem((BLK, BLK), f32),
        flat=vmem((up(NBLK + height, 64), BLK), f32),
        sib_out=vmem((windows, height, BLK), bf16),
        sib_in=vmem((windows, height, BLK), bf16),
        far_out=vmem((windows, height, BLK), bf16),
        far_in=vmem((windows, height, BLK), bf16),
        st=vmem((12, group, 8, BLK), f32),
        st16=vmem((2, group, 16, BLK), f32),
    )
    result.update(
        fast_out_box=vmem((3, HALF, BLK), f32),
        slow_out_box=vmem((3, slow_rows, BLK), f32),
        fast_grad_box=vmem((3, HALF, BLK), f32),
        slow_grad_box=vmem((3, slow_rows, BLK), f32),
        fast_out_end=vmem((C_FAST * halves, BLK), f32),
        slow_out_end=vmem((share * slow_frames * halves, BLK), f32),
        fast_grad_end=vmem((C_FAST * halves, BLK), f32),
        slow_grad_end=vmem((share * slow_frames * halves, BLK), f32),
        end_grad=vmem((height, BLK), f32),
        p_send=dma(()),
        p_recv=dma((devices // 2,)),
        p_sibling=dma(()),
        gather_sems=dma((4, 3)),
        ex_send=dma(()),
        ex_recv=dma((EXCHANGES,)),
        box_send=dma(()),
        box_recv=dma((4,)),
        sum_sems=dma((3,)),
        sib_recv=dma((windows,)),
        local=dma((16,)),
    )
    return result


def main_kernel(cfg, *refs):
    nd, nm, frames, slow_frames, share, slots = cfg
    n_out = len(outputs(cfg))
    args, results, held = refs[:7], refs[7 : 7 + n_out], refs[7 + n_out :]
    crop_in, owner_in, master_in, fast_in, slow_in, fcot_in, scot_in = args
    R = types.SimpleNamespace(**dict(zip(scratch(cfg), held, strict=True)))
    p = Place(nd, nm)
    devices = nd * nm
    halves = POS // BLK
    rows = up(slots + 15, 16)
    tiles = rows // 16
    slow_rows, fast_rows = slow_frames * HALF, frames * HALF
    per_group = frames // GROUPS
    group_rows = per_group * HALF
    slabs = share == BLK
    me = p.dp * nm + p.mp
    partner = p.a * p.nb + p.off_b(1)

    members = nd * p.nb
    member = p.dp * p.nb + p.b
    group_peers = [
        p.dev(p.off_x(i), lax.rem(p.c + k, 2), p.a, p.off_b(j))
        for i in reversed(range(p.nx))
        for j in reversed(range(p.nb))
        for k in range(2)
        if i or j or k
    ]
    near = [p.dev(p.x, p.c, p.off_a(i), p.b) for i in range(1, p.na)]
    barrier = pltpu.get_barrier_semaphore()
    for device in group_peers + near:
        pl.semaphore_signal(barrier, inc=1, device_id=device, device_id_type=MESH)

    local_copies = []

    def fetch(source, target):
        copy = pltpu.make_async_copy(source, target, R.local.at[len(local_copies)])
        copy.start()
        local_copies.append(copy)
        return copy

    get_owner = fetch(owner_in, R.owner_v)
    get_owner_s = fetch(owner_in, R.owner_s)
    get_master = fetch(master_in, R.shift.at[pl.ds(16, slots)])
    get_fast = fetch(fast_in, R.fast_v)
    get_slow = fetch(slow_in, R.slow_v)
    get_fcot = fetch(fcot_in, R.fcot_v)
    get_scot = fetch(scot_in, R.scot_v)

    crop = crop_in[0]
    R.mask_all[...] = position_mask(crop)
    R.mask[...] = R.mask_all[pl.ds(pl.multiple_of(p.b * HALF, HALF), HALF), :]
    tall = crop.astype(f32)
    area = tall * tall * (1.0 / COLUMNS)
    xt_ref, xs_ref, fc_ref, sc_ref = R.xt, R.xs, R.fc, R.sc
    for f in (0, 1, frames + 2, frames + 3):
        xt_ref[f] = jnp.zeros((HALF, BLK), bf16)
    two_in, two_back = R.two_in, R.two_back
    for ref in (two_in, two_back):
        ref[:HALF] = jnp.zeros((HALF, 256), bf16)
        ref[(slow_frames + 1) * HALF :] = jnp.zeros((HALF, 256), bf16)

    get_owner.wait()
    spot = lax.broadcasted_iota(jnp.int32, (8, BLK), 0) * BLK
    spot = spot + lax.broadcasted_iota(jnp.int32, (8, BLK), 1)
    lowest = jnp.full((8, BLK), NBLK, jnp.int32)
    number = jnp.zeros((8, BLK), jnp.int32)
    whole = NBLK // 1024 * 1024
    for i in range(0, whole, 1024):
        mine = R.owner_v[pl.ds(i, 1024)].reshape(8, BLK) == me
        lowest = jnp.minimum(lowest, jnp.where(mine, spot + i, NBLK))
        number = number + jnp.where(mine, 1, 0)
    for i in range(whole, NBLK // BLK * BLK, BLK):
        mine = R.owner_v[pl.ds(i, BLK)].reshape(1, BLK) == me
        mine = mine & (spot < BLK)
        lowest = jnp.minimum(lowest, jnp.where(mine, spot + i, NBLK))
        number = number + jnp.where(mine, 1, 0)
    get_owner_s.wait()

    def last_ones(i, found):
        first, n = found
        mine = R.owner_s[i] == me
        return jnp.where(mine, jnp.minimum(first, i), first), n + jnp.where(mine, 1, 0)

    found = jnp.min(lowest), jnp.sum(number)
    my_start, my_count = lax.fori_loop(NBLK // BLK * BLK, NBLK, last_ones, found)
    line = lax.broadcasted_iota(jnp.int32, (8, BLK), 0)
    R.info[...] = jnp.where(line == 0, my_start, my_count)
    shift = lax.rem(my_start, 16)
    get_master.wait()
    moved = R.shift[pl.ds(16 - shift, rows), :]
    row = lax.broadcasted_iota(jnp.int32, (rows, BLK), 0)
    own = (row >= shift) & (row < shift + my_count)
    p_ref = R.p

    def p_slot(slot):
        return p_ref.at[pl.ds(slot * tiles, tiles)]

    p_slot(me)[...] = jnp.where(own, moved, 0.0).astype(bf16).reshape(tiles, 16, BLK)

    pl.semaphore_wait(barrier, len(group_peers) + len(near))
    p_sends = []

    def view(x, c, a, b):
        return p_slot(p.slot(x, c, a, b))

    def came(source):
        x, c, a, b = source
        return R.p_recv.at[x * nm + a * p.nb + b]

    def pass_on(source, along_a=(), along_b=False, along_x=False, along_c=False):
        piece, sem = view(*source), came(source)
        to = []
        for i in along_a:
            to += [p.dev(p.x, p.c, p.off_a(i), p.b)]
        if along_x:
            to += [p.dev(p.off_x(i), p.c, p.a, p.b) for i in range(1, p.nx)]
        if along_b:
            to += [p.dev(p.x, p.c, p.a, p.off_b(1))]
        for device in to:
            remote(piece, piece, R.p_send, sem, device)
            p_sends.append(device)
        if along_c:
            device = p.dev(p.x, 1 - p.c, p.a, p.b)
            remote(piece, piece, R.p_send, R.p_sibling, device)
            p_sends.append(device)

    def take(source):
        arrived(view(*source), came(source))

    here = (p.x, p.c, p.a, p.b)
    pass_on(here, along_a=range(1, p.na), along_b=True, along_x=True, along_c=True)

    turned_ref = R.turned

    def half_of(b):
        return pl.ds(pl.multiple_of(b * HALF, HALF), HALF)

    def own_frame(slot, other, source):
        turned_ref[...] = source[...].astype(f32).T * R.mask_all[...]
        slot[...] = turned_ref[half_of(p.b), :].astype(bf16)
        other[...] = turned_ref[half_of(p.off_b(1)), :].astype(bf16)

    def own_slow(slot, other, source):
        stage = R.stage
        stage[...] = source[...].astype(f32)
        for s in range(slow_frames):
            at = slice(s * HALF, (s + 1) * HALF)
            for h in range(halves):
                part = stage[pl.ds(h * slow_frames + s, share, stride=halves * slow_frames), :]
                if slabs:
                    here = slice(h * BLK, (h + 1) * BLK)
                    turned_ref[here, :] = part.T * R.mask_all[here, :]
                else:
                    turned_ref[h * share : (h + 1) * share, :] = part
            if slabs:
                slot[at, :] = turned_ref[half_of(p.b), :].astype(bf16)
                other[at, :] = turned_ref[half_of(p.off_b(1)), :].astype(bf16)
            else:
                for ref, b in ((R.piece, p.b), (other, p.off_b(1))):
                    mine = pl.ds(pl.multiple_of(b * share, share), share)
                    ref[:, at] = turned_ref[mine, :].astype(bf16)
        if not slabs:
            pltpu.sync_copy(R.piece, slot)

    def from_natural(natural, wide):
        ranks = BLK // share

        def block(i, _):
            s, j = i // SLABS, lax.rem(i, SLABS)
            at_row = pl.ds(pl.multiple_of(s * HALF, HALF), HALF)
            for k in range(ranks):
                pltpu.sync_copy(
                    natural.at[j * ranks + k, :, at_row],
                    R.turn.at[pl.ds(k * share, share)],
                )
            piece = R.turn[...].astype(f32).T * R.mask[...]
            wide[j, at_row, :] = piece.astype(bf16)
            return 0

        lax.fori_loop(0, slow_frames * SLABS, block, 0)

    def gather(which, array, other, skip=0):
        sems = [R.gather_sems.at[which, i] for i in range(3)]
        return Gather(p, array, other, skip, *sems)

    x_gather = gather(0, xt_ref, R.x_other, 2)
    fc_gather = gather(1, fc_ref, R.fc_other)
    xs_gather = gather(2, xs_ref if slabs else results[6], R.xs_other)
    sc_gather = gather(3, sc_ref if slabs else results[7], R.sc_other)
    get_fast.wait()
    own_frame(x_gather.view(p.mp), R.x_other, R.fast_v)
    x_gather.start()
    get_slow.wait()
    own_slow(xs_gather.view(p.mp), R.xs_other, R.slow_v)

    steps = [1 << i for i in reversed(range(max(1, (slots - 1).bit_length())))]
    owner_s, run_device, run_start, run_count = (R.owner_s, R.run_device, R.run_start, R.run_count)

    def run(k, at):
        device = owner_s[jnp.minimum(at, NBLK - 1)]
        n = jnp.int32(1)
        for step in steps:
            more = n + step
            last = at + more - 1
            inside = owner_s[jnp.minimum(last, NBLK - 1)] == device
            n = jnp.where((more <= slots) & (last < NBLK) & inside, more, n)
        run_device[k] = device
        run_start[k] = at
        run_count[k] = n
        return at + n

    lax.fori_loop(0, devices, run, jnp.int32(0))

    targets = [(i, j) for i in range(p.nx) for j in range(p.nb)]
    owners = [p.slot(p.off_x(i), c, p.a, p.off_b(j)) for c in (p.c, 1 - p.c) for i, j in targets]

    def find(k, found):
        return [jnp.where(run_device[k] == d, run_start[k], at) for d, at in zip(owners, found)]

    for i, at in enumerate(lax.fori_loop(0, devices, find, [jnp.int32(0)] * len(owners))):
        R.win_start[i] = at

    for i in range(1, p.na):
        source = (p.x, p.c, p.off_a(p.na - i), p.b)
        take(source)
        pass_on(source, along_b=True, along_x=True, along_c=True)
    x_gather.relay()
    xs_gather.start()

    def tile_of(k):
        return run_device[k] * tiles - run_start[k] // 16

    def table(k, found):
        start, last = run_start[k], run_start[k] + run_count[k] - 1
        final = jnp.minimum(spot * 16 + 15, NBLK - 1)
        holds = (final >= start) & (final <= last)
        tile = jnp.where(spot == start // 16, devices * tiles + k, spot + tile_of(k))
        return jnp.where(holds, tile, found)

    R.table_v[...] = lax.fori_loop(0, devices, table, jnp.zeros((8, BLK), jnp.int32))
    get_table = fetch(R.table_v, R.table_s)

    across = p.na // 2
    for i in range(p.na):
        source = (p.x, p.c, p.off_a(p.na - i), p.off_b(1))
        take(source)
        pass_on(source, along_x=i < across, along_c=True)
        for j in range(1, p.nx):
            source = (p.off_x(j), p.c, p.off_a(p.na - i), p.b)
            take(source)
            pass_on(source, along_b=i >= across, along_c=True)
    xs_gather.relay()
    get_fcot.wait()
    own_frame(fc_gather.view(p.mp), R.fc_other, R.fcot_v)
    get_scot.wait()
    own_slow(sc_gather.view(p.mp), R.sc_other, R.scot_v)
    for i in range(p.na):
        for k in range(1, p.nx):
            source = (p.off_x(k), p.c, p.off_a(p.na - i), p.off_b(1))
            take(source)
            pass_on(source, along_c=True)
    sc_gather.start()
    arrived(p_ref.at[pl.ds(0, devices // 2 * tiles)], R.p_sibling)
    get_table.wait()

    def tile_rows(t):
        return pl.ds(pl.multiple_of(t * 16, 16), 16)

    q_ref = R.q

    def first_tile(k, before):
        tile = p_ref[run_device[k] * tiles].astype(f32)
        shared = lax.rem(run_start[k], 16) != 0
        tile = tile + jnp.where(shared, before, 0.0)
        q_ref[k] = tile.astype(bf16)
        last = (run_start[k] + run_count[k] - 1) // 16
        alone = last == run_start[k] // 16
        return jnp.where(alone, tile, p_ref[tile_of(k) + last].astype(f32))

    lax.fori_loop(0, devices, first_tile, jnp.zeros((16, BLK), f32))
    flat_ref, table_s = R.flat, R.table_s

    def lay_out(first_block, end_block):
        first, end = first_block // 16, up(end_block, 16) // 16

        def one(t):
            source = table_s[t // BLK, lax.rem(t, BLK)]
            plain = p_ref[jnp.minimum(source, devices * tiles - 1)]
            shared = q_ref[jnp.maximum(source - devices * tiles, 0)]
            tile = jnp.where(source < devices * tiles, plain, shared)
            flat_ref[tile_rows(t), :] = tile.astype(f32)

        def eight(i, _):
            for k in range(8):
                one(first + i * 8 + k)
            return 0

        lax.fori_loop(0, (end - first) // 8, eight, 0)
        for t in range(first + (end - first) // 8 * 8, end):
            one(t)

    def matrix(out_ref, at, height, blocks):
        lay_out(at, at + height * blocks)
        for j in range(blocks):
            for o in range(0, height, 256):
                out_ref[o : o + 256, j * BLK : (j + 1) * BLK] = flat_ref[
                    pl.ds(at + o * blocks + j, 256, stride=blocks), :
                ].astype(bf16)

    group = lane_group()
    square_ref = R.square
    lat_w, s1_w, s2_w, s3_w = R.lat_w, R.s1_w, R.s2_w, R.s3_w
    f1_w, f2_w, f3_w, vec_ref = R.f1_w, R.f2_w, R.f3_w, R.vec

    def spread_rows(at, height):
        for r in range(GROUPS):
            part = jnp.where(group == r, flat_ref[at : at + height // GROUPS, :], 0.0)
            square_ref[pl.ds(r, height // GROUPS, stride=GROUPS), :] = fold_lanes(part)
        return square_ref[:height, :]

    def fast_weights():
        lay_out(AT_F1, AT_LAT)
        for k in range(3):
            tap = flat_ref[pl.ds(AT_F1 + k, B_FAST, stride=3), :].astype(bf16)
            for g in range(GROUPS):
                f1_w[g * B_FAST : (g + 1) * B_FAST, k * BLK : (k + 1) * BLK] = tap
        two = spread_rows(AT_F2, B_FAST)
        for g in range(GROUPS):
            f2_w[g * B_FAST : (g + 1) * B_FAST, :] = jnp.where(group == g, two, 0.0).astype(bf16)
        f3_w[...] = spread_rows(AT_F3, C_FAST).astype(bf16)

    matrix(lat_w, AT_LAT, C_LAT, 5)
    lay_out(AT_VEC, NBLK)
    vec_ref[...] = flat_ref[AT_VEC : AT_VEC + 32, :]
    x_gather.finish()

    zb, latb, s2b, dz, da1, wide_ref = (R.zb, R.latb, R.s2b, R.dz, R.da1, R.wide)
    c1, c2, c3, e, e3, da3 = (R.c1, R.c2, R.c3, R.e, R.e3, R.da3)
    a1p, a2p, h1p, h2p, d1p, d2p, ep, a3, e3f, da3f = (R.a1p, R.a2p, R.h1p, R.h2p, R.d1p, R.d2p, R.ep, R.a3, R.e3f, R.da3f)
    mask_ref, st_ref, st16_ref = R.mask, R.st, R.st16
    s1b = two_in.at[pl.ds(HALF, slow_rows)]
    da2 = two_back.at[pl.ds(HALF, slow_rows)]

    def stat(which):
        return (st_ref, which) if which < 12 else (st16_ref, which - 12)

    def exchange(which):
        ref, at = stat(which)
        own = ref.at[at, member]
        for device in group_peers:
            remote(own, own, R.ex_send, R.ex_recv.at[which], device)

    def exchanged(which):
        ref, at = stat(which)
        arrived(ref.at[at, pl.ds(0, members - 1)], R.ex_recv.at[which])
        total = ref[at, 0]
        for i in range(1, members):
            total = total + ref[at, i]
        return total

    def put(which, at, vector):
        ref, index = stat(which)
        for j in range(vector.shape[1] // BLK):
            ref[index, member, at + j : at + j + 1, :] = vector[:, j * BLK : (j + 1) * BLK]

    def fill(which, at, value):
        ref, index = stat(which)
        ref[index, member, at:8, :] = jnp.full((8 - at, BLK), value, f32)

    def row_of(block, at, n):
        return jnp.concatenate([block[at + j : at + j + 1, :] for j in range(n)], 1)

    def vectors(place):
        g, b, n = place
        return row_of(vec_ref[...], g, n), row_of(vec_ref[...], b, n)

    def rows_at(i, size):
        return pl.ds(pl.multiple_of(i * size, size), size)

    def mask_at(i, width):
        part = mask_ref[pl.ds(pl.multiple_of(lax.rem(i * RC, HALF), RC), RC), :]
        return jnp.concatenate([part] * (width // BLK), 1) if width > BLK else part

    def eights(v):
        return jnp.sum(v.reshape(v.shape[0] // 8, 8, v.shape[1]), 0)

    def total_row(v):
        return jnp.sum(v, 0, keepdims=True)

    def affine(sums, squares, count, gain, bias):
        mean = sums / count
        scale = lax.rsqrt(squares / count - mean * mean + norm_eps)
        grow = gain * scale
        return mean, scale, grow, bias - mean * grow

    def loop(n, body, start):
        return lax.fori_loop(0, n, body, start, unroll=n if n <= 8 else 4)

    def sums_of(ref, n_rows, width):
        def body(i, acc):
            v = ref[rows_at(i, RC), :].astype(f32)
            return acc[0] + eights(v), acc[1] + eights(v * v)

        zero = jnp.zeros((8, width), f32)
        one, two = loop(n_rows // RC, body, (zero, zero))
        return total_row(one), total_row(two)

    def activate(src, dst, n_rows, width, grow, base):
        def body(i, _):
            at = rows_at(i, RC)
            pre = src[at, :].astype(f32) * grow + base
            dst[at, :] = (gelu(pre) * mask_at(i, width)).astype(bf16)
            return 0

        loop(n_rows // RC, body, 0)

    def slopes(src, incoming, n_rows, width, norm):
        mean, scale, grow, base = norm

        def body(i, acc):
            at = rows_at(i, RC)
            a = src[at, :].astype(f32)
            d = gelu_slope(a * grow + base) * incoming[at, :] * mask_at(i, width)
            incoming[at, :] = d
            return acc[0] + eights(d), acc[1] + eights(d * ((a - mean) * scale))

        zero = jnp.zeros((8, width), f32)
        one, two = loop(n_rows // RC, body, (zero, zero))
        return total_row(one), total_row(two)

    def back_vectors(bias_sum, gain_sum, count, norm):
        mean, scale, grow, base = norm
        k1 = grow * gain_sum / count
        return grow * bias_sum / count - k1 * (mean * scale), k1 * scale

    def raw_grads(src, pres, dst, n_rows, width, norm, q0, q1):
        grow = norm[2]

        def body(i, _):
            at = rows_at(i, RC)
            a = src[at, :].astype(f32)
            da = grow * pres[at, :] - mask_at(i, width) * (q0 + a * q1)
            dst[at, :] = da.astype(bf16)
            return 0

        loop(n_rows // RC, body, 0)

    def put_vector(row, vector):
        for j in range(vector.shape[1] // BLK):
            at = AT_VEC + row + j
            flat_ref[at : at + 1, :] = vector[:, j * BLK : (j + 1) * BLK]

    def put_pair(which, one, two, place=None):
        put(which, 0, one)
        put(which, one.shape[1] // BLK, two)
        if place is not None:
            put_vector(place[0], two)
            put_vector(place[1], one)

    slow_chunks = [slice(i, i + CH) for i in range(0, slow_rows, CH)]
    group_chunks = [slice(i, i + CH) for i in range(0, group_rows, CH)]

    def all_slabs(ref, at):
        return jnp.concatenate([ref[j, at, :] for j in range(SLABS)], 1)

    boxes = (
        (R.fast_out_box, R.fast_out_end),
        (R.slow_out_box, R.slow_out_end),
        (R.fast_grad_box, R.fast_grad_end),
        (R.slow_grad_box, R.slow_grad_end),
    )

    def box(which, kind):
        return boxes[which][0].at[kind]

    def hand_over(which):
        box_sems = R.box_send, R.box_recv.at[which]
        remote(box(which, SENT), box(which, GOT), *box_sems, (p.dp, partner))

    deliveries = []

    def deliver(source, which):
        sem = R.local.at[len(local_copies) + len(deliveries)]
        copy = pltpu.make_async_copy(source, results[which], sem)
        copy.start()
        deliveries.append(copy)

    def to_channels(block):
        turned = block.T
        if slabs:
            return turned
        lane_shift = lax.rem(p.mp * share, BLK)
        return sum(
            jnp.where(lane_shift == k * share, turned[k * share : (k + 1) * share, :], 0.0)
            for k in range(BLK // share)
        )

    def complete(which):
        ref, end = boxes[which]
        arrived(box(which, GOT), R.box_recv.at[which])
        fast = which in (FAST_OUT, FAST_GRAD)
        n = 1 if fast else slow_frames
        for s in range(n):
            at = slice(s * HALF, (s + 1) * HALF)
            for h in range(halves):
                block = jnp.where(p.b == h, ref[MINE, at, :], ref[GOT, at, :])
                block = block.T if fast else to_channels(block)
                end[pl.ds(s * halves + h, block.shape[0], stride=n * halves), :] = block
        deliver(end, which)

    for s in range(slow_frames):
        for k in range(5):
            wide_ref[s * HALF : (s + 1) * HALF, k * BLK : (k + 1) * BLK] = xt_ref[4 * s + k]
    for at in slow_chunks:
        zb[at, :] = dot_nt(wide_ref[at, :], lat_w[...]).astype(bf16)
    put_pair(EX_LAT, *sums_of(zb, slow_rows, C_LAT))
    fill(EX_LAT, 4, area)
    exchange(EX_LAT)

    fast_weights()

    def fast_rows_of(ref, first_frame, at):
        f = first_frame + at.start // HALF
        return jnp.concatenate([ref[f + i] for i in range(CH // HALF)], 0)

    for at in group_chunks:
        total = jnp.zeros((CH, BLK), f32)
        for g in range(GROUPS):
            window = jnp.concatenate(
                [fast_rows_of(xt_ref, g * per_group + 1 + k, at) for k in range(3)], 1
            )
            total = total + jnp.where(group == g, dot_nt(window, f1_w[...]), 0.0)
        a1p[at, :] = total

    def put_folded(which, one, two):
        put(which, 0, fold_lanes(one))
        put(which, 1, fold_lanes(two))

    put_folded(EX_F1, *sums_of(a1p, group_rows, BLK))
    fill(EX_F1, 2, area)
    exchange(EX_F1)
    sc_gather.relay()
    fc_gather.start()

    matrix(s1_w, AT_S1, B_SLOW, 10)
    xs_gather.finish()
    if not slabs:
        from_natural(results[6], xs_ref)

    for at in slow_chunks:
        c1[at, :] = dot_nt(all_slabs(xs_ref, at), s1_w[:, :C_SLOW])

    total = exchanged(EX_LAT)
    area_all = total[4:5, :]
    slow_count = jnp.concatenate([area_all * float(slow_frames)] * 2, 1)
    slow_count8 = jnp.concatenate([slow_count] * 4, 1)
    fast_count = area_all * float(frames)
    lat_norm = affine(row_of(total, 0, 2), row_of(total, 2, 2), slow_count, *vectors(V_LAT))
    activate(zb, latb, slow_rows, C_LAT, lat_norm[2], lat_norm[3])
    for at in slow_chunks:
        c1[at, :] = c1[at, :] + dot_nt(latb[at, :], s1_w[:, C_SLOW:])
    put_pair(EX_S1, *sums_of(c1, slow_rows, B_SLOW))
    fill(EX_S1, 4, 0.0)
    exchange(EX_S1)

    matrix(s2_w, AT_S2, B_SLOW, 6)
    fc_gather.relay()
    matrix(s3_w, AT_S3, C_SLOW, 2)

    packed = vec_ref[0:1, :]

    def spread(which):
        return fold_lanes(jnp.where(group == which, packed, 0.0))

    def exchanged_two(which):
        total = exchanged(which)
        return total[0:1, :], total[1:2, :]

    f1_norm = affine(*exchanged_two(EX_F1), fast_count, spread(0), spread(1))
    activate(a1p, h1p, group_rows, BLK, f1_norm[2], f1_norm[3])
    for at in group_chunks:
        a2p[at, :] = dot_nt(h1p[at, :], f2_w[...])
    put_folded(EX_F2, *sums_of(a2p, group_rows, BLK))
    fill(EX_F2, 2, 0.0)
    exchange(EX_F2)

    total = exchanged(EX_S1)
    s1_norm = affine(row_of(total, 0, 2), row_of(total, 2, 2), slow_count, *vectors(V_S1))
    activate(c1, s1b, slow_rows, B_SLOW, s1_norm[2], s1_norm[3])

    def shifted(ref, at, k):
        return ref[at.start + k * HALF : at.stop + k * HALF, :]

    for at in slow_chunks:
        window = jnp.concatenate([shifted(two_in, at, k) for k in range(3)], 1)
        c2[at, :] = dot_nt(window, s2_w[...])
    put_pair(EX_S2, *sums_of(c2, slow_rows, B_SLOW))
    fill(EX_S2, 4, 0.0)
    exchange(EX_S2)

    f2_norm = affine(*exchanged_two(EX_F2), fast_count, spread(2), spread(3))
    activate(a2p, h2p, group_rows, BLK, f2_norm[2], f2_norm[3])
    for g in range(GROUPS):
        for at in group_chunks:
            part = jnp.where(group == g, h2p[at, :], 0.0).astype(bf16)
            here = slice(g * group_rows + at.start, g * group_rows + at.stop)
            a3[here, :] = dot_nt(part, f3_w[...])
    put_pair(EX_F3, *sums_of(a3, fast_rows, BLK))
    fill(EX_F3, 2, 0.0)
    exchange(EX_F3)

    total = exchanged(EX_S2)
    s2_norm = affine(row_of(total, 0, 2), row_of(total, 2, 2), slow_count, *vectors(V_S2))
    activate(c2, s2b, slow_rows, B_SLOW, s2_norm[2], s2_norm[3])
    quarter = C_SLOW // 4
    quarters = [slice(n * quarter, (n + 1) * quarter) for n in range(4)]
    for n, lanes in enumerate(quarters):
        for at in slow_chunks:
            c3[at, lanes] = dot_nt(s2b[at, :], s3_w[lanes, :])
        one, two = sums_of(c3.at[:, lanes], slow_rows, quarter)
        put(EX_S3, 2 * n, one)
        put(EX_S3, 8 + 2 * n, two)
    exchange(EX_S3)

    f3_norm = affine(*exchanged_two(EX_F3), fast_count, *vectors(V_F3))
    for rank, kind in ((partner, SENT), (p.mp, MINE)):
        pre = a3[rows_at(rank, HALF), :] * f3_norm[2] + f3_norm[3]
        pre = pre + xt_ref[rank + 2].astype(f32)
        R.fast_out_box[kind] = gelu(pre) * mask_ref[...]
    hand_over(FAST_OUT)
    sc_gather.finish()
    if not slabs:
        from_natural(results[7], sc_ref)
    total = exchanged(EX_S3)
    s3_norm = affine(row_of(total, 0, 8), row_of(total, 8, 8), slow_count8, *vectors(V_S3))

    def pair_of(ref, n, at):
        return jnp.concatenate([ref[2 * n, at, :], ref[2 * n + 1, at, :]], 1).astype(f32)

    for n, lanes in enumerate(quarters):
        norm = [v[:, lanes] for v in s3_norm]

        def slow_slopes(i, acc, n=n, lanes=lanes, norm=norm):
            at = rows_at(i, RC)
            a = c3[at, lanes]
            pre = a * norm[2] + norm[3] + pair_of(xs_ref, n, at)
            d = gelu_slope(pre) * pair_of(sc_ref, n, at)
            e3[at, lanes] = d
            return acc[0] + eights(d), acc[1] + eights(d * ((a - norm[0]) * norm[1]))

        zero = jnp.zeros((8, quarter), f32)
        one, two = loop(slow_rows // RC, slow_slopes, (zero, zero))
        one, two = total_row(one), total_row(two)
        put(EX_BS3, 2 * n, one)
        put(EX_BS3, 8 + 2 * n, two)
        put_vector(V_S3[0] + 2 * n, two)
        put_vector(V_S3[1] + 2 * n, one)
    exchange(EX_BS3)

    fc_gather.finish()

    def fast_slopes(i, acc):
        mean, scale, grow, base = f3_norm
        at = rows_at(i, RC)
        f, here = i // (HALF // RC), rows_at(lax.rem(i, HALF // RC), RC)
        a = a3[at, :]
        x = xt_ref[f + 2, here, :].astype(f32)
        d = gelu_slope(a * grow + base + x) * fc_ref[f, here, :].astype(f32)
        e3f[at, :] = d
        return acc[0] + eights(d), acc[1] + eights(d * ((a - mean) * scale))

    zero = jnp.zeros((8, BLK), f32)
    one, two = loop(fast_rows // RC, fast_slopes, (zero, zero))
    put_pair(EX_BF3, total_row(one), total_row(two), V_F3)
    fill(EX_BF3, 2, 0.0)
    exchange(EX_BF3)

    def slow_place(rank):
        slab = rank * share // BLK
        return slab, pl.ds(pl.multiple_of(slab * BLK, BLK), BLK)

    def slow_result(kind, rank):
        slab, lanes = slow_place(rank)
        grow, base = (
            sum(jnp.where(slab == k, v[:, k * BLK : (k + 1) * BLK], 0.0) for k in range(SLABS))
            for v in s3_norm[2:]
        )
        for s in range(slow_frames):
            at = slice(s * HALF, (s + 1) * HALF)
            pre = c3[at, lanes] * grow + base + xs_ref[slab, at, :].astype(f32)
            R.slow_out_box[kind, at, :] = gelu(pre) * mask_ref[...]

    def slow_input_grad(kind, rank):
        slab, lanes = slow_place(rank)
        for s in range(slow_frames):
            at = slice(s * HALF, (s + 1) * HALF)
            value = e3[at, lanes] + dot_nn(da1[at, :], s1_w[:, lanes])
            R.slow_grad_box[kind, at, :] = value * mask_ref[...]

    slow_result(SENT, partner)
    hand_over(SLOW_OUT)

    total = exchanged(EX_BS3)
    q0, q1 = back_vectors(row_of(total, 0, 8), row_of(total, 8, 8), slow_count8, s3_norm)
    for lanes in quarters:
        norm = [v[:, lanes] for v in s3_norm]
        raw_grads(
            c3.at[:, lanes], e3.at[:, lanes], da3.at[:, lanes], slow_rows, quarter, norm,
            q0[:, lanes], q1[:, lanes]
        )
    for at in slow_chunks:
        e[at, :] = dot_nn(da3[at, :], s3_w[...])
    put_pair(EX_B2, *slopes(c2, e, slow_rows, B_SLOW, s2_norm), V_S2)
    fill(EX_B2, 4, 0.0)
    exchange(EX_B2)

    q0, q1 = back_vectors(*exchanged_two(EX_BF3), fast_count, f3_norm)
    raw_grads(a3, e3f, da3f, fast_rows, BLK, f3_norm, q0, q1)
    for at in group_chunks:
        total = jnp.zeros((CH, BLK), f32)
        for g in range(GROUPS):
            here = slice(g * group_rows + at.start, g * group_rows + at.stop)
            total = total + jnp.where(group == g, dot_nn(da3f[here, :], f3_w[...]), 0.0)
        ep[at, :] = total
    one, two = slopes(a2p, ep, group_rows, BLK, f2_norm)
    put_folded(EX_BF2, one, two)
    fill(EX_BF2, 2, 0.0)
    exchange(EX_BF2)
    vec_two = jnp.where(group == 2, fold_lanes(two), 0.0)
    vec_two = vec_two + jnp.where(group == 3, fold_lanes(one), 0.0)

    def to_flat(at, blocks, offset, lane, value):
        for j in range(value.shape[1] // BLK):
            here = pl.ds(at + offset * blocks + lane + j, value.shape[0], stride=blocks)
            flat_ref[here, :] = value[:, j * BLK : (j + 1) * BLK]

    for n, lanes in enumerate(quarters):
        to_flat(AT_S3, 2, n * quarter, 0, dot_tn(da3[:, lanes], s2b[...]))

    total = exchanged(EX_B2)
    q0, q1 = back_vectors(row_of(total, 0, 2), row_of(total, 2, 2), slow_count, s2_norm)
    raw_grads(c2, e, da2, slow_rows, B_SLOW, s2_norm, q0, q1)
    for at in slow_chunks:
        e[at, :] = functools.reduce(
            lambda u, v: u + v,
            [
                dot_nn(shifted(two_back, at, 2 - k), s2_w[:, k * B_SLOW : (k + 1) * B_SLOW])
                for k in range(3)
            ],
        )
    put_pair(EX_B1, *slopes(c1, e, slow_rows, B_SLOW, s1_norm), V_S1)
    fill(EX_B1, 4, 0.0)
    exchange(EX_B1)

    q0, q1 = back_vectors(*exchanged_two(EX_BF2), fast_count, f2_norm)
    raw_grads(a2p, ep, d2p, group_rows, BLK, f2_norm, q0, q1)
    for at in group_chunks:
        ep[at, :] = dot_nn(d2p[at, :], f2_w[...])
    one, two = slopes(a1p, ep, group_rows, BLK, f1_norm)
    put_folded(EX_BF1, one, two)
    fill(EX_BF1, 2, 0.0)
    exchange(EX_BF1)
    vec_one = jnp.where(group == 0, fold_lanes(two), 0.0)
    vec_one = vec_one + jnp.where(group == 1, fold_lanes(one), 0.0)
    put_vector(0, vec_one + vec_two)

    everything = slice(0, slow_rows)
    for k in range(3):
        part = dot_tn(two_back[HALF : HALF + slow_rows, :], shifted(two_in, everything, k))
        to_flat(AT_S2, 6, 0, 2 * k, part)

    total = jnp.zeros((BLK, BLK), f32)
    for g in range(GROUPS):
        at = slice(g * group_rows, (g + 1) * group_rows)
        total = total + jnp.where(group == g, dot_tn(da3f[at, :], h2p[...]), 0.0)

    def to_blocks(value, at):
        n = value.shape[0] // GROUPS
        square_ref[: value.shape[0], :] = fold_lanes(value)
        flat_ref[at : at + n, :] = sum(
            jnp.where(group == r, square_ref[pl.ds(r, n, stride=GROUPS), :], 0.0)
            for r in range(GROUPS)
        )

    to_blocks(total, AT_F3)
    square = dot_tn(d2p[...], h1p[...])
    to_blocks(
        sum(
            jnp.where(group == g, square[g * B_FAST : (g + 1) * B_FAST, :], 0.0)
            for g in range(GROUPS)
        ),
        AT_F2,
    )

    total = exchanged(EX_B1)
    q0, q1 = back_vectors(row_of(total, 0, 2), row_of(total, 2, 2), slow_count, s1_norm)
    raw_grads(c1, e, da1, slow_rows, B_SLOW, s1_norm, q0, q1)
    for at in slow_chunks:
        e[at, :] = dot_nn(da1[at, :], s1_w[:, C_SLOW:])
    put_pair(EX_BLAT, *slopes(zb, e, slow_rows, C_LAT, lat_norm), V_LAT)
    fill(EX_BLAT, 4, 0.0)
    exchange(EX_BLAT)

    q0, q1 = back_vectors(*exchanged_two(EX_BF1), fast_count, f1_norm)
    raw_grads(a1p, ep, d1p, group_rows, BLK, f1_norm, q0, q1)
    for k in range(3):
        tap = jnp.zeros((B_FAST, BLK), f32)
        for g in range(GROUPS):
            first = g * per_group + k + 1
            right = jnp.concatenate([xt_ref[first + i] for i in range(per_group)], 0)
            part = dot_tn(d1p[...], right)
            tap = tap + part[g * B_FAST : (g + 1) * B_FAST, :]
        to_flat(AT_F1, 3, 0, k, tap)

    for n in range(4):
        right = jnp.concatenate([xs_ref[2 * n], xs_ref[2 * n + 1]], 1)
        to_flat(AT_S1, 10, 0, 2 * n, dot_tn(da1[...], right))
    to_flat(AT_S1, 10, 0, 8, dot_tn(da1[...], latb[...]))

    def frame_grad(rank):
        grad = e3f[rows_at(rank, HALF), :]
        for k in range(3):
            f = rank - k + 1
            there = (f >= 0) & (f < frames)
            g, j = f // per_group, lax.rem(f, per_group)
            g, j = jnp.where(there, g, 0), jnp.where(there, j, 0)
            left = jnp.where((group == g) & there, d1p[rows_at(j, HALF), :], 0.0).astype(bf16)
            grad = grad + dot_nn(left, f1_w[:, k * BLK : (k + 1) * BLK])
        return grad

    def lateral_grad(rank):
        later, s = lax.rem(rank + 2, 4), (rank + 2) // 4
        grad = jnp.zeros((HALF, BLK), f32)
        for tap, at, there in (
            (later, s, s < slow_frames),
            (later + 4, s - 1, (later == 0) & (s > 0)),
        ):
            tap, at = jnp.where(there, tap, 0), jnp.where(there, at, 0)
            left = jnp.where(there, dz[rows_at(at, HALF), :], 0.0).astype(bf16)
            weight = lat_w[:, pl.ds(pl.multiple_of(tap * BLK, BLK), BLK)]
            grad = grad + dot_nn(left, weight)
        return grad

    slow_input_grad(SENT, partner)
    hand_over(SLOW_GRAD)

    total = exchanged(EX_BLAT)
    q0, q1 = back_vectors(row_of(total, 0, 2), row_of(total, 2, 2), slow_count, lat_norm)
    raw_grads(zb, e, dz, slow_rows, C_LAT, lat_norm, q0, q1)
    to_flat(AT_LAT, 5, 0, 0, dot_tn(dz[...], wide_ref[...]))

    height = up(slots, 16)
    sib_out, sib_in, far_out, far_in = (R.sib_out, R.sib_in, R.far_out, R.far_in)
    sib_send, far_send, far_recv = (R.sum_sems.at[i] for i in range(3))
    sib_recv = R.sib_recv

    def window_of(c, o):
        return flat_ref[pl.ds(R.win_start[c * len(targets) + o], height), :]

    order = [*range(1, len(targets)), 0]
    for o in order:
        sib_out[o] = window_of(1, o).astype(bf16)
        sibling = p.dev(p.x, 1 - p.c, p.a, p.b)
        remote(sib_out.at[o], sib_in.at[o], sib_send, sib_recv.at[o], sibling)

    def fast_input_grad(kind, rank):
        R.fast_grad_box[kind] = (frame_grad(rank) + lateral_grad(rank)) * mask_ref[...]

    fast_input_grad(SENT, partner)
    hand_over(FAST_GRAD)
    for o in order:
        arrived(sib_in.at[o], sib_recv.at[o])
        both = window_of(0, o) + sib_in[o].astype(f32)
        if o:
            far_out[o] = both.astype(bf16)
            x, b = p.off_x(targets[o][0]), p.off_b(targets[o][1])
            remote(far_out.at[o], far_in.at[o], far_send, far_recv, p.dev(x, p.c, p.a, b))
        else:
            total = both
    complete(FAST_OUT)
    slow_result(MINE, p.mp)
    complete(SLOW_OUT)
    slow_input_grad(MINE, p.mp)
    complete(SLOW_GRAD)
    fast_input_grad(MINE, p.mp)
    complete(FAST_GRAD)
    arrived(far_in.at[pl.ds(1, len(targets) - 1)], far_recv)
    for o in range(1, len(targets)):
        total = total + far_in[o].astype(f32)
    R.end_grad[...] = total
    deliver(R.end_grad, 4)
    deliver(R.info, 5)

    sent = len(p_sends)
    while sent:
        n = min(sent, devices)
        arrived(p_ref.at[pl.ds(0, n * tiles)], R.p_send)
        sent -= n
    for each in (x_gather, xs_gather, fc_gather, sc_gather):
        each.drain()
    arrived(flat_ref.at[pl.ds(0, (members - 1) * (12 * 8 + 2 * 16))], R.ex_send)
    arrived(flat_ref.at[pl.ds(0, 2 * HALF + 2 * slow_rows)], R.box_send)
    arrived(sib_out, sib_send)
    arrived(far_out.at[pl.ds(1, len(targets) - 1)], far_send)
    for copy in deliveries:
        copy.wait()


def call_main(cfg, crop, owner, master, fast, slow, fcot, scot):
    smem = pl.BlockSpec(memory_space=pltpu.SMEM)
    hbm = pl.BlockSpec(memory_space=pltpu.HBM)
    outs = outputs(cfg)
    return pl.pallas_call(
        functools.partial(main_kernel, cfg),
        out_shape=tuple(jax.ShapeDtypeStruct(s, t) for s, t in outs),
        in_specs=[smem] + [hbm] * 6,
        out_specs=tuple(hbm for _ in outs),
        scratch_shapes=list(scratch(cfg).values()),
        compiler_params=pltpu.CompilerParams(
            collective_id=0, has_side_effects=True, vmem_limit_bytes=62 << 20
        ),
        name="block",
    )(crop, owner, master, fast, slow, fcot, scot)[:6]


def adam_kernel(cfg, *refs):
    nd, nm, frames, slow_frames, share, slots = cfg
    inputs, results, (sems, *held) = refs[:9], refs[9:17], refs[17:]
    run, grad, master, one, two = held[:5]
    w_out, one_out, two_out, low_out = held[9:]
    fetches = [
        pltpu.make_async_copy(source, target, sems.at[i])
        for i, (source, target) in enumerate(zip(inputs, held[:9], strict=True))
    ]
    for copy in fetches:
        copy.start()
    stores = [
        pltpu.make_async_copy(source, target, sems.at[9 + i])
        for i, (source, target) in enumerate(zip(held[9:] + held[5:9], results, strict=True))
    ]
    fetches[0].wait()
    start, count = run[0:1, :], run[1:2, :]
    row = lax.broadcasted_iota(jnp.int32, (slots, BLK), 0)
    living = row < count
    block = row + start
    rate = jnp.full((slots, BLK), 0.2, f32)
    for at, width in (
        (AT_VEC, B_SLOW),
        (AT_S3, 3 * B_SLOW),
        (AT_S2, C_SLOW + C_LAT),
        (AT_S1, 5 * C_FAST),
        (AT_LAT, B_FAST),
        (AT_F2, 3 * C_FAST),
    ):
        rate = jnp.where(block < at, 0.5 / math.sqrt(width), rate)
    decay = jnp.where(block < AT_VEC, decay_rate, 0.0)
    for copy in fetches[5:]:
        copy.wait()
    for copy in stores[4:]:
        copy.start()
    for copy in fetches[1:5]:
        copy.wait()
    g = grad[:slots, :]
    first = beta_first * one[...] + (1.0 - beta_first) * g
    second = beta_second * two[...] + (1.0 - beta_second) * g * g
    lift_one = 1.0 - beta_first**STEP
    lift_two = 1.0 - beta_second**STEP
    update = first / lift_one / (jnp.sqrt(second / lift_two) + adam_eps)
    weight = master[...]
    weight = jnp.where(living, weight - rate * (update + decay * weight), 0.0)
    w_out[...] = weight
    one_out[...] = jnp.where(living, first, 0.0)
    two_out[...] = jnp.where(living, second, 0.0)
    low_out[...] = weight.astype(bf16)
    for copy in stores[:4]:
        copy.start()
    for copy in stores:
        copy.wait()


def call_adam(cfg, run, grad, master, one, two, passed):
    arrays = (run, grad, master, one, two, *passed)
    hbm = pl.BlockSpec(memory_space=pltpu.HBM)
    new = [jax.ShapeDtypeStruct(master.shape, t) for t in (f32, f32, f32, bf16)]
    results = new + [jax.ShapeDtypeStruct(a.shape, a.dtype) for a in passed]
    held = [pltpu.VMEM(a.shape, a.dtype) for a in (*arrays, *new)]
    return pl.pallas_call(
        functools.partial(adam_kernel, cfg),
        out_shape=tuple(results),
        in_specs=[hbm] * len(arrays),
        out_specs=(hbm,) * len(results),
        scratch_shapes=[pltpu.SemaphoreType.DMA((len(arrays) + len(results),)), *held],
        compiler_params=pltpu.CompilerParams(vmem_limit_bytes=62 << 20),
        name="adam",
    )(*arrays)


def solution(mesh):
    nd, nm = mesh.shape["dp"], mesh.shape["mp"]

    def local(fast_in, slow_in, fast_cot, slow_cot, crop, owner, master, one, two):
        share, slow_frames = slow_in.shape[0], slow_in.shape[1]
        cfg = (nd, nm, fast_in.shape[1] * nm, slow_frames, share, master.shape[0])

        def halves(array):
            split = array.reshape(share, slow_frames, POS // BLK, BLK)
            return split.transpose(0, 2, 1, 3).reshape(-1, BLK)

        *passed, grad, run = call_main(
            cfg,
            crop,
            owner,
            master,
            fast_in.reshape(C_FAST, POS),
            halves(slow_in),
            fast_cot.reshape(C_FAST, POS),
            halves(slow_cot),
        )
        new = call_adam(cfg, run, grad, master, one, two, passed)
        return (
            new[4].reshape(fast_in.shape),
            new[5].reshape(slow_in.shape),
            new[6].reshape(fast_in.shape),
            new[7].reshape(slow_in.shape),
            *new[:4],
        )

    return jax.shard_map(
        local,
        mesh=mesh,
        in_specs=(
            P(None, "mp", "dp", None),
            P("mp", None, "dp", None),
            P(None, "mp", "dp", None),
            P("mp", None, "dp", None),
            P("dp"),
            P(),
            P(("dp", "mp"), None),
            P(("dp", "mp"), None),
            P(("dp", "mp"), None),
        ),
        out_specs=(
            P(None, "mp", "dp", None),
            P("mp", None, "dp", None),
            P(None, "mp", "dp", None),
            P("mp", None, "dp", None),
            P(("dp", "mp"), None),
            P(("dp", "mp"), None),
            P(("dp", "mp"), None),
            P(("dp", "mp"), None),
        ),
        check_vma=False,
    )
```

```python
import functools
import math
import types

import jax
import jax.numpy as jnp
from jax import lax
from jax.experimental import pallas as pl
from jax.experimental.pallas import tpu as pltpu
from jax.sharding import PartitionSpec as P

C_FAST = 128
B_FAST = 32
C_SLOW = 1024
B_SLOW = 256
C_LAT = 256
TILE = 16
POS = TILE * TILE
BLK = 128
STEP = 10
NBLK = 7591

norm_eps = 1e-05
beta_first = 0.5
beta_second = 0.5
adam_eps = 1e-08
decay_rate = 0.05

MESH = pl.DeviceIdType.MESH
f32 = jnp.float32
bf16 = jnp.bfloat16
RC = 32
CH = 256
GROUPS = BLK // B_FAST
COLUMNS = 2
HALF = POS // COLUMNS
SLABS = C_SLOW // BLK

AT_F1 = 0
AT_F2 = AT_F1 + B_FAST * 3 * C_FAST // BLK
AT_F3 = AT_F2 + B_FAST * B_FAST // BLK
AT_LAT = AT_F3 + C_FAST * B_FAST // BLK
AT_S1 = AT_LAT + C_LAT * 5 * C_FAST // BLK
AT_S2 = AT_S1 + B_SLOW * (C_SLOW + C_LAT) // BLK
AT_S3 = AT_S2 + B_SLOW * 3 * B_SLOW // BLK
AT_VEC = AT_S3 + C_SLOW * B_SLOW // BLK
V_F3 = (1, 2, 1)
V_LAT = (3, 5, 2)
V_S1 = (7, 9, 2)
V_S2 = (11, 13, 2)
V_S3 = (15, 23, 8)


def up(n, m):
    return (n + m - 1) // m * m


def dot_nt(a, b):
    return lax.dot_general(a, b, (((1,), (1,)), ((), ())), preferred_element_type=f32)


def dot_tn(a, b):
    return lax.dot_general(a, b, (((0,), (0,)), ((), ())), preferred_element_type=f32)


def dot_nn(a, b):
    return lax.dot_general(a, b, (((1,), (0,)), ((), ())), preferred_element_type=f32)


G0 = math.sqrt(2.0 / math.pi)
G1 = 0.044715


def gelu(x):
    t = jnp.tanh(x * (G0 + (G0 * G1) * (x * x)))
    return 0.5 * x * (1.0 + t)


def gelu_slope(x):
    xx = x * x
    t = jnp.tanh(x * (G0 + (G0 * G1) * xx))
    return 0.5 * (1.0 + t) + (0.5 * x) * (1.0 - t * t) * (G0 + (3.0 * G0 * G1) * xx)


def position_mask(crop):
    spot = lax.broadcasted_iota(jnp.int32, (POS, BLK), 0)
    inside = (spot // TILE < crop) & (lax.rem(spot, TILE) < crop)
    return jnp.where(inside, 1.0, 0.0).astype(f32)


def lane_group():
    return lax.broadcasted_iota(jnp.int32, (1, BLK), 1) // B_FAST


def fold_lanes(v):
    v = v + pltpu.roll(v, B_FAST, 1)
    return v + pltpu.roll(v, 2 * B_FAST, 1)


def remote(source, target, send_sem, recv_sem, device):
    pltpu.make_async_remote_copy(
        src_ref=source,
        dst_ref=target,
        send_sem=send_sem,
        recv_sem=recv_sem,
        device_id=device,
        device_id_type=MESH,
    ).start()


def arrived(view, sem):
    pltpu.make_async_copy(view, view, sem).wait()


class Place:
    def __init__(self, nd, nm):
        self.nd, self.nm = nd, nm
        self.nx = nd // 2
        self.nb = COLUMNS
        self.na = nm // self.nb
        self.dp = lax.axis_index("dp")
        self.mp = lax.axis_index("mp")
        self.x, self.c = self.dp // 2, lax.rem(self.dp, 2)
        self.a, self.b = self.mp // self.nb, lax.rem(self.mp, self.nb)

    def off_a(self, i):
        return lax.rem(self.a + i, self.na)

    def off_b(self, i):
        return lax.rem(self.b + i, self.nb)

    def off_x(self, i):
        return lax.rem(self.x + i, self.nx)

    def dev(self, x, c, a, b):
        return (x * 2 + c, a * self.nb + b)

    def slot(self, x, c, a, b):
        return (x * 2 + c) * self.nm + a * self.nb + b


class Gather:
    def __init__(self, place, slabs, other, skip, send, near, far):
        self.p, self.slabs, self.other, self.skip = place, slabs, other, skip
        self.sems = send, near, far

    def view(self, rank):
        return self.slabs.at[rank + self.skip]

    def along(self, rank):
        p, (send, near, far) = self.p, self.sems
        for i in range(1, p.na):
            device = (p.dp, p.off_a(i) * p.nb + p.b)
            remote(self.view(rank), self.view(rank), send, far, device)

    def start(self):
        p, (send, near, far) = self.p, self.sems
        remote(self.other, self.view(p.mp), send, near, (p.dp, p.a * p.nb + p.off_b(1)))
        self.along(p.mp)

    def relay(self):
        p, (send, near, far) = self.p, self.sems
        rank = p.a * p.nb + p.off_b(1)
        arrived(self.view(rank), near)
        self.along(rank)

    def finish(self):
        arrived(self.slabs.at[pl.ds(0, (self.p.na - 1) * self.p.nb)], self.sems[2])

    def drain(self):
        arrived(self.slabs.at[pl.ds(0, self.p.nm - 1)], self.sems[0])


EX_LAT, EX_S1, EX_S2, EX_B2, EX_B1, EX_BLAT = range(6)
EX_F1, EX_F2, EX_F3, EX_BF3, EX_BF2, EX_BF1 = range(6, 12)
EX_S3, EX_BS3 = 12, 13
EXCHANGES = 14

FAST_OUT, SLOW_OUT, FAST_GRAD, SLOW_GRAD = range(4)
SENT, MINE, GOT = range(3)


def outputs(cfg):
    nd, nm, frames, slow_frames, share, slots = cfg
    halves = POS // BLK
    fast, slow = (C_FAST * halves, BLK), (share * slow_frames * halves, BLK)
    result = [(fast, f32), (slow, f32), (fast, f32), (slow, f32), ((up(slots, 16), BLK), f32)]
    result += [((8, BLK), jnp.int32)] + [((slots, BLK), f32)] * 3
    if share != BLK:
        result += [((nm, share, slow_frames * HALF), bf16)] * 2
    return result


def scratch(cfg):
    nd, nm, frames, slow_frames, share, slots = cfg
    devices, group = nd * nm, nd * COLUMNS
    rows = up(slots + 15, 16)
    height = up(slots, 16)
    halves = POS // BLK
    slow_rows, fast_rows = slow_frames * HALF, frames * HALF
    group_rows = fast_rows // GROUPS
    windows = group // 2
    vmem, smem, dma = pltpu.VMEM, pltpu.SMEM, pltpu.SemaphoreType.DMA
    piece = (slow_rows, BLK) if share == BLK else (share, slow_rows)
    result = dict(
        owner_v=vmem((NBLK,), jnp.int32),
        owner_s=smem((NBLK,), jnp.int32),
        run_device=smem((devices,), jnp.int32),
        run_start=smem((devices,), jnp.int32),
        run_count=smem((devices,), jnp.int32),
        win_start=smem((group,), jnp.int32),
        table_v=vmem((8, BLK), jnp.int32),
        table_s=smem((8, BLK), jnp.int32),
        shift=vmem((rows + 16, BLK), f32),
        p=vmem((devices * (rows // 16), 16, BLK), bf16),
        q=vmem((devices, 16, BLK), bf16),
        fast_v=vmem((C_FAST, POS), bf16),
        slow_v=vmem((share * slow_frames * halves, BLK), bf16),
        fcot_v=vmem((C_FAST, POS), bf16),
        scot_v=vmem((share * slow_frames * halves, BLK), bf16),
        stage=vmem((share * slow_frames * halves, BLK), f32),
        turned=vmem((POS, BLK), f32),
        x_other=vmem((HALF, BLK), bf16),
        fc_other=vmem((HALF, BLK), bf16),
        xs_other=vmem(piece, bf16),
        sc_other=vmem(piece, bf16),
        xt=vmem((frames + 4, HALF, BLK), bf16),
        xs=vmem((SLABS, slow_rows, BLK), bf16),
        fc=vmem((frames, HALF, BLK), bf16),
        sc=vmem((SLABS, slow_rows, BLK), bf16),
        wide=vmem((slow_rows, 5 * C_FAST), bf16),
        lat_w=vmem((C_LAT, 5 * C_FAST), bf16),
        s1_w=vmem((B_SLOW, C_SLOW + C_LAT), bf16),
        s2_w=vmem((B_SLOW, 3 * B_SLOW), bf16),
        s3_w=vmem((C_SLOW, B_SLOW), bf16),
        f1_w=vmem((BLK, 3 * C_FAST), bf16),
        f2_w=vmem((BLK, BLK), bf16),
        f3_w=vmem((BLK, BLK), bf16),
        vec=vmem((32, BLK), f32),
        mask_all=vmem((POS, BLK), f32),
        mask=vmem((HALF, BLK), f32),
    )
    if share != BLK:
        result.update(
            piece=vmem(piece, bf16),
            turn=vmem((BLK, HALF), bf16),
        )
    result.update(
        zb=vmem((slow_rows, 256), bf16),
        latb=vmem((slow_rows, 256), bf16),
        s2b=vmem((slow_rows, 256), bf16),
        dz=vmem((slow_rows, 256), bf16),
        da1=vmem((slow_rows, 256), bf16),
    )
    result.update(
        two_in=vmem(((slow_frames + 2) * HALF, 256), bf16),
        two_back=vmem(((slow_frames + 2) * HALF, 256), bf16),
        c1=vmem((slow_rows, 256), f32),
        c2=vmem((slow_rows, 256), f32),
        c3=vmem((slow_rows, C_SLOW), f32),
        e=vmem((slow_rows, 256), f32),
        e3=vmem((slow_rows, C_SLOW), f32),
        da3=vmem((slow_rows, C_SLOW), bf16),
        a1p=vmem((group_rows, BLK), f32),
        a2p=vmem((group_rows, BLK), f32),
        h1p=vmem((group_rows, BLK), bf16),
        h2p=vmem((group_rows, BLK), bf16),
        d1p=vmem((group_rows, BLK), bf16),
        d2p=vmem((group_rows, BLK), bf16),
        ep=vmem((group_rows, BLK), f32),
        a3=vmem((fast_rows, BLK), f32),
        e3f=vmem((fast_rows, BLK), f32),
        da3f=vmem((fast_rows, BLK), bf16),
        square=vmem((BLK, BLK), f32),
        flat=vmem((up(NBLK + height, 64), BLK), f32),
        sib_out=vmem((windows, height, BLK), bf16),
        sib_in=vmem((windows, height, BLK), bf16),
        far_out=vmem((windows, height, BLK), bf16),
        far_in=vmem((windows, height, BLK), bf16),
        st=vmem((12, group, 8, BLK), f32),
        st16=vmem((2, group, 16, BLK), f32),
    )
    result.update(
        fast_out_box=vmem((3, HALF, BLK), f32),
        slow_out_box=vmem((3, slow_rows, BLK), f32),
        fast_grad_box=vmem((3, HALF, BLK), f32),
        slow_grad_box=vmem((3, slow_rows, BLK), f32),
        p_send=dma(()),
        p_recv=dma((devices // 2,)),
        p_sibling=dma(()),
        gather_sems=dma((4, 3)),
        ex_send=dma(()),
        ex_recv=dma((EXCHANGES,)),
        box_send=dma(()),
        box_recv=dma((4,)),
        sum_sems=dma((3,)),
        sib_recv=dma((windows,)),
        local=dma((16,)),
    )
    return result


def main_kernel(cfg, *refs):
    nd, nm, frames, slow_frames, share, slots = cfg
    n_out = len(outputs(cfg))
    args, results, held = refs[:9], refs[9 : 9 + n_out], refs[9 + n_out :]
    crop_in, owner_in, master_in, first_in, second_in, fast_in, slow_in, fcot_in, scot_in = args
    R = types.SimpleNamespace(**dict(zip(scratch(cfg), held, strict=True)))
    p = Place(nd, nm)
    devices = nd * nm
    halves = POS // BLK
    rows = up(slots + 15, 16)
    tiles = rows // 16
    slow_rows, fast_rows = slow_frames * HALF, frames * HALF
    per_group = frames // GROUPS
    group_rows = per_group * HALF
    slabs = share == BLK
    me = p.dp * nm + p.mp
    partner = p.a * p.nb + p.off_b(1)

    members = nd * p.nb
    member = p.dp * p.nb + p.b
    group_peers = [
        p.dev(p.off_x(i), lax.rem(p.c + k, 2), p.a, p.off_b(j))
        for i in reversed(range(p.nx))
        for j in reversed(range(p.nb))
        for k in range(2)
        if i or j or k
    ]
    near = [p.dev(p.x, p.c, p.off_a(i), p.b) for i in range(1, p.na)]
    barrier = pltpu.get_barrier_semaphore()
    for device in group_peers + near:
        pl.semaphore_signal(barrier, inc=1, device_id=device, device_id_type=MESH)

    local_copies = []

    def fetch(source, target):
        copy = pltpu.make_async_copy(source, target, R.local.at[len(local_copies)])
        copy.start()
        local_copies.append(copy)
        return copy

    get_owner = fetch(owner_in, R.owner_v)
    get_owner_s = fetch(owner_in, R.owner_s)
    get_master = fetch(master_in, R.shift.at[pl.ds(16, slots)])
    get_fast = fetch(fast_in, R.fast_v)
    get_slow = fetch(slow_in, R.slow_v)
    get_fcot = fetch(fcot_in, R.fcot_v)
    get_scot = fetch(scot_in, R.scot_v)
    kept = [fetch(a, results[6 + i]) for i, a in enumerate((master_in, first_in, second_in))]

    crop = crop_in[0]
    R.mask_all[...] = position_mask(crop)
    R.mask[...] = R.mask_all[pl.ds(pl.multiple_of(p.b * HALF, HALF), HALF), :]
    tall = crop.astype(f32)
    area = tall * tall * (1.0 / COLUMNS)
    xt_ref, xs_ref, fc_ref, sc_ref = R.xt, R.xs, R.fc, R.sc
    for f in (0, 1, frames + 2, frames + 3):
        xt_ref[f] = jnp.zeros((HALF, BLK), bf16)
    two_in, two_back = R.two_in, R.two_back
    for ref in (two_in, two_back):
        ref[:HALF] = jnp.zeros((HALF, 256), bf16)
        ref[(slow_frames + 1) * HALF :] = jnp.zeros((HALF, 256), bf16)

    get_owner.wait()
    spot = lax.broadcasted_iota(jnp.int32, (8, BLK), 0) * BLK
    spot = spot + lax.broadcasted_iota(jnp.int32, (8, BLK), 1)
    lowest = jnp.full((8, BLK), NBLK, jnp.int32)
    number = jnp.zeros((8, BLK), jnp.int32)
    whole = NBLK // 1024 * 1024
    for i in range(0, whole, 1024):
        mine = R.owner_v[pl.ds(i, 1024)].reshape(8, BLK) == me
        lowest = jnp.minimum(lowest, jnp.where(mine, spot + i, NBLK))
        number = number + jnp.where(mine, 1, 0)
    for i in range(whole, NBLK // BLK * BLK, BLK):
        mine = R.owner_v[pl.ds(i, BLK)].reshape(1, BLK) == me
        mine = mine & (spot < BLK)
        lowest = jnp.minimum(lowest, jnp.where(mine, spot + i, NBLK))
        number = number + jnp.where(mine, 1, 0)
    get_owner_s.wait()

    def last_ones(i, found):
        first, n = found
        mine = R.owner_s[i] == me
        return jnp.where(mine, jnp.minimum(first, i), first), n + jnp.where(mine, 1, 0)

    found = jnp.min(lowest), jnp.sum(number)
    my_start, my_count = lax.fori_loop(NBLK // BLK * BLK, NBLK, last_ones, found)
    line = lax.broadcasted_iota(jnp.int32, (8, BLK), 0)
    results[5][...] = jnp.where(line == 0, my_start, my_count)
    shift = lax.rem(my_start, 16)
    get_master.wait()
    moved = R.shift[pl.ds(16 - shift, rows), :]
    row = lax.broadcasted_iota(jnp.int32, (rows, BLK), 0)
    own = (row >= shift) & (row < shift + my_count)
    p_ref = R.p

    def p_slot(slot):
        return p_ref.at[pl.ds(slot * tiles, tiles)]

    p_slot(me)[...] = jnp.where(own, moved, 0.0).astype(bf16).reshape(tiles, 16, BLK)

    pl.semaphore_wait(barrier, len(group_peers) + len(near))
    p_sends = []

    def view(x, c, a, b):
        return p_slot(p.slot(x, c, a, b))

    def came(source):
        x, c, a, b = source
        return R.p_recv.at[x * nm + a * p.nb + b]

    def pass_on(source, along_a=(), along_b=False, along_x=False, along_c=False):
        piece, sem = view(*source), came(source)
        to = []
        for i in along_a:
            to += [p.dev(p.x, p.c, p.off_a(i), p.b)]
        if along_x:
            to += [p.dev(p.off_x(i), p.c, p.a, p.b) for i in range(1, p.nx)]
        if along_b:
            to += [p.dev(p.x, p.c, p.a, p.off_b(1))]
        for device in to:
            remote(piece, piece, R.p_send, sem, device)
            p_sends.append(device)
        if along_c:
            device = p.dev(p.x, 1 - p.c, p.a, p.b)
            remote(piece, piece, R.p_send, R.p_sibling, device)
            p_sends.append(device)

    def take(source):
        arrived(view(*source), came(source))

    here = (p.x, p.c, p.a, p.b)
    pass_on(here, along_a=range(1, p.na), along_b=True, along_x=True, along_c=True)

    turned_ref = R.turned

    def half_of(b):
        return pl.ds(pl.multiple_of(b * HALF, HALF), HALF)

    def own_frame(slot, other, source):
        turned_ref[...] = source[...].astype(f32).T * R.mask_all[...]
        slot[...] = turned_ref[half_of(p.b), :].astype(bf16)
        other[...] = turned_ref[half_of(p.off_b(1)), :].astype(bf16)

    def own_slow(slot, other, source):
        stage = R.stage
        stage[...] = source[...].astype(f32)
        for s in range(slow_frames):
            at = slice(s * HALF, (s + 1) * HALF)
            for h in range(halves):
                part = stage[pl.ds(h * slow_frames + s, share, stride=halves * slow_frames), :]
                if slabs:
                    here = slice(h * BLK, (h + 1) * BLK)
                    turned_ref[here, :] = part.T * R.mask_all[here, :]
                else:
                    turned_ref[h * share : (h + 1) * share, :] = part
            if slabs:
                slot[at, :] = turned_ref[half_of(p.b), :].astype(bf16)
                other[at, :] = turned_ref[half_of(p.off_b(1)), :].astype(bf16)
            else:
                for ref, b in ((R.piece, p.b), (other, p.off_b(1))):
                    mine = pl.ds(pl.multiple_of(b * share, share), share)
                    ref[:, at] = turned_ref[mine, :].astype(bf16)
        if not slabs:
            pltpu.sync_copy(R.piece, slot)

    def from_natural(natural, wide):
        ranks = BLK // share

        def block(i, _):
            s, j = i // SLABS, lax.rem(i, SLABS)
            at_row = pl.ds(pl.multiple_of(s * HALF, HALF), HALF)
            for k in range(ranks):
                pltpu.sync_copy(
                    natural.at[j * ranks + k, :, at_row],
                    R.turn.at[pl.ds(k * share, share)],
                )
            piece = R.turn[...].astype(f32).T * R.mask[...]
            wide[j, at_row, :] = piece.astype(bf16)
            return 0

        lax.fori_loop(0, slow_frames * SLABS, block, 0)

    def gather(which, array, other, skip=0):
        sems = [R.gather_sems.at[which, i] for i in range(3)]
        return Gather(p, array, other, skip, *sems)

    x_gather = gather(0, xt_ref, R.x_other, 2)
    fc_gather = gather(1, fc_ref, R.fc_other)
    xs_gather = gather(2, xs_ref if slabs else results[9], R.xs_other)
    sc_gather = gather(3, sc_ref if slabs else results[10], R.sc_other)
    get_fast.wait()
    own_frame(x_gather.view(p.mp), R.x_other, R.fast_v)
    x_gather.start()
    get_slow.wait()
    own_slow(xs_gather.view(p.mp), R.xs_other, R.slow_v)

    steps = [1 << i for i in reversed(range(max(1, (slots - 1).bit_length())))]
    owner_s, run_device, run_start, run_count = (R.owner_s, R.run_device, R.run_start, R.run_count)

    def run(k, at):
        device = owner_s[jnp.minimum(at, NBLK - 1)]
        n = jnp.int32(1)
        for step in steps:
            more = n + step
            last = at + more - 1
            inside = owner_s[jnp.minimum(last, NBLK - 1)] == device
            n = jnp.where((more <= slots) & (last < NBLK) & inside, more, n)
        run_device[k] = device
        run_start[k] = at
        run_count[k] = n
        return at + n

    lax.fori_loop(0, devices, run, jnp.int32(0))

    targets = [(i, j) for i in range(p.nx) for j in range(p.nb)]
    owners = [p.slot(p.off_x(i), c, p.a, p.off_b(j)) for c in (p.c, 1 - p.c) for i, j in targets]

    def find(k, found):
        return [jnp.where(run_device[k] == d, run_start[k], at) for d, at in zip(owners, found)]

    for i, at in enumerate(lax.fori_loop(0, devices, find, [jnp.int32(0)] * len(owners))):
        R.win_start[i] = at

    for i in range(1, p.na):
        source = (p.x, p.c, p.off_a(p.na - i), p.b)
        take(source)
        pass_on(source, along_b=True, along_x=True, along_c=True)
    x_gather.relay()
    xs_gather.start()

    def tile_of(k):
        return run_device[k] * tiles - run_start[k] // 16

    def table(k, found):
        start, last = run_start[k], run_start[k] + run_count[k] - 1
        final = jnp.minimum(spot * 16 + 15, NBLK - 1)
        holds = (final >= start) & (final <= last)
        tile = jnp.where(spot == start // 16, devices * tiles + k, spot + tile_of(k))
        return jnp.where(holds, tile, found)

    R.table_v[...] = lax.fori_loop(0, devices, table, jnp.zeros((8, BLK), jnp.int32))
    get_table = fetch(R.table_v, R.table_s)

    across = p.na // 2
    for i in range(p.na):
        source = (p.x, p.c, p.off_a(p.na - i), p.off_b(1))
        take(source)
        pass_on(source, along_x=i < across, along_c=True)
        for j in range(1, p.nx):
            source = (p.off_x(j), p.c, p.off_a(p.na - i), p.b)
            take(source)
            pass_on(source, along_b=i >= across, along_c=True)
    xs_gather.relay()
    get_fcot.wait()
    own_frame(fc_gather.view(p.mp), R.fc_other, R.fcot_v)
    get_scot.wait()
    own_slow(sc_gather.view(p.mp), R.sc_other, R.scot_v)
    for i in range(p.na):
        for k in range(1, p.nx):
            source = (p.off_x(k), p.c, p.off_a(p.na - i), p.off_b(1))
            take(source)
            pass_on(source, along_c=True)
    sc_gather.start()
    arrived(p_ref.at[pl.ds(0, devices // 2 * tiles)], R.p_sibling)
    get_table.wait()
    sc_gather.relay()

    def tile_rows(t):
        return pl.ds(pl.multiple_of(t * 16, 16), 16)

    q_ref = R.q

    def first_tile(k, before):
        tile = p_ref[run_device[k] * tiles].astype(f32)
        shared = lax.rem(run_start[k], 16) != 0
        tile = tile + jnp.where(shared, before, 0.0)
        q_ref[k] = tile.astype(bf16)
        last = (run_start[k] + run_count[k] - 1) // 16
        alone = last == run_start[k] // 16
        return jnp.where(alone, tile, p_ref[tile_of(k) + last].astype(f32))

    lax.fori_loop(0, devices, first_tile, jnp.zeros((16, BLK), f32))
    flat_ref, table_s = R.flat, R.table_s

    def lay_out(first_block, end_block):
        first, end = first_block // 16, up(end_block, 16) // 16

        def one(t):
            source = table_s[t // BLK, lax.rem(t, BLK)]
            plain = p_ref[jnp.minimum(source, devices * tiles - 1)]
            shared = q_ref[jnp.maximum(source - devices * tiles, 0)]
            tile = jnp.where(source < devices * tiles, plain, shared)
            flat_ref[tile_rows(t), :] = tile.astype(f32)

        def eight(i, _):
            for k in range(8):
                one(first + i * 8 + k)
            return 0

        lax.fori_loop(0, (end - first) // 8, eight, 0)
        for t in range(first + (end - first) // 8 * 8, end):
            one(t)

    def matrix(out_ref, at, height, blocks):
        lay_out(at, at + height * blocks)
        for j in range(blocks):
            for o in range(0, height, 256):
                out_ref[o : o + 256, j * BLK : (j + 1) * BLK] = flat_ref[
                    pl.ds(at + o * blocks + j, 256, stride=blocks), :
                ].astype(bf16)

    group = lane_group()
    square_ref = R.square
    lat_w, s1_w, s2_w, s3_w = R.lat_w, R.s1_w, R.s2_w, R.s3_w
    f1_w, f2_w, f3_w, vec_ref = R.f1_w, R.f2_w, R.f3_w, R.vec

    def spread_rows(at, height):
        for r in range(GROUPS):
            part = jnp.where(group == r, flat_ref[at : at + height // GROUPS, :], 0.0)
            square_ref[pl.ds(r, height // GROUPS, stride=GROUPS), :] = fold_lanes(part)
        return square_ref[:height, :]

    def fast_weights():
        lay_out(AT_F1, AT_LAT)
        for k in range(3):
            tap = flat_ref[pl.ds(AT_F1 + k, B_FAST, stride=3), :].astype(bf16)
            for g in range(GROUPS):
                f1_w[g * B_FAST : (g + 1) * B_FAST, k * BLK : (k + 1) * BLK] = tap
        two = spread_rows(AT_F2, B_FAST)
        for g in range(GROUPS):
            f2_w[g * B_FAST : (g + 1) * B_FAST, :] = jnp.where(group == g, two, 0.0).astype(bf16)
        f3_w[...] = spread_rows(AT_F3, C_FAST).astype(bf16)

    matrix(lat_w, AT_LAT, C_LAT, 5)
    lay_out(AT_VEC, NBLK)
    vec_ref[...] = flat_ref[AT_VEC : AT_VEC + 32, :]
    x_gather.finish()

    zb, latb, s2b, dz, da1, wide_ref = (R.zb, R.latb, R.s2b, R.dz, R.da1, R.wide)
    c1, c2, c3, e, e3, da3 = (R.c1, R.c2, R.c3, R.e, R.e3, R.da3)
    a1p, a2p, h1p, h2p, d1p, d2p, ep, a3, e3f, da3f = (R.a1p, R.a2p, R.h1p, R.h2p, R.d1p, R.d2p, R.ep, R.a3, R.e3f, R.da3f)
    mask_ref, st_ref, st16_ref = R.mask, R.st, R.st16
    s1b = two_in.at[pl.ds(HALF, slow_rows)]
    da2 = two_back.at[pl.ds(HALF, slow_rows)]

    def stat(which):
        return (st_ref, which) if which < 12 else (st16_ref, which - 12)

    def exchange(which):
        ref, at = stat(which)
        own = ref.at[at, member]
        for device in group_peers:
            remote(own, own, R.ex_send, R.ex_recv.at[which], device)

    def exchanged(which):
        ref, at = stat(which)
        arrived(ref.at[at, pl.ds(0, members - 1)], R.ex_recv.at[which])
        total = ref[at, 0]
        for i in range(1, members):
            total = total + ref[at, i]
        return total

    def put(which, at, vector):
        ref, index = stat(which)
        for j in range(vector.shape[1] // BLK):
            ref[index, member, at + j : at + j + 1, :] = vector[:, j * BLK : (j + 1) * BLK]

    def fill(which, at, value):
        ref, index = stat(which)
        ref[index, member, at:8, :] = jnp.full((8 - at, BLK), value, f32)

    def row_of(block, at, n):
        return jnp.concatenate([block[at + j : at + j + 1, :] for j in range(n)], 1)

    def vectors(place):
        g, b, n = place
        return row_of(vec_ref[...], g, n), row_of(vec_ref[...], b, n)

    def rows_at(i, size):
        return pl.ds(pl.multiple_of(i * size, size), size)

    def mask_at(i, width):
        part = mask_ref[pl.ds(pl.multiple_of(lax.rem(i * RC, HALF), RC), RC), :]
        return jnp.concatenate([part] * (width // BLK), 1) if width > BLK else part

    def eights(v):
        return jnp.sum(v.reshape(v.shape[0] // 8, 8, v.shape[1]), 0)

    def total_row(v):
        return jnp.sum(v, 0, keepdims=True)

    def affine(sums, squares, count, gain, bias):
        mean = sums / count
        scale = lax.rsqrt(squares / count - mean * mean + norm_eps)
        grow = gain * scale
        return mean, scale, grow, bias - mean * grow

    def loop(n, body, start):
        return lax.fori_loop(0, n, body, start, unroll=n if n <= 8 else 4)

    def sums_of(ref, n_rows, width):
        def body(i, acc):
            v = ref[rows_at(i, RC), :].astype(f32)
            return acc[0] + eights(v), acc[1] + eights(v * v)

        zero = jnp.zeros((8, width), f32)
        one, two = loop(n_rows // RC, body, (zero, zero))
        return total_row(one), total_row(two)

    def activate(src, dst, n_rows, width, grow, base):
        def body(i, _):
            at = rows_at(i, RC)
            pre = src[at, :].astype(f32) * grow + base
            dst[at, :] = (gelu(pre) * mask_at(i, width)).astype(bf16)
            return 0

        loop(n_rows // RC, body, 0)

    def slopes(src, incoming, n_rows, width, norm):
        mean, scale, grow, base = norm

        def body(i, acc):
            at = rows_at(i, RC)
            a = src[at, :].astype(f32)
            d = gelu_slope(a * grow + base) * incoming[at, :] * mask_at(i, width)
            incoming[at, :] = d
            return acc[0] + eights(d), acc[1] + eights(d * ((a - mean) * scale))

        zero = jnp.zeros((8, width), f32)
        one, two = loop(n_rows // RC, body, (zero, zero))
        return total_row(one), total_row(two)

    def back_vectors(bias_sum, gain_sum, count, norm):
        mean, scale, grow, base = norm
        k1 = grow * gain_sum / count
        return grow * bias_sum / count - k1 * (mean * scale), k1 * scale

    def raw_grads(src, pres, dst, n_rows, width, norm, q0, q1):
        grow = norm[2]

        def body(i, _):
            at = rows_at(i, RC)
            a = src[at, :].astype(f32)
            da = grow * pres[at, :] - mask_at(i, width) * (q0 + a * q1)
            dst[at, :] = da.astype(bf16)
            return 0

        loop(n_rows // RC, body, 0)

    def put_vector(row, vector):
        for j in range(vector.shape[1] // BLK):
            at = AT_VEC + row + j
            flat_ref[at : at + 1, :] = vector[:, j * BLK : (j + 1) * BLK]

    def put_pair(which, one, two, place=None):
        put(which, 0, one)
        put(which, one.shape[1] // BLK, two)
        if place is not None:
            put_vector(place[0], two)
            put_vector(place[1], one)

    slow_chunks = [slice(i, i + CH) for i in range(0, slow_rows, CH)]
    group_chunks = [slice(i, i + CH) for i in range(0, group_rows, CH)]

    def all_slabs(ref, at):
        return jnp.concatenate([ref[j, at, :] for j in range(SLABS)], 1)

    boxes = (
        (R.fast_out_box, results[0]),
        (R.slow_out_box, results[1]),
        (R.fast_grad_box, results[2]),
        (R.slow_grad_box, results[3]),
    )

    def box(which, kind):
        return boxes[which][0].at[kind]

    def hand_over(which):
        box_sems = R.box_send, R.box_recv.at[which]
        remote(box(which, SENT), box(which, GOT), *box_sems, (p.dp, partner))

    def to_channels(block):
        turned = block.T
        if slabs:
            return turned
        lane_shift = lax.rem(p.mp * share, BLK)
        return sum(
            jnp.where(lane_shift == k * share, turned[k * share : (k + 1) * share, :], 0.0)
            for k in range(BLK // share)
        )

    def complete(which):
        ref, end = boxes[which]
        arrived(box(which, GOT), R.box_recv.at[which])
        fast = which in (FAST_OUT, FAST_GRAD)
        n = 1 if fast else slow_frames
        for s in range(n):
            at = slice(s * HALF, (s + 1) * HALF)
            for h in range(halves):
                block = jnp.where(p.b == h, ref[MINE, at, :], ref[GOT, at, :])
                block = block.T if fast else to_channels(block)
                end[pl.ds(s * halves + h, block.shape[0], stride=n * halves), :] = block

    for s in range(slow_frames):
        for k in range(5):
            wide_ref[s * HALF : (s + 1) * HALF, k * BLK : (k + 1) * BLK] = xt_ref[4 * s + k]
    for at in slow_chunks:
        zb[at, :] = dot_nt(wide_ref[at, :], lat_w[...]).astype(bf16)
    put_pair(EX_LAT, *sums_of(zb, slow_rows, C_LAT))
    fill(EX_LAT, 4, area)
    exchange(EX_LAT)

    fast_weights()

    def fast_rows_of(ref, first_frame, at):
        f = first_frame + at.start // HALF
        return jnp.concatenate([ref[f + i] for i in range(CH // HALF)], 0)

    for at in group_chunks:
        total = jnp.zeros((CH, BLK), f32)
        for g in range(GROUPS):
            window = jnp.concatenate(
                [fast_rows_of(xt_ref, g * per_group + 1 + k, at) for k in range(3)], 1
            )
            total = total + jnp.where(group == g, dot_nt(window, f1_w[...]), 0.0)
        a1p[at, :] = total

    def put_folded(which, one, two):
        put(which, 0, fold_lanes(one))
        put(which, 1, fold_lanes(two))

    put_folded(EX_F1, *sums_of(a1p, group_rows, BLK))
    fill(EX_F1, 2, area)
    exchange(EX_F1)

    matrix(s1_w, AT_S1, B_SLOW, 10)
    xs_gather.finish()
    if not slabs:
        from_natural(results[9], xs_ref)

    for at in slow_chunks:
        c1[at, :] = dot_nt(all_slabs(xs_ref, at), s1_w[:, :C_SLOW])

    total = exchanged(EX_LAT)
    area_all = total[4:5, :]
    slow_count = jnp.concatenate([area_all * float(slow_frames)] * 2, 1)
    slow_count8 = jnp.concatenate([slow_count] * 4, 1)
    fast_count = area_all * float(frames)
    lat_norm = affine(row_of(total, 0, 2), row_of(total, 2, 2), slow_count, *vectors(V_LAT))
    activate(zb, latb, slow_rows, C_LAT, lat_norm[2], lat_norm[3])
    for at in slow_chunks:
        c1[at, :] = c1[at, :] + dot_nt(latb[at, :], s1_w[:, C_SLOW:])
    put_pair(EX_S1, *sums_of(c1, slow_rows, B_SLOW))
    fill(EX_S1, 4, 0.0)
    exchange(EX_S1)

    matrix(s2_w, AT_S2, B_SLOW, 6)
    fc_gather.start()
    matrix(s3_w, AT_S3, C_SLOW, 2)

    packed = vec_ref[0:1, :]

    def spread(which):
        return fold_lanes(jnp.where(group == which, packed, 0.0))

    def exchanged_two(which):
        total = exchanged(which)
        return total[0:1, :], total[1:2, :]

    f1_norm = affine(*exchanged_two(EX_F1), fast_count, spread(0), spread(1))
    activate(a1p, h1p, group_rows, BLK, f1_norm[2], f1_norm[3])
    for at in group_chunks:
        a2p[at, :] = dot_nt(h1p[at, :], f2_w[...])
    put_folded(EX_F2, *sums_of(a2p, group_rows, BLK))
    fill(EX_F2, 2, 0.0)
    exchange(EX_F2)

    total = exchanged(EX_S1)
    s1_norm = affine(row_of(total, 0, 2), row_of(total, 2, 2), slow_count, *vectors(V_S1))
    activate(c1, s1b, slow_rows, B_SLOW, s1_norm[2], s1_norm[3])

    def shifted(ref, at, k):
        return ref[at.start + k * HALF : at.stop + k * HALF, :]

    for at in slow_chunks:
        window = jnp.concatenate([shifted(two_in, at, k) for k in range(3)], 1)
        c2[at, :] = dot_nt(window, s2_w[...])
    put_pair(EX_S2, *sums_of(c2, slow_rows, B_SLOW))
    fill(EX_S2, 4, 0.0)
    exchange(EX_S2)

    fc_gather.relay()

    f2_norm = affine(*exchanged_two(EX_F2), fast_count, spread(2), spread(3))
    activate(a2p, h2p, group_rows, BLK, f2_norm[2], f2_norm[3])
    for g in range(GROUPS):
        for at in group_chunks:
            part = jnp.where(group == g, h2p[at, :], 0.0).astype(bf16)
            here = slice(g * group_rows + at.start, g * group_rows + at.stop)
            a3[here, :] = dot_nt(part, f3_w[...])
    put_pair(EX_F3, *sums_of(a3, fast_rows, BLK))
    fill(EX_F3, 2, 0.0)
    exchange(EX_F3)

    total = exchanged(EX_S2)
    s2_norm = affine(row_of(total, 0, 2), row_of(total, 2, 2), slow_count, *vectors(V_S2))
    activate(c2, s2b, slow_rows, B_SLOW, s2_norm[2], s2_norm[3])
    quarter = C_SLOW // 4
    quarters = [slice(n * quarter, (n + 1) * quarter) for n in range(4)]
    for n, lanes in enumerate(quarters):
        for at in slow_chunks:
            c3[at, lanes] = dot_nt(s2b[at, :], s3_w[lanes, :])
        one, two = sums_of(c3.at[:, lanes], slow_rows, quarter)
        put(EX_S3, 2 * n, one)
        put(EX_S3, 8 + 2 * n, two)
    exchange(EX_S3)

    f3_norm = affine(*exchanged_two(EX_F3), fast_count, *vectors(V_F3))
    for rank, kind in ((partner, SENT), (p.mp, MINE)):
        pre = a3[rows_at(rank, HALF), :] * f3_norm[2] + f3_norm[3]
        pre = pre + xt_ref[rank + 2].astype(f32)
        R.fast_out_box[kind] = gelu(pre) * mask_ref[...]
    hand_over(FAST_OUT)
    sc_gather.finish()
    if not slabs:
        from_natural(results[10], sc_ref)
    total = exchanged(EX_S3)
    s3_norm = affine(row_of(total, 0, 8), row_of(total, 8, 8), slow_count8, *vectors(V_S3))

    def pair_of(ref, n, at):
        return jnp.concatenate([ref[2 * n, at, :], ref[2 * n + 1, at, :]], 1).astype(f32)

    for n, lanes in enumerate(quarters):
        norm = [v[:, lanes] for v in s3_norm]

        def slow_slopes(i, acc, n=n, lanes=lanes, norm=norm):
            at = rows_at(i, RC)
            a = c3[at, lanes]
            pre = a * norm[2] + norm[3] + pair_of(xs_ref, n, at)
            d = gelu_slope(pre) * pair_of(sc_ref, n, at)
            e3[at, lanes] = d
            return acc[0] + eights(d), acc[1] + eights(d * ((a - norm[0]) * norm[1]))

        zero = jnp.zeros((8, quarter), f32)
        one, two = loop(slow_rows // RC, slow_slopes, (zero, zero))
        one, two = total_row(one), total_row(two)
        put(EX_BS3, 2 * n, one)
        put(EX_BS3, 8 + 2 * n, two)
        put_vector(V_S3[0] + 2 * n, two)
        put_vector(V_S3[1] + 2 * n, one)
    exchange(EX_BS3)

    fc_gather.finish()

    def fast_slopes(i, acc):
        mean, scale, grow, base = f3_norm
        at = rows_at(i, RC)
        f, here = i // (HALF // RC), rows_at(lax.rem(i, HALF // RC), RC)
        a = a3[at, :]
        x = xt_ref[f + 2, here, :].astype(f32)
        d = gelu_slope(a * grow + base + x) * fc_ref[f, here, :].astype(f32)
        e3f[at, :] = d
        return acc[0] + eights(d), acc[1] + eights(d * ((a - mean) * scale))

    zero = jnp.zeros((8, BLK), f32)
    one, two = loop(fast_rows // RC, fast_slopes, (zero, zero))
    put_pair(EX_BF3, total_row(one), total_row(two), V_F3)
    fill(EX_BF3, 2, 0.0)
    exchange(EX_BF3)

    def slow_place(rank):
        slab = rank * share // BLK
        return slab, pl.ds(pl.multiple_of(slab * BLK, BLK), BLK)

    def slow_result(kind, rank):
        slab, lanes = slow_place(rank)
        grow, base = (
            sum(jnp.where(slab == k, v[:, k * BLK : (k + 1) * BLK], 0.0) for k in range(SLABS))
            for v in s3_norm[2:]
        )
        for s in range(slow_frames):
            at = slice(s * HALF, (s + 1) * HALF)
            pre = c3[at, lanes] * grow + base + xs_ref[slab, at, :].astype(f32)
            R.slow_out_box[kind, at, :] = gelu(pre) * mask_ref[...]

    def slow_input_grad(kind, rank):
        slab, lanes = slow_place(rank)
        for s in range(slow_frames):
            at = slice(s * HALF, (s + 1) * HALF)
            value = e3[at, lanes] + dot_nn(da1[at, :], s1_w[:, lanes])
            R.slow_grad_box[kind, at, :] = value * mask_ref[...]

    slow_result(SENT, partner)
    hand_over(SLOW_OUT)

    total = exchanged(EX_BS3)
    q0, q1 = back_vectors(row_of(total, 0, 8), row_of(total, 8, 8), slow_count8, s3_norm)
    for lanes in quarters:
        norm = [v[:, lanes] for v in s3_norm]
        raw_grads(
            c3.at[:, lanes], e3.at[:, lanes], da3.at[:, lanes], slow_rows, quarter, norm,
            q0[:, lanes], q1[:, lanes]
        )
    for at in slow_chunks:
        e[at, :] = dot_nn(da3[at, :], s3_w[...])
    put_pair(EX_B2, *slopes(c2, e, slow_rows, B_SLOW, s2_norm), V_S2)
    fill(EX_B2, 4, 0.0)
    exchange(EX_B2)

    q0, q1 = back_vectors(*exchanged_two(EX_BF3), fast_count, f3_norm)
    raw_grads(a3, e3f, da3f, fast_rows, BLK, f3_norm, q0, q1)
    for at in group_chunks:
        total = jnp.zeros((CH, BLK), f32)
        for g in range(GROUPS):
            here = slice(g * group_rows + at.start, g * group_rows + at.stop)
            total = total + jnp.where(group == g, dot_nn(da3f[here, :], f3_w[...]), 0.0)
        ep[at, :] = total
    one, two = slopes(a2p, ep, group_rows, BLK, f2_norm)
    put_folded(EX_BF2, one, two)
    fill(EX_BF2, 2, 0.0)
    exchange(EX_BF2)
    vec_two = jnp.where(group == 2, fold_lanes(two), 0.0)
    vec_two = vec_two + jnp.where(group == 3, fold_lanes(one), 0.0)

    def to_flat(at, blocks, offset, lane, value):
        for j in range(value.shape[1] // BLK):
            here = pl.ds(at + offset * blocks + lane + j, value.shape[0], stride=blocks)
            flat_ref[here, :] = value[:, j * BLK : (j + 1) * BLK]

    for n, lanes in enumerate(quarters):
        to_flat(AT_S3, 2, n * quarter, 0, dot_tn(da3[:, lanes], s2b[...]))

    total = exchanged(EX_B2)
    q0, q1 = back_vectors(row_of(total, 0, 2), row_of(total, 2, 2), slow_count, s2_norm)
    raw_grads(c2, e, da2, slow_rows, B_SLOW, s2_norm, q0, q1)
    for at in slow_chunks:
        e[at, :] = functools.reduce(
            lambda u, v: u + v,
            [
                dot_nn(shifted(two_back, at, 2 - k), s2_w[:, k * B_SLOW : (k + 1) * B_SLOW])
                for k in range(3)
            ],
        )
    put_pair(EX_B1, *slopes(c1, e, slow_rows, B_SLOW, s1_norm), V_S1)
    fill(EX_B1, 4, 0.0)
    exchange(EX_B1)

    q0, q1 = back_vectors(*exchanged_two(EX_BF2), fast_count, f2_norm)
    raw_grads(a2p, ep, d2p, group_rows, BLK, f2_norm, q0, q1)
    for at in group_chunks:
        ep[at, :] = dot_nn(d2p[at, :], f2_w[...])
    one, two = slopes(a1p, ep, group_rows, BLK, f1_norm)
    put_folded(EX_BF1, one, two)
    fill(EX_BF1, 2, 0.0)
    exchange(EX_BF1)
    vec_one = jnp.where(group == 0, fold_lanes(two), 0.0)
    vec_one = vec_one + jnp.where(group == 1, fold_lanes(one), 0.0)
    put_vector(0, vec_one + vec_two)

    everything = slice(0, slow_rows)
    for k in range(3):
        part = dot_tn(two_back[HALF : HALF + slow_rows, :], shifted(two_in, everything, k))
        to_flat(AT_S2, 6, 0, 2 * k, part)

    total = jnp.zeros((BLK, BLK), f32)
    for g in range(GROUPS):
        at = slice(g * group_rows, (g + 1) * group_rows)
        total = total + jnp.where(group == g, dot_tn(da3f[at, :], h2p[...]), 0.0)

    def to_blocks(value, at):
        n = value.shape[0] // GROUPS
        square_ref[: value.shape[0], :] = fold_lanes(value)
        flat_ref[at : at + n, :] = sum(
            jnp.where(group == r, square_ref[pl.ds(r, n, stride=GROUPS), :], 0.0)
            for r in range(GROUPS)
        )

    to_blocks(total, AT_F3)
    square = dot_tn(d2p[...], h1p[...])
    to_blocks(
        sum(
            jnp.where(group == g, square[g * B_FAST : (g + 1) * B_FAST, :], 0.0)
            for g in range(GROUPS)
        ),
        AT_F2,
    )

    total = exchanged(EX_B1)
    q0, q1 = back_vectors(row_of(total, 0, 2), row_of(total, 2, 2), slow_count, s1_norm)
    raw_grads(c1, e, da1, slow_rows, B_SLOW, s1_norm, q0, q1)
    for at in slow_chunks:
        e[at, :] = dot_nn(da1[at, :], s1_w[:, C_SLOW:])
    put_pair(EX_BLAT, *slopes(zb, e, slow_rows, C_LAT, lat_norm), V_LAT)
    fill(EX_BLAT, 4, 0.0)
    exchange(EX_BLAT)

    q0, q1 = back_vectors(*exchanged_two(EX_BF1), fast_count, f1_norm)
    raw_grads(a1p, ep, d1p, group_rows, BLK, f1_norm, q0, q1)
    for k in range(3):
        tap = jnp.zeros((B_FAST, BLK), f32)
        for g in range(GROUPS):
            first = g * per_group + k + 1
            right = jnp.concatenate([xt_ref[first + i] for i in range(per_group)], 0)
            part = dot_tn(d1p[...], right)
            tap = tap + part[g * B_FAST : (g + 1) * B_FAST, :]
        to_flat(AT_F1, 3, 0, k, tap)

    for n in range(4):
        right = jnp.concatenate([xs_ref[2 * n], xs_ref[2 * n + 1]], 1)
        to_flat(AT_S1, 10, 0, 2 * n, dot_tn(da1[...], right))
    to_flat(AT_S1, 10, 0, 8, dot_tn(da1[...], latb[...]))

    def frame_grad(rank):
        grad = e3f[rows_at(rank, HALF), :]
        for k in range(3):
            f = rank - k + 1
            there = (f >= 0) & (f < frames)
            g, j = f // per_group, lax.rem(f, per_group)
            g, j = jnp.where(there, g, 0), jnp.where(there, j, 0)
            left = jnp.where((group == g) & there, d1p[rows_at(j, HALF), :], 0.0).astype(bf16)
            grad = grad + dot_nn(left, f1_w[:, k * BLK : (k + 1) * BLK])
        return grad

    def lateral_grad(rank):
        later, s = lax.rem(rank + 2, 4), (rank + 2) // 4
        grad = jnp.zeros((HALF, BLK), f32)
        for tap, at, there in (
            (later, s, s < slow_frames),
            (later + 4, s - 1, (later == 0) & (s > 0)),
        ):
            tap, at = jnp.where(there, tap, 0), jnp.where(there, at, 0)
            left = jnp.where(there, dz[rows_at(at, HALF), :], 0.0).astype(bf16)
            weight = lat_w[:, pl.ds(pl.multiple_of(tap * BLK, BLK), BLK)]
            grad = grad + dot_nn(left, weight)
        return grad

    slow_input_grad(SENT, partner)
    hand_over(SLOW_GRAD)

    total = exchanged(EX_BLAT)
    q0, q1 = back_vectors(row_of(total, 0, 2), row_of(total, 2, 2), slow_count, lat_norm)
    raw_grads(zb, e, dz, slow_rows, C_LAT, lat_norm, q0, q1)
    to_flat(AT_LAT, 5, 0, 0, dot_tn(dz[...], wide_ref[...]))

    height = up(slots, 16)
    sib_out, sib_in, far_out, far_in = (R.sib_out, R.sib_in, R.far_out, R.far_in)
    sib_send, far_send, far_recv = (R.sum_sems.at[i] for i in range(3))
    sib_recv = R.sib_recv

    def window_of(c, o):
        return flat_ref[pl.ds(R.win_start[c * len(targets) + o], height), :]

    order = [*range(1, len(targets)), 0]
    for o in order:
        sib_out[o] = window_of(1, o).astype(bf16)
        sibling = p.dev(p.x, 1 - p.c, p.a, p.b)
        remote(sib_out.at[o], sib_in.at[o], sib_send, sib_recv.at[o], sibling)

    def fast_input_grad(kind, rank):
        R.fast_grad_box[kind] = (frame_grad(rank) + lateral_grad(rank)) * mask_ref[...]

    fast_input_grad(SENT, partner)
    hand_over(FAST_GRAD)
    for o in order:
        arrived(sib_in.at[o], sib_recv.at[o])
        both = window_of(0, o) + sib_in[o].astype(f32)
        if o:
            far_out[o] = both.astype(bf16)
            x, b = p.off_x(targets[o][0]), p.off_b(targets[o][1])
            remote(far_out.at[o], far_in.at[o], far_send, far_recv, p.dev(x, p.c, p.a, b))
        else:
            total = both
    complete(FAST_OUT)
    slow_result(MINE, p.mp)
    complete(SLOW_OUT)
    slow_input_grad(MINE, p.mp)
    complete(SLOW_GRAD)
    fast_input_grad(MINE, p.mp)
    complete(FAST_GRAD)
    arrived(far_in.at[pl.ds(1, len(targets) - 1)], far_recv)
    for o in range(1, len(targets)):
        total = total + far_in[o].astype(f32)
    results[4][...] = total

    sent = len(p_sends)
    while sent:
        n = min(sent, devices)
        arrived(p_ref.at[pl.ds(0, n * tiles)], R.p_send)
        sent -= n
    for copy in kept:
        copy.wait()
    for each in (x_gather, xs_gather, fc_gather, sc_gather):
        each.drain()
    arrived(flat_ref.at[pl.ds(0, (members - 1) * (12 * 8 + 2 * 16))], R.ex_send)
    arrived(flat_ref.at[pl.ds(0, 2 * HALF + 2 * slow_rows)], R.box_send)
    arrived(sib_out, sib_send)
    arrived(far_out.at[pl.ds(1, len(targets) - 1)], far_send)


def call_main(cfg, *args):
    smem = pl.BlockSpec(memory_space=pltpu.SMEM)
    hbm = pl.BlockSpec(memory_space=pltpu.HBM)
    vmem = pl.BlockSpec(memory_space=pltpu.VMEM)
    outs = outputs(cfg)
    return pl.pallas_call(
        functools.partial(main_kernel, cfg),
        out_shape=tuple((pltpu.VMEM if i < 9 else jax.ShapeDtypeStruct)(s, t) for i, (s, t) in enumerate(outs)),
        in_specs=[smem] + [hbm] * 8,
        out_specs=(vmem,) * 9 + (hbm,) * (len(outs) - 9),
        scratch_shapes=list(scratch(cfg).values()),
        compiler_params=pltpu.CompilerParams(
            collective_id=0, has_side_effects=True, vmem_limit_bytes=56 << 20
        ),
        name="block",
    )(*args)[:9]


def adam_kernel(cfg, *refs):
    nd, nm, frames, slow_frames, share, slots = cfg
    inputs, results, sems, held = refs[:9], refs[9:17], refs[17], refs[18:]
    run, grad, master, one, two = inputs[:5]
    w_out, one_out, two_out, low_out = held
    stores = [
        pltpu.make_async_copy(source, target, sems.at[i])
        for i, (source, target) in enumerate(zip(held + inputs[5:], results, strict=True))
    ]
    for copy in stores[4:]:
        copy.start()
    start, count = run[0:1, :], run[1:2, :]
    row = lax.broadcasted_iota(jnp.int32, (slots, BLK), 0)
    living = row < count
    block = row + start
    rate = jnp.full((slots, BLK), 0.2, f32)
    for at, width in (
        (AT_VEC, B_SLOW),
        (AT_S3, 3 * B_SLOW),
        (AT_S2, C_SLOW + C_LAT),
        (AT_S1, 5 * C_FAST),
        (AT_LAT, B_FAST),
        (AT_F2, 3 * C_FAST),
    ):
        rate = jnp.where(block < at, 0.5 / math.sqrt(width), rate)
    decay = jnp.where(block < AT_VEC, decay_rate, 0.0)
    g = grad[:slots, :]
    first = beta_first * one[...] + (1.0 - beta_first) * g
    second = beta_second * two[...] + (1.0 - beta_second) * g * g
    lift_one = 1.0 - beta_first**STEP
    lift_two = 1.0 - beta_second**STEP
    update = first / lift_one / (jnp.sqrt(second / lift_two) + adam_eps)
    weight = master[...]
    weight = jnp.where(living, weight - rate * (update + decay * weight), 0.0)
    w_out[...] = weight
    one_out[...] = jnp.where(living, first, 0.0)
    two_out[...] = jnp.where(living, second, 0.0)
    low_out[...] = weight.astype(bf16)
    for copy in stores[:4]:
        copy.start()
    for copy in stores:
        copy.wait()


def call_adam(cfg, run, grad, master, one, two, passed):
    arrays = (run, grad, master, one, two, *passed)
    hbm = pl.BlockSpec(memory_space=pltpu.HBM)
    vmem = pl.BlockSpec(memory_space=pltpu.VMEM)
    new = [jax.ShapeDtypeStruct(master.shape, t) for t in (f32, f32, f32, bf16)]
    results = new + [jax.ShapeDtypeStruct(a.shape, a.dtype) for a in passed]
    return pl.pallas_call(
        functools.partial(adam_kernel, cfg),
        out_shape=tuple(results),
        in_specs=[vmem] * len(arrays),
        out_specs=(hbm,) * len(results),
        scratch_shapes=[
            pltpu.SemaphoreType.DMA((len(results),)),
            *[pltpu.VMEM(a.shape, a.dtype) for a in new],
        ],
        compiler_params=pltpu.CompilerParams(vmem_limit_bytes=16 << 20),
        name="adam",
    )(*arrays)


def solution(mesh):
    nd, nm = mesh.shape["dp"], mesh.shape["mp"]

    def local(fast_in, slow_in, fast_cot, slow_cot, crop, owner, master, one, two):
        share, slow_frames = slow_in.shape[0], slow_in.shape[1]
        cfg = (nd, nm, fast_in.shape[1] * nm, slow_frames, share, master.shape[0])

        def halves(array):
            split = array.reshape(share, slow_frames, POS // BLK, BLK)
            return split.transpose(0, 2, 1, 3).reshape(-1, BLK)

        *passed, grad, run, master, one, two = call_main(
            cfg,
            crop,
            owner,
            master,
            one,
            two,
            fast_in.reshape(C_FAST, POS),
            halves(slow_in),
            fast_cot.reshape(C_FAST, POS),
            halves(slow_cot),
        )
        new = call_adam(cfg, run, grad, master, one, two, passed)
        return (
            new[4].reshape(fast_in.shape),
            new[5].reshape(slow_in.shape),
            new[6].reshape(fast_in.shape),
            new[7].reshape(slow_in.shape),
            *new[:4],
        )

    return jax.shard_map(
        local,
        mesh=mesh,
        in_specs=(
            P(None, "mp", "dp", None),
            P("mp", None, "dp", None),
            P(None, "mp", "dp", None),
            P("mp", None, "dp", None),
            P("dp"),
            P(),
            P(("dp", "mp"), None),
            P(("dp", "mp"), None),
            P(("dp", "mp"), None),
        ),
        out_specs=(
            P(None, "mp", "dp", None),
            P("mp", None, "dp", None),
            P(None, "mp", "dp", None),
            P("mp", None, "dp", None),
            P(("dp", "mp"), None),
            P(("dp", "mp"), None),
            P(("dp", "mp"), None),
            P(("dp", "mp"), None),
        ),
        check_vma=False,
    )
```

```python
import functools
import math
import types

import jax
import jax.numpy as jnp
from jax import lax
from jax.experimental import pallas as pl
from jax.experimental.pallas import tpu as pltpu
from jax.sharding import PartitionSpec as P

C_FAST = 128
B_FAST = 32
C_SLOW = 1024
B_SLOW = 256
C_LAT = 256
TILE = 16
POS = TILE * TILE
BLK = 128
STEP = 10
NBLK = 7591

norm_eps = 1e-05
beta_first = 0.5
beta_second = 0.5
adam_eps = 1e-08
decay_rate = 0.05

MESH = pl.DeviceIdType.MESH
f32 = jnp.float32
bf16 = jnp.bfloat16
RC = 32
CH = 256
GROUPS = BLK // B_FAST
COLUMNS = 2
HALF = POS // COLUMNS
SLABS = C_SLOW // BLK

AT_F1 = 0
AT_F2 = AT_F1 + B_FAST * 3 * C_FAST // BLK
AT_F3 = AT_F2 + B_FAST * B_FAST // BLK
AT_LAT = AT_F3 + C_FAST * B_FAST // BLK
AT_S1 = AT_LAT + C_LAT * 5 * C_FAST // BLK
AT_S2 = AT_S1 + B_SLOW * (C_SLOW + C_LAT) // BLK
AT_S3 = AT_S2 + B_SLOW * 3 * B_SLOW // BLK
AT_VEC = AT_S3 + C_SLOW * B_SLOW // BLK
V_F3 = (1, 2, 1)
V_LAT = (3, 5, 2)
V_S1 = (7, 9, 2)
V_S2 = (11, 13, 2)
V_S3 = (15, 23, 8)


def up(n, m):
    return (n + m - 1) // m * m


def dot_nt(a, b):
    return lax.dot_general(a, b, (((1,), (1,)), ((), ())), preferred_element_type=f32)


def dot_tn(a, b):
    return lax.dot_general(a, b, (((0,), (0,)), ((), ())), preferred_element_type=f32)


def dot_nn(a, b):
    return lax.dot_general(a, b, (((1,), (0,)), ((), ())), preferred_element_type=f32)


G0 = math.sqrt(2.0 / math.pi)
G1 = 0.044715


def gelu(x):
    t = jnp.tanh(x * (G0 + (G0 * G1) * (x * x)))
    return 0.5 * x * (1.0 + t)


def gelu_slope(x):
    xx = x * x
    t = jnp.tanh(x * (G0 + (G0 * G1) * xx))
    return 0.5 * (1.0 + t) + (0.5 * x) * (1.0 - t * t) * (G0 + (3.0 * G0 * G1) * xx)


def position_mask(crop):
    spot = lax.broadcasted_iota(jnp.int32, (POS, BLK), 0)
    inside = (spot // TILE < crop) & (lax.rem(spot, TILE) < crop)
    return jnp.where(inside, 1.0, 0.0).astype(f32)


def lane_group():
    return lax.broadcasted_iota(jnp.int32, (1, BLK), 1) // B_FAST


def fold_lanes(v):
    v = v + pltpu.roll(v, B_FAST, 1)
    return v + pltpu.roll(v, 2 * B_FAST, 1)


def remote(source, target, send_sem, recv_sem, device):
    pltpu.make_async_remote_copy(
        src_ref=source,
        dst_ref=target,
        send_sem=send_sem,
        recv_sem=recv_sem,
        device_id=device,
        device_id_type=MESH,
    ).start()


def arrived(view, sem):
    pltpu.make_async_copy(view, view, sem).wait()


class Place:
    def __init__(self, nd, nm):
        self.nd, self.nm = nd, nm
        self.nx = nd // 2
        self.nb = COLUMNS
        self.na = nm // self.nb
        self.dp = lax.axis_index("dp")
        self.mp = lax.axis_index("mp")
        self.x, self.c = self.dp // 2, lax.rem(self.dp, 2)
        self.a, self.b = self.mp // self.nb, lax.rem(self.mp, self.nb)

    def off_a(self, i):
        return lax.rem(self.a + i, self.na)

    def off_b(self, i):
        return lax.rem(self.b + i, self.nb)

    def off_x(self, i):
        return lax.rem(self.x + i, self.nx)

    def dev(self, x, c, a, b):
        return (x * 2 + c, a * self.nb + b)

    def slot(self, x, c, a, b):
        return (x * 2 + c) * self.nm + a * self.nb + b


class Gather:
    def __init__(self, place, slabs, other, skip, send, near, far):
        self.p, self.slabs, self.other, self.skip = place, slabs, other, skip
        self.sems = send, near, far

    def view(self, rank):
        return self.slabs.at[rank + self.skip]

    def along(self, rank):
        p, (send, near, far) = self.p, self.sems
        for i in range(1, p.na):
            device = (p.dp, p.off_a(i) * p.nb + p.b)
            remote(self.view(rank), self.view(rank), send, far, device)

    def start(self):
        p, (send, near, far) = self.p, self.sems
        remote(self.other, self.view(p.mp), send, near, (p.dp, p.a * p.nb + p.off_b(1)))
        self.along(p.mp)

    def relay(self):
        p, (send, near, far) = self.p, self.sems
        rank = p.a * p.nb + p.off_b(1)
        arrived(self.view(rank), near)
        self.along(rank)

    def pass_on(self, i):
        pass

    def finish(self):
        arrived(self.slabs.at[pl.ds(0, (self.p.na - 1) * self.p.nb)], self.sems[2])

    def drain(self):
        arrived(self.slabs.at[pl.ds(0, self.p.nm - 1)], self.sems[0])


class TreeGather(Gather):
    def __init__(self, place, slabs, other, skip, send, near, mate, *more):
        super().__init__(place, slabs, other, skip, send, near, mate)
        self.cross, self.relayed = more[:2], more[2]
        a = place.a
        self.inner = (a == 1) | (a == 2)
        self.mate = a + 1 - 2 * lax.rem(a, 2)
        self.over_there = 2 - a // 2
        self.other_half = 2 - a // 2 * 2

    def along(self, rank, i=0):
        p, piece = self.p, self.view(rank)
        for a, recv in ((self.mate, self.sems[2]), (self.over_there, self.cross[i])):
            remote(piece, piece, self.sems[0], recv, (p.dp, a * p.nb + p.b))

    def relay(self):
        p = self.p
        rank = p.a * p.nb + p.off_b(1)
        arrived(self.view(rank), self.sems[1])
        self.along(rank, 1)

    def pass_on(self, i):
        p = self.p

        @pl.when(self.inner)
        def _():
            arrived(self.slabs.at[pl.ds(0, 2)], self.cross[i])
            for k in range(2):
                piece = self.view((self.other_half + k) * p.nb + p.off_b(i))
                to = (p.dp, self.mate * p.nb + p.b)
                remote(piece, piece, self.relayed, self.cross[i], to)

    def finish(self):
        arrived(self.slabs.at[pl.ds(0, self.p.nb)], self.sems[2])

        @pl.when(~self.inner)
        def _():
            for cross in self.cross:
                arrived(self.slabs.at[pl.ds(0, 2)], cross)

    def drain(self):
        arrived(self.slabs.at[pl.ds(0, 1 + 2 * self.p.nb)], self.sems[0])

        @pl.when(self.inner)
        def _():
            arrived(self.slabs.at[pl.ds(0, 2 * self.p.nb)], self.relayed)


EX_LAT, EX_S1, EX_S2, EX_B2, EX_B1, EX_BLAT = range(6)
EX_F1, EX_F2, EX_F3, EX_BF3, EX_BF2, EX_BF1 = range(6, 12)
EX_S3, EX_BS3 = 12, 13
EXCHANGES = 14

FAST_OUT, SLOW_OUT, FAST_GRAD, SLOW_GRAD = range(4)
SENT, MINE, GOT = range(3)


def outputs(cfg):
    nd, nm, frames, slow_frames, share, slots = cfg
    halves = POS // BLK
    fast, slow = (C_FAST * halves, BLK), (share * slow_frames * halves, BLK)
    result = [(fast, f32), (slow, f32), (fast, f32), (slow, f32), ((up(slots, 16), BLK), f32)]
    result += [((8, BLK), jnp.int32)] + [((slots, BLK), f32)] * 3
    if share != BLK:
        result += [((nm, share, slow_frames * HALF), bf16)] * 2
    return result


def scratch(cfg):
    nd, nm, frames, slow_frames, share, slots = cfg
    devices, group = nd * nm, nd * COLUMNS
    rows = up(slots + 15, 16)
    height = up(slots, 16)
    halves = POS // BLK
    slow_rows, fast_rows = slow_frames * HALF, frames * HALF
    group_rows = fast_rows // GROUPS
    windows = group // 2
    vmem, smem, dma = pltpu.VMEM, pltpu.SMEM, pltpu.SemaphoreType.DMA
    piece = (slow_rows, BLK) if share == BLK else (share, slow_rows)
    result = dict(
        owner_v=vmem((NBLK,), jnp.int32),
        owner_s=smem((NBLK,), jnp.int32),
        run_device=smem((devices,), jnp.int32),
        run_start=smem((devices,), jnp.int32),
        run_count=smem((devices,), jnp.int32),
        win_start=smem((group,), jnp.int32),
        table_v=vmem((8, BLK), jnp.int32),
        table_s=smem((8, BLK), jnp.int32),
        shift=vmem((rows + 16, BLK), f32),
        p=vmem((devices * (rows // 16), 16, BLK), bf16),
        q=vmem((devices, 16, BLK), bf16),
        fast_v=vmem((C_FAST, POS), bf16),
        slow_v=vmem((share * slow_frames * halves, BLK), bf16),
        fcot_v=vmem((C_FAST, POS), bf16),
        scot_v=vmem((share * slow_frames * halves, BLK), bf16),
        stage=vmem((share * slow_frames * halves, BLK), f32),
        turned=vmem((POS, BLK), f32),
        x_other=vmem((HALF, BLK), bf16),
        fc_other=vmem((HALF, BLK), bf16),
        xs_other=vmem(piece, bf16),
        sc_other=vmem(piece, bf16),
        xt=vmem((frames + 4, HALF, BLK), bf16),
        xs=vmem((SLABS, slow_rows, BLK), bf16),
        fc=vmem((frames, HALF, BLK), bf16),
        sc=vmem((SLABS, slow_rows, BLK), bf16),
        wide=vmem((slow_rows, 5 * C_FAST), bf16),
        lat_w=vmem((C_LAT, 5 * C_FAST), bf16),
        s1_w=vmem((B_SLOW, C_SLOW + C_LAT), bf16),
        s2_w=vmem((B_SLOW, 3 * B_SLOW), bf16),
        s3_w=vmem((C_SLOW, B_SLOW), bf16),
        f1_w=vmem((BLK, 3 * C_FAST), bf16),
        f2_w=vmem((BLK, BLK), bf16),
        f3_w=vmem((BLK, BLK), bf16),
        vec=vmem((32, BLK), f32),
        mask_all=vmem((POS, BLK), f32),
        mask=vmem((HALF, BLK), f32),
    )
    if share != BLK:
        result.update(
            piece=vmem(piece, bf16),
            turn=vmem((BLK, HALF), bf16),
        )
    result.update(
        zb=vmem((slow_rows, 256), bf16),
        latb=vmem((slow_rows, 256), bf16),
        s2b=vmem((slow_rows, 256), bf16),
        dz=vmem((slow_rows, 256), bf16),
        da1=vmem((slow_rows, 256), bf16),
    )
    result.update(
        two_in=vmem(((slow_frames + 2) * HALF, 256), bf16),
        two_back=vmem(((slow_frames + 2) * HALF, 256), bf16),
        c1=vmem((slow_rows, 256), f32),
        c2=vmem((slow_rows, 256), f32),
        c3=vmem((slow_rows, C_SLOW), f32),
        e=vmem((slow_rows, 256), f32),
        e3=vmem((slow_rows, C_SLOW), f32),
        da3=vmem((slow_rows, C_SLOW), bf16),
        a1p=vmem((group_rows, BLK), f32),
        a2p=vmem((group_rows, BLK), f32),
        h1p=vmem((group_rows, BLK), bf16),
        h2p=vmem((group_rows, BLK), bf16),
        d1p=vmem((group_rows, BLK), bf16),
        d2p=vmem((group_rows, BLK), bf16),
        ep=vmem((group_rows, BLK), f32),
        a3=vmem((fast_rows, BLK), f32),
        e3f=vmem((fast_rows, BLK), f32),
        da3f=vmem((fast_rows, BLK), bf16),
        square=vmem((BLK, BLK), f32),
        flat=vmem((up(NBLK + height, 64), BLK), f32),
        sib_out=vmem((windows, height, BLK), bf16),
        sib_in=vmem((windows, height, BLK), bf16),
        far_out=vmem((windows, height, BLK), bf16),
        far_in=vmem((windows, height, BLK), bf16),
        st=vmem((12, group, 8, BLK), f32),
        st16=vmem((2, group, 16, BLK), f32),
    )
    result.update(
        fast_out_box=vmem((3, HALF, BLK), f32),
        slow_out_box=vmem((3, slow_rows, BLK), f32),
        fast_grad_box=vmem((3, HALF, BLK), f32),
        slow_grad_box=vmem((3, slow_rows, BLK), f32),
        p_send=dma(()),
        p_recv=dma((devices // 2,)),
        p_sibling=dma(()),
        gather_sems=dma((4, 6)),
        ex_send=dma(()),
        ex_recv=dma((EXCHANGES,)),
        box_send=dma(()),
        box_recv=dma((4,)),
        sum_sems=dma((3,)),
        sib_recv=dma((windows,)),
        local=dma((16,)),
    )
    return result


def main_kernel(cfg, *refs):
    nd, nm, frames, slow_frames, share, slots = cfg
    n_out = len(outputs(cfg))
    args, results, held = refs[:9], refs[9 : 9 + n_out], refs[9 + n_out :]
    crop_in, owner_in, master_in, first_in, second_in, fast_in, slow_in, fcot_in, scot_in = args
    R = types.SimpleNamespace(**dict(zip(scratch(cfg), held, strict=True)))
    p = Place(nd, nm)
    devices = nd * nm
    halves = POS // BLK
    rows = up(slots + 15, 16)
    tiles = rows // 16
    slow_rows, fast_rows = slow_frames * HALF, frames * HALF
    per_group = frames // GROUPS
    group_rows = per_group * HALF
    slabs = share == BLK
    me = p.dp * nm + p.mp
    partner = p.a * p.nb + p.off_b(1)

    members = nd * p.nb
    member = p.dp * p.nb + p.b
    group_peers = [
        p.dev(p.off_x(i), lax.rem(p.c + k, 2), p.a, p.off_b(j))
        for i in reversed(range(p.nx))
        for j in reversed(range(p.nb))
        for k in range(2)
        if i or j or k
    ]
    near = [p.dev(p.x, p.c, p.off_a(i), p.b) for i in range(1, p.na)]
    barrier = pltpu.get_barrier_semaphore()
    for device in group_peers + near:
        pl.semaphore_signal(barrier, inc=1, device_id=device, device_id_type=MESH)

    local_copies = []

    def fetch(source, target):
        copy = pltpu.make_async_copy(source, target, R.local.at[len(local_copies)])
        copy.start()
        local_copies.append(copy)
        return copy

    get_owner = fetch(owner_in, R.owner_v)
    get_owner_s = fetch(owner_in, R.owner_s)
    get_master = fetch(master_in, R.shift.at[pl.ds(16, slots)])
    get_fast = fetch(fast_in, R.fast_v)
    get_slow = fetch(slow_in, R.slow_v)
    get_fcot = fetch(fcot_in, R.fcot_v)
    get_scot = fetch(scot_in, R.scot_v)
    kept = [fetch(a, results[6 + i]) for i, a in enumerate((master_in, first_in, second_in))]

    crop = crop_in[0]
    R.mask_all[...] = position_mask(crop)
    R.mask[...] = R.mask_all[pl.ds(pl.multiple_of(p.b * HALF, HALF), HALF), :]
    tall = crop.astype(f32)
    area = tall * tall * (1.0 / COLUMNS)
    xt_ref, xs_ref, fc_ref, sc_ref = R.xt, R.xs, R.fc, R.sc
    for f in (0, 1, frames + 2, frames + 3):
        xt_ref[f] = jnp.zeros((HALF, BLK), bf16)
    two_in, two_back = R.two_in, R.two_back
    for ref in (two_in, two_back):
        ref[:HALF] = jnp.zeros((HALF, 256), bf16)
        ref[(slow_frames + 1) * HALF :] = jnp.zeros((HALF, 256), bf16)

    get_owner.wait()
    spot = lax.broadcasted_iota(jnp.int32, (8, BLK), 0) * BLK
    spot = spot + lax.broadcasted_iota(jnp.int32, (8, BLK), 1)
    lowest = jnp.full((8, BLK), NBLK, jnp.int32)
    number = jnp.zeros((8, BLK), jnp.int32)
    whole = NBLK // 1024 * 1024
    for i in range(0, whole, 1024):
        mine = R.owner_v[pl.ds(i, 1024)].reshape(8, BLK) == me
        lowest = jnp.minimum(lowest, jnp.where(mine, spot + i, NBLK))
        number = number + jnp.where(mine, 1, 0)
    for i in range(whole, NBLK // BLK * BLK, BLK):
        mine = R.owner_v[pl.ds(i, BLK)].reshape(1, BLK) == me
        mine = mine & (spot < BLK)
        lowest = jnp.minimum(lowest, jnp.where(mine, spot + i, NBLK))
        number = number + jnp.where(mine, 1, 0)
    get_owner_s.wait()

    def last_ones(i, found):
        first, n = found
        mine = R.owner_s[i] == me
        return jnp.where(mine, jnp.minimum(first, i), first), n + jnp.where(mine, 1, 0)

    found = jnp.min(lowest), jnp.sum(number)
    my_start, my_count = lax.fori_loop(NBLK // BLK * BLK, NBLK, last_ones, found)
    line = lax.broadcasted_iota(jnp.int32, (8, BLK), 0)
    results[5][...] = jnp.where(line == 0, my_start, my_count)
    shift = lax.rem(my_start, 16)
    get_master.wait()
    moved = R.shift[pl.ds(16 - shift, rows), :]
    row = lax.broadcasted_iota(jnp.int32, (rows, BLK), 0)
    own = (row >= shift) & (row < shift + my_count)
    p_ref = R.p

    def p_slot(slot):
        return p_ref.at[pl.ds(slot * tiles, tiles)]

    p_slot(me)[...] = jnp.where(own, moved, 0.0).astype(bf16).reshape(tiles, 16, BLK)

    pl.semaphore_wait(barrier, len(group_peers) + len(near))
    p_sends = []

    def view(x, c, a, b):
        return p_slot(p.slot(x, c, a, b))

    def came(source):
        x, c, a, b = source
        return R.p_recv.at[x * nm + a * p.nb + b]

    def pass_on(source, along_a=(), along_b=False, along_x=False, along_c=False):
        piece, sem = view(*source), came(source)
        to = []
        for i in along_a:
            to += [p.dev(p.x, p.c, p.off_a(i), p.b)]
        if along_x:
            to += [p.dev(p.off_x(i), p.c, p.a, p.b) for i in range(1, p.nx)]
        if along_b:
            to += [p.dev(p.x, p.c, p.a, p.off_b(1))]
        for device in to:
            remote(piece, piece, R.p_send, sem, device)
            p_sends.append(device)
        if along_c:
            device = p.dev(p.x, 1 - p.c, p.a, p.b)
            remote(piece, piece, R.p_send, R.p_sibling, device)
            p_sends.append(device)

    def take(source):
        arrived(view(*source), came(source))

    here = (p.x, p.c, p.a, p.b)
    pass_on(here, along_a=range(1, p.na), along_b=True, along_x=True, along_c=True)

    turned_ref = R.turned

    def half_of(b):
        return pl.ds(pl.multiple_of(b * HALF, HALF), HALF)

    def own_frame(slot, other, source):
        turned_ref[...] = source[...].astype(f32).T * R.mask_all[...]
        slot[...] = turned_ref[half_of(p.b), :].astype(bf16)
        other[...] = turned_ref[half_of(p.off_b(1)), :].astype(bf16)

    def own_slow(slot, other, source):
        stage = R.stage
        stage[...] = source[...].astype(f32)
        for s in range(slow_frames):
            at = slice(s * HALF, (s + 1) * HALF)
            for h in range(halves):
                part = stage[pl.ds(h * slow_frames + s, share, stride=halves * slow_frames), :]
                if slabs:
                    here = slice(h * BLK, (h + 1) * BLK)
                    turned_ref[here, :] = part.T * R.mask_all[here, :]
                else:
                    turned_ref[h * share : (h + 1) * share, :] = part
            if slabs:
                slot[at, :] = turned_ref[half_of(p.b), :].astype(bf16)
                other[at, :] = turned_ref[half_of(p.off_b(1)), :].astype(bf16)
            else:
                for ref, b in ((R.piece, p.b), (other, p.off_b(1))):
                    mine = pl.ds(pl.multiple_of(b * share, share), share)
                    ref[:, at] = turned_ref[mine, :].astype(bf16)
        if not slabs:
            pltpu.sync_copy(R.piece, slot)

    def from_natural(natural, wide):
        ranks = BLK // share

        def block(i, _):
            s, j = i // SLABS, lax.rem(i, SLABS)
            at_row = pl.ds(pl.multiple_of(s * HALF, HALF), HALF)
            for k in range(ranks):
                pltpu.sync_copy(
                    natural.at[j * ranks + k, :, at_row],
                    R.turn.at[pl.ds(k * share, share)],
                )
            piece = R.turn[...].astype(f32).T * R.mask[...]
            wide[j, at_row, :] = piece.astype(bf16)
            return 0

        lax.fori_loop(0, slow_frames * SLABS, block, 0)

    def gather(kind, which, array, other, skip=0):
        sems = [R.gather_sems.at[which, i] for i in range(3 if kind is Gather else 6)]
        return kind(p, array, other, skip, *sems)

    tree = TreeGather if p.na == 4 else Gather
    x_gather = gather(tree, 0, xt_ref, R.x_other, 2)
    fc_gather = gather(Gather, 1, fc_ref, R.fc_other)
    xs_gather = gather(Gather, 2, xs_ref if slabs else results[9], R.xs_other)
    sc_gather = gather(Gather, 3, sc_ref if slabs else results[10], R.sc_other)
    get_fast.wait()
    own_frame(x_gather.view(p.mp), R.x_other, R.fast_v)
    x_gather.start()
    get_slow.wait()
    own_slow(xs_gather.view(p.mp), R.xs_other, R.slow_v)

    steps = [1 << i for i in reversed(range(max(1, (slots - 1).bit_length())))]
    owner_s, run_device, run_start, run_count = (R.owner_s, R.run_device, R.run_start, R.run_count)

    def run(k, at):
        device = owner_s[jnp.minimum(at, NBLK - 1)]
        n = jnp.int32(1)
        for step in steps:
            more = n + step
            last = at + more - 1
            inside = owner_s[jnp.minimum(last, NBLK - 1)] == device
            n = jnp.where((more <= slots) & (last < NBLK) & inside, more, n)
        run_device[k] = device
        run_start[k] = at
        run_count[k] = n
        return at + n

    lax.fori_loop(0, devices, run, jnp.int32(0))

    targets = [(i, j) for i in range(p.nx) for j in range(p.nb)]
    owners = [p.slot(p.off_x(i), c, p.a, p.off_b(j)) for c in (p.c, 1 - p.c) for i, j in targets]

    def find(k, found):
        return [jnp.where(run_device[k] == d, run_start[k], at) for d, at in zip(owners, found)]

    for i, at in enumerate(lax.fori_loop(0, devices, find, [jnp.int32(0)] * len(owners))):
        R.win_start[i] = at

    for i in range(1, p.na):
        source = (p.x, p.c, p.off_a(p.na - i), p.b)
        take(source)
        pass_on(source, along_b=True, along_x=True, along_c=True)
    x_gather.relay()
    xs_gather.start()

    def tile_of(k):
        return run_device[k] * tiles - run_start[k] // 16

    def table(k, found):
        start, last = run_start[k], run_start[k] + run_count[k] - 1
        final = jnp.minimum(spot * 16 + 15, NBLK - 1)
        holds = (final >= start) & (final <= last)
        tile = jnp.where(spot == start // 16, devices * tiles + k, spot + tile_of(k))
        return jnp.where(holds, tile, found)

    R.table_v[...] = lax.fori_loop(0, devices, table, jnp.zeros((8, BLK), jnp.int32))
    get_table = fetch(R.table_v, R.table_s)
    x_gather.pass_on(0)
    x_gather.pass_on(1)

    across = p.na // 2
    for i in range(p.na):
        source = (p.x, p.c, p.off_a(p.na - i), p.off_b(1))
        take(source)
        pass_on(source, along_x=i < across, along_c=True)
        for j in range(1, p.nx):
            source = (p.off_x(j), p.c, p.off_a(p.na - i), p.b)
            take(source)
            pass_on(source, along_b=i >= across, along_c=True)
    xs_gather.relay()
    get_fcot.wait()
    own_frame(fc_gather.view(p.mp), R.fc_other, R.fcot_v)
    get_scot.wait()
    own_slow(sc_gather.view(p.mp), R.sc_other, R.scot_v)
    for i in range(p.na):
        for k in range(1, p.nx):
            source = (p.off_x(k), p.c, p.off_a(p.na - i), p.off_b(1))
            take(source)
            pass_on(source, along_c=True)
    sc_gather.start()
    arrived(p_ref.at[pl.ds(0, devices // 2 * tiles)], R.p_sibling)
    get_table.wait()
    sc_gather.relay()

    def tile_rows(t):
        return pl.ds(pl.multiple_of(t * 16, 16), 16)

    q_ref = R.q

    def first_tile(k, before):
        tile = p_ref[run_device[k] * tiles].astype(f32)
        shared = lax.rem(run_start[k], 16) != 0
        tile = tile + jnp.where(shared, before, 0.0)
        q_ref[k] = tile.astype(bf16)
        last = (run_start[k] + run_count[k] - 1) // 16
        alone = last == run_start[k] // 16
        return jnp.where(alone, tile, p_ref[tile_of(k) + last].astype(f32))

    lax.fori_loop(0, devices, first_tile, jnp.zeros((16, BLK), f32))
    flat_ref, table_s = R.flat, R.table_s

    def lay_out(first_block, end_block):
        first, end = first_block // 16, up(end_block, 16) // 16

        def one(t):
            source = table_s[t // BLK, lax.rem(t, BLK)]
            plain = p_ref[jnp.minimum(source, devices * tiles - 1)]
            shared = q_ref[jnp.maximum(source - devices * tiles, 0)]
            tile = jnp.where(source < devices * tiles, plain, shared)
            flat_ref[tile_rows(t), :] = tile.astype(f32)

        def eight(i, _):
            for k in range(8):
                one(first + i * 8 + k)
            return 0

        lax.fori_loop(0, (end - first) // 8, eight, 0)
        for t in range(first + (end - first) // 8 * 8, end):
            one(t)

    def matrix(out_ref, at, height, blocks):
        lay_out(at, at + height * blocks)
        for j in range(blocks):
            for o in range(0, height, 256):
                out_ref[o : o + 256, j * BLK : (j + 1) * BLK] = flat_ref[
                    pl.ds(at + o * blocks + j, 256, stride=blocks), :
                ].astype(bf16)

    group = lane_group()
    square_ref = R.square
    lat_w, s1_w, s2_w, s3_w = R.lat_w, R.s1_w, R.s2_w, R.s3_w
    f1_w, f2_w, f3_w, vec_ref = R.f1_w, R.f2_w, R.f3_w, R.vec

    def spread_rows(at, height):
        for r in range(GROUPS):
            part = jnp.where(group == r, flat_ref[at : at + height // GROUPS, :], 0.0)
            square_ref[pl.ds(r, height // GROUPS, stride=GROUPS), :] = fold_lanes(part)
        return square_ref[:height, :]

    def fast_weights():
        lay_out(AT_F1, AT_LAT)
        for k in range(3):
            tap = flat_ref[pl.ds(AT_F1 + k, B_FAST, stride=3), :].astype(bf16)
            for g in range(GROUPS):
                f1_w[g * B_FAST : (g + 1) * B_FAST, k * BLK : (k + 1) * BLK] = tap
        two = spread_rows(AT_F2, B_FAST)
        for g in range(GROUPS):
            f2_w[g * B_FAST : (g + 1) * B_FAST, :] = jnp.where(group == g, two, 0.0).astype(bf16)
        f3_w[...] = spread_rows(AT_F3, C_FAST).astype(bf16)

    matrix(lat_w, AT_LAT, C_LAT, 5)
    lay_out(AT_VEC, NBLK)
    vec_ref[...] = flat_ref[AT_VEC : AT_VEC + 32, :]
    x_gather.finish()

    zb, latb, s2b, dz, da1, wide_ref = (R.zb, R.latb, R.s2b, R.dz, R.da1, R.wide)
    c1, c2, c3, e, e3, da3 = (R.c1, R.c2, R.c3, R.e, R.e3, R.da3)
    a1p, a2p, h1p, h2p, d1p, d2p, ep, a3, e3f, da3f = (R.a1p, R.a2p, R.h1p, R.h2p, R.d1p, R.d2p, R.ep, R.a3, R.e3f, R.da3f)
    mask_ref, st_ref, st16_ref = R.mask, R.st, R.st16
    s1b = two_in.at[pl.ds(HALF, slow_rows)]
    da2 = two_back.at[pl.ds(HALF, slow_rows)]

    def stat(which):
        return (st_ref, which) if which < 12 else (st16_ref, which - 12)

    def exchange(which):
        ref, at = stat(which)
        own = ref.at[at, member]
        for device in group_peers:
            remote(own, own, R.ex_send, R.ex_recv.at[which], device)

    def exchanged(which):
        ref, at = stat(which)
        arrived(ref.at[at, pl.ds(0, members - 1)], R.ex_recv.at[which])
        total = ref[at, 0]
        for i in range(1, members):
            total = total + ref[at, i]
        return total

    def put(which, at, vector):
        ref, index = stat(which)
        for j in range(vector.shape[1] // BLK):
            ref[index, member, at + j : at + j + 1, :] = vector[:, j * BLK : (j + 1) * BLK]

    def fill(which, at, value):
        ref, index = stat(which)
        ref[index, member, at:8, :] = jnp.full((8 - at, BLK), value, f32)

    def row_of(block, at, n):
        return jnp.concatenate([block[at + j : at + j + 1, :] for j in range(n)], 1)

    def vectors(place):
        g, b, n = place
        return row_of(vec_ref[...], g, n), row_of(vec_ref[...], b, n)

    def rows_at(i, size):
        return pl.ds(pl.multiple_of(i * size, size), size)

    def mask_at(i, width):
        part = mask_ref[pl.ds(pl.multiple_of(lax.rem(i * RC, HALF), RC), RC), :]
        return jnp.concatenate([part] * (width // BLK), 1) if width > BLK else part

    def eights(v):
        return jnp.sum(v.reshape(v.shape[0] // 8, 8, v.shape[1]), 0)

    def total_row(v):
        return jnp.sum(v, 0, keepdims=True)

    def affine(sums, squares, count, gain, bias):
        mean = sums / count
        scale = lax.rsqrt(squares / count - mean * mean + norm_eps)
        grow = gain * scale
        return mean, scale, grow, bias - mean * grow

    def loop(n, body, start):
        return lax.fori_loop(0, n, body, start, unroll=n if n <= 8 else 4)

    def sums_of(ref, n_rows, width):
        def body(i, acc):
            v = ref[rows_at(i, RC), :].astype(f32)
            return acc[0] + eights(v), acc[1] + eights(v * v)

        zero = jnp.zeros((8, width), f32)
        one, two = loop(n_rows // RC, body, (zero, zero))
        return total_row(one), total_row(two)

    def activate(src, dst, n_rows, width, grow, base):
        def body(i, _):
            at = rows_at(i, RC)
            pre = src[at, :].astype(f32) * grow + base
            dst[at, :] = (gelu(pre) * mask_at(i, width)).astype(bf16)
            return 0

        loop(n_rows // RC, body, 0)

    def slopes(src, incoming, n_rows, width, norm):
        mean, scale, grow, base = norm

        def body(i, acc):
            at = rows_at(i, RC)
            a = src[at, :].astype(f32)
            d = gelu_slope(a * grow + base) * incoming[at, :] * mask_at(i, width)
            incoming[at, :] = d
            return acc[0] + eights(d), acc[1] + eights(d * ((a - mean) * scale))

        zero = jnp.zeros((8, width), f32)
        one, two = loop(n_rows // RC, body, (zero, zero))
        return total_row(one), total_row(two)

    def back_vectors(bias_sum, gain_sum, count, norm):
        mean, scale, grow, base = norm
        k1 = grow * gain_sum / count
        return grow * bias_sum / count - k1 * (mean * scale), k1 * scale

    def raw_grads(src, pres, dst, n_rows, width, norm, q0, q1):
        grow = norm[2]

        def body(i, _):
            at = rows_at(i, RC)
            a = src[at, :].astype(f32)
            da = grow * pres[at, :] - mask_at(i, width) * (q0 + a * q1)
            dst[at, :] = da.astype(bf16)
            return 0

        loop(n_rows // RC, body, 0)

    def put_vector(row, vector):
        for j in range(vector.shape[1] // BLK):
            at = AT_VEC + row + j
            flat_ref[at : at + 1, :] = vector[:, j * BLK : (j + 1) * BLK]

    def put_pair(which, one, two, place=None):
        put(which, 0, one)
        put(which, one.shape[1] // BLK, two)
        if place is not None:
            put_vector(place[0], two)
            put_vector(place[1], one)

    slow_chunks = [slice(i, i + CH) for i in range(0, slow_rows, CH)]
    group_chunks = [slice(i, i + CH) for i in range(0, group_rows, CH)]

    def all_slabs(ref, at):
        return jnp.concatenate([ref[j, at, :] for j in range(SLABS)], 1)

    boxes = (
        (R.fast_out_box, results[0]),
        (R.slow_out_box, results[1]),
        (R.fast_grad_box, results[2]),
        (R.slow_grad_box, results[3]),
    )

    def box(which, kind):
        return boxes[which][0].at[kind]

    def hand_over(which):
        box_sems = R.box_send, R.box_recv.at[which]
        remote(box(which, SENT), box(which, GOT), *box_sems, (p.dp, partner))

    def to_channels(block):
        turned = block.T
        if slabs:
            return turned
        lane_shift = lax.rem(p.mp * share, BLK)
        return sum(
            jnp.where(lane_shift == k * share, turned[k * share : (k + 1) * share, :], 0.0)
            for k in range(BLK // share)
        )

    def complete(which):
        ref, end = boxes[which]
        arrived(box(which, GOT), R.box_recv.at[which])
        fast = which in (FAST_OUT, FAST_GRAD)
        n = 1 if fast else slow_frames
        for s in range(n):
            at = slice(s * HALF, (s + 1) * HALF)
            for h in range(halves):
                block = jnp.where(p.b == h, ref[MINE, at, :], ref[GOT, at, :])
                block = block.T if fast else to_channels(block)
                end[pl.ds(s * halves + h, block.shape[0], stride=n * halves), :] = block

    for s in range(slow_frames):
        for k in range(5):
            wide_ref[s * HALF : (s + 1) * HALF, k * BLK : (k + 1) * BLK] = xt_ref[4 * s + k]
    for at in slow_chunks:
        zb[at, :] = dot_nt(wide_ref[at, :], lat_w[...]).astype(bf16)
    put_pair(EX_LAT, *sums_of(zb, slow_rows, C_LAT))
    fill(EX_LAT, 4, area)
    exchange(EX_LAT)

    fast_weights()

    def fast_rows_of(ref, first_frame, at):
        f = first_frame + at.start // HALF
        return jnp.concatenate([ref[f + i] for i in range(CH // HALF)], 0)

    for at in group_chunks:
        total = jnp.zeros((CH, BLK), f32)
        for g in range(GROUPS):
            window = jnp.concatenate(
                [fast_rows_of(xt_ref, g * per_group + 1 + k, at) for k in range(3)], 1
            )
            total = total + jnp.where(group == g, dot_nt(window, f1_w[...]), 0.0)
        a1p[at, :] = total

    def put_folded(which, one, two):
        put(which, 0, fold_lanes(one))
        put(which, 1, fold_lanes(two))

    put_folded(EX_F1, *sums_of(a1p, group_rows, BLK))
    fill(EX_F1, 2, area)
    exchange(EX_F1)

    matrix(s1_w, AT_S1, B_SLOW, 10)
    xs_gather.finish()
    if not slabs:
        from_natural(results[9], xs_ref)

    for at in slow_chunks:
        c1[at, :] = dot_nt(all_slabs(xs_ref, at), s1_w[:, :C_SLOW])

    total = exchanged(EX_LAT)
    area_all = total[4:5, :]
    slow_count = jnp.concatenate([area_all * float(slow_frames)] * 2, 1)
    slow_count8 = jnp.concatenate([slow_count] * 4, 1)
    fast_count = area_all * float(frames)
    lat_norm = affine(row_of(total, 0, 2), row_of(total, 2, 2), slow_count, *vectors(V_LAT))
    activate(zb, latb, slow_rows, C_LAT, lat_norm[2], lat_norm[3])
    for at in slow_chunks:
        c1[at, :] = c1[at, :] + dot_nt(latb[at, :], s1_w[:, C_SLOW:])
    put_pair(EX_S1, *sums_of(c1, slow_rows, B_SLOW))
    fill(EX_S1, 4, 0.0)
    exchange(EX_S1)

    matrix(s2_w, AT_S2, B_SLOW, 6)
    fc_gather.start()
    matrix(s3_w, AT_S3, C_SLOW, 2)

    packed = vec_ref[0:1, :]

    def spread(which):
        return fold_lanes(jnp.where(group == which, packed, 0.0))

    def exchanged_two(which):
        total = exchanged(which)
        return total[0:1, :], total[1:2, :]

    f1_norm = affine(*exchanged_two(EX_F1), fast_count, spread(0), spread(1))
    activate(a1p, h1p, group_rows, BLK, f1_norm[2], f1_norm[3])
    for at in group_chunks:
        a2p[at, :] = dot_nt(h1p[at, :], f2_w[...])
    put_folded(EX_F2, *sums_of(a2p, group_rows, BLK))
    fill(EX_F2, 2, 0.0)
    exchange(EX_F2)

    total = exchanged(EX_S1)
    s1_norm = affine(row_of(total, 0, 2), row_of(total, 2, 2), slow_count, *vectors(V_S1))
    activate(c1, s1b, slow_rows, B_SLOW, s1_norm[2], s1_norm[3])

    def shifted(ref, at, k):
        return ref[at.start + k * HALF : at.stop + k * HALF, :]

    for at in slow_chunks:
        window = jnp.concatenate([shifted(two_in, at, k) for k in range(3)], 1)
        c2[at, :] = dot_nt(window, s2_w[...])
    put_pair(EX_S2, *sums_of(c2, slow_rows, B_SLOW))
    fill(EX_S2, 4, 0.0)
    exchange(EX_S2)

    fc_gather.relay()

    f2_norm = affine(*exchanged_two(EX_F2), fast_count, spread(2), spread(3))
    activate(a2p, h2p, group_rows, BLK, f2_norm[2], f2_norm[3])
    for g in range(GROUPS):
        for at in group_chunks:
            part = jnp.where(group == g, h2p[at, :], 0.0).astype(bf16)
            here = slice(g * group_rows + at.start, g * group_rows + at.stop)
            a3[here, :] = dot_nt(part, f3_w[...])
    put_pair(EX_F3, *sums_of(a3, fast_rows, BLK))
    fill(EX_F3, 2, 0.0)
    exchange(EX_F3)

    total = exchanged(EX_S2)
    s2_norm = affine(row_of(total, 0, 2), row_of(total, 2, 2), slow_count, *vectors(V_S2))
    activate(c2, s2b, slow_rows, B_SLOW, s2_norm[2], s2_norm[3])
    quarter = C_SLOW // 4
    quarters = [slice(n * quarter, (n + 1) * quarter) for n in range(4)]
    for n, lanes in enumerate(quarters):
        for at in slow_chunks:
            c3[at, lanes] = dot_nt(s2b[at, :], s3_w[lanes, :])
        one, two = sums_of(c3.at[:, lanes], slow_rows, quarter)
        put(EX_S3, 2 * n, one)
        put(EX_S3, 8 + 2 * n, two)
    exchange(EX_S3)

    f3_norm = affine(*exchanged_two(EX_F3), fast_count, *vectors(V_F3))
    for rank, kind in ((partner, SENT), (p.mp, MINE)):
        pre = a3[rows_at(rank, HALF), :] * f3_norm[2] + f3_norm[3]
        pre = pre + xt_ref[rank + 2].astype(f32)
        R.fast_out_box[kind] = gelu(pre) * mask_ref[...]
    hand_over(FAST_OUT)
    sc_gather.finish()
    if not slabs:
        from_natural(results[10], sc_ref)
    total = exchanged(EX_S3)
    s3_norm = affine(row_of(total, 0, 8), row_of(total, 8, 8), slow_count8, *vectors(V_S3))

    def pair_of(ref, n, at):
        return jnp.concatenate([ref[2 * n, at, :], ref[2 * n + 1, at, :]], 1).astype(f32)

    for n, lanes in enumerate(quarters):
        norm = [v[:, lanes] for v in s3_norm]

        def slow_slopes(i, acc, n=n, lanes=lanes, norm=norm):
            at = rows_at(i, RC)
            a = c3[at, lanes]
            pre = a * norm[2] + norm[3] + pair_of(xs_ref, n, at)
            d = gelu_slope(pre) * pair_of(sc_ref, n, at)
            e3[at, lanes] = d
            return acc[0] + eights(d), acc[1] + eights(d * ((a - norm[0]) * norm[1]))

        zero = jnp.zeros((8, quarter), f32)
        one, two = loop(slow_rows // RC, slow_slopes, (zero, zero))
        one, two = total_row(one), total_row(two)
        put(EX_BS3, 2 * n, one)
        put(EX_BS3, 8 + 2 * n, two)
        put_vector(V_S3[0] + 2 * n, two)
        put_vector(V_S3[1] + 2 * n, one)
    exchange(EX_BS3)

    fc_gather.finish()

    def fast_slopes(i, acc):
        mean, scale, grow, base = f3_norm
        at = rows_at(i, RC)
        f, here = i // (HALF // RC), rows_at(lax.rem(i, HALF // RC), RC)
        a = a3[at, :]
        x = xt_ref[f + 2, here, :].astype(f32)
        d = gelu_slope(a * grow + base + x) * fc_ref[f, here, :].astype(f32)
        e3f[at, :] = d
        return acc[0] + eights(d), acc[1] + eights(d * ((a - mean) * scale))

    zero = jnp.zeros((8, BLK), f32)
    one, two = loop(fast_rows // RC, fast_slopes, (zero, zero))
    put_pair(EX_BF3, total_row(one), total_row(two), V_F3)
    fill(EX_BF3, 2, 0.0)
    exchange(EX_BF3)

    def slow_place(rank):
        slab = rank * share // BLK
        return slab, pl.ds(pl.multiple_of(slab * BLK, BLK), BLK)

    def slow_result(kind, rank):
        slab, lanes = slow_place(rank)
        grow, base = (
            sum(jnp.where(slab == k, v[:, k * BLK : (k + 1) * BLK], 0.0) for k in range(SLABS))
            for v in s3_norm[2:]
        )
        for s in range(slow_frames):
            at = slice(s * HALF, (s + 1) * HALF)
            pre = c3[at, lanes] * grow + base + xs_ref[slab, at, :].astype(f32)
            R.slow_out_box[kind, at, :] = gelu(pre) * mask_ref[...]

    def slow_input_grad(kind, rank):
        slab, lanes = slow_place(rank)
        for s in range(slow_frames):
            at = slice(s * HALF, (s + 1) * HALF)
            value = e3[at, lanes] + dot_nn(da1[at, :], s1_w[:, lanes])
            R.slow_grad_box[kind, at, :] = value * mask_ref[...]

    slow_result(SENT, partner)
    hand_over(SLOW_OUT)

    total = exchanged(EX_BS3)
    q0, q1 = back_vectors(row_of(total, 0, 8), row_of(total, 8, 8), slow_count8, s3_norm)
    for lanes in quarters:
        norm = [v[:, lanes] for v in s3_norm]
        raw_grads(
            c3.at[:, lanes], e3.at[:, lanes], da3.at[:, lanes], slow_rows, quarter, norm,
            q0[:, lanes], q1[:, lanes]
        )
    for at in slow_chunks:
        e[at, :] = dot_nn(da3[at, :], s3_w[...])
    put_pair(EX_B2, *slopes(c2, e, slow_rows, B_SLOW, s2_norm), V_S2)
    fill(EX_B2, 4, 0.0)
    exchange(EX_B2)

    q0, q1 = back_vectors(*exchanged_two(EX_BF3), fast_count, f3_norm)
    raw_grads(a3, e3f, da3f, fast_rows, BLK, f3_norm, q0, q1)
    for at in group_chunks:
        total = jnp.zeros((CH, BLK), f32)
        for g in range(GROUPS):
            here = slice(g * group_rows + at.start, g * group_rows + at.stop)
            total = total + jnp.where(group == g, dot_nn(da3f[here, :], f3_w[...]), 0.0)
        ep[at, :] = total
    one, two = slopes(a2p, ep, group_rows, BLK, f2_norm)
    put_folded(EX_BF2, one, two)
    fill(EX_BF2, 2, 0.0)
    exchange(EX_BF2)
    vec_two = jnp.where(group == 2, fold_lanes(two), 0.0)
    vec_two = vec_two + jnp.where(group == 3, fold_lanes(one), 0.0)

    def to_flat(at, blocks, offset, lane, value):
        for j in range(value.shape[1] // BLK):
            here = pl.ds(at + offset * blocks + lane + j, value.shape[0], stride=blocks)
            flat_ref[here, :] = value[:, j * BLK : (j + 1) * BLK]

    for n, lanes in enumerate(quarters):
        to_flat(AT_S3, 2, n * quarter, 0, dot_tn(da3[:, lanes], s2b[...]))

    total = exchanged(EX_B2)
    q0, q1 = back_vectors(row_of(total, 0, 2), row_of(total, 2, 2), slow_count, s2_norm)
    raw_grads(c2, e, da2, slow_rows, B_SLOW, s2_norm, q0, q1)
    for at in slow_chunks:
        e[at, :] = functools.reduce(
            lambda u, v: u + v,
            [
                dot_nn(shifted(two_back, at, 2 - k), s2_w[:, k * B_SLOW : (k + 1) * B_SLOW])
                for k in range(3)
            ],
        )
    put_pair(EX_B1, *slopes(c1, e, slow_rows, B_SLOW, s1_norm), V_S1)
    fill(EX_B1, 4, 0.0)
    exchange(EX_B1)

    q0, q1 = back_vectors(*exchanged_two(EX_BF2), fast_count, f2_norm)
    raw_grads(a2p, ep, d2p, group_rows, BLK, f2_norm, q0, q1)
    for at in group_chunks:
        ep[at, :] = dot_nn(d2p[at, :], f2_w[...])
    one, two = slopes(a1p, ep, group_rows, BLK, f1_norm)
    put_folded(EX_BF1, one, two)
    fill(EX_BF1, 2, 0.0)
    exchange(EX_BF1)
    vec_one = jnp.where(group == 0, fold_lanes(two), 0.0)
    vec_one = vec_one + jnp.where(group == 1, fold_lanes(one), 0.0)
    put_vector(0, vec_one + vec_two)

    everything = slice(0, slow_rows)
    for k in range(3):
        part = dot_tn(two_back[HALF : HALF + slow_rows, :], shifted(two_in, everything, k))
        to_flat(AT_S2, 6, 0, 2 * k, part)

    total = jnp.zeros((BLK, BLK), f32)
    for g in range(GROUPS):
        at = slice(g * group_rows, (g + 1) * group_rows)
        total = total + jnp.where(group == g, dot_tn(da3f[at, :], h2p[...]), 0.0)

    def to_blocks(value, at):
        n = value.shape[0] // GROUPS
        square_ref[: value.shape[0], :] = fold_lanes(value)
        flat_ref[at : at + n, :] = sum(
            jnp.where(group == r, square_ref[pl.ds(r, n, stride=GROUPS), :], 0.0)
            for r in range(GROUPS)
        )

    to_blocks(total, AT_F3)
    square = dot_tn(d2p[...], h1p[...])
    to_blocks(
        sum(
            jnp.where(group == g, square[g * B_FAST : (g + 1) * B_FAST, :], 0.0)
            for g in range(GROUPS)
        ),
        AT_F2,
    )

    total = exchanged(EX_B1)
    q0, q1 = back_vectors(row_of(total, 0, 2), row_of(total, 2, 2), slow_count, s1_norm)
    raw_grads(c1, e, da1, slow_rows, B_SLOW, s1_norm, q0, q1)
    for at in slow_chunks:
        e[at, :] = dot_nn(da1[at, :], s1_w[:, C_SLOW:])
    put_pair(EX_BLAT, *slopes(zb, e, slow_rows, C_LAT, lat_norm), V_LAT)
    fill(EX_BLAT, 4, 0.0)
    exchange(EX_BLAT)

    q0, q1 = back_vectors(*exchanged_two(EX_BF1), fast_count, f1_norm)
    raw_grads(a1p, ep, d1p, group_rows, BLK, f1_norm, q0, q1)
    for k in range(3):
        tap = jnp.zeros((B_FAST, BLK), f32)
        for g in range(GROUPS):
            first = g * per_group + k + 1
            right = jnp.concatenate([xt_ref[first + i] for i in range(per_group)], 0)
            part = dot_tn(d1p[...], right)
            tap = tap + part[g * B_FAST : (g + 1) * B_FAST, :]
        to_flat(AT_F1, 3, 0, k, tap)

    for n in range(4):
        right = jnp.concatenate([xs_ref[2 * n], xs_ref[2 * n + 1]], 1)
        to_flat(AT_S1, 10, 0, 2 * n, dot_tn(da1[...], right))
    to_flat(AT_S1, 10, 0, 8, dot_tn(da1[...], latb[...]))

    def frame_grad(rank):
        grad = e3f[rows_at(rank, HALF), :]
        for k in range(3):
            f = rank - k + 1
            there = (f >= 0) & (f < frames)
            g, j = f // per_group, lax.rem(f, per_group)
            g, j = jnp.where(there, g, 0), jnp.where(there, j, 0)
            left = jnp.where((group == g) & there, d1p[rows_at(j, HALF), :], 0.0).astype(bf16)
            grad = grad + dot_nn(left, f1_w[:, k * BLK : (k + 1) * BLK])
        return grad

    def lateral_grad(rank):
        later, s = lax.rem(rank + 2, 4), (rank + 2) // 4
        grad = jnp.zeros((HALF, BLK), f32)
        for tap, at, there in (
            (later, s, s < slow_frames),
            (later + 4, s - 1, (later == 0) & (s > 0)),
        ):
            tap, at = jnp.where(there, tap, 0), jnp.where(there, at, 0)
            left = jnp.where(there, dz[rows_at(at, HALF), :], 0.0).astype(bf16)
            weight = lat_w[:, pl.ds(pl.multiple_of(tap * BLK, BLK), BLK)]
            grad = grad + dot_nn(left, weight)
        return grad

    slow_input_grad(SENT, partner)
    hand_over(SLOW_GRAD)

    total = exchanged(EX_BLAT)
    q0, q1 = back_vectors(row_of(total, 0, 2), row_of(total, 2, 2), slow_count, lat_norm)
    raw_grads(zb, e, dz, slow_rows, C_LAT, lat_norm, q0, q1)
    to_flat(AT_LAT, 5, 0, 0, dot_tn(dz[...], wide_ref[...]))

    height = up(slots, 16)
    sib_out, sib_in, far_out, far_in = (R.sib_out, R.sib_in, R.far_out, R.far_in)
    sib_send, far_send, far_recv = (R.sum_sems.at[i] for i in range(3))
    sib_recv = R.sib_recv

    def window_of(c, o):
        return flat_ref[pl.ds(R.win_start[c * len(targets) + o], height), :]

    order = [*range(1, len(targets)), 0]
    for o in order:
        sib_out[o] = window_of(1, o).astype(bf16)
        sibling = p.dev(p.x, 1 - p.c, p.a, p.b)
        remote(sib_out.at[o], sib_in.at[o], sib_send, sib_recv.at[o], sibling)

    def fast_input_grad(kind, rank):
        R.fast_grad_box[kind] = (frame_grad(rank) + lateral_grad(rank)) * mask_ref[...]

    fast_input_grad(SENT, partner)
    hand_over(FAST_GRAD)
    for o in order:
        arrived(sib_in.at[o], sib_recv.at[o])
        both = window_of(0, o) + sib_in[o].astype(f32)
        if o:
            far_out[o] = both.astype(bf16)
            x, b = p.off_x(targets[o][0]), p.off_b(targets[o][1])
            remote(far_out.at[o], far_in.at[o], far_send, far_recv, p.dev(x, p.c, p.a, b))
        else:
            total = both
    complete(FAST_OUT)
    slow_result(MINE, p.mp)
    complete(SLOW_OUT)
    slow_input_grad(MINE, p.mp)
    complete(SLOW_GRAD)
    fast_input_grad(MINE, p.mp)
    complete(FAST_GRAD)
    arrived(far_in.at[pl.ds(1, len(targets) - 1)], far_recv)
    for o in range(1, len(targets)):
        total = total + far_in[o].astype(f32)
    results[4][...] = total

    sent = len(p_sends)
    while sent:
        n = min(sent, devices)
        arrived(p_ref.at[pl.ds(0, n * tiles)], R.p_send)
        sent -= n
    for copy in kept:
        copy.wait()
    for each in (x_gather, xs_gather, fc_gather, sc_gather):
        each.drain()
    arrived(flat_ref.at[pl.ds(0, (members - 1) * (12 * 8 + 2 * 16))], R.ex_send)
    arrived(flat_ref.at[pl.ds(0, 2 * HALF + 2 * slow_rows)], R.box_send)
    arrived(sib_out, sib_send)
    arrived(far_out.at[pl.ds(1, len(targets) - 1)], far_send)


def call_main(cfg, *args):
    smem = pl.BlockSpec(memory_space=pltpu.SMEM)
    hbm = pl.BlockSpec(memory_space=pltpu.HBM)
    vmem = pl.BlockSpec(memory_space=pltpu.VMEM)
    outs = outputs(cfg)
    return pl.pallas_call(
        functools.partial(main_kernel, cfg),
        out_shape=tuple((pltpu.VMEM if i < 9 else jax.ShapeDtypeStruct)(s, t) for i, (s, t) in enumerate(outs)),
        in_specs=[smem] + [hbm] * 8,
        out_specs=(vmem,) * 9 + (hbm,) * (len(outs) - 9),
        scratch_shapes=list(scratch(cfg).values()),
        compiler_params=pltpu.CompilerParams(
            collective_id=0, has_side_effects=True, vmem_limit_bytes=56 << 20
        ),
        name="block",
    )(*args)[:9]


def adam_kernel(cfg, *refs):
    nd, nm, frames, slow_frames, share, slots = cfg
    inputs, results, sems, held = refs[:9], refs[9:17], refs[17], refs[18:]
    run, grad, master, one, two = inputs[:5]
    w_out, one_out, two_out, low_out = held
    stores = [
        pltpu.make_async_copy(source, target, sems.at[i])
        for i, (source, target) in enumerate(zip(held + inputs[5:], results, strict=True))
    ]
    for copy in stores[4:]:
        copy.start()
    start, count = run[0:1, :], run[1:2, :]
    row = lax.broadcasted_iota(jnp.int32, (slots, BLK), 0)
    living = row < count
    block = row + start
    rate = jnp.full((slots, BLK), 0.2, f32)
    for at, width in (
        (AT_VEC, B_SLOW),
        (AT_S3, 3 * B_SLOW),
        (AT_S2, C_SLOW + C_LAT),
        (AT_S1, 5 * C_FAST),
        (AT_LAT, B_FAST),
        (AT_F2, 3 * C_FAST),
    ):
        rate = jnp.where(block < at, 0.5 / math.sqrt(width), rate)
    decay = jnp.where(block < AT_VEC, decay_rate, 0.0)
    g = grad[:slots, :]
    first = beta_first * one[...] + (1.0 - beta_first) * g
    second = beta_second * two[...] + (1.0 - beta_second) * g * g
    lift_one = 1.0 - beta_first**STEP
    lift_two = 1.0 - beta_second**STEP
    update = first / lift_one / (jnp.sqrt(second / lift_two) + adam_eps)
    weight = master[...]
    weight = jnp.where(living, weight - rate * (update + decay * weight), 0.0)
    w_out[...] = weight
    one_out[...] = jnp.where(living, first, 0.0)
    two_out[...] = jnp.where(living, second, 0.0)
    low_out[...] = weight.astype(bf16)
    for copy in stores[:4]:
        copy.start()
    for copy in stores:
        copy.wait()


def call_adam(cfg, run, grad, master, one, two, passed):
    arrays = (run, grad, master, one, two, *passed)
    hbm = pl.BlockSpec(memory_space=pltpu.HBM)
    vmem = pl.BlockSpec(memory_space=pltpu.VMEM)
    new = [jax.ShapeDtypeStruct(master.shape, t) for t in (f32, f32, f32, bf16)]
    results = new + [jax.ShapeDtypeStruct(a.shape, a.dtype) for a in passed]
    return pl.pallas_call(
        functools.partial(adam_kernel, cfg),
        out_shape=tuple(results),
        in_specs=[vmem] * len(arrays),
        out_specs=(hbm,) * len(results),
        scratch_shapes=[
            pltpu.SemaphoreType.DMA((len(results),)),
            *[pltpu.VMEM(a.shape, a.dtype) for a in new],
        ],
        compiler_params=pltpu.CompilerParams(vmem_limit_bytes=16 << 20),
        name="adam",
    )(*arrays)


def solution(mesh):
    nd, nm = mesh.shape["dp"], mesh.shape["mp"]

    def local(fast_in, slow_in, fast_cot, slow_cot, crop, owner, master, one, two):
        share, slow_frames = slow_in.shape[0], slow_in.shape[1]
        cfg = (nd, nm, fast_in.shape[1] * nm, slow_frames, share, master.shape[0])

        def halves(array):
            split = array.reshape(share, slow_frames, POS // BLK, BLK)
            return split.transpose(0, 2, 1, 3).reshape(-1, BLK)

        *passed, grad, run, master, one, two = call_main(
            cfg,
            crop,
            owner,
            master,
            one,
            two,
            fast_in.reshape(C_FAST, POS),
            halves(slow_in),
            fast_cot.reshape(C_FAST, POS),
            halves(slow_cot),
        )
        new = call_adam(cfg, run, grad, master, one, two, passed)
        return (
            new[4].reshape(fast_in.shape),
            new[5].reshape(slow_in.shape),
            new[6].reshape(fast_in.shape),
            new[7].reshape(slow_in.shape),
            *new[:4],
        )

    return jax.shard_map(
        local,
        mesh=mesh,
        in_specs=(
            P(None, "mp", "dp", None),
            P("mp", None, "dp", None),
            P(None, "mp", "dp", None),
            P("mp", None, "dp", None),
            P("dp"),
            P(),
            P(("dp", "mp"), None),
            P(("dp", "mp"), None),
            P(("dp", "mp"), None),
        ),
        out_specs=(
            P(None, "mp", "dp", None),
            P("mp", None, "dp", None),
            P(None, "mp", "dp", None),
            P("mp", None, "dp", None),
            P(("dp", "mp"), None),
            P(("dp", "mp"), None),
            P(("dp", "mp"), None),
            P(("dp", "mp"), None),
        ),
        check_vma=False,
    )
```

```python
import functools
import math
import types

import jax
import jax.numpy as jnp
from jax import lax
from jax.experimental import pallas as pl
from jax.experimental.pallas import tpu as pltpu
from jax.sharding import PartitionSpec as P

C_FAST = 128
B_FAST = 32
C_SLOW = 1024
B_SLOW = 256
C_LAT = 256
TILE = 16
POS = TILE * TILE
BLK = 128
STEP = 10
NBLK = 7591

norm_eps = 1e-05
beta_first = 0.5
beta_second = 0.5
adam_eps = 1e-08
decay_rate = 0.05

MESH = pl.DeviceIdType.MESH
f32 = jnp.float32
bf16 = jnp.bfloat16
RC = 32
CH = 256
GROUPS = BLK // B_FAST
COLUMNS = 2
HALF = POS // COLUMNS
SLABS = C_SLOW // BLK

AT_F1 = 0
AT_F2 = AT_F1 + B_FAST * 3 * C_FAST // BLK
AT_F3 = AT_F2 + B_FAST * B_FAST // BLK
AT_LAT = AT_F3 + C_FAST * B_FAST // BLK
AT_S1 = AT_LAT + C_LAT * 5 * C_FAST // BLK
AT_S2 = AT_S1 + B_SLOW * (C_SLOW + C_LAT) // BLK
AT_S3 = AT_S2 + B_SLOW * 3 * B_SLOW // BLK
AT_VEC = AT_S3 + C_SLOW * B_SLOW // BLK
V_F3 = (1, 2, 1)
V_LAT = (3, 5, 2)
V_S1 = (7, 9, 2)
V_S2 = (11, 13, 2)
V_S3 = (15, 23, 8)


def up(n, m):
    return (n + m - 1) // m * m


def dot_nt(a, b):
    return lax.dot_general(a, b, (((1,), (1,)), ((), ())), preferred_element_type=f32)


def dot_tn(a, b):
    return lax.dot_general(a, b, (((0,), (0,)), ((), ())), preferred_element_type=f32)


def dot_nn(a, b):
    return lax.dot_general(a, b, (((1,), (0,)), ((), ())), preferred_element_type=f32)


G0 = math.sqrt(2.0 / math.pi)
G1 = 0.044715


def gelu(x):
    t = jnp.tanh(x * (G0 + (G0 * G1) * (x * x)))
    return 0.5 * x * (1.0 + t)


def gelu_slope(x):
    xx = x * x
    t = jnp.tanh(x * (G0 + (G0 * G1) * xx))
    return 0.5 * (1.0 + t) + (0.5 * x) * (1.0 - t * t) * (G0 + (3.0 * G0 * G1) * xx)


def position_mask(crop):
    spot = lax.broadcasted_iota(jnp.int32, (POS, BLK), 0)
    inside = (spot // TILE < crop) & (lax.rem(spot, TILE) < crop)
    return jnp.where(inside, 1.0, 0.0).astype(f32)


def lane_group():
    return lax.broadcasted_iota(jnp.int32, (1, BLK), 1) // B_FAST


def fold_lanes(v):
    v = v + pltpu.roll(v, B_FAST, 1)
    return v + pltpu.roll(v, 2 * B_FAST, 1)


def remote(source, target, send_sem, recv_sem, device):
    pltpu.make_async_remote_copy(
        src_ref=source,
        dst_ref=target,
        send_sem=send_sem,
        recv_sem=recv_sem,
        device_id=device,
        device_id_type=MESH,
    ).start()


def arrived(view, sem):
    pltpu.make_async_copy(view, view, sem).wait()


class Place:
    def __init__(self, nd, nm):
        self.nd, self.nm = nd, nm
        self.nx = nd // 2
        self.nb = COLUMNS
        self.na = nm // self.nb
        self.dp = lax.axis_index("dp")
        self.mp = lax.axis_index("mp")
        self.x, self.c = self.dp // 2, lax.rem(self.dp, 2)
        self.a, self.b = self.mp // self.nb, lax.rem(self.mp, self.nb)

    def off_a(self, i):
        return lax.rem(self.a + i, self.na)

    def off_b(self, i):
        return lax.rem(self.b + i, self.nb)

    def off_x(self, i):
        return lax.rem(self.x + i, self.nx)

    def dev(self, x, c, a, b):
        return (x * 2 + c, a * self.nb + b)

    def slot(self, x, c, a, b):
        return (x * 2 + c) * self.nm + a * self.nb + b


class Gather:
    def __init__(self, place, slabs, other, skip, send, near, far):
        self.p, self.slabs, self.other, self.skip = place, slabs, other, skip
        self.sems = send, near, far

    def view(self, rank):
        return self.slabs.at[rank + self.skip]

    def along(self, rank):
        p, (send, near, far) = self.p, self.sems
        for i in range(1, p.na):
            device = (p.dp, p.off_a(i) * p.nb + p.b)
            remote(self.view(rank), self.view(rank), send, far, device)

    def start(self):
        p, (send, near, far) = self.p, self.sems
        remote(self.other, self.view(p.mp), send, near, (p.dp, p.a * p.nb + p.off_b(1)))
        self.along(p.mp)

    def relay(self):
        p, (send, near, far) = self.p, self.sems
        rank = p.a * p.nb + p.off_b(1)
        arrived(self.view(rank), near)
        self.along(rank)

    def pass_on(self, i):
        pass

    def finish(self):
        arrived(self.slabs.at[pl.ds(0, (self.p.na - 1) * self.p.nb)], self.sems[2])

    def drain(self):
        arrived(self.slabs.at[pl.ds(0, self.p.nm - 1)], self.sems[0])


class TreeGather(Gather):
    def __init__(self, place, slabs, other, skip, send, near, mate, *more):
        super().__init__(place, slabs, other, skip, send, near, mate)
        self.cross, self.relayed = more[:2], more[2]
        a = place.a
        self.inner = (a == 1) | (a == 2)
        self.mate = a + 1 - 2 * lax.rem(a, 2)
        self.over_there = 2 - a // 2
        self.other_half = 2 - a // 2 * 2

    def along(self, rank, i=0):
        p, piece = self.p, self.view(rank)
        for a, recv in ((self.mate, self.sems[2]), (self.over_there, self.cross[i])):
            remote(piece, piece, self.sems[0], recv, (p.dp, a * p.nb + p.b))

    def relay(self):
        p = self.p
        rank = p.a * p.nb + p.off_b(1)
        arrived(self.view(rank), self.sems[1])
        self.along(rank, 1)

    def pass_on(self, i):
        p = self.p

        @pl.when(self.inner)
        def _():
            arrived(self.slabs.at[pl.ds(0, 2)], self.cross[i])
            for k in range(2):
                piece = self.view((self.other_half + k) * p.nb + p.off_b(i))
                to = (p.dp, self.mate * p.nb + p.b)
                remote(piece, piece, self.relayed, self.cross[i], to)

    def finish(self):
        arrived(self.slabs.at[pl.ds(0, self.p.nb)], self.sems[2])

        @pl.when(~self.inner)
        def _():
            for cross in self.cross:
                arrived(self.slabs.at[pl.ds(0, 2)], cross)

    def drain(self):
        arrived(self.slabs.at[pl.ds(0, 1 + 2 * self.p.nb)], self.sems[0])

        @pl.when(self.inner)
        def _():
            arrived(self.slabs.at[pl.ds(0, 2 * self.p.nb)], self.relayed)


EX_LAT, EX_S1, EX_S2, EX_B2, EX_B1, EX_BLAT = range(6)
EX_F1, EX_F2, EX_F3, EX_BF3, EX_BF2, EX_BF1 = range(6, 12)
EX_S3, EX_BS3 = 12, 13
EXCHANGES = 14

FAST_OUT, SLOW_OUT, FAST_GRAD, SLOW_GRAD = range(4)
SENT, MINE, GOT = range(3)


def outputs(cfg):
    nd, nm, frames, slow_frames, share, slots = cfg
    halves = POS // BLK
    fast, slow = (C_FAST * halves, BLK), (share * slow_frames * halves, BLK)
    result = [(fast, f32), (slow, f32), (fast, f32), (slow, f32), ((up(slots, 16), BLK), f32)]
    result += [((8, BLK), jnp.int32)] + [((slots, BLK), f32)] * 3
    if share != BLK:
        result += [((nm, share, slow_frames * HALF), bf16)] * 2
    return result


def scratch(cfg):
    nd, nm, frames, slow_frames, share, slots = cfg
    devices, group = nd * nm, nd * COLUMNS
    rows = up(slots + 15, 16)
    height = up(slots, 16)
    halves = POS // BLK
    slow_rows, fast_rows = slow_frames * HALF, frames * HALF
    group_rows = fast_rows // GROUPS
    windows = group // 2
    vmem, smem, dma = pltpu.VMEM, pltpu.SMEM, pltpu.SemaphoreType.DMA
    piece = (slow_rows, BLK) if share == BLK else (share, slow_rows)
    result = dict(
        owner_v=vmem((NBLK,), jnp.int32),
        owner_s=smem((NBLK,), jnp.int32),
        run_device=smem((devices,), jnp.int32),
        run_start=smem((devices,), jnp.int32),
        run_count=smem((devices,), jnp.int32),
        win_start=smem((group,), jnp.int32),
        table_v=vmem((8, BLK), jnp.int32),
        table_s=smem((8, BLK), jnp.int32),
        shift=vmem((rows + 16, BLK), f32),
        p=vmem((devices * (rows // 16), 16, BLK), bf16),
        q=vmem((devices, 16, BLK), bf16),
        fast_v=vmem((C_FAST, POS), bf16),
        slow_v=vmem((share * slow_frames * halves, BLK), bf16),
        fcot_v=vmem((C_FAST, POS), bf16),
        scot_v=vmem((share * slow_frames * halves, BLK), bf16),
        stage=vmem((share * slow_frames * halves, BLK), f32),
        turned=vmem((POS, BLK), f32),
        x_other=vmem((HALF, BLK), bf16),
        fc_other=vmem((HALF, BLK), bf16),
        xs_other=vmem(piece, bf16),
        sc_other=vmem(piece, bf16),
        xt=vmem((frames + 4, HALF, BLK), bf16),
        xs=vmem((SLABS, slow_rows, BLK), bf16),
        fc=vmem((frames, HALF, BLK), bf16),
        sc=vmem((SLABS, slow_rows, BLK), bf16),
        wide=vmem((slow_rows, 5 * C_FAST), bf16),
        lat_w=vmem((C_LAT, 5 * C_FAST), bf16),
        s1_w=vmem((B_SLOW, C_SLOW + C_LAT), bf16),
        s2_w=vmem((B_SLOW, 3 * B_SLOW), bf16),
        s3_w=vmem((C_SLOW, B_SLOW), bf16),
        f1_w=vmem((BLK, 3 * C_FAST), bf16),
        f2_w=vmem((BLK, BLK), bf16),
        f3_w=vmem((BLK, BLK), bf16),
        vec=vmem((32, BLK), f32),
        mask_all=vmem((POS, BLK), f32),
        mask=vmem((HALF, BLK), f32),
    )
    if share != BLK:
        result.update(
            piece=vmem(piece, bf16),
            turn=vmem((BLK, HALF), bf16),
        )
    result.update(
        zb=vmem((slow_rows, 256), bf16),
        latb=vmem((slow_rows, 256), bf16),
        s2b=vmem((slow_rows, 256), bf16),
        dz=vmem((slow_rows, 256), bf16),
        da1=vmem((slow_rows, 256), bf16),
    )
    result.update(
        two_in=vmem(((slow_frames + 2) * HALF, 256), bf16),
        two_back=vmem(((slow_frames + 2) * HALF, 256), bf16),
        c1=vmem((slow_rows, 256), f32),
        c2=vmem((slow_rows, 256), f32),
        c3=vmem((slow_rows, C_SLOW), f32),
        e=vmem((slow_rows, 256), f32),
        e3=vmem((slow_rows, C_SLOW), f32),
        da3=vmem((slow_rows, C_SLOW), bf16),
        a1p=vmem((group_rows, BLK), f32),
        a2p=vmem((group_rows, BLK), f32),
        h1p=vmem((group_rows, BLK), bf16),
        h2p=vmem((group_rows, BLK), bf16),
        d1p=vmem((group_rows, BLK), bf16),
        d2p=vmem((group_rows, BLK), bf16),
        ep=vmem((group_rows, BLK), f32),
        a3=vmem((fast_rows, BLK), f32),
        e3f=vmem((fast_rows, BLK), f32),
        da3f=vmem((fast_rows, BLK), bf16),
        square=vmem((BLK, BLK), f32),
        flat=vmem((up(NBLK + height, 64), BLK), f32),
        sib_out=vmem((windows, height, BLK), bf16),
        sib_in=vmem((windows, height, BLK), bf16),
        far_out=vmem((windows, height, BLK), bf16),
        far_in=vmem((windows, height, BLK), bf16),
        st=vmem((12, group, 8, BLK), f32),
        st16=vmem((2, group, 16, BLK), f32),
    )
    result.update(
        fast_out_box=vmem((3, HALF, BLK), f32),
        slow_out_box=vmem((3, slow_rows, BLK), f32),
        fast_grad_box=vmem((3, HALF, BLK), f32),
        slow_grad_box=vmem((3, slow_rows, BLK), f32),
        p_send=dma(()),
        p_recv=dma((devices // 2,)),
        p_sibling=dma(()),
        gather_sems=dma((4, 6)),
        ex_send=dma(()),
        ex_recv=dma((EXCHANGES,)),
        box_send=dma(()),
        box_recv=dma((4,)),
        sum_sems=dma((3,)),
        sib_recv=dma((windows,)),
        local=dma((16,)),
    )
    return result


def main_kernel(cfg, *refs):
    nd, nm, frames, slow_frames, share, slots = cfg
    n_out = len(outputs(cfg))
    args, results, held = refs[:9], refs[9 : 9 + n_out], refs[9 + n_out :]
    crop_in, owner_in, master_in, first_in, second_in, fast_in, slow_in, fcot_in, scot_in = args
    R = types.SimpleNamespace(**dict(zip(scratch(cfg), held, strict=True)))
    p = Place(nd, nm)
    devices = nd * nm
    halves = POS // BLK
    rows = up(slots + 15, 16)
    tiles = rows // 16
    slow_rows, fast_rows = slow_frames * HALF, frames * HALF
    per_group = frames // GROUPS
    group_rows = per_group * HALF
    slabs = share == BLK
    me = p.dp * nm + p.mp
    partner = p.a * p.nb + p.off_b(1)

    members = nd * p.nb
    member = p.dp * p.nb + p.b
    group_peers = [
        p.dev(p.off_x(i), lax.rem(p.c + k, 2), p.a, p.off_b(j))
        for i in reversed(range(p.nx))
        for j in reversed(range(p.nb))
        for k in range(2)
        if i or j or k
    ]
    near = [p.dev(p.x, p.c, p.off_a(i), p.b) for i in range(1, p.na)]
    barrier = pltpu.get_barrier_semaphore()
    for device in group_peers + near:
        pl.semaphore_signal(barrier, inc=1, device_id=device, device_id_type=MESH)

    local_copies = []

    def fetch(source, target):
        copy = pltpu.make_async_copy(source, target, R.local.at[len(local_copies)])
        copy.start()
        local_copies.append(copy)
        return copy

    get_owner = fetch(owner_in, R.owner_v)
    get_owner_s = fetch(owner_in, R.owner_s)
    get_master = fetch(master_in, R.shift.at[pl.ds(16, slots)])
    get_fast = fetch(fast_in, R.fast_v)
    get_slow = fetch(slow_in, R.slow_v)
    get_fcot = fetch(fcot_in, R.fcot_v)
    get_scot = fetch(scot_in, R.scot_v)
    kept = [fetch(a, results[6 + i]) for i, a in enumerate((master_in, first_in, second_in))]

    crop = crop_in[0]
    R.mask_all[...] = position_mask(crop)
    R.mask[...] = R.mask_all[pl.ds(pl.multiple_of(p.b * HALF, HALF), HALF), :]
    tall = crop.astype(f32)
    area = tall * tall * (1.0 / COLUMNS)
    xt_ref, xs_ref, fc_ref, sc_ref = R.xt, R.xs, R.fc, R.sc
    for f in (0, 1, frames + 2, frames + 3):
        xt_ref[f] = jnp.zeros((HALF, BLK), bf16)
    two_in, two_back = R.two_in, R.two_back
    for ref in (two_in, two_back):
        ref[:HALF] = jnp.zeros((HALF, 256), bf16)
        ref[(slow_frames + 1) * HALF :] = jnp.zeros((HALF, 256), bf16)

    get_owner.wait()
    spot = lax.broadcasted_iota(jnp.int32, (8, BLK), 0) * BLK
    spot = spot + lax.broadcasted_iota(jnp.int32, (8, BLK), 1)
    lowest = jnp.full((8, BLK), NBLK, jnp.int32)
    number = jnp.zeros((8, BLK), jnp.int32)
    whole = NBLK // 1024 * 1024
    for i in range(0, whole, 1024):
        mine = R.owner_v[pl.ds(i, 1024)].reshape(8, BLK) == me
        lowest = jnp.minimum(lowest, jnp.where(mine, spot + i, NBLK))
        number = number + jnp.where(mine, 1, 0)
    for i in range(whole, NBLK // BLK * BLK, BLK):
        mine = R.owner_v[pl.ds(i, BLK)].reshape(1, BLK) == me
        mine = mine & (spot < BLK)
        lowest = jnp.minimum(lowest, jnp.where(mine, spot + i, NBLK))
        number = number + jnp.where(mine, 1, 0)
    get_owner_s.wait()

    def last_ones(i, found):
        first, n = found
        mine = R.owner_s[i] == me
        return jnp.where(mine, jnp.minimum(first, i), first), n + jnp.where(mine, 1, 0)

    found = jnp.min(lowest), jnp.sum(number)
    my_start, my_count = lax.fori_loop(NBLK // BLK * BLK, NBLK, last_ones, found)
    line = lax.broadcasted_iota(jnp.int32, (8, BLK), 0)
    results[5][...] = jnp.where(line == 0, my_start, my_count)
    shift = lax.rem(my_start, 16)
    get_master.wait()
    moved = R.shift[pl.ds(16 - shift, rows), :]
    row = lax.broadcasted_iota(jnp.int32, (rows, BLK), 0)
    own = (row >= shift) & (row < shift + my_count)
    p_ref = R.p

    def p_slot(slot):
        return p_ref.at[pl.ds(slot * tiles, tiles)]

    p_slot(me)[...] = jnp.where(own, moved, 0.0).astype(bf16).reshape(tiles, 16, BLK)

    pl.semaphore_wait(barrier, len(group_peers) + len(near))
    p_sends = []

    def view(x, c, a, b):
        return p_slot(p.slot(x, c, a, b))

    def came(source):
        x, c, a, b = source
        return R.p_recv.at[x * nm + a * p.nb + b]

    def pass_on(source, along_a=(), along_b=False, along_x=False, along_c=False):
        piece, sem = view(*source), came(source)
        to = []
        for i in along_a:
            to += [p.dev(p.x, p.c, p.off_a(i), p.b)]
        if along_x:
            to += [p.dev(p.off_x(i), p.c, p.a, p.b) for i in range(1, p.nx)]
        if along_b:
            to += [p.dev(p.x, p.c, p.a, p.off_b(1))]
        for device in to:
            remote(piece, piece, R.p_send, sem, device)
            p_sends.append(device)
        if along_c:
            device = p.dev(p.x, 1 - p.c, p.a, p.b)
            remote(piece, piece, R.p_send, R.p_sibling, device)
            p_sends.append(device)

    def take(source):
        arrived(view(*source), came(source))

    here = (p.x, p.c, p.a, p.b)
    pass_on(here, along_a=range(1, p.na), along_b=True, along_x=True, along_c=True)

    turned_ref = R.turned

    def half_of(b):
        return pl.ds(pl.multiple_of(b * HALF, HALF), HALF)

    def own_frame(slot, other, source):
        turned_ref[...] = source[...].astype(f32).T * R.mask_all[...]
        slot[...] = turned_ref[half_of(p.b), :].astype(bf16)
        other[...] = turned_ref[half_of(p.off_b(1)), :].astype(bf16)

    def own_slow(slot, other, source):
        stage = R.stage
        stage[...] = source[...].astype(f32)
        for s in range(slow_frames):
            at = slice(s * HALF, (s + 1) * HALF)
            for h in range(halves):
                part = stage[pl.ds(h * slow_frames + s, share, stride=halves * slow_frames), :]
                if slabs:
                    here = slice(h * BLK, (h + 1) * BLK)
                    turned_ref[here, :] = part.T * R.mask_all[here, :]
                else:
                    turned_ref[h * share : (h + 1) * share, :] = part
            if slabs:
                slot[at, :] = turned_ref[half_of(p.b), :].astype(bf16)
                other[at, :] = turned_ref[half_of(p.off_b(1)), :].astype(bf16)
            else:
                for ref, b in ((R.piece, p.b), (other, p.off_b(1))):
                    mine = pl.ds(pl.multiple_of(b * share, share), share)
                    ref[:, at] = turned_ref[mine, :].astype(bf16)
        if not slabs:
            pltpu.sync_copy(R.piece, slot)

    def from_natural(natural, wide):
        ranks = BLK // share

        def block(i, _):
            s, j = i // SLABS, lax.rem(i, SLABS)
            at_row = pl.ds(pl.multiple_of(s * HALF, HALF), HALF)
            for k in range(ranks):
                pltpu.sync_copy(
                    natural.at[j * ranks + k, :, at_row],
                    R.turn.at[pl.ds(k * share, share)],
                )
            piece = R.turn[...].astype(f32).T * R.mask[...]
            wide[j, at_row, :] = piece.astype(bf16)
            return 0

        lax.fori_loop(0, slow_frames * SLABS, block, 0)

    def gather(kind, which, array, other, skip=0):
        sems = [R.gather_sems.at[which, i] for i in range(3 if kind is Gather else 6)]
        return kind(p, array, other, skip, *sems)

    tree = TreeGather if p.na == 4 else Gather
    x_gather = gather(tree, 0, xt_ref, R.x_other, 2)
    fc_gather = gather(Gather, 1, fc_ref, R.fc_other)
    xs_gather = gather(Gather, 2, xs_ref if slabs else results[9], R.xs_other)
    sc_gather = gather(Gather, 3, sc_ref if slabs else results[10], R.sc_other)
    get_fast.wait()
    own_frame(x_gather.view(p.mp), R.x_other, R.fast_v)
    x_gather.start()
    get_slow.wait()
    own_slow(xs_gather.view(p.mp), R.xs_other, R.slow_v)

    steps = [1 << i for i in reversed(range(max(1, (slots - 1).bit_length())))]
    owner_s, run_device, run_start, run_count = (R.owner_s, R.run_device, R.run_start, R.run_count)

    def run(k, at):
        device = owner_s[jnp.minimum(at, NBLK - 1)]
        n = jnp.int32(1)
        for step in steps:
            more = n + step
            last = at + more - 1
            inside = owner_s[jnp.minimum(last, NBLK - 1)] == device
            n = jnp.where((more <= slots) & (last < NBLK) & inside, more, n)
        run_device[k] = device
        run_start[k] = at
        run_count[k] = n
        return at + n

    lax.fori_loop(0, devices, run, jnp.int32(0))

    targets = [(i, j) for i in range(p.nx) for j in range(p.nb)]
    owners = [p.slot(p.off_x(i), c, p.a, p.off_b(j)) for c in (p.c, 1 - p.c) for i, j in targets]

    def find(k, found):
        return [jnp.where(run_device[k] == d, run_start[k], at) for d, at in zip(owners, found)]

    for i, at in enumerate(lax.fori_loop(0, devices, find, [jnp.int32(0)] * len(owners))):
        R.win_start[i] = at

    for i in range(1, p.na):
        source = (p.x, p.c, p.off_a(p.na - i), p.b)
        take(source)
        pass_on(source, along_b=True, along_x=True, along_c=True)
    x_gather.relay()
    xs_gather.start()

    def tile_of(k):
        return run_device[k] * tiles - run_start[k] // 16

    def table(k, found):
        start, last = run_start[k], run_start[k] + run_count[k] - 1
        final = jnp.minimum(spot * 16 + 15, NBLK - 1)
        holds = (final >= start) & (final <= last)
        tile = jnp.where(spot == start // 16, devices * tiles + k, spot + tile_of(k))
        return jnp.where(holds, tile, found)

    R.table_v[...] = lax.fori_loop(0, devices, table, jnp.zeros((8, BLK), jnp.int32))
    get_table = fetch(R.table_v, R.table_s)
    x_gather.pass_on(0)
    x_gather.pass_on(1)

    across = p.na // 2
    for i in range(p.na):
        source = (p.x, p.c, p.off_a(p.na - i), p.off_b(1))
        take(source)
        pass_on(source, along_x=i < across, along_c=True)
        for j in range(1, p.nx):
            source = (p.off_x(j), p.c, p.off_a(p.na - i), p.b)
            take(source)
            pass_on(source, along_b=i >= across, along_c=True)
    xs_gather.relay()
    get_fcot.wait()
    own_frame(fc_gather.view(p.mp), R.fc_other, R.fcot_v)
    get_scot.wait()
    own_slow(sc_gather.view(p.mp), R.sc_other, R.scot_v)
    sc_gather.start()
    for i in range(p.na):
        for k in range(1, p.nx):
            source = (p.off_x(k), p.c, p.off_a(p.na - i), p.off_b(1))
            take(source)
            pass_on(source, along_c=True)
    arrived(p_ref.at[pl.ds(0, devices // 2 * tiles)], R.p_sibling)
    get_table.wait()
    sc_gather.relay()

    def tile_rows(t):
        return pl.ds(pl.multiple_of(t * 16, 16), 16)

    q_ref = R.q

    def first_tile(k, before):
        tile = p_ref[run_device[k] * tiles].astype(f32)
        shared = lax.rem(run_start[k], 16) != 0
        tile = tile + jnp.where(shared, before, 0.0)
        q_ref[k] = tile.astype(bf16)
        last = (run_start[k] + run_count[k] - 1) // 16
        alone = last == run_start[k] // 16
        return jnp.where(alone, tile, p_ref[tile_of(k) + last].astype(f32))

    lax.fori_loop(0, devices, first_tile, jnp.zeros((16, BLK), f32))
    flat_ref, table_s = R.flat, R.table_s

    def lay_out(first_block, end_block):
        first, end = first_block // 16, up(end_block, 16) // 16

        def one(t):
            source = table_s[t // BLK, lax.rem(t, BLK)]
            plain = p_ref[jnp.minimum(source, devices * tiles - 1)]
            shared = q_ref[jnp.maximum(source - devices * tiles, 0)]
            tile = jnp.where(source < devices * tiles, plain, shared)
            flat_ref[tile_rows(t), :] = tile.astype(f32)

        def eight(i, _):
            for k in range(8):
                one(first + i * 8 + k)
            return 0

        lax.fori_loop(0, (end - first) // 8, eight, 0)
        for t in range(first + (end - first) // 8 * 8, end):
            one(t)

    def matrix(out_ref, at, height, blocks):
        lay_out(at, at + height * blocks)
        for j in range(blocks):
            for o in range(0, height, 256):
                out_ref[o : o + 256, j * BLK : (j + 1) * BLK] = flat_ref[
                    pl.ds(at + o * blocks + j, 256, stride=blocks), :
                ].astype(bf16)

    group = lane_group()
    square_ref = R.square
    lat_w, s1_w, s2_w, s3_w = R.lat_w, R.s1_w, R.s2_w, R.s3_w
    f1_w, f2_w, f3_w, vec_ref = R.f1_w, R.f2_w, R.f3_w, R.vec

    def spread_rows(at, height):
        for r in range(GROUPS):
            part = jnp.where(group == r, flat_ref[at : at + height // GROUPS, :], 0.0)
            square_ref[pl.ds(r, height // GROUPS, stride=GROUPS), :] = fold_lanes(part)
        return square_ref[:height, :]

    def fast_weights():
        lay_out(AT_F1, AT_LAT)
        for k in range(3):
            tap = flat_ref[pl.ds(AT_F1 + k, B_FAST, stride=3), :].astype(bf16)
            for g in range(GROUPS):
                f1_w[g * B_FAST : (g + 1) * B_FAST, k * BLK : (k + 1) * BLK] = tap
        two = spread_rows(AT_F2, B_FAST)
        for g in range(GROUPS):
            f2_w[g * B_FAST : (g + 1) * B_FAST, :] = jnp.where(group == g, two, 0.0).astype(bf16)
        f3_w[...] = spread_rows(AT_F3, C_FAST).astype(bf16)

    matrix(lat_w, AT_LAT, C_LAT, 5)
    lay_out(AT_VEC, NBLK)
    vec_ref[...] = flat_ref[AT_VEC : AT_VEC + 32, :]
    x_gather.finish()

    zb, latb, s2b, dz, da1, wide_ref = (R.zb, R.latb, R.s2b, R.dz, R.da1, R.wide)
    c1, c2, c3, e, e3, da3 = (R.c1, R.c2, R.c3, R.e, R.e3, R.da3)
    a1p, a2p, h1p, h2p, d1p, d2p, ep, a3, e3f, da3f = (R.a1p, R.a2p, R.h1p, R.h2p, R.d1p, R.d2p, R.ep, R.a3, R.e3f, R.da3f)
    mask_ref, st_ref, st16_ref = R.mask, R.st, R.st16
    s1b = two_in.at[pl.ds(HALF, slow_rows)]
    da2 = two_back.at[pl.ds(HALF, slow_rows)]

    def stat(which):
        return (st_ref, which) if which < 12 else (st16_ref, which - 12)

    def exchange(which):
        ref, at = stat(which)
        own = ref.at[at, member]
        for device in group_peers:
            remote(own, own, R.ex_send, R.ex_recv.at[which], device)

    def exchanged(which):
        ref, at = stat(which)
        arrived(ref.at[at, pl.ds(0, members - 1)], R.ex_recv.at[which])
        total = ref[at, 0]
        for i in range(1, members):
            total = total + ref[at, i]
        return total

    def put(which, at, vector):
        ref, index = stat(which)
        for j in range(vector.shape[1] // BLK):
            ref[index, member, at + j : at + j + 1, :] = vector[:, j * BLK : (j + 1) * BLK]

    def fill(which, at, value):
        ref, index = stat(which)
        ref[index, member, at:8, :] = jnp.full((8 - at, BLK), value, f32)

    def row_of(block, at, n):
        return jnp.concatenate([block[at + j : at + j + 1, :] for j in range(n)], 1)

    def vectors(place):
        g, b, n = place
        return row_of(vec_ref[...], g, n), row_of(vec_ref[...], b, n)

    def rows_at(i, size):
        return pl.ds(pl.multiple_of(i * size, size), size)

    def mask_at(i, width):
        part = mask_ref[pl.ds(pl.multiple_of(lax.rem(i * RC, HALF), RC), RC), :]
        return jnp.concatenate([part] * (width // BLK), 1) if width > BLK else part

    def eights(v):
        return jnp.sum(v.reshape(v.shape[0] // 8, 8, v.shape[1]), 0)

    def total_row(v):
        return jnp.sum(v, 0, keepdims=True)

    def affine(sums, squares, count, gain, bias):
        mean = sums / count
        scale = lax.rsqrt(squares / count - mean * mean + norm_eps)
        grow = gain * scale
        return mean, scale, grow, bias - mean * grow

    def loop(n, body, start):
        return lax.fori_loop(0, n, body, start, unroll=n if n <= 8 else 4)

    def sums_of(ref, n_rows, width):
        def body(i, acc):
            v = ref[rows_at(i, RC), :].astype(f32)
            return acc[0] + eights(v), acc[1] + eights(v * v)

        zero = jnp.zeros((8, width), f32)
        one, two = loop(n_rows // RC, body, (zero, zero))
        return total_row(one), total_row(two)

    def activate(src, dst, n_rows, width, grow, base):
        def body(i, _):
            at = rows_at(i, RC)
            pre = src[at, :].astype(f32) * grow + base
            dst[at, :] = (gelu(pre) * mask_at(i, width)).astype(bf16)
            return 0

        loop(n_rows // RC, body, 0)

    def slopes(src, incoming, n_rows, width, norm):
        mean, scale, grow, base = norm

        def body(i, acc):
            at = rows_at(i, RC)
            a = src[at, :].astype(f32)
            d = gelu_slope(a * grow + base) * incoming[at, :] * mask_at(i, width)
            incoming[at, :] = d
            return acc[0] + eights(d), acc[1] + eights(d * ((a - mean) * scale))

        zero = jnp.zeros((8, width), f32)
        one, two = loop(n_rows // RC, body, (zero, zero))
        return total_row(one), total_row(two)

    def back_vectors(bias_sum, gain_sum, count, norm):
        mean, scale, grow, base = norm
        k1 = grow * gain_sum / count
        return grow * bias_sum / count - k1 * (mean * scale), k1 * scale

    def raw_grads(src, pres, dst, n_rows, width, norm, q0, q1):
        grow = norm[2]

        def body(i, _):
            at = rows_at(i, RC)
            a = src[at, :].astype(f32)
            da = grow * pres[at, :] - mask_at(i, width) * (q0 + a * q1)
            dst[at, :] = da.astype(bf16)
            return 0

        loop(n_rows // RC, body, 0)

    def put_vector(row, vector):
        for j in range(vector.shape[1] // BLK):
            at = AT_VEC + row + j
            flat_ref[at : at + 1, :] = vector[:, j * BLK : (j + 1) * BLK]

    def put_pair(which, one, two, place=None):
        put(which, 0, one)
        put(which, one.shape[1] // BLK, two)
        if place is not None:
            put_vector(place[0], two)
            put_vector(place[1], one)

    slow_chunks = [slice(i, i + CH) for i in range(0, slow_rows, CH)]
    group_chunks = [slice(i, i + CH) for i in range(0, group_rows, CH)]

    def all_slabs(ref, at):
        return jnp.concatenate([ref[j, at, :] for j in range(SLABS)], 1)

    boxes = (
        (R.fast_out_box, results[0]),
        (R.slow_out_box, results[1]),
        (R.fast_grad_box, results[2]),
        (R.slow_grad_box, results[3]),
    )

    def box(which, kind):
        return boxes[which][0].at[kind]

    def hand_over(which):
        box_sems = R.box_send, R.box_recv.at[which]
        remote(box(which, SENT), box(which, GOT), *box_sems, (p.dp, partner))

    def to_channels(block):
        turned = block.T
        if slabs:
            return turned
        lane_shift = lax.rem(p.mp * share, BLK)
        return sum(
            jnp.where(lane_shift == k * share, turned[k * share : (k + 1) * share, :], 0.0)
            for k in range(BLK // share)
        )

    def complete(which):
        ref, end = boxes[which]
        arrived(box(which, GOT), R.box_recv.at[which])
        fast = which in (FAST_OUT, FAST_GRAD)
        n = 1 if fast else slow_frames
        for s in range(n):
            at = slice(s * HALF, (s + 1) * HALF)
            for h in range(halves):
                block = jnp.where(p.b == h, ref[MINE, at, :], ref[GOT, at, :])
                block = block.T if fast else to_channels(block)
                end[pl.ds(s * halves + h, block.shape[0], stride=n * halves), :] = block

    for s in range(slow_frames):
        for k in range(5):
            wide_ref[s * HALF : (s + 1) * HALF, k * BLK : (k + 1) * BLK] = xt_ref[4 * s + k]
    for at in slow_chunks:
        zb[at, :] = dot_nt(wide_ref[at, :], lat_w[...]).astype(bf16)
    put_pair(EX_LAT, *sums_of(zb, slow_rows, C_LAT))
    fill(EX_LAT, 4, area)
    exchange(EX_LAT)

    fast_weights()

    def fast_rows_of(ref, first_frame, at):
        f = first_frame + at.start // HALF
        return jnp.concatenate([ref[f + i] for i in range(CH // HALF)], 0)

    for at in group_chunks:
        total = jnp.zeros((CH, BLK), f32)
        for g in range(GROUPS):
            window = jnp.concatenate(
                [fast_rows_of(xt_ref, g * per_group + 1 + k, at) for k in range(3)], 1
            )
            total = total + jnp.where(group == g, dot_nt(window, f1_w[...]), 0.0)
        a1p[at, :] = total

    def put_folded(which, one, two):
        put(which, 0, fold_lanes(one))
        put(which, 1, fold_lanes(two))

    put_folded(EX_F1, *sums_of(a1p, group_rows, BLK))
    fill(EX_F1, 2, area)
    exchange(EX_F1)

    matrix(s1_w, AT_S1, B_SLOW, 10)
    xs_gather.finish()
    if not slabs:
        from_natural(results[9], xs_ref)

    for at in slow_chunks:
        c1[at, :] = dot_nt(all_slabs(xs_ref, at), s1_w[:, :C_SLOW])

    total = exchanged(EX_LAT)
    area_all = total[4:5, :]
    slow_count = jnp.concatenate([area_all * float(slow_frames)] * 2, 1)
    slow_count8 = jnp.concatenate([slow_count] * 4, 1)
    fast_count = area_all * float(frames)
    lat_norm = affine(row_of(total, 0, 2), row_of(total, 2, 2), slow_count, *vectors(V_LAT))
    activate(zb, latb, slow_rows, C_LAT, lat_norm[2], lat_norm[3])
    for at in slow_chunks:
        c1[at, :] = c1[at, :] + dot_nt(latb[at, :], s1_w[:, C_SLOW:])
    put_pair(EX_S1, *sums_of(c1, slow_rows, B_SLOW))
    fill(EX_S1, 4, 0.0)
    exchange(EX_S1)

    matrix(s2_w, AT_S2, B_SLOW, 6)
    fc_gather.start()
    matrix(s3_w, AT_S3, C_SLOW, 2)

    packed = vec_ref[0:1, :]

    def spread(which):
        return fold_lanes(jnp.where(group == which, packed, 0.0))

    def exchanged_two(which):
        total = exchanged(which)
        return total[0:1, :], total[1:2, :]

    f1_norm = affine(*exchanged_two(EX_F1), fast_count, spread(0), spread(1))
    activate(a1p, h1p, group_rows, BLK, f1_norm[2], f1_norm[3])
    for at in group_chunks:
        a2p[at, :] = dot_nt(h1p[at, :], f2_w[...])
    put_folded(EX_F2, *sums_of(a2p, group_rows, BLK))
    fill(EX_F2, 2, 0.0)
    exchange(EX_F2)

    total = exchanged(EX_S1)
    s1_norm = affine(row_of(total, 0, 2), row_of(total, 2, 2), slow_count, *vectors(V_S1))
    activate(c1, s1b, slow_rows, B_SLOW, s1_norm[2], s1_norm[3])

    def shifted(ref, at, k):
        return ref[at.start + k * HALF : at.stop + k * HALF, :]

    for at in slow_chunks:
        window = jnp.concatenate([shifted(two_in, at, k) for k in range(3)], 1)
        c2[at, :] = dot_nt(window, s2_w[...])
    put_pair(EX_S2, *sums_of(c2, slow_rows, B_SLOW))
    fill(EX_S2, 4, 0.0)
    exchange(EX_S2)

    fc_gather.relay()

    f2_norm = affine(*exchanged_two(EX_F2), fast_count, spread(2), spread(3))
    activate(a2p, h2p, group_rows, BLK, f2_norm[2], f2_norm[3])
    for g in range(GROUPS):
        for at in group_chunks:
            part = jnp.where(group == g, h2p[at, :], 0.0).astype(bf16)
            here = slice(g * group_rows + at.start, g * group_rows + at.stop)
            a3[here, :] = dot_nt(part, f3_w[...])
    put_pair(EX_F3, *sums_of(a3, fast_rows, BLK))
    fill(EX_F3, 2, 0.0)
    exchange(EX_F3)

    total = exchanged(EX_S2)
    s2_norm = affine(row_of(total, 0, 2), row_of(total, 2, 2), slow_count, *vectors(V_S2))
    activate(c2, s2b, slow_rows, B_SLOW, s2_norm[2], s2_norm[3])
    quarter = C_SLOW // 4
    quarters = [slice(n * quarter, (n + 1) * quarter) for n in range(4)]
    for n, lanes in enumerate(quarters):
        for at in slow_chunks:
            c3[at, lanes] = dot_nt(s2b[at, :], s3_w[lanes, :])
        one, two = sums_of(c3.at[:, lanes], slow_rows, quarter)
        put(EX_S3, 2 * n, one)
        put(EX_S3, 8 + 2 * n, two)
    exchange(EX_S3)

    f3_norm = affine(*exchanged_two(EX_F3), fast_count, *vectors(V_F3))
    for rank, kind in ((partner, SENT), (p.mp, MINE)):
        pre = a3[rows_at(rank, HALF), :] * f3_norm[2] + f3_norm[3]
        pre = pre + xt_ref[rank + 2].astype(f32)
        R.fast_out_box[kind] = gelu(pre) * mask_ref[...]
    hand_over(FAST_OUT)
    sc_gather.finish()
    if not slabs:
        from_natural(results[10], sc_ref)
    total = exchanged(EX_S3)
    s3_norm = affine(row_of(total, 0, 8), row_of(total, 8, 8), slow_count8, *vectors(V_S3))

    def pair_of(ref, n, at):
        return jnp.concatenate([ref[2 * n, at, :], ref[2 * n + 1, at, :]], 1).astype(f32)

    for n, lanes in enumerate(quarters):
        norm = [v[:, lanes] for v in s3_norm]

        def slow_slopes(i, acc, n=n, lanes=lanes, norm=norm):
            at = rows_at(i, RC)
            a = c3[at, lanes]
            pre = a * norm[2] + norm[3] + pair_of(xs_ref, n, at)
            d = gelu_slope(pre) * pair_of(sc_ref, n, at)
            e3[at, lanes] = d
            return acc[0] + eights(d), acc[1] + eights(d * ((a - norm[0]) * norm[1]))

        zero = jnp.zeros((8, quarter), f32)
        one, two = loop(slow_rows // RC, slow_slopes, (zero, zero))
        one, two = total_row(one), total_row(two)
        put(EX_BS3, 2 * n, one)
        put(EX_BS3, 8 + 2 * n, two)
        put_vector(V_S3[0] + 2 * n, two)
        put_vector(V_S3[1] + 2 * n, one)
    exchange(EX_BS3)

    fc_gather.finish()

    def fast_slopes(i, acc):
        mean, scale, grow, base = f3_norm
        at = rows_at(i, RC)
        f, here = i // (HALF // RC), rows_at(lax.rem(i, HALF // RC), RC)
        a = a3[at, :]
        x = xt_ref[f + 2, here, :].astype(f32)
        d = gelu_slope(a * grow + base + x) * fc_ref[f, here, :].astype(f32)
        e3f[at, :] = d
        return acc[0] + eights(d), acc[1] + eights(d * ((a - mean) * scale))

    zero = jnp.zeros((8, BLK), f32)
    one, two = loop(fast_rows // RC, fast_slopes, (zero, zero))
    put_pair(EX_BF3, total_row(one), total_row(two), V_F3)
    fill(EX_BF3, 2, 0.0)
    exchange(EX_BF3)

    def slow_place(rank):
        slab = rank * share // BLK
        return slab, pl.ds(pl.multiple_of(slab * BLK, BLK), BLK)

    def slow_result(kind, rank):
        slab, lanes = slow_place(rank)
        grow, base = (
            sum(jnp.where(slab == k, v[:, k * BLK : (k + 1) * BLK], 0.0) for k in range(SLABS))
            for v in s3_norm[2:]
        )
        for s in range(slow_frames):
            at = slice(s * HALF, (s + 1) * HALF)
            pre = c3[at, lanes] * grow + base + xs_ref[slab, at, :].astype(f32)
            R.slow_out_box[kind, at, :] = gelu(pre) * mask_ref[...]

    def slow_input_grad(kind, rank):
        slab, lanes = slow_place(rank)
        for s in range(slow_frames):
            at = slice(s * HALF, (s + 1) * HALF)
            value = e3[at, lanes] + dot_nn(da1[at, :], s1_w[:, lanes])
            R.slow_grad_box[kind, at, :] = value * mask_ref[...]

    slow_result(SENT, partner)
    hand_over(SLOW_OUT)

    total = exchanged(EX_BS3)
    q0, q1 = back_vectors(row_of(total, 0, 8), row_of(total, 8, 8), slow_count8, s3_norm)
    for lanes in quarters:
        norm = [v[:, lanes] for v in s3_norm]
        raw_grads(
            c3.at[:, lanes], e3.at[:, lanes], da3.at[:, lanes], slow_rows, quarter, norm,
            q0[:, lanes], q1[:, lanes]
        )
    for at in slow_chunks:
        e[at, :] = dot_nn(da3[at, :], s3_w[...])
    put_pair(EX_B2, *slopes(c2, e, slow_rows, B_SLOW, s2_norm), V_S2)
    fill(EX_B2, 4, 0.0)
    exchange(EX_B2)

    q0, q1 = back_vectors(*exchanged_two(EX_BF3), fast_count, f3_norm)
    raw_grads(a3, e3f, da3f, fast_rows, BLK, f3_norm, q0, q1)
    for at in group_chunks:
        total = jnp.zeros((CH, BLK), f32)
        for g in range(GROUPS):
            here = slice(g * group_rows + at.start, g * group_rows + at.stop)
            total = total + jnp.where(group == g, dot_nn(da3f[here, :], f3_w[...]), 0.0)
        ep[at, :] = total
    one, two = slopes(a2p, ep, group_rows, BLK, f2_norm)
    put_folded(EX_BF2, one, two)
    fill(EX_BF2, 2, 0.0)
    exchange(EX_BF2)
    vec_two = jnp.where(group == 2, fold_lanes(two), 0.0)
    vec_two = vec_two + jnp.where(group == 3, fold_lanes(one), 0.0)

    def to_flat(at, blocks, offset, lane, value):
        for j in range(value.shape[1] // BLK):
            here = pl.ds(at + offset * blocks + lane + j, value.shape[0], stride=blocks)
            flat_ref[here, :] = value[:, j * BLK : (j + 1) * BLK]

    for n, lanes in enumerate(quarters):
        to_flat(AT_S3, 2, n * quarter, 0, dot_tn(da3[:, lanes], s2b[...]))

    total = exchanged(EX_B2)
    q0, q1 = back_vectors(row_of(total, 0, 2), row_of(total, 2, 2), slow_count, s2_norm)
    raw_grads(c2, e, da2, slow_rows, B_SLOW, s2_norm, q0, q1)
    for at in slow_chunks:
        e[at, :] = functools.reduce(
            lambda u, v: u + v,
            [
                dot_nn(shifted(two_back, at, 2 - k), s2_w[:, k * B_SLOW : (k + 1) * B_SLOW])
                for k in range(3)
            ],
        )
    put_pair(EX_B1, *slopes(c1, e, slow_rows, B_SLOW, s1_norm), V_S1)
    fill(EX_B1, 4, 0.0)
    exchange(EX_B1)

    q0, q1 = back_vectors(*exchanged_two(EX_BF2), fast_count, f2_norm)
    raw_grads(a2p, ep, d2p, group_rows, BLK, f2_norm, q0, q1)
    for at in group_chunks:
        ep[at, :] = dot_nn(d2p[at, :], f2_w[...])
    one, two = slopes(a1p, ep, group_rows, BLK, f1_norm)
    put_folded(EX_BF1, one, two)
    fill(EX_BF1, 2, 0.0)
    exchange(EX_BF1)
    vec_one = jnp.where(group == 0, fold_lanes(two), 0.0)
    vec_one = vec_one + jnp.where(group == 1, fold_lanes(one), 0.0)
    put_vector(0, vec_one + vec_two)

    everything = slice(0, slow_rows)
    for k in range(3):
        part = dot_tn(two_back[HALF : HALF + slow_rows, :], shifted(two_in, everything, k))
        to_flat(AT_S2, 6, 0, 2 * k, part)

    total = jnp.zeros((BLK, BLK), f32)
    for g in range(GROUPS):
        at = slice(g * group_rows, (g + 1) * group_rows)
        total = total + jnp.where(group == g, dot_tn(da3f[at, :], h2p[...]), 0.0)

    def to_blocks(value, at):
        n = value.shape[0] // GROUPS
        square_ref[: value.shape[0], :] = fold_lanes(value)
        flat_ref[at : at + n, :] = sum(
            jnp.where(group == r, square_ref[pl.ds(r, n, stride=GROUPS), :], 0.0)
            for r in range(GROUPS)
        )

    to_blocks(total, AT_F3)
    square = dot_tn(d2p[...], h1p[...])
    to_blocks(
        sum(
            jnp.where(group == g, square[g * B_FAST : (g + 1) * B_FAST, :], 0.0)
            for g in range(GROUPS)
        ),
        AT_F2,
    )

    total = exchanged(EX_B1)
    q0, q1 = back_vectors(row_of(total, 0, 2), row_of(total, 2, 2), slow_count, s1_norm)
    raw_grads(c1, e, da1, slow_rows, B_SLOW, s1_norm, q0, q1)
    for at in slow_chunks:
        e[at, :] = dot_nn(da1[at, :], s1_w[:, C_SLOW:])
    put_pair(EX_BLAT, *slopes(zb, e, slow_rows, C_LAT, lat_norm), V_LAT)
    fill(EX_BLAT, 4, 0.0)
    exchange(EX_BLAT)

    q0, q1 = back_vectors(*exchanged_two(EX_BF1), fast_count, f1_norm)
    raw_grads(a1p, ep, d1p, group_rows, BLK, f1_norm, q0, q1)
    for k in range(3):
        tap = jnp.zeros((B_FAST, BLK), f32)
        for g in range(GROUPS):
            first = g * per_group + k + 1
            right = jnp.concatenate([xt_ref[first + i] for i in range(per_group)], 0)
            part = dot_tn(d1p[...], right)
            tap = tap + part[g * B_FAST : (g + 1) * B_FAST, :]
        to_flat(AT_F1, 3, 0, k, tap)

    for n in range(4):
        right = jnp.concatenate([xs_ref[2 * n], xs_ref[2 * n + 1]], 1)
        to_flat(AT_S1, 10, 0, 2 * n, dot_tn(da1[...], right))
    to_flat(AT_S1, 10, 0, 8, dot_tn(da1[...], latb[...]))

    def frame_grad(rank):
        grad = e3f[rows_at(rank, HALF), :]
        for k in range(3):
            f = rank - k + 1
            there = (f >= 0) & (f < frames)
            g, j = f // per_group, lax.rem(f, per_group)
            g, j = jnp.where(there, g, 0), jnp.where(there, j, 0)
            left = jnp.where((group == g) & there, d1p[rows_at(j, HALF), :], 0.0).astype(bf16)
            grad = grad + dot_nn(left, f1_w[:, k * BLK : (k + 1) * BLK])
        return grad

    def lateral_grad(rank):
        later, s = lax.rem(rank + 2, 4), (rank + 2) // 4
        grad = jnp.zeros((HALF, BLK), f32)
        for tap, at, there in (
            (later, s, s < slow_frames),
            (later + 4, s - 1, (later == 0) & (s > 0)),
        ):
            tap, at = jnp.where(there, tap, 0), jnp.where(there, at, 0)
            left = jnp.where(there, dz[rows_at(at, HALF), :], 0.0).astype(bf16)
            weight = lat_w[:, pl.ds(pl.multiple_of(tap * BLK, BLK), BLK)]
            grad = grad + dot_nn(left, weight)
        return grad

    slow_input_grad(SENT, partner)
    hand_over(SLOW_GRAD)

    total = exchanged(EX_BLAT)
    q0, q1 = back_vectors(row_of(total, 0, 2), row_of(total, 2, 2), slow_count, lat_norm)
    raw_grads(zb, e, dz, slow_rows, C_LAT, lat_norm, q0, q1)
    to_flat(AT_LAT, 5, 0, 0, dot_tn(dz[...], wide_ref[...]))

    height = up(slots, 16)
    sib_out, sib_in, far_out, far_in = (R.sib_out, R.sib_in, R.far_out, R.far_in)
    sib_send, far_send, far_recv = (R.sum_sems.at[i] for i in range(3))
    sib_recv = R.sib_recv

    def window_of(c, o):
        return flat_ref[pl.ds(R.win_start[c * len(targets) + o], height), :]

    order = [*range(1, len(targets)), 0]
    for o in order:
        sib_out[o] = window_of(1, o).astype(bf16)
        sibling = p.dev(p.x, 1 - p.c, p.a, p.b)
        remote(sib_out.at[o], sib_in.at[o], sib_send, sib_recv.at[o], sibling)

    def fast_input_grad(kind, rank):
        R.fast_grad_box[kind] = (frame_grad(rank) + lateral_grad(rank)) * mask_ref[...]

    fast_input_grad(SENT, partner)
    hand_over(FAST_GRAD)
    for o in order:
        arrived(sib_in.at[o], sib_recv.at[o])
        both = window_of(0, o) + sib_in[o].astype(f32)
        if o:
            far_out[o] = both.astype(bf16)
            x, b = p.off_x(targets[o][0]), p.off_b(targets[o][1])
            remote(far_out.at[o], far_in.at[o], far_send, far_recv, p.dev(x, p.c, p.a, b))
        else:
            total = both
    complete(FAST_OUT)
    slow_result(MINE, p.mp)
    complete(SLOW_OUT)
    slow_input_grad(MINE, p.mp)
    complete(SLOW_GRAD)
    fast_input_grad(MINE, p.mp)
    complete(FAST_GRAD)
    arrived(far_in.at[pl.ds(1, len(targets) - 1)], far_recv)
    for o in range(1, len(targets)):
        total = total + far_in[o].astype(f32)
    results[4][...] = total

    sent = len(p_sends)
    while sent:
        n = min(sent, devices)
        arrived(p_ref.at[pl.ds(0, n * tiles)], R.p_send)
        sent -= n
    for copy in kept:
        copy.wait()
    for each in (x_gather, xs_gather, fc_gather, sc_gather):
        each.drain()
    arrived(flat_ref.at[pl.ds(0, (members - 1) * (12 * 8 + 2 * 16))], R.ex_send)
    arrived(flat_ref.at[pl.ds(0, 2 * HALF + 2 * slow_rows)], R.box_send)
    arrived(sib_out, sib_send)
    arrived(far_out.at[pl.ds(1, len(targets) - 1)], far_send)


def call_main(cfg, *args):
    smem = pl.BlockSpec(memory_space=pltpu.SMEM)
    hbm = pl.BlockSpec(memory_space=pltpu.HBM)
    vmem = pl.BlockSpec(memory_space=pltpu.VMEM)
    outs = outputs(cfg)
    return pl.pallas_call(
        functools.partial(main_kernel, cfg),
        out_shape=tuple((pltpu.VMEM if i < 9 else jax.ShapeDtypeStruct)(s, t) for i, (s, t) in enumerate(outs)),
        in_specs=[smem] + [hbm] * 8,
        out_specs=(vmem,) * 9 + (hbm,) * (len(outs) - 9),
        scratch_shapes=list(scratch(cfg).values()),
        compiler_params=pltpu.CompilerParams(
            collective_id=0, has_side_effects=True, vmem_limit_bytes=56 << 20
        ),
        name="block",
    )(*args)[:9]


def adam_kernel(cfg, *refs):
    nd, nm, frames, slow_frames, share, slots = cfg
    inputs, results, sems, held = refs[:9], refs[9:17], refs[17], refs[18:]
    run, grad, master, one, two = inputs[:5]
    w_out, one_out, two_out, low_out = held
    stores = [
        pltpu.make_async_copy(source, target, sems.at[i])
        for i, (source, target) in enumerate(zip(held + inputs[5:], results, strict=True))
    ]
    for copy in stores[4:]:
        copy.start()
    start, count = run[0:1, :], run[1:2, :]
    row = lax.broadcasted_iota(jnp.int32, (slots, BLK), 0)
    living = row < count
    block = row + start
    rate = jnp.full((slots, BLK), 0.2, f32)
    for at, width in (
        (AT_VEC, B_SLOW),
        (AT_S3, 3 * B_SLOW),
        (AT_S2, C_SLOW + C_LAT),
        (AT_S1, 5 * C_FAST),
        (AT_LAT, B_FAST),
        (AT_F2, 3 * C_FAST),
    ):
        rate = jnp.where(block < at, 0.5 / math.sqrt(width), rate)
    decay = jnp.where(block < AT_VEC, decay_rate, 0.0)
    g = grad[:slots, :]
    first = beta_first * one[...] + (1.0 - beta_first) * g
    second = beta_second * two[...] + (1.0 - beta_second) * g * g
    lift_one = 1.0 - beta_first**STEP
    lift_two = 1.0 - beta_second**STEP
    update = first / lift_one / (jnp.sqrt(second / lift_two) + adam_eps)
    weight = master[...]
    weight = jnp.where(living, weight - rate * (update + decay * weight), 0.0)
    w_out[...] = weight
    one_out[...] = jnp.where(living, first, 0.0)
    two_out[...] = jnp.where(living, second, 0.0)
    low_out[...] = weight.astype(bf16)
    for copy in stores[:4]:
        copy.start()
    for copy in stores:
        copy.wait()


def call_adam(cfg, run, grad, master, one, two, passed):
    arrays = (run, grad, master, one, two, *passed)
    hbm = pl.BlockSpec(memory_space=pltpu.HBM)
    vmem = pl.BlockSpec(memory_space=pltpu.VMEM)
    new = [jax.ShapeDtypeStruct(master.shape, t) for t in (f32, f32, f32, bf16)]
    results = new + [jax.ShapeDtypeStruct(a.shape, a.dtype) for a in passed]
    return pl.pallas_call(
        functools.partial(adam_kernel, cfg),
        out_shape=tuple(results),
        in_specs=[vmem] * len(arrays),
        out_specs=(hbm,) * len(results),
        scratch_shapes=[
            pltpu.SemaphoreType.DMA((len(results),)),
            *[pltpu.VMEM(a.shape, a.dtype) for a in new],
        ],
        compiler_params=pltpu.CompilerParams(vmem_limit_bytes=16 << 20),
        name="adam",
    )(*arrays)


def solution(mesh):
    nd, nm = mesh.shape["dp"], mesh.shape["mp"]

    def local(fast_in, slow_in, fast_cot, slow_cot, crop, owner, master, one, two):
        share, slow_frames = slow_in.shape[0], slow_in.shape[1]
        cfg = (nd, nm, fast_in.shape[1] * nm, slow_frames, share, master.shape[0])

        def halves(array):
            split = array.reshape(share, slow_frames, POS // BLK, BLK)
            return split.transpose(0, 2, 1, 3).reshape(-1, BLK)

        *passed, grad, run, master, one, two = call_main(
            cfg,
            crop,
            owner,
            master,
            one,
            two,
            fast_in.reshape(C_FAST, POS),
            halves(slow_in),
            fast_cot.reshape(C_FAST, POS),
            halves(slow_cot),
        )
        new = call_adam(cfg, run, grad, master, one, two, passed)
        return (
            new[4].reshape(fast_in.shape),
            new[5].reshape(slow_in.shape),
            new[6].reshape(fast_in.shape),
            new[7].reshape(slow_in.shape),
            *new[:4],
        )

    return jax.shard_map(
        local,
        mesh=mesh,
        in_specs=(
            P(None, "mp", "dp", None),
            P("mp", None, "dp", None),
            P(None, "mp", "dp", None),
            P("mp", None, "dp", None),
            P("dp"),
            P(),
            P(("dp", "mp"), None),
            P(("dp", "mp"), None),
            P(("dp", "mp"), None),
        ),
        out_specs=(
            P(None, "mp", "dp", None),
            P("mp", None, "dp", None),
            P(None, "mp", "dp", None),
            P("mp", None, "dp", None),
            P(("dp", "mp"), None),
            P(("dp", "mp"), None),
            P(("dp", "mp"), None),
            P(("dp", "mp"), None),
        ),
        check_vma=False,
    )
```

```python
import functools
import math
import types

import jax
import jax.numpy as jnp
from jax import lax
from jax.experimental import pallas as pl
from jax.experimental.pallas import tpu as pltpu
from jax.sharding import PartitionSpec as P

C_FAST = 128
B_FAST = 32
C_SLOW = 1024
B_SLOW = 256
C_LAT = 256
TILE = 16
POS = TILE * TILE
BLK = 128
STEP = 10
NBLK = 7591

norm_eps = 1e-05
beta_first = 0.5
beta_second = 0.5
adam_eps = 1e-08
decay_rate = 0.05

MESH = pl.DeviceIdType.MESH
f32 = jnp.float32
bf16 = jnp.bfloat16
RC = 64
CH = 256
GROUPS = BLK // B_FAST
COLUMNS = 2
HALF = POS // COLUMNS
SLABS = C_SLOW // BLK

AT_F1 = 0
AT_F2 = AT_F1 + B_FAST * 3 * C_FAST // BLK
AT_F3 = AT_F2 + B_FAST * B_FAST // BLK
AT_LAT = AT_F3 + C_FAST * B_FAST // BLK
AT_S1 = AT_LAT + C_LAT * 5 * C_FAST // BLK
AT_S2 = AT_S1 + B_SLOW * (C_SLOW + C_LAT) // BLK
AT_S3 = AT_S2 + B_SLOW * 3 * B_SLOW // BLK
AT_VEC = AT_S3 + C_SLOW * B_SLOW // BLK
V_F3 = (1, 2, 1)
V_LAT = (3, 5, 2)
V_S1 = (7, 9, 2)
V_S2 = (11, 13, 2)
V_S3 = (15, 23, 8)


def up(n, m):
    return (n + m - 1) // m * m


def dot_nt(a, b):
    return lax.dot_general(a, b, (((1,), (1,)), ((), ())), preferred_element_type=f32)


def dot_tn(a, b):
    return lax.dot_general(a, b, (((0,), (0,)), ((), ())), preferred_element_type=f32)


def dot_nn(a, b):
    return lax.dot_general(a, b, (((1,), (0,)), ((), ())), preferred_element_type=f32)


G0 = math.sqrt(2.0 / math.pi)
G1 = 0.044715


def gelu(x):
    t = jnp.tanh(x * (G0 + (G0 * G1) * (x * x)))
    return 0.5 * x * (1.0 + t)


def gelu_slope(x):
    xx = x * x
    t = jnp.tanh(x * (G0 + (G0 * G1) * xx))
    return 0.5 * (1.0 + t) + (0.5 * x) * (1.0 - t * t) * (G0 + (3.0 * G0 * G1) * xx)


def position_mask(crop):
    spot = lax.broadcasted_iota(jnp.int32, (POS, BLK), 0)
    inside = (spot // TILE < crop) & (lax.rem(spot, TILE) < crop)
    return jnp.where(inside, 1.0, 0.0).astype(f32)


def lane_group():
    return lax.broadcasted_iota(jnp.int32, (1, BLK), 1) // B_FAST


def fold_lanes(v):
    v = v + pltpu.roll(v, B_FAST, 1)
    return v + pltpu.roll(v, 2 * B_FAST, 1)


def remote(source, target, send_sem, recv_sem, device):
    pltpu.make_async_remote_copy(
        src_ref=source,
        dst_ref=target,
        send_sem=send_sem,
        recv_sem=recv_sem,
        device_id=device,
        device_id_type=MESH,
    ).start()


def arrived(view, sem):
    pltpu.make_async_copy(view, view, sem).wait()


class Place:
    def __init__(self, nd, nm):
        self.nd, self.nm = nd, nm
        self.nx = nd // 2
        self.nb = COLUMNS
        self.na = nm // self.nb
        self.dp = lax.axis_index("dp")
        self.mp = lax.axis_index("mp")
        self.x, self.c = self.dp // 2, lax.rem(self.dp, 2)
        self.a, self.b = self.mp // self.nb, lax.rem(self.mp, self.nb)

    def off_a(self, i):
        return lax.rem(self.a + i, self.na)

    def off_b(self, i):
        return lax.rem(self.b + i, self.nb)

    def off_x(self, i):
        return lax.rem(self.x + i, self.nx)

    def dev(self, x, c, a, b):
        return (x * 2 + c, a * self.nb + b)

    def slot(self, x, c, a, b):
        return (x * 2 + c) * self.nm + a * self.nb + b


class Gather:
    def __init__(self, place, slabs, other, skip, send, near, far):
        self.p, self.slabs, self.other, self.skip = place, slabs, other, skip
        self.sems = send, near, far

    def view(self, rank):
        return self.slabs.at[rank + self.skip]

    def along(self, rank):
        p, (send, near, far) = self.p, self.sems
        for i in range(1, p.na):
            device = (p.dp, p.off_a(i) * p.nb + p.b)
            remote(self.view(rank), self.view(rank), send, far, device)

    def start(self):
        p, (send, near, far) = self.p, self.sems
        remote(self.other, self.view(p.mp), send, near, (p.dp, p.a * p.nb + p.off_b(1)))
        self.along(p.mp)

    def relay(self):
        p, (send, near, far) = self.p, self.sems
        rank = p.a * p.nb + p.off_b(1)
        arrived(self.view(rank), near)
        self.along(rank)

    def pass_on(self, i):
        pass

    def finish(self):
        arrived(self.slabs.at[pl.ds(0, (self.p.na - 1) * self.p.nb)], self.sems[2])

    def drain(self):
        arrived(self.slabs.at[pl.ds(0, self.p.nm - 1)], self.sems[0])


class TreeGather(Gather):
    def __init__(self, place, slabs, other, skip, send, near, mate, *more):
        super().__init__(place, slabs, other, skip, send, near, mate)
        self.cross, self.relayed = more[:2], more[2]
        a = place.a
        self.inner = (a == 1) | (a == 2)
        self.mate = a + 1 - 2 * lax.rem(a, 2)
        self.over_there = 2 - a // 2
        self.other_half = 2 - a // 2 * 2

    def along(self, rank, i=0):
        p, piece = self.p, self.view(rank)
        for a, recv in ((self.mate, self.sems[2]), (self.over_there, self.cross[i])):
            remote(piece, piece, self.sems[0], recv, (p.dp, a * p.nb + p.b))

    def relay(self):
        p = self.p
        rank = p.a * p.nb + p.off_b(1)
        arrived(self.view(rank), self.sems[1])
        self.along(rank, 1)

    def pass_on(self, i):
        p = self.p

        @pl.when(self.inner)
        def _():
            arrived(self.slabs.at[pl.ds(0, 2)], self.cross[i])
            for k in range(2):
                piece = self.view((self.other_half + k) * p.nb + p.off_b(i))
                to = (p.dp, self.mate * p.nb + p.b)
                remote(piece, piece, self.relayed, self.cross[i], to)

    def finish(self):
        arrived(self.slabs.at[pl.ds(0, self.p.nb)], self.sems[2])

        @pl.when(~self.inner)
        def _():
            for cross in self.cross:
                arrived(self.slabs.at[pl.ds(0, 2)], cross)

    def drain(self):
        arrived(self.slabs.at[pl.ds(0, 1 + 2 * self.p.nb)], self.sems[0])

        @pl.when(self.inner)
        def _():
            arrived(self.slabs.at[pl.ds(0, 2 * self.p.nb)], self.relayed)


EX_LAT, EX_S1, EX_S2, EX_B2, EX_B1, EX_BLAT = range(6)
EX_F1, EX_F2, EX_F3, EX_BF3, EX_BF2, EX_BF1 = range(6, 12)
EX_S3, EX_BS3 = 12, 13
EXCHANGES = 14

FAST_OUT, SLOW_OUT, FAST_GRAD, SLOW_GRAD = range(4)
SENT, MINE, GOT = range(3)


def outputs(cfg):
    nd, nm, frames, slow_frames, share, slots = cfg
    halves = POS // BLK
    fast, slow = (C_FAST * halves, BLK), (share * slow_frames * halves, BLK)
    result = [(fast, f32), (slow, f32), (fast, f32), (slow, f32), ((up(slots, 16), BLK), f32)]
    result += [((8, BLK), jnp.int32)] + [((slots, BLK), f32)] * 3
    if share != BLK:
        result += [((nm, share, slow_frames * HALF), bf16)] * 2
    return result


def scratch(cfg):
    nd, nm, frames, slow_frames, share, slots = cfg
    devices, group = nd * nm, nd * COLUMNS
    rows = up(slots + 15, 16)
    height = up(slots, 16)
    halves = POS // BLK
    slow_rows, fast_rows = slow_frames * HALF, frames * HALF
    group_rows = fast_rows // GROUPS
    windows = group // 2
    vmem, smem, dma = pltpu.VMEM, pltpu.SMEM, pltpu.SemaphoreType.DMA
    piece = (slow_rows, BLK) if share == BLK else (share, slow_rows)
    result = dict(
        owner_v=vmem((NBLK,), jnp.int32),
        owner_s=smem((NBLK,), jnp.int32),
        run_device=smem((devices,), jnp.int32),
        run_start=smem((devices,), jnp.int32),
        run_count=smem((devices,), jnp.int32),
        win_start=smem((group,), jnp.int32),
        table_v=vmem((8, BLK), jnp.int32),
        table_s=smem((8, BLK), jnp.int32),
        shift=vmem((rows + 16, BLK), f32),
        p=vmem((devices * (rows // 16), 16, BLK), bf16),
        q=vmem((devices, 16, BLK), bf16),
        fast_v=vmem((C_FAST, POS), bf16),
        slow_v=vmem((share * slow_frames * halves, BLK), bf16),
        fcot_v=vmem((C_FAST, POS), bf16),
        scot_v=vmem((share * slow_frames * halves, BLK), bf16),
        stage=vmem((share * slow_frames * halves, BLK), f32),
        turned=vmem((POS, BLK), f32),
        x_other=vmem((HALF, BLK), bf16),
        fc_other=vmem((HALF, BLK), bf16),
        xs_other=vmem(piece, bf16),
        sc_other=vmem(piece, bf16),
        xt=vmem((frames + 4, HALF, BLK), bf16),
        xs=vmem((SLABS, slow_rows, BLK), bf16),
        fc=vmem((frames, HALF, BLK), bf16),
        sc=vmem((SLABS, slow_rows, BLK), bf16),
        wide=vmem((slow_rows, 5 * C_FAST), bf16),
        lat_w=vmem((C_LAT, 5 * C_FAST), bf16),
        s1_w=vmem((B_SLOW, C_SLOW + C_LAT), bf16),
        s2_w=vmem((B_SLOW, 3 * B_SLOW), bf16),
        s3_w=vmem((C_SLOW, B_SLOW), bf16),
        f1_w=vmem((BLK, 3 * C_FAST), bf16),
        f2_w=vmem((BLK, BLK), bf16),
        f3_w=vmem((BLK, BLK), bf16),
        vec=vmem((32, BLK), f32),
        mask_all=vmem((POS, BLK), f32),
        mask=vmem((HALF, BLK), f32),
    )
    if share != BLK:
        result.update(
            piece=vmem(piece, bf16),
            turn=vmem((BLK, HALF), bf16),
        )
    result.update(
        zb=vmem((slow_rows, 256), bf16),
        latb=vmem((slow_rows, 256), bf16),
        s2b=vmem((slow_rows, 256), bf16),
        dz=vmem((slow_rows, 256), bf16),
        da1=vmem((slow_rows, 256), bf16),
    )
    result.update(
        two_in=vmem(((slow_frames + 2) * HALF, 256), bf16),
        two_back=vmem(((slow_frames + 2) * HALF, 256), bf16),
        c1=vmem((slow_rows, 256), f32),
        c2=vmem((slow_rows, 256), f32),
        c3=vmem((slow_rows, C_SLOW), f32),
        e=vmem((slow_rows, 256), f32),
        e3=vmem((slow_rows, C_SLOW), f32),
        da3=vmem((slow_rows, C_SLOW), bf16),
        a1p=vmem((group_rows, BLK), f32),
        a2p=vmem((group_rows, BLK), f32),
        h1p=vmem((group_rows, BLK), bf16),
        h2p=vmem((group_rows, BLK), bf16),
        d1p=vmem((group_rows, BLK), bf16),
        d2p=vmem((group_rows, BLK), bf16),
        ep=vmem((group_rows, BLK), f32),
        a3=vmem((fast_rows, BLK), f32),
        e3f=vmem((fast_rows, BLK), f32),
        da3f=vmem((fast_rows, BLK), bf16),
        square=vmem((BLK, BLK), f32),
        flat=vmem((up(NBLK + height, 64), BLK), f32),
        sib_out=vmem((windows, height, BLK), bf16),
        sib_in=vmem((windows, height, BLK), bf16),
        far_out=vmem((windows, height, BLK), bf16),
        far_in=vmem((windows, height, BLK), bf16),
        st=vmem((12, group, 8, BLK), f32),
        st16=vmem((2, group, 16, BLK), f32),
    )
    result.update(
        fast_out_box=vmem((3, HALF, BLK), f32),
        slow_out_box=vmem((3, slow_rows, BLK), f32),
        fast_grad_box=vmem((3, HALF, BLK), f32),
        slow_grad_box=vmem((3, slow_rows, BLK), f32),
        p_send=dma(()),
        p_recv=dma((devices // 2,)),
        p_sibling=dma(()),
        gather_sems=dma((15,)),
        ex_send=dma(()),
        ex_recv=dma((EXCHANGES,)),
        box_send=dma(()),
        box_recv=dma((4,)),
        sum_sems=dma((3,)),
        sib_recv=dma((windows,)),
        local=dma((11,)),
    )
    return result


def main_kernel(cfg, *refs):
    nd, nm, frames, slow_frames, share, slots = cfg
    n_out = len(outputs(cfg))
    args, results, held = refs[:9], refs[9 : 9 + n_out], refs[9 + n_out :]
    crop_in, owner_in, master_in, first_in, second_in, fast_in, slow_in, fcot_in, scot_in = args
    R = types.SimpleNamespace(**dict(zip(scratch(cfg), held, strict=True)))
    p = Place(nd, nm)
    devices = nd * nm
    halves = POS // BLK
    rows = up(slots + 15, 16)
    tiles = rows // 16
    slow_rows, fast_rows = slow_frames * HALF, frames * HALF
    per_group = frames // GROUPS
    group_rows = per_group * HALF
    slabs = share == BLK
    me = p.dp * nm + p.mp
    partner = p.a * p.nb + p.off_b(1)

    members = nd * p.nb
    member = p.dp * p.nb + p.b
    group_peers = [
        p.dev(p.off_x(i), lax.rem(p.c + k, 2), p.a, p.off_b(j))
        for i in reversed(range(p.nx))
        for j in reversed(range(p.nb))
        for k in range(2)
        if i or j or k
    ]
    near = [p.dev(p.x, p.c, p.off_a(i), p.b) for i in range(1, p.na)]
    barrier = pltpu.get_barrier_semaphore()
    for device in group_peers + near:
        pl.semaphore_signal(barrier, inc=1, device_id=device, device_id_type=MESH)

    local_copies = []

    def fetch(source, target):
        copy = pltpu.make_async_copy(source, target, R.local.at[len(local_copies)])
        copy.start()
        local_copies.append(copy)
        return copy

    get_owner = fetch(owner_in, R.owner_v)
    get_owner_s = fetch(owner_in, R.owner_s)
    get_master = fetch(master_in, R.shift.at[pl.ds(16, slots)])
    get_fast = fetch(fast_in, R.fast_v)
    get_slow = fetch(slow_in, R.slow_v)
    get_fcot = fetch(fcot_in, R.fcot_v)
    get_scot = fetch(scot_in, R.scot_v)
    kept = [fetch(a, results[6 + i]) for i, a in enumerate((master_in, first_in, second_in))]

    crop = crop_in[0]
    R.mask_all[...] = position_mask(crop)
    R.mask[...] = R.mask_all[pl.ds(pl.multiple_of(p.b * HALF, HALF), HALF), :]
    tall = crop.astype(f32)
    area = tall * tall * (1.0 / COLUMNS)
    xt_ref, xs_ref, fc_ref, sc_ref = R.xt, R.xs, R.fc, R.sc
    for f in (0, 1, frames + 2, frames + 3):
        xt_ref[f] = jnp.zeros((HALF, BLK), bf16)
    two_in, two_back = R.two_in, R.two_back
    for ref in (two_in, two_back):
        ref[:HALF] = jnp.zeros((HALF, 256), bf16)
        ref[(slow_frames + 1) * HALF :] = jnp.zeros((HALF, 256), bf16)

    get_owner.wait()
    spot = lax.broadcasted_iota(jnp.int32, (8, BLK), 0) * BLK
    spot = spot + lax.broadcasted_iota(jnp.int32, (8, BLK), 1)
    lowest = jnp.full((8, BLK), NBLK, jnp.int32)
    number = jnp.zeros((8, BLK), jnp.int32)
    whole = NBLK // 1024 * 1024
    for i in range(0, whole, 1024):
        mine = R.owner_v[pl.ds(i, 1024)].reshape(8, BLK) == me
        lowest = jnp.minimum(lowest, jnp.where(mine, spot + i, NBLK))
        number = number + jnp.where(mine, 1, 0)
    for i in range(whole, NBLK // BLK * BLK, BLK):
        mine = R.owner_v[pl.ds(i, BLK)].reshape(1, BLK) == me
        mine = mine & (spot < BLK)
        lowest = jnp.minimum(lowest, jnp.where(mine, spot + i, NBLK))
        number = number + jnp.where(mine, 1, 0)
    get_owner_s.wait()

    def last_ones(i, found):
        first, n = found
        mine = R.owner_s[i] == me
        return jnp.where(mine, jnp.minimum(first, i), first), n + jnp.where(mine, 1, 0)

    found = jnp.min(lowest), jnp.sum(number)
    my_start, my_count = lax.fori_loop(NBLK // BLK * BLK, NBLK, last_ones, found)
    line = lax.broadcasted_iota(jnp.int32, (8, BLK), 0)
    results[5][...] = jnp.where(line == 0, my_start, my_count)
    shift = lax.rem(my_start, 16)
    get_master.wait()
    moved = R.shift[pl.ds(16 - shift, rows), :]
    row = lax.broadcasted_iota(jnp.int32, (rows, BLK), 0)
    own = (row >= shift) & (row < shift + my_count)
    p_ref = R.p

    def p_slot(slot):
        return p_ref.at[pl.ds(slot * tiles, tiles)]

    p_slot(me)[...] = jnp.where(own, moved, 0.0).astype(bf16).reshape(tiles, 16, BLK)

    pl.semaphore_wait(barrier, len(group_peers) + len(near))
    p_sends = []

    def view(x, c, a, b):
        return p_slot(p.slot(x, c, a, b))

    def came(source):
        x, c, a, b = source
        return R.p_recv.at[x * nm + a * p.nb + b]

    def pass_on(source, along_a=(), along_b=False, along_x=False, along_c=False):
        piece, sem = view(*source), came(source)
        to = []
        for i in along_a:
            to += [p.dev(p.x, p.c, p.off_a(i), p.b)]
        if along_x:
            to += [p.dev(p.off_x(i), p.c, p.a, p.b) for i in range(1, p.nx)]
        if along_b:
            to += [p.dev(p.x, p.c, p.a, p.off_b(1))]
        for device in to:
            remote(piece, piece, R.p_send, sem, device)
            p_sends.append(device)
        if along_c:
            device = p.dev(p.x, 1 - p.c, p.a, p.b)
            remote(piece, piece, R.p_send, R.p_sibling, device)
            p_sends.append(device)

    def take(source):
        arrived(view(*source), came(source))

    here = (p.x, p.c, p.a, p.b)
    pass_on(here, along_a=range(1, p.na), along_b=True, along_x=True, along_c=True)

    turned_ref = R.turned

    def half_of(b):
        return pl.ds(pl.multiple_of(b * HALF, HALF), HALF)

    def own_frame(slot, other, source):
        turned_ref[...] = source[...].astype(f32).T * R.mask_all[...]
        slot[...] = turned_ref[half_of(p.b), :].astype(bf16)
        other[...] = turned_ref[half_of(p.off_b(1)), :].astype(bf16)

    def own_slow(slot, other, source):
        stage = R.stage
        stage[...] = source[...].astype(f32)
        for s in range(slow_frames):
            at = slice(s * HALF, (s + 1) * HALF)
            for h in range(halves):
                part = stage[pl.ds(h * slow_frames + s, share, stride=halves * slow_frames), :]
                if slabs:
                    here = slice(h * BLK, (h + 1) * BLK)
                    turned_ref[here, :] = part.T * R.mask_all[here, :]
                else:
                    turned_ref[h * share : (h + 1) * share, :] = part
            if slabs:
                slot[at, :] = turned_ref[half_of(p.b), :].astype(bf16)
                other[at, :] = turned_ref[half_of(p.off_b(1)), :].astype(bf16)
            else:
                for ref, b in ((R.piece, p.b), (other, p.off_b(1))):
                    mine = pl.ds(pl.multiple_of(b * share, share), share)
                    ref[:, at] = turned_ref[mine, :].astype(bf16)
        if not slabs:
            pltpu.sync_copy(R.piece, slot)

    def from_natural(natural, wide):
        ranks = BLK // share

        def block(i, _):
            s, j = i // SLABS, lax.rem(i, SLABS)
            at_row = pl.ds(pl.multiple_of(s * HALF, HALF), HALF)
            for k in range(ranks):
                pltpu.sync_copy(
                    natural.at[j * ranks + k, :, at_row],
                    R.turn.at[pl.ds(k * share, share)],
                )
            piece = R.turn[...].astype(f32).T * R.mask[...]
            wide[j, at_row, :] = piece.astype(bf16)
            return 0

        lax.fori_loop(0, slow_frames * SLABS, block, 0)

    def gather(kind, which, array, other, skip=0):
        first = which * 3 + 3 if which else 0
        sems = [R.gather_sems.at[first + i] for i in range(3 if kind is Gather else 6)]
        return kind(p, array, other, skip, *sems)

    tree = TreeGather if p.na == 4 else Gather
    x_gather = gather(tree, 0, xt_ref, R.x_other, 2)
    fc_gather = gather(Gather, 1, fc_ref, R.fc_other)
    xs_gather = gather(Gather, 2, xs_ref if slabs else results[9], R.xs_other)
    sc_gather = gather(Gather, 3, sc_ref if slabs else results[10], R.sc_other)
    get_fast.wait()
    own_frame(x_gather.view(p.mp), R.x_other, R.fast_v)
    x_gather.start()
    get_slow.wait()
    own_slow(xs_gather.view(p.mp), R.xs_other, R.slow_v)

    steps = [1 << i for i in reversed(range(max(1, (slots - 1).bit_length())))]
    owner_s, run_device, run_start, run_count = (R.owner_s, R.run_device, R.run_start, R.run_count)

    def run(k, at):
        device = owner_s[jnp.minimum(at, NBLK - 1)]
        n = jnp.int32(1)
        for step in steps:
            more = n + step
            last = at + more - 1
            inside = owner_s[jnp.minimum(last, NBLK - 1)] == device
            n = jnp.where((more <= slots) & (last < NBLK) & inside, more, n)
        run_device[k] = device
        run_start[k] = at
        run_count[k] = n
        return at + n

    lax.fori_loop(0, devices, run, jnp.int32(0))

    targets = [(i, j) for i in range(p.nx) for j in range(p.nb)]
    owners = [p.slot(p.off_x(i), c, p.a, p.off_b(j)) for c in (p.c, 1 - p.c) for i, j in targets]

    def find(k, found):
        return [jnp.where(run_device[k] == d, run_start[k], at) for d, at in zip(owners, found)]

    for i, at in enumerate(lax.fori_loop(0, devices, find, [jnp.int32(0)] * len(owners))):
        R.win_start[i] = at

    for i in range(1, p.na):
        source = (p.x, p.c, p.off_a(p.na - i), p.b)
        take(source)
        pass_on(source, along_b=True, along_x=True, along_c=True)
    x_gather.relay()
    xs_gather.start()

    def tile_of(k):
        return run_device[k] * tiles - run_start[k] // 16

    def table(k, found):
        start, last = run_start[k], run_start[k] + run_count[k] - 1
        final = jnp.minimum(spot * 16 + 15, NBLK - 1)
        holds = (final >= start) & (final <= last)
        tile = jnp.where(spot == start // 16, devices * tiles + k, spot + tile_of(k))
        return jnp.where(holds, tile, found)

    R.table_v[...] = lax.fori_loop(0, devices, table, jnp.zeros((8, BLK), jnp.int32))
    get_table = fetch(R.table_v, R.table_s)
    x_gather.pass_on(0)
    x_gather.pass_on(1)

    across = p.na // 2
    for i in range(p.na):
        source = (p.x, p.c, p.off_a(p.na - i), p.off_b(1))
        take(source)
        pass_on(source, along_x=i < across, along_c=True)
        for j in range(1, p.nx):
            source = (p.off_x(j), p.c, p.off_a(p.na - i), p.b)
            take(source)
            pass_on(source, along_b=i >= across, along_c=True)
    xs_gather.relay()
    get_fcot.wait()
    own_frame(fc_gather.view(p.mp), R.fc_other, R.fcot_v)
    get_scot.wait()
    own_slow(sc_gather.view(p.mp), R.sc_other, R.scot_v)
    sc_gather.start()
    for i in range(p.na):
        for k in range(1, p.nx):
            source = (p.off_x(k), p.c, p.off_a(p.na - i), p.off_b(1))
            take(source)
            pass_on(source, along_c=True)
    arrived(p_ref.at[pl.ds(0, devices // 2 * tiles)], R.p_sibling)
    get_table.wait()
    sc_gather.relay()

    def tile_rows(t):
        return pl.ds(pl.multiple_of(t * 16, 16), 16)

    q_ref = R.q

    def first_tile(k, before):
        tile = p_ref[run_device[k] * tiles].astype(f32)
        shared = lax.rem(run_start[k], 16) != 0
        tile = tile + jnp.where(shared, before, 0.0)
        q_ref[k] = tile.astype(bf16)
        last = (run_start[k] + run_count[k] - 1) // 16
        alone = last == run_start[k] // 16
        return jnp.where(alone, tile, p_ref[tile_of(k) + last].astype(f32))

    lax.fori_loop(0, devices, first_tile, jnp.zeros((16, BLK), f32))
    flat_ref, table_s = R.flat, R.table_s

    def lay_out(first_block, end_block):
        first, end = first_block // 16, up(end_block, 16) // 16

        def one(t):
            source = table_s[t // BLK, lax.rem(t, BLK)]
            plain = p_ref[jnp.minimum(source, devices * tiles - 1)]
            shared = q_ref[jnp.maximum(source - devices * tiles, 0)]
            tile = jnp.where(source < devices * tiles, plain, shared)
            flat_ref[tile_rows(t), :] = tile.astype(f32)

        def eight(i, _):
            for k in range(8):
                one(first + i * 8 + k)
            return 0

        lax.fori_loop(0, (end - first) // 8, eight, 0)
        for t in range(first + (end - first) // 8 * 8, end):
            one(t)

    def matrix(out_ref, at, height, blocks):
        lay_out(at, at + height * blocks)
        for j in range(blocks):
            for o in range(0, height, 256):
                out_ref[o : o + 256, j * BLK : (j + 1) * BLK] = flat_ref[
                    pl.ds(at + o * blocks + j, 256, stride=blocks), :
                ].astype(bf16)

    group = lane_group()
    square_ref = R.square
    lat_w, s1_w, s2_w, s3_w = R.lat_w, R.s1_w, R.s2_w, R.s3_w
    f1_w, f2_w, f3_w, vec_ref = R.f1_w, R.f2_w, R.f3_w, R.vec

    def spread_rows(at, height):
        for r in range(GROUPS):
            part = jnp.where(group == r, flat_ref[at : at + height // GROUPS, :], 0.0)
            square_ref[pl.ds(r, height // GROUPS, stride=GROUPS), :] = fold_lanes(part)
        return square_ref[:height, :]

    def fast_weights():
        lay_out(AT_F1, AT_LAT)
        for k in range(3):
            tap = flat_ref[pl.ds(AT_F1 + k, B_FAST, stride=3), :].astype(bf16)
            for g in range(GROUPS):
                f1_w[g * B_FAST : (g + 1) * B_FAST, k * BLK : (k + 1) * BLK] = tap
        two = spread_rows(AT_F2, B_FAST)
        for g in range(GROUPS):
            f2_w[g * B_FAST : (g + 1) * B_FAST, :] = jnp.where(group == g, two, 0.0).astype(bf16)
        f3_w[...] = spread_rows(AT_F3, C_FAST).astype(bf16)

    matrix(lat_w, AT_LAT, C_LAT, 5)
    lay_out(AT_VEC, NBLK)
    vec_ref[...] = flat_ref[AT_VEC : AT_VEC + 32, :]
    x_gather.finish()

    zb, latb, s2b, dz, da1, wide_ref = (R.zb, R.latb, R.s2b, R.dz, R.da1, R.wide)
    c1, c2, c3, e, e3, da3 = (R.c1, R.c2, R.c3, R.e, R.e3, R.da3)
    a1p, a2p, h1p, h2p, d1p, d2p, ep, a3, e3f, da3f = (R.a1p, R.a2p, R.h1p, R.h2p, R.d1p, R.d2p, R.ep, R.a3, R.e3f, R.da3f)
    mask_ref, st_ref, st16_ref = R.mask, R.st, R.st16
    s1b = two_in.at[pl.ds(HALF, slow_rows)]
    da2 = two_back.at[pl.ds(HALF, slow_rows)]

    def stat(which):
        return (st_ref, which) if which < 12 else (st16_ref, which - 12)

    def exchange(which):
        ref, at = stat(which)
        own = ref.at[at, member]
        for device in group_peers:
            remote(own, own, R.ex_send, R.ex_recv.at[which], device)

    def exchanged(which):
        ref, at = stat(which)
        arrived(ref.at[at, pl.ds(0, members - 1)], R.ex_recv.at[which])
        total = ref[at, 0]
        for i in range(1, members):
            total = total + ref[at, i]
        return total

    def put(which, at, vector):
        ref, index = stat(which)
        for j in range(vector.shape[1] // BLK):
            ref[index, member, at + j : at + j + 1, :] = vector[:, j * BLK : (j + 1) * BLK]

    def fill(which, at, value):
        ref, index = stat(which)
        ref[index, member, at:8, :] = jnp.full((8 - at, BLK), value, f32)

    def row_of(block, at, n):
        return jnp.concatenate([block[at + j : at + j + 1, :] for j in range(n)], 1)

    def vectors(place):
        g, b, n = place
        return row_of(vec_ref[...], g, n), row_of(vec_ref[...], b, n)

    def rows_at(i, size):
        return pl.ds(pl.multiple_of(i * size, size), size)

    def mask_at(i, width):
        part = mask_ref[pl.ds(pl.multiple_of(lax.rem(i * RC, HALF), RC), RC), :]
        return jnp.concatenate([part] * (width // BLK), 1) if width > BLK else part

    def eights(v):
        return jnp.sum(v.reshape(v.shape[0] // 8, 8, v.shape[1]), 0)

    def total_row(v):
        return jnp.sum(v, 0, keepdims=True)

    def affine(sums, squares, count, gain, bias):
        mean = sums / count
        scale = lax.rsqrt(squares / count - mean * mean + norm_eps)
        grow = gain * scale
        return mean, scale, grow, bias - mean * grow

    def loop(n, body, start):
        return lax.fori_loop(0, n, body, start, unroll=n if n <= 8 else 4)

    def sums_of(ref, n_rows, width):
        def body(i, acc):
            v = ref[rows_at(i, RC), :].astype(f32)
            return acc[0] + eights(v), acc[1] + eights(v * v)

        zero = jnp.zeros((8, width), f32)
        one, two = loop(n_rows // RC, body, (zero, zero))
        return total_row(one), total_row(two)

    def activate(src, dst, n_rows, width, grow, base):
        def body(i, _):
            at = rows_at(i, RC)
            pre = src[at, :].astype(f32) * grow + base
            dst[at, :] = (gelu(pre) * mask_at(i, width)).astype(bf16)
            return 0

        loop(n_rows // RC, body, 0)

    def slopes(src, incoming, n_rows, width, norm):
        mean, scale, grow, base = norm

        def body(i, acc):
            at = rows_at(i, RC)
            a = src[at, :].astype(f32)
            d = gelu_slope(a * grow + base) * incoming[at, :] * mask_at(i, width)
            incoming[at, :] = d
            return acc[0] + eights(d), acc[1] + eights(d * ((a - mean) * scale))

        zero = jnp.zeros((8, width), f32)
        one, two = loop(n_rows // RC, body, (zero, zero))
        return total_row(one), total_row(two)

    def back_vectors(bias_sum, gain_sum, count, norm):
        mean, scale, grow, base = norm
        k1 = grow * gain_sum / count
        return grow * bias_sum / count - k1 * (mean * scale), k1 * scale

    def raw_grads(src, pres, dst, n_rows, width, norm, q0, q1):
        grow = norm[2]

        def body(i, _):
            at = rows_at(i, RC)
            a = src[at, :].astype(f32)
            da = grow * pres[at, :] - mask_at(i, width) * (q0 + a * q1)
            dst[at, :] = da.astype(bf16)
            return 0

        loop(n_rows // RC, body, 0)

    def put_vector(row, vector):
        for j in range(vector.shape[1] // BLK):
            at = AT_VEC + row + j
            flat_ref[at : at + 1, :] = vector[:, j * BLK : (j + 1) * BLK]

    def put_pair(which, one, two, place=None):
        put(which, 0, one)
        put(which, one.shape[1] // BLK, two)
        if place is not None:
            put_vector(place[0], two)
            put_vector(place[1], one)

    slow_chunks = [slice(i, i + CH) for i in range(0, slow_rows, CH)]
    group_chunks = [slice(i, i + CH) for i in range(0, group_rows, CH)]

    def all_slabs(ref, at):
        return jnp.concatenate([ref[j, at, :] for j in range(SLABS)], 1)

    boxes = (
        (R.fast_out_box, results[0]),
        (R.slow_out_box, results[1]),
        (R.fast_grad_box, results[2]),
        (R.slow_grad_box, results[3]),
    )

    def box(which, kind):
        return boxes[which][0].at[kind]

    def hand_over(which):
        box_sems = R.box_send, R.box_recv.at[which]
        remote(box(which, SENT), box(which, GOT), *box_sems, (p.dp, partner))

    def to_channels(block):
        turned = block.T
        if slabs:
            return turned
        lane_shift = lax.rem(p.mp * share, BLK)
        return sum(
            jnp.where(lane_shift == k * share, turned[k * share : (k + 1) * share, :], 0.0)
            for k in range(BLK // share)
        )

    def complete(which):
        ref, end = boxes[which]
        arrived(box(which, GOT), R.box_recv.at[which])
        fast = which in (FAST_OUT, FAST_GRAD)
        n = 1 if fast else slow_frames
        for s in range(n):
            at = slice(s * HALF, (s + 1) * HALF)
            for h in range(halves):
                block = jnp.where(p.b == h, ref[MINE, at, :], ref[GOT, at, :])
                block = block.T if fast else to_channels(block)
                end[pl.ds(s * halves + h, block.shape[0], stride=n * halves), :] = block

    for s in range(slow_frames):
        for k in range(5):
            wide_ref[s * HALF : (s + 1) * HALF, k * BLK : (k + 1) * BLK] = xt_ref[4 * s + k]
    for at in slow_chunks:
        zb[at, :] = dot_nt(wide_ref[at, :], lat_w[...]).astype(bf16)
    put_pair(EX_LAT, *sums_of(zb, slow_rows, C_LAT))
    fill(EX_LAT, 4, area)
    exchange(EX_LAT)

    fast_weights()

    def fast_rows_of(ref, first_frame, at):
        f = first_frame + at.start // HALF
        return jnp.concatenate([ref[f + i] for i in range(CH // HALF)], 0)

    for at in group_chunks:
        total = jnp.zeros((CH, BLK), f32)
        for g in range(GROUPS):
            window = jnp.concatenate(
                [fast_rows_of(xt_ref, g * per_group + 1 + k, at) for k in range(3)], 1
            )
            total = total + jnp.where(group == g, dot_nt(window, f1_w[...]), 0.0)
        a1p[at, :] = total

    def put_folded(which, one, two):
        put(which, 0, fold_lanes(one))
        put(which, 1, fold_lanes(two))

    put_folded(EX_F1, *sums_of(a1p, group_rows, BLK))
    fill(EX_F1, 2, area)
    exchange(EX_F1)

    matrix(s1_w, AT_S1, B_SLOW, 10)
    xs_gather.finish()
    if not slabs:
        from_natural(results[9], xs_ref)

    for at in slow_chunks:
        c1[at, :] = dot_nt(all_slabs(xs_ref, at), s1_w[:, :C_SLOW])

    total = exchanged(EX_LAT)
    area_all = total[4:5, :]
    slow_count = jnp.concatenate([area_all * float(slow_frames)] * 2, 1)
    slow_count8 = jnp.concatenate([slow_count] * 4, 1)
    fast_count = area_all * float(frames)
    lat_norm = affine(row_of(total, 0, 2), row_of(total, 2, 2), slow_count, *vectors(V_LAT))
    activate(zb, latb, slow_rows, C_LAT, lat_norm[2], lat_norm[3])
    for at in slow_chunks:
        c1[at, :] = c1[at, :] + dot_nt(latb[at, :], s1_w[:, C_SLOW:])
    put_pair(EX_S1, *sums_of(c1, slow_rows, B_SLOW))
    fill(EX_S1, 4, 0.0)
    exchange(EX_S1)

    matrix(s2_w, AT_S2, B_SLOW, 6)
    fc_gather.start()
    matrix(s3_w, AT_S3, C_SLOW, 2)

    packed = vec_ref[0:1, :]

    def spread(which):
        return fold_lanes(jnp.where(group == which, packed, 0.0))

    def exchanged_two(which):
        total = exchanged(which)
        return total[0:1, :], total[1:2, :]

    f1_norm = affine(*exchanged_two(EX_F1), fast_count, spread(0), spread(1))
    activate(a1p, h1p, group_rows, BLK, f1_norm[2], f1_norm[3])
    for at in group_chunks:
        a2p[at, :] = dot_nt(h1p[at, :], f2_w[...])
    put_folded(EX_F2, *sums_of(a2p, group_rows, BLK))
    fill(EX_F2, 2, 0.0)
    exchange(EX_F2)

    total = exchanged(EX_S1)
    s1_norm = affine(row_of(total, 0, 2), row_of(total, 2, 2), slow_count, *vectors(V_S1))
    activate(c1, s1b, slow_rows, B_SLOW, s1_norm[2], s1_norm[3])

    def shifted(ref, at, k):
        return ref[at.start + k * HALF : at.stop + k * HALF, :]

    for at in slow_chunks:
        window = jnp.concatenate([shifted(two_in, at, k) for k in range(3)], 1)
        c2[at, :] = dot_nt(window, s2_w[...])
    put_pair(EX_S2, *sums_of(c2, slow_rows, B_SLOW))
    fill(EX_S2, 4, 0.0)
    exchange(EX_S2)

    fc_gather.relay()

    f2_norm = affine(*exchanged_two(EX_F2), fast_count, spread(2), spread(3))
    activate(a2p, h2p, group_rows, BLK, f2_norm[2], f2_norm[3])
    for g in range(GROUPS):
        for at in group_chunks:
            part = jnp.where(group == g, h2p[at, :], 0.0).astype(bf16)
            here = slice(g * group_rows + at.start, g * group_rows + at.stop)
            a3[here, :] = dot_nt(part, f3_w[...])
    put_pair(EX_F3, *sums_of(a3, fast_rows, BLK))
    fill(EX_F3, 2, 0.0)
    exchange(EX_F3)

    total = exchanged(EX_S2)
    s2_norm = affine(row_of(total, 0, 2), row_of(total, 2, 2), slow_count, *vectors(V_S2))
    activate(c2, s2b, slow_rows, B_SLOW, s2_norm[2], s2_norm[3])
    quarter = C_SLOW // 4
    quarters = [slice(n * quarter, (n + 1) * quarter) for n in range(4)]
    for n, lanes in enumerate(quarters):
        for at in slow_chunks:
            c3[at, lanes] = dot_nt(s2b[at, :], s3_w[lanes, :])
        one, two = sums_of(c3.at[:, lanes], slow_rows, quarter)
        put(EX_S3, 2 * n, one)
        put(EX_S3, 8 + 2 * n, two)
    exchange(EX_S3)

    f3_norm = affine(*exchanged_two(EX_F3), fast_count, *vectors(V_F3))
    for rank, kind in ((partner, SENT), (p.mp, MINE)):
        pre = a3[rows_at(rank, HALF), :] * f3_norm[2] + f3_norm[3]
        pre = pre + xt_ref[rank + 2].astype(f32)
        R.fast_out_box[kind] = gelu(pre) * mask_ref[...]
    hand_over(FAST_OUT)
    sc_gather.finish()
    if not slabs:
        from_natural(results[10], sc_ref)
    total = exchanged(EX_S3)
    s3_norm = affine(row_of(total, 0, 8), row_of(total, 8, 8), slow_count8, *vectors(V_S3))

    def pair_of(ref, n, at):
        return jnp.concatenate([ref[2 * n, at, :], ref[2 * n + 1, at, :]], 1).astype(f32)

    for n, lanes in enumerate(quarters):
        norm = [v[:, lanes] for v in s3_norm]

        def slow_slopes(i, acc, n=n, lanes=lanes, norm=norm):
            at = rows_at(i, RC)
            a = c3[at, lanes]
            pre = a * norm[2] + norm[3] + pair_of(xs_ref, n, at)
            d = gelu_slope(pre) * pair_of(sc_ref, n, at)
            e3[at, lanes] = d
            return acc[0] + eights(d), acc[1] + eights(d * ((a - norm[0]) * norm[1]))

        zero = jnp.zeros((8, quarter), f32)
        one, two = loop(slow_rows // RC, slow_slopes, (zero, zero))
        one, two = total_row(one), total_row(two)
        put(EX_BS3, 2 * n, one)
        put(EX_BS3, 8 + 2 * n, two)
        put_vector(V_S3[0] + 2 * n, two)
        put_vector(V_S3[1] + 2 * n, one)
    exchange(EX_BS3)

    fc_gather.finish()

    def fast_slopes(i, acc):
        mean, scale, grow, base = f3_norm
        at = rows_at(i, RC)
        f, here = i // (HALF // RC), rows_at(lax.rem(i, HALF // RC), RC)
        a = a3[at, :]
        x = xt_ref[f + 2, here, :].astype(f32)
        d = gelu_slope(a * grow + base + x) * fc_ref[f, here, :].astype(f32)
        e3f[at, :] = d
        return acc[0] + eights(d), acc[1] + eights(d * ((a - mean) * scale))

    zero = jnp.zeros((8, BLK), f32)
    one, two = loop(fast_rows // RC, fast_slopes, (zero, zero))
    put_pair(EX_BF3, total_row(one), total_row(two), V_F3)
    fill(EX_BF3, 2, 0.0)
    exchange(EX_BF3)

    def slow_place(rank):
        slab = rank * share // BLK
        return slab, pl.ds(pl.multiple_of(slab * BLK, BLK), BLK)

    def slow_result(kind, rank):
        slab, lanes = slow_place(rank)
        grow, base = (
            sum(jnp.where(slab == k, v[:, k * BLK : (k + 1) * BLK], 0.0) for k in range(SLABS))
            for v in s3_norm[2:]
        )
        for s in range(slow_frames):
            at = slice(s * HALF, (s + 1) * HALF)
            pre = c3[at, lanes] * grow + base + xs_ref[slab, at, :].astype(f32)
            R.slow_out_box[kind, at, :] = gelu(pre) * mask_ref[...]

    def slow_input_grad(kind, rank):
        slab, lanes = slow_place(rank)
        for s in range(slow_frames):
            at = slice(s * HALF, (s + 1) * HALF)
            value = e3[at, lanes] + dot_nn(da1[at, :], s1_w[:, lanes])
            R.slow_grad_box[kind, at, :] = value * mask_ref[...]

    slow_result(SENT, partner)
    hand_over(SLOW_OUT)

    total = exchanged(EX_BS3)
    q0, q1 = back_vectors(row_of(total, 0, 8), row_of(total, 8, 8), slow_count8, s3_norm)
    for lanes in quarters:
        norm = [v[:, lanes] for v in s3_norm]
        raw_grads(
            c3.at[:, lanes], e3.at[:, lanes], da3.at[:, lanes], slow_rows, quarter, norm,
            q0[:, lanes], q1[:, lanes]
        )
    for at in slow_chunks:
        e[at, :] = dot_nn(da3[at, :], s3_w[...])
    put_pair(EX_B2, *slopes(c2, e, slow_rows, B_SLOW, s2_norm), V_S2)
    fill(EX_B2, 4, 0.0)
    exchange(EX_B2)

    q0, q1 = back_vectors(*exchanged_two(EX_BF3), fast_count, f3_norm)
    raw_grads(a3, e3f, da3f, fast_rows, BLK, f3_norm, q0, q1)
    for at in group_chunks:
        total = jnp.zeros((CH, BLK), f32)
        for g in range(GROUPS):
            here = slice(g * group_rows + at.start, g * group_rows + at.stop)
            total = total + jnp.where(group == g, dot_nn(da3f[here, :], f3_w[...]), 0.0)
        ep[at, :] = total
    one, two = slopes(a2p, ep, group_rows, BLK, f2_norm)
    put_folded(EX_BF2, one, two)
    fill(EX_BF2, 2, 0.0)
    exchange(EX_BF2)
    vec_two = jnp.where(group == 2, fold_lanes(two), 0.0)
    vec_two = vec_two + jnp.where(group == 3, fold_lanes(one), 0.0)

    def to_flat(at, blocks, offset, lane, value):
        for j in range(value.shape[1] // BLK):
            here = pl.ds(at + offset * blocks + lane + j, value.shape[0], stride=blocks)
            flat_ref[here, :] = value[:, j * BLK : (j + 1) * BLK]

    for n, lanes in enumerate(quarters):
        to_flat(AT_S3, 2, n * quarter, 0, dot_tn(da3[:, lanes], s2b[...]))

    total = exchanged(EX_B2)
    q0, q1 = back_vectors(row_of(total, 0, 2), row_of(total, 2, 2), slow_count, s2_norm)
    raw_grads(c2, e, da2, slow_rows, B_SLOW, s2_norm, q0, q1)
    for at in slow_chunks:
        e[at, :] = functools.reduce(
            lambda u, v: u + v,
            [
                dot_nn(shifted(two_back, at, 2 - k), s2_w[:, k * B_SLOW : (k + 1) * B_SLOW])
                for k in range(3)
            ],
        )
    put_pair(EX_B1, *slopes(c1, e, slow_rows, B_SLOW, s1_norm), V_S1)
    fill(EX_B1, 4, 0.0)
    exchange(EX_B1)

    q0, q1 = back_vectors(*exchanged_two(EX_BF2), fast_count, f2_norm)
    raw_grads(a2p, ep, d2p, group_rows, BLK, f2_norm, q0, q1)
    for at in group_chunks:
        ep[at, :] = dot_nn(d2p[at, :], f2_w[...])
    one, two = slopes(a1p, ep, group_rows, BLK, f1_norm)
    put_folded(EX_BF1, one, two)
    fill(EX_BF1, 2, 0.0)
    exchange(EX_BF1)
    vec_one = jnp.where(group == 0, fold_lanes(two), 0.0)
    vec_one = vec_one + jnp.where(group == 1, fold_lanes(one), 0.0)
    put_vector(0, vec_one + vec_two)

    everything = slice(0, slow_rows)
    for k in range(3):
        part = dot_tn(two_back[HALF : HALF + slow_rows, :], shifted(two_in, everything, k))
        to_flat(AT_S2, 6, 0, 2 * k, part)

    total = jnp.zeros((BLK, BLK), f32)
    for g in range(GROUPS):
        at = slice(g * group_rows, (g + 1) * group_rows)
        total = total + jnp.where(group == g, dot_tn(da3f[at, :], h2p[...]), 0.0)

    def to_blocks(value, at):
        n = value.shape[0] // GROUPS
        square_ref[: value.shape[0], :] = fold_lanes(value)
        flat_ref[at : at + n, :] = sum(
            jnp.where(group == r, square_ref[pl.ds(r, n, stride=GROUPS), :], 0.0)
            for r in range(GROUPS)
        )

    to_blocks(total, AT_F3)
    square = dot_tn(d2p[...], h1p[...])
    to_blocks(
        sum(
            jnp.where(group == g, square[g * B_FAST : (g + 1) * B_FAST, :], 0.0)
            for g in range(GROUPS)
        ),
        AT_F2,
    )

    total = exchanged(EX_B1)
    q0, q1 = back_vectors(row_of(total, 0, 2), row_of(total, 2, 2), slow_count, s1_norm)
    raw_grads(c1, e, da1, slow_rows, B_SLOW, s1_norm, q0, q1)
    for at in slow_chunks:
        e[at, :] = dot_nn(da1[at, :], s1_w[:, C_SLOW:])
    put_pair(EX_BLAT, *slopes(zb, e, slow_rows, C_LAT, lat_norm), V_LAT)
    fill(EX_BLAT, 4, 0.0)
    exchange(EX_BLAT)

    q0, q1 = back_vectors(*exchanged_two(EX_BF1), fast_count, f1_norm)
    raw_grads(a1p, ep, d1p, group_rows, BLK, f1_norm, q0, q1)
    for k in range(3):
        tap = jnp.zeros((B_FAST, BLK), f32)
        for g in range(GROUPS):
            first = g * per_group + k + 1
            right = jnp.concatenate([xt_ref[first + i] for i in range(per_group)], 0)
            part = dot_tn(d1p[...], right)
            tap = tap + part[g * B_FAST : (g + 1) * B_FAST, :]
        to_flat(AT_F1, 3, 0, k, tap)

    for n in range(4):
        right = jnp.concatenate([xs_ref[2 * n], xs_ref[2 * n + 1]], 1)
        to_flat(AT_S1, 10, 0, 2 * n, dot_tn(da1[...], right))
    to_flat(AT_S1, 10, 0, 8, dot_tn(da1[...], latb[...]))

    def frame_grad(rank):
        grad = e3f[rows_at(rank, HALF), :]
        for k in range(3):
            f = rank - k + 1
            there = (f >= 0) & (f < frames)
            g, j = f // per_group, lax.rem(f, per_group)
            g, j = jnp.where(there, g, 0), jnp.where(there, j, 0)
            left = jnp.where((group == g) & there, d1p[rows_at(j, HALF), :], 0.0).astype(bf16)
            grad = grad + dot_nn(left, f1_w[:, k * BLK : (k + 1) * BLK])
        return grad

    def lateral_grad(rank):
        later, s = lax.rem(rank + 2, 4), (rank + 2) // 4
        grad = jnp.zeros((HALF, BLK), f32)
        for tap, at, there in (
            (later, s, s < slow_frames),
            (later + 4, s - 1, (later == 0) & (s > 0)),
        ):
            tap, at = jnp.where(there, tap, 0), jnp.where(there, at, 0)
            left = jnp.where(there, dz[rows_at(at, HALF), :], 0.0).astype(bf16)
            weight = lat_w[:, pl.ds(pl.multiple_of(tap * BLK, BLK), BLK)]
            grad = grad + dot_nn(left, weight)
        return grad

    slow_input_grad(SENT, partner)
    hand_over(SLOW_GRAD)

    total = exchanged(EX_BLAT)
    q0, q1 = back_vectors(row_of(total, 0, 2), row_of(total, 2, 2), slow_count, lat_norm)
    raw_grads(zb, e, dz, slow_rows, C_LAT, lat_norm, q0, q1)
    to_flat(AT_LAT, 5, 0, 0, dot_tn(dz[...], wide_ref[...]))

    height = up(slots, 16)
    sib_out, sib_in, far_out, far_in = (R.sib_out, R.sib_in, R.far_out, R.far_in)
    sib_send, far_send, far_recv = (R.sum_sems.at[i] for i in range(3))
    sib_recv = R.sib_recv

    def window_of(c, o):
        return flat_ref[pl.ds(R.win_start[c * len(targets) + o], height), :]

    order = [*reversed(range(len(targets)))]
    for o in order:
        sib_out[o] = window_of(1, o).astype(bf16)
        sibling = p.dev(p.x, 1 - p.c, p.a, p.b)
        remote(sib_out.at[o], sib_in.at[o], sib_send, sib_recv.at[o], sibling)

    def fast_input_grad(kind, rank):
        R.fast_grad_box[kind] = (frame_grad(rank) + lateral_grad(rank)) * mask_ref[...]

    fast_input_grad(SENT, partner)
    hand_over(FAST_GRAD)
    for o in order:
        arrived(sib_in.at[o], sib_recv.at[o])
        both = window_of(0, o) + sib_in[o].astype(f32)
        if o:
            far_out[o] = both.astype(bf16)
            x, b = p.off_x(targets[o][0]), p.off_b(targets[o][1])
            remote(far_out.at[o], far_in.at[o], far_send, far_recv, p.dev(x, p.c, p.a, b))
        else:
            total = both
    complete(FAST_OUT)
    slow_result(MINE, p.mp)
    complete(SLOW_OUT)
    slow_input_grad(MINE, p.mp)
    complete(SLOW_GRAD)
    fast_input_grad(MINE, p.mp)
    complete(FAST_GRAD)
    arrived(far_in.at[pl.ds(1, len(targets) - 1)], far_recv)
    for o in range(1, len(targets)):
        total = total + far_in[o].astype(f32)
    results[4][...] = total

    sent = len(p_sends)
    while sent:
        n = min(sent, devices)
        arrived(p_ref.at[pl.ds(0, n * tiles)], R.p_send)
        sent -= n
    for copy in kept:
        copy.wait()
    for each in (x_gather, xs_gather, fc_gather, sc_gather):
        each.drain()
    arrived(flat_ref.at[pl.ds(0, (members - 1) * (12 * 8 + 2 * 16))], R.ex_send)
    arrived(flat_ref.at[pl.ds(0, 2 * HALF + 2 * slow_rows)], R.box_send)
    arrived(sib_out, sib_send)
    arrived(far_out.at[pl.ds(1, len(targets) - 1)], far_send)


def call_main(cfg, *args):
    smem = pl.BlockSpec(memory_space=pltpu.SMEM)
    hbm = pl.BlockSpec(memory_space=pltpu.HBM)
    vmem = pl.BlockSpec(memory_space=pltpu.VMEM)
    outs = outputs(cfg)
    return pl.pallas_call(
        functools.partial(main_kernel, cfg),
        out_shape=tuple((pltpu.VMEM if i < 9 else jax.ShapeDtypeStruct)(s, t) for i, (s, t) in enumerate(outs)),
        in_specs=[smem] + [hbm] * 8,
        out_specs=(vmem,) * 9 + (hbm,) * (len(outs) - 9),
        scratch_shapes=list(scratch(cfg).values()),
        compiler_params=pltpu.CompilerParams(
            collective_id=0, has_side_effects=True, vmem_limit_bytes=56 << 20
        ),
        name="block",
    )(*args)[:9]


def adam_kernel(cfg, *refs):
    nd, nm, frames, slow_frames, share, slots = cfg
    inputs, results, sems, held = refs[:9], refs[9:17], refs[17], refs[18:]
    run, grad, master, one, two = inputs[:5]
    w_out, one_out, two_out, low_out = held
    stores = [
        pltpu.make_async_copy(source, target, sems.at[i])
        for i, (source, target) in enumerate(zip(held + inputs[5:], results, strict=True))
    ]
    for copy in stores[4:]:
        copy.start()
    start, count = run[0:1, :], run[1:2, :]
    row = lax.broadcasted_iota(jnp.int32, (slots, BLK), 0)
    living = row < count
    block = row + start
    rate = jnp.full((slots, BLK), 0.2, f32)
    for at, width in (
        (AT_VEC, B_SLOW),
        (AT_S3, 3 * B_SLOW),
        (AT_S2, C_SLOW + C_LAT),
        (AT_S1, 5 * C_FAST),
        (AT_LAT, B_FAST),
        (AT_F2, 3 * C_FAST),
    ):
        rate = jnp.where(block < at, 0.5 / math.sqrt(width), rate)
    decay = jnp.where(block < AT_VEC, decay_rate, 0.0)
    g = grad[:slots, :]
    first = beta_first * one[...] + (1.0 - beta_first) * g
    second = beta_second * two[...] + (1.0 - beta_second) * g * g
    lift_one = 1.0 - beta_first**STEP
    lift_two = 1.0 - beta_second**STEP
    update = first / lift_one / (jnp.sqrt(second / lift_two) + adam_eps)
    weight = master[...]
    weight = jnp.where(living, weight - rate * (update + decay * weight), 0.0)
    w_out[...] = weight
    one_out[...] = jnp.where(living, first, 0.0)
    two_out[...] = jnp.where(living, second, 0.0)
    low_out[...] = weight.astype(bf16)
    for copy in stores[:4]:
        copy.start()
    for copy in stores:
        copy.wait()


def call_adam(cfg, run, grad, master, one, two, passed):
    arrays = (run, grad, master, one, two, *passed)
    hbm = pl.BlockSpec(memory_space=pltpu.HBM)
    vmem = pl.BlockSpec(memory_space=pltpu.VMEM)
    new = [jax.ShapeDtypeStruct(master.shape, t) for t in (f32, f32, f32, bf16)]
    results = new + [jax.ShapeDtypeStruct(a.shape, a.dtype) for a in passed]
    return pl.pallas_call(
        functools.partial(adam_kernel, cfg),
        out_shape=tuple(results),
        in_specs=[vmem] * len(arrays),
        out_specs=(hbm,) * len(results),
        scratch_shapes=[
            pltpu.SemaphoreType.DMA((len(results),)),
            *[pltpu.VMEM(a.shape, a.dtype) for a in new],
        ],
        compiler_params=pltpu.CompilerParams(vmem_limit_bytes=16 << 20),
        name="adam",
    )(*arrays)


def solution(mesh):
    nd, nm = mesh.shape["dp"], mesh.shape["mp"]

    def local(fast_in, slow_in, fast_cot, slow_cot, crop, owner, master, one, two):
        share, slow_frames = slow_in.shape[0], slow_in.shape[1]
        cfg = (nd, nm, fast_in.shape[1] * nm, slow_frames, share, master.shape[0])

        def halves(array):
            split = array.reshape(share, slow_frames, POS // BLK, BLK)
            return split.transpose(0, 2, 1, 3).reshape(-1, BLK)

        *passed, grad, run, master, one, two = call_main(
            cfg,
            crop,
            owner,
            master,
            one,
            two,
            fast_in.reshape(C_FAST, POS),
            halves(slow_in),
            fast_cot.reshape(C_FAST, POS),
            halves(slow_cot),
        )
        new = call_adam(cfg, run, grad, master, one, two, passed)
        return (
            new[4].reshape(fast_in.shape),
            new[5].reshape(slow_in.shape),
            new[6].reshape(fast_in.shape),
            new[7].reshape(slow_in.shape),
            *new[:4],
        )

    return jax.shard_map(
        local,
        mesh=mesh,
        in_specs=(
            P(None, "mp", "dp", None),
            P("mp", None, "dp", None),
            P(None, "mp", "dp", None),
            P("mp", None, "dp", None),
            P("dp"),
            P(),
            P(("dp", "mp"), None),
            P(("dp", "mp"), None),
            P(("dp", "mp"), None),
        ),
        out_specs=(
            P(None, "mp", "dp", None),
            P("mp", None, "dp", None),
            P(None, "mp", "dp", None),
            P("mp", None, "dp", None),
            P(("dp", "mp"), None),
            P(("dp", "mp"), None),
            P(("dp", "mp"), None),
            P(("dp", "mp"), None),
        ),
        check_vma=False,
    )
```
